32 devices in a mesh: groups: 2 (over y), expert: 4 (over z), mp: 4 (over x, core).
Axes of the slice: x: 2, y: 2, z: 4, core: 2. Of those that a mesh axis runs over, the one named last changes fastest.
Arguments:
- tokens: bfloat16 [2048, 1024], P(('groups', 'expert')), parts along dimension 0, may hold values from -6 to 6
- encoder_states: bfloat16 [8, 2, 512, 1024], P(('groups', 'expert'), None, None, 'mp'), parts along dimension 0, may hold values from -64 to 64
- source_owner: int32 [8], P(('groups', 'expert')), parts along dimension 0, may hold values from 0 to 3
- query_weight: bfloat16 [1024, 1024], P(None, 'mp'), may hold values from -0.1875 to 0.1875
- output_weight: bfloat16 [1024, 1024], P('mp'), may hold values from -0.1875 to 0.1875
- router_weight: bfloat16 [1024, 4], replicated, may hold values from -0.1875 to 0.1875
- expert_choice: int32 [2048, 2], P(('groups', 'expert')), parts along dimension 0, may hold values from 0 to 3, all different within a row; in each aligned block of 256 rows (0 to 255, 256 to 511, ...) at most 192 rows name the same one
- expand_weight: bfloat16 [4, 1024, 4096], P('expert', None, 'mp'), may hold values from -0.1875 to 0.1875
- shrink_weight: bfloat16 [4, 4096, 1024], P('expert', 'mp'), may hold values from -0.09375 to 0.09375
Outputs:
- layer_out: bfloat16 [2048, 1024], P(('groups', 'expert'), 'mp'), parts along dimension 0
The draws below stay inside these ranges and needn't reach their ends.
There are 2 independent parts, one for each index of `groups`. The reference program is written for one: setup_inputs(seed, part) draws one part's arguments, and reference() takes and returns one part's arrays. A program takes and returns all parts, laid end to end along the dimension named above; an argument that names none is the same for every part. Nothing has to cross between parts.
Inputs may be any that keep to these rules, and one draw needn't show every extreme that they name: `expert_choice`: in each aligned block of 256 rows (the rows of one device) no expert is named more than 192 times, a bound that some block reaches; the two experts of a row differ.
All inputs are finite; a program needn't handle non-finite values.
Results may differ from the reference program's by a relative error of at most 0.0072.
Values may be sent and summed in bfloat16 or wider, within the bound.
No kernel may reach another device: no remote copies, remote signals or barrier semaphores. Data moves between devices by JAX's collectives and lax.ppermute only.
A program may use at most 64 MiB of HBM per device.

```python
import math
import jax
import jax.numpy as jnp
import numpy as np
from jax import lax

D = 1024
HEADS = 8
HEAD_DIM = 128
FF = 4096
SRC_LEN = 512
TOK_DEV = 256
EXPERTS = 4
TOKENS = 1024
CAP = 192
N_EXPERT = 4


def draw_encoder_states(key, part):
    key = jax.random.fold_in(key, 7)
    first_key, second_key = jax.random.split(key, 2)
    normal_keys = jax.random.normal(first_key, (N_EXPERT, SRC_LEN, D), jnp.float32)
    values = jnp.clip(jax.random.normal(second_key, (N_EXPERT, SRC_LEN, D), jnp.float32), -8.0, 8.0)
    scaled_keys = 2.0 * normal_keys
    scaled_keys = jnp.clip(scaled_keys, -64.0, 64.0)
    return jnp.stack([scaled_keys, values], axis=1).astype(jnp.bfloat16)


def plant(values, key, least, largest):
    longest = values.shape.index(max(values.shape))
    spots = []
    for shift in (0, 1):
        where = [jax.random.randint(jax.random.fold_in(key, axis), (), 0, length) for axis, length in enumerate(values.shape)]
        where[longest] = (where[longest] + shift) % values.shape[longest]
        spots.append(tuple(where))
    return values.at[spots[0]].set(least).at[spots[1]].set(largest)


def block_levels(key, extent, pieces, least, largest):
    level = 1.0
    for dim, blocks in pieces:
        steps = jax.random.uniform(jax.random.fold_in(jax.random.fold_in(key, 6), dim), (blocks,), jnp.float32, least / len(pieces), largest / len(pieces))
        level = level * jnp.repeat(jnp.exp(steps), extent[dim] // blocks).reshape((-1,) + (1,) * (len(extent) - 1 - dim))
    return level


def deal_out(key, own, number, rows, number_of, top, most, slope):
    ranking = jax.random.permutation(key, number_of)
    packed, common = portions_of(number_of, rows * top, most, slope, True), portions_of(number_of, rows * top, most, slope, False)
    places = jnp.arange(number_of)

    def named(tallies, offset_by):
        used = int((tallies > 0).sum())
        fixed = max(1, used // 4)
        passed = fixed + (places - fixed + offset_by * (used - fixed)) % max(1, number_of - fixed)
        return jnp.zeros((number_of,), jnp.int32).at[ranking[jnp.where(places < fixed, places, passed)]].set(jnp.asarray(tallies, jnp.int32))

    tallies = jnp.where(number % 4 == 0, named(packed, number // 4), named(common, number - number // 4 - 1))
    mixed = jax.random.permutation(jax.random.fold_in(own, 3), number_of)
    donor, taker = mixed[0:number_of // 2 * 2:2], mixed[1:number_of // 2 * 2:2]
    slack = jnp.minimum(tallies[donor] - 1, most - tallies[taker]) // 2
    slack = jnp.where((donor == ranking[0]) | (taker == ranking[0]) | (tallies[taker] == 0), 0, jnp.maximum(slack, 0))
    passed = jax.random.randint(jax.random.fold_in(own, 4), (number_of // 2,), 0, 1 << 20) % (slack + 1)
    tallies = tallies.at[donor].add(-passed).at[taker].add(passed)
    members = jnp.searchsorted(jnp.cumsum(tallies), jnp.arange(rows * top), side="right").astype(jnp.int32)
    table = members.reshape(top, rows).T
    table = table[jax.random.permutation(jax.random.fold_in(own, 1), rows)]
    offset_by = jax.random.randint(jax.random.fold_in(own, 2), (rows, 1), 0, top)
    return jnp.take_along_axis(table, (jnp.arange(top)[None, :] + offset_by) % top, axis=1)


def portions_of(amount, total, limit, slope, full):
    loads = [(1 << 20) // math.isqrt(standing ** slope) + 1 for standing in range(1, amount + 1)]
    largest = limit if full else min(limit, max(-(-total // amount), total * loads[0] // sum(loads)))
    least = 1 if total - largest >= amount - 1 else 0
    holding, rest = [largest] + [least] * (amount - 1), total - largest - least * (amount - 1)
    while rest > 0:
        free = [i for i in range(1, amount) if holding[i] < largest] or [i for i in range(1, amount) if holding[i] < limit]
        whole, remaining = sum([loads[i] for i in free]), rest
        for i in free:
            more = min(limit - holding[i], max(1, remaining * loads[i] // whole), rest)
            holding[i] = holding[i] + more
            rest = rest - more
    return np.array(holding)


def noise(stream_key, dims, width, bound, cuts=(), kind=jnp.bfloat16):
    loudness = block_levels(stream_key, dims, cuts, -0.22, 0.18) if cuts else 1.0
    result = jax.random.normal(stream_key, dims, jnp.float32) * width * loudness
    return jnp.minimum(jnp.maximum(result, -bound), bound).astype(kind)


def setup_inputs(seed: int = 0, part: int = 0) -> dict:
    streams_of = jax.random.split(jax.random.key(seed), 10)
    part_splits = jax.random.split(jax.random.fold_in(streams_of[9], part), 10)
    tokens = noise(part_splits[0], (TOKENS, D), 1.0, 6.0, ((0, 4),))
    encoder_states = draw_encoder_states(jax.random.fold_in(jax.random.fold_in(streams_of[9], part), 71), part)
    source_owner = plant(jax.random.randint(part_splits[2], (N_EXPERT,), 0, N_EXPERT), jax.random.fold_in(part_splits[2], 1), 0, N_EXPERT - 1).astype(jnp.int32)
    query_weight = noise(streams_of[3], (D, D), D ** -0.5, 0.1875, ((1, 4),))
    output_weight = noise(streams_of[4], (D, D), D ** -0.5, 0.1875, ((0, 4),))
    router_weight = noise(streams_of[5], (D, EXPERTS), D ** -0.5, 0.1875)
    expert_choice_keys = jax.random.split(jax.random.fold_in(part_splits[6], 1), TOKENS // TOK_DEV)
    expert_choice_turns = jax.random.permutation(jax.random.fold_in(part_splits[6], 3), TOKENS // TOK_DEV)
    expert_choice = jax.vmap(lambda own, number: deal_out(jax.random.fold_in(part_splits[6], 2), own, number, TOK_DEV, EXPERTS, 2, CAP, 2))(expert_choice_keys, expert_choice_turns).reshape((TOKENS, 2))
    expand_weight = noise(streams_of[7], (EXPERTS, D, FF), D ** -0.5, 0.1875, ((0, 4), (2, 4)))
    shrink_weight = noise(streams_of[8], (EXPERTS, FF, D), FF ** -0.5, 0.09375, ((0, 4), (1, 4)))
    return dict(tokens=tokens, encoder_states=encoder_states, source_owner=source_owner, query_weight=query_weight, output_weight=output_weight, router_weight=router_weight, expert_choice=expert_choice, expand_weight=expand_weight, shrink_weight=shrink_weight)


def attend_block(query_block, source):
    key_heads = source[0].astype(jnp.float32).reshape(SRC_LEN, HEADS, HEAD_DIM)
    value_heads = source[1].astype(jnp.float32).reshape(SRC_LEN, HEADS, HEAD_DIM)
    query_heads = query_block.astype(jnp.float32).reshape(-1, HEADS, HEAD_DIM)
    scores = jnp.einsum("thd,shd->hts", query_heads, key_heads) * (HEAD_DIM ** -0.5)
    weights = jnp.exp(scores - jnp.max(scores, axis=2, keepdims=True))
    weights = (weights / jnp.sum(weights, axis=2, keepdims=True)).astype(jnp.bfloat16)
    context = jnp.einsum("hts,shd->thd", weights.astype(jnp.float32), value_heads)
    return context.reshape(-1, D).astype(jnp.bfloat16)


def reference(tokens, encoder_states, source_owner, query_weight, output_weight, router_weight, expert_choice, expand_weight, shrink_weight):
    queries = jnp.dot(tokens, query_weight, preferred_element_type=jnp.float32).astype(jnp.bfloat16)
    blocks = queries.reshape(N_EXPERT, TOK_DEV, D)

    def one_block(inputs):
        block, owner = inputs
        source = lax.dynamic_index_in_dim(encoder_states, owner, 0, keepdims=False)
        return attend_block(block, source)

    context = lax.map(one_block, (blocks, source_owner.astype(jnp.int32))).reshape(TOKENS, D)
    attention = jnp.dot(context, output_weight, preferred_element_type=jnp.float32)
    state = (tokens.astype(jnp.float32) + attention).astype(jnp.bfloat16)
    logits = jnp.dot(state, router_weight, preferred_element_type=jnp.float32)
    picked = jnp.take_along_axis(logits, expert_choice, axis=1)
    gate_first = jax.nn.sigmoid(picked[:, 0] - picked[:, 1])
    gate_second = jax.nn.sigmoid(picked[:, 1] - picked[:, 0])
    flat_choice = expert_choice.reshape(-1)
    most_rows = N_EXPERT * CAP

    def run_expert(inputs):
        number, expand, shrink = inputs
        matches = flat_choice == number
        hits = jnp.nonzero(matches, size=most_rows, fill_value=0)[0].astype(jnp.int32)
        live = jnp.arange(most_rows, dtype=jnp.int32) < jnp.sum(matches.astype(jnp.int32))
        routed = state[hits // 2].astype(jnp.float32)
        hidden = jnp.maximum(jnp.dot(routed, expand.astype(jnp.float32)), 0.0).astype(jnp.bfloat16)
        output = jnp.dot(hidden.astype(jnp.float32), shrink.astype(jnp.float32)).astype(jnp.bfloat16)
        target = jnp.where(live, hits, 2 * TOKENS).astype(jnp.int32)
        return output, target

    outputs, targets = lax.map(run_expert, (jnp.arange(EXPERTS, dtype=jnp.int32), expand_weight, shrink_weight))
    placed = jnp.zeros((2 * TOKENS, D), jnp.bfloat16).at[targets.reshape(-1)].set(outputs.reshape(-1, D), mode="drop")
    results = placed.reshape(TOKENS, 2, D).astype(jnp.float32)
    combined = state.astype(jnp.float32) + gate_first[:, None] * results[:, 0] + gate_second[:, None] * results[:, 1]
    return combined.astype(jnp.bfloat16)
```

```python
import functools

import jax
import jax.numpy as jnp
from jax import lax
from jax.experimental import pallas as pl
from jax.experimental.pallas import tpu as pltpu
from jax.sharding import PartitionSpec as P

HEAD_DIM = 128
DIRECT = 8
F32, BF16 = jnp.float32, jnp.bfloat16
PARAMS = pltpu.CompilerParams(vmem_limit_bytes=40 * 2**20)
SCALARS = pl.BlockSpec(memory_space=pltpu.SMEM)
WHOLE = pl.BlockSpec(memory_space=pltpu.VMEM)


def dot(a, b, dims=((1,), (0,))):
    return lax.dot_general(a, b, (dims, ((), ())), preferred_element_type=F32)


def query_kernel(tokens, weight, out):
    out[...] = dot(tokens[...], weight[...]).astype(BF16)


def attend_kernel(queries, source, out):
    for head in range(queries.shape[1] // HEAD_DIM):
        part = slice(head * HEAD_DIM, (head + 1) * HEAD_DIM)
        scores = dot(queries[:, part], source[0, :, part], ((1,), (1,)))
        top = jnp.max(scores, axis=1, keepdims=True)
        weights = jnp.exp((scores - top) * HEAD_DIM**-0.5)
        total = jnp.sum(weights, axis=1, keepdims=True)
        context = dot(weights.astype(BF16), source[1, :, part])
        out[:, part] = (context / total).astype(BF16)


def attend(queries, source, block):
    rows, width = queries.shape
    return pl.pallas_call(
        attend_kernel,
        grid=(rows // block,),
        in_specs=[
            pl.BlockSpec((block, width), lambda i: (i, 0)),
            pl.BlockSpec(source.shape, lambda i: (0, 0, 0)),
        ],
        out_specs=pl.BlockSpec((block, width), lambda i: (i, 0)),
        out_shape=jax.ShapeDtypeStruct((rows, width), BF16),
        compiler_params=PARAMS,
        name="attend",
    )(queries, source)


def route_kernel(experts, ids, choice, choice_t, dispatch, first, second):
    tokens = choice.shape[0]
    parts, slots = dispatch.shape[0], dispatch.shape[1]
    capacity = slots * parts // experts
    wide = lax.broadcasted_iota(jnp.int32, (tokens, experts), 1)
    tall = lax.broadcasted_iota(jnp.int32, (experts, tokens), 0)
    c0, c1 = choice[:, 0:1], choice[:, 1:2]
    r0, r1 = choice_t[0:1, :], choice_t[1:2, :]
    named = ((wide == c0) | (wide == c1)).astype(BF16)
    named_t = ((tall == r0) | (tall == r1)).astype(BF16)
    i = lax.broadcasted_iota(jnp.int32, (tokens, tokens), 0)
    j = lax.broadcasted_iota(jnp.int32, (tokens, tokens), 1)
    rank = dot((j < i).astype(BF16), named).astype(jnp.int32)
    rank_t = dot(named_t, (i < j).astype(BF16)).astype(jnp.int32)
    place0 = c0 * capacity + jnp.sum(jnp.where(wide == c0, rank, 0), axis=1, keepdims=True)
    place1 = c1 * capacity + jnp.sum(jnp.where(wide == c1, rank, 0), axis=1, keepdims=True)
    across0 = r0 * capacity + jnp.sum(jnp.where(tall == r0, rank_t, 0), axis=0, keepdims=True)
    across1 = r1 * capacity + jnp.sum(jnp.where(tall == r1, rank_t, 0), axis=0, keepdims=True)
    lane = lax.broadcasted_iota(jnp.int32, (tokens, slots), 1)
    row = lax.broadcasted_iota(jnp.int32, (slots, tokens), 0)
    for k in range(parts):
        base = (ids[0] ^ k) * capacity if parts > 1 else 0
        dispatch[k] = ((row + base == across0) | (row + base == across1)).astype(BF16)
        first[k] = (lane + base == place0).astype(BF16)
        second[k] = (lane + base == place1).astype(BF16)


def route(ids, choice, experts, parts, capacity):
    tokens = choice.shape[0]
    slots = experts * capacity // parts
    return pl.pallas_call(
        functools.partial(route_kernel, experts),
        in_specs=[SCALARS, WHOLE, WHOLE],
        out_specs=[WHOLE] * 3,
        out_shape=[
            jax.ShapeDtypeStruct((parts, slots, tokens), BF16),
            jax.ShapeDtypeStruct((parts, tokens, slots), BF16),
            jax.ShapeDtypeStruct((parts, tokens, slots), BF16),
        ],
        compiler_params=PARAMS,
        name="route",
    )(ids, choice, choice.T)


def state_kernel(count, away, *refs):
    ids, tokens, dispatch = refs[:3]
    contexts, weights = refs[3 : 3 + count], refs[3 + count : 3 + 2 * count]
    state = refs[3 + 2 * count]
    outs = refs[4 + 2 * count :]
    total = tokens[...].astype(F32)
    for context, weight in zip(contexts, weights):
        total += dot(context[...], weight[...])
    state[...] = total.astype(BF16)
    half = state.shape[1] // 2
    mine = state[:, pl.ds(pl.multiple_of((ids[1] & 1) * half, half), half)]
    for out, k in zip(outs, away):
        out[...] = dot(dispatch[k], mine).astype(BF16)


def make_state(ids, tokens, dispatch, contexts, weights, away):
    slots = dispatch.shape[1]
    features = tokens.shape[1]
    return pl.pallas_call(
        functools.partial(state_kernel, len(contexts), away),
        in_specs=[SCALARS] + [WHOLE] * (2 + 2 * len(contexts)),
        out_specs=[WHOLE] * (1 + len(away)),
        out_shape=[jax.ShapeDtypeStruct(tokens.shape, BF16)]
        + [jax.ShapeDtypeStruct((slots, features // 2), BF16)] * len(away),
        compiler_params=PARAMS,
        name="state",
    )(ids, tokens, dispatch, *contexts, *weights)


def home_kernel(experts, ids, state, dispatch, router, choice, own_a, own_b, gates, columns):
    half = own_a.shape[1]
    core = ids[1] & 1
    own_a[...] = dot(dispatch[0], state[:, pl.ds(pl.multiple_of(core * half, half), half)]).astype(BF16)
    own_b[...] = dot(dispatch[0], state[:, pl.ds(pl.multiple_of((1 - core) * half, half), half)]).astype(BF16)
    logits = dot(state[...], router[...])
    wide = lax.broadcasted_iota(jnp.int32, logits.shape, 1)
    first = jnp.sum(jnp.where(wide == choice[:, 0:1], logits, 0.0), axis=1, keepdims=True)
    second = jnp.sum(jnp.where(wide == choice[:, 1:2], logits, 0.0), axis=1, keepdims=True)
    gates[:, 0:1] = jax.nn.sigmoid(first - second)
    gates[:, 1:2] = jax.nn.sigmoid(second - first)
    width = columns.shape[1]
    columns[...] = state[:, pl.ds(pl.multiple_of(ids[1] * width, width), width)].astype(F32)


def at_home(ids, state, dispatch, router, choice, experts, width):
    tokens, features = state.shape
    slots = dispatch.shape[1]
    return pl.pallas_call(
        functools.partial(home_kernel, experts),
        in_specs=[SCALARS] + [WHOLE] * 4,
        out_specs=[WHOLE] * 4,
        out_shape=[
            jax.ShapeDtypeStruct((slots, features // 2), BF16),
            jax.ShapeDtypeStruct((slots, features // 2), BF16),
            jax.ShapeDtypeStruct((tokens, 2), F32),
            jax.ShapeDtypeStruct((tokens, width), F32),
        ],
        compiler_params=PARAMS,
        name="home",
    )(ids, state, dispatch, router, choice)


def expert_kernel(ids, mine, other, expand, shrink, keep, give, total):
    step, steps = pl.program_id(0), pl.num_programs(0)
    half = mine.shape[1]
    core = ids[1] & 1
    hidden = dot(mine[...], expand[pl.ds(pl.multiple_of(core * half, half), half), :])
    hidden += dot(other[...], expand[pl.ds(pl.multiple_of((1 - core) * half, half), half), :])
    hidden = jnp.maximum(hidden, 0.0).astype(BF16)
    product = dot(hidden, shrink[...])

    @pl.when(step == 0)
    def _():
        total[...] = product

    @pl.when(step > 0)
    def _():
        total[...] += product

    @pl.when(step == steps - 1)
    def _():
        parts = keep.shape[0]
        width = keep.shape[2]
        for j in range(parts):
            at = (ids[1] ^ (2 * j)) * width
            keep[j] = total[:, pl.ds(pl.multiple_of(at, width), width)]
            at = (ids[1] ^ (2 * j) ^ 1) * width
            give[j] = total[:, pl.ds(pl.multiple_of(at, width), width)].astype(BF16)


def run_expert(ids, mine, other, expand, shrink, parts):
    rows, half = mine.shape
    features, units = expand.shape
    tile = min(256, units)
    width = features // (2 * parts)
    return pl.pallas_call(
        expert_kernel,
        grid=(units // tile,),
        in_specs=[
            SCALARS,
            pl.BlockSpec((rows, half), lambda i: (0, 0)),
            pl.BlockSpec((rows, half), lambda i: (0, 0)),
            pl.BlockSpec((features, tile), lambda i: (0, i)),
            pl.BlockSpec((tile, features), lambda i: (i, 0)),
        ],
        out_specs=[pl.BlockSpec((parts, rows, width), lambda i: (0, 0, 0))] * 2,
        out_shape=[
            jax.ShapeDtypeStruct((parts, rows, width), F32),
            jax.ShapeDtypeStruct((parts, rows, width), BF16),
        ],
        scratch_shapes=[pltpu.VMEM((rows, features), F32)],
        compiler_params=PARAMS,
        name="expert",
    )(ids, mine, other, expand, shrink)


def combine_kernel(count, gates, base, first, second, *refs):
    parts, out = refs[:count], refs[count]
    total = parts[0][...].astype(F32)
    for part in parts[1:]:
        total += part[...].astype(F32)
    total = total.astype(BF16)
    result = base[...] + gates[:, 0:1] * dot(first[...], total) + gates[:, 1:2] * dot(second[...], total)
    out[...] = result.astype(out.dtype)


def combine(gates, base, first, second, parts, dtype):
    return pl.pallas_call(
        functools.partial(combine_kernel, len(parts)),
        in_specs=[WHOLE] * (4 + len(parts)),
        out_specs=WHOLE,
        out_shape=jax.ShapeDtypeStruct(base.shape, dtype),
        compiler_params=PARAMS,
        name="combine",
    )(gates, base, first, second, *parts)


def local(
    tokens,
    encoder_states,
    source_owner,
    query_weight,
    output_weight,
    router_weight,
    expert_choice,
    expand_weight,
    shrink_weight,
):
    token_count, features = tokens.shape
    groups = lax.axis_size("expert")
    slices = lax.axis_size("mp")
    here, column = lax.axis_index("expert"), lax.axis_index("mp")
    ids = jnp.stack([here, column]).astype(jnp.int32)
    width = features // slices
    experts = expand_weight.shape[0] * groups
    capacity = max(2, 3 * token_count // experts)
    direct = groups <= DIRECT
    pairs = slices // 2

    def hop(value, along_expert, along_mp):
        if along_expert == 0 and along_mp == 0:
            return value
        moves = [
            (e * slices + m, (e ^ along_expert) * slices + (m ^ along_mp))
            for e in range(groups)
            for m in range(slices)
        ]
        return lax.ppermute(value, ("expert", "mp"), moves)

    def spread(value):
        parts = value.reshape(groups, -1, value.shape[-1])
        return lax.all_to_all(parts, "expert", 0, 0, tiled=True).reshape(value.shape)

    steps = range(groups) if direct else [0]
    dispatch, first, second = route(ids, expert_choice, experts, len(steps), capacity)

    queries = pl.pallas_call(
        query_kernel,
        in_specs=[WHOLE] * 2,
        out_specs=WHOLE,
        out_shape=jax.ShapeDtypeStruct((token_count, width), BF16),
        compiler_params=PARAMS,
        name="query",
    )(tokens, query_weight)
    owner = source_owner[0]
    if direct:
        context = attend(queries, encoder_states[0], token_count)
        for k in range(1, groups):
            back = hop(attend(hop(queries, k, 0), encoder_states[0], token_count), k, 0)
            context = jnp.where(owner == here ^ k, back, context)
    else:
        asked = lax.all_gather(queries, "expert", axis=0, tiled=True)
        back = spread(attend(asked, encoder_states[0], token_count))
        context = lax.dynamic_slice_in_dim(back, owner * token_count, token_count, 0)

    weights = [output_weight]
    bit = 1
    while bit < slices:
        bit *= 2
    while bit > 1:
        bit //= 2
        weights = weights + [hop(weight, 0, bit) for weight in weights]
    order = [0]
    bit = slices
    while bit > 1:
        bit //= 2
        order = order + [index ^ bit for index in order]
    contexts = [hop(context, 0, index) for index in order]

    away = tuple(range(1, groups)) if direct else (0,)
    state, *leaving = make_state(ids, tokens, dispatch, contexts, weights, away)
    own_a, own_b, gates, columns = at_home(ids, state, dispatch, router_weight, expert_choice, experts, width)

    results = columns
    for k in steps:
        if not direct:
            mine = spread(leaving[0])
            other = hop(mine, 0, 1)
        elif k == 0:
            mine, other = own_a, own_b
        else:
            mine = hop(leaving[k - 1], k, 0)
            other = hop(mine, 0, 1)
        keep, give = run_expert(ids, mine, other, expand_weight[0], shrink_weight[0], pairs)
        summed = (keep + hop(give, 0, 1).astype(F32)).astype(BF16)
        parts = []
        for j in range(pairs):
            if direct:
                parts.append(hop(summed[j], k, 2 * j))
            else:
                parts.append(hop(spread(summed[j]), 0, 2 * j))
        last = k == steps[-1]
        results = combine(gates, results, first[k], second[k], parts, BF16 if last else F32)
    return results


def solution(mesh):
    return jax.shard_map(
        local,
        mesh=mesh,
        in_specs=(
            P(("groups", "expert"), None),
            P(("groups", "expert"), None, None, "mp"),
            P(("groups", "expert")),
            P(None, "mp"),
            P("mp", None),
            P(),
            P(("groups", "expert"), None),
            P("expert", None, "mp"),
            P("expert", "mp", None),
        ),
        out_specs=P(("groups", "expert"), "mp"),
        check_vma=False,
    )
```

```python
import functools

import jax
import jax.numpy as jnp
from jax import lax
from jax.experimental import pallas as pl
from jax.experimental.pallas import tpu as pltpu
from jax.sharding import PartitionSpec as P

HEAD_DIM = 128
DIRECT = 8
CUTS = 4
TILE = 256
F32, BF16 = jnp.float32, jnp.bfloat16
PARAMS = pltpu.CompilerParams(vmem_limit_bytes=40 * 2**20)
SCALARS = pl.BlockSpec(memory_space=pltpu.SMEM)
WHOLE = pl.BlockSpec(memory_space=pltpu.VMEM)


def dot(a, b, dims=((1,), (0,))):
    return lax.dot_general(a, b, (dims, ((), ())), preferred_element_type=F32)


def in_hbm(value):
    return pltpu.with_memory_space_constraint(value, pltpu.HBM)


def query_kernel(tokens, weight, out, tokens_here, weight_here, sems):
    features = tokens.shape[1]
    depth = features // CUTS
    copies = []
    for i in range(CUTS):
        part = pl.ds(i * depth, depth)
        copies.append(
            (
                pltpu.make_async_copy(tokens.at[:, part], tokens_here.at[:, part], sems.at[0, i]),
                pltpu.make_async_copy(weight.at[part, :], weight_here.at[part, :], sems.at[1, i]),
            )
        )
    for pair in copies:
        for copy in pair:
            copy.start()
    total = jnp.zeros(out.shape, F32)
    for i, pair in enumerate(copies):
        for copy in pair:
            copy.wait()
        part = slice(i * depth, (i + 1) * depth)
        total += dot(tokens_here[:, part], weight_here[part, :])
    out[...] = total.astype(BF16)


def ask(tokens, weight):
    return pl.pallas_call(
        query_kernel,
        in_specs=[pl.BlockSpec(memory_space=pltpu.HBM)] * 2,
        out_specs=WHOLE,
        out_shape=jax.ShapeDtypeStruct((tokens.shape[0], weight.shape[1]), BF16),
        scratch_shapes=[
            pltpu.VMEM(tokens.shape, BF16),
            pltpu.VMEM(weight.shape, BF16),
            pltpu.SemaphoreType.DMA((2, CUTS)),
        ],
        compiler_params=PARAMS,
        name="query",
    )(in_hbm(tokens), in_hbm(weight))


def stage_kernel(source, out, sems):
    copies = [
        pltpu.make_async_copy(source.at[:, rows], out.at[:, rows], sems.at[i])
        for i, rows in enumerate(
            pl.ds(i * (source.shape[1] // CUTS), source.shape[1] // CUTS) for i in range(CUTS)
        )
    ]
    for copy in copies:
        copy.start()
    for copy in copies:
        copy.wait()


def stage(source):
    return pl.pallas_call(
        stage_kernel,
        in_specs=[pl.BlockSpec(memory_space=pltpu.HBM)],
        out_specs=WHOLE,
        out_shape=jax.ShapeDtypeStruct(source.shape, source.dtype),
        scratch_shapes=[pltpu.SemaphoreType.DMA((CUTS,))],
        compiler_params=PARAMS,
        name="stage",
    )(in_hbm(source))


def attend_kernel(queries, source, out):
    for head in range(queries.shape[1] // HEAD_DIM):
        part = slice(head * HEAD_DIM, (head + 1) * HEAD_DIM)
        scores = dot(queries[:, part], source[0, :, part], ((1,), (1,)))
        top = jnp.max(scores, axis=1, keepdims=True)
        weights = jnp.exp((scores - top) * HEAD_DIM**-0.5)
        total = jnp.sum(weights, axis=1, keepdims=True)
        context = dot(weights.astype(BF16), source[1, :, part])
        out[:, part] = (context / total).astype(BF16)


def attend(queries, source, block):
    rows, width = queries.shape
    if rows == block:
        return pl.pallas_call(
            attend_kernel,
            in_specs=[WHOLE] * 2,
            out_specs=WHOLE,
            out_shape=jax.ShapeDtypeStruct((rows, width), BF16),
            compiler_params=PARAMS,
            name="attend",
        )(queries, source)
    return pl.pallas_call(
        attend_kernel,
        grid=(rows // block,),
        in_specs=[
            pl.BlockSpec((block, width), lambda i: (i, 0)),
            pl.BlockSpec(source.shape, lambda i: (0, 0, 0)),
        ],
        out_specs=pl.BlockSpec((block, width), lambda i: (i, 0)),
        out_shape=jax.ShapeDtypeStruct((rows, width), BF16),
        compiler_params=PARAMS,
        name="attend",
    )(queries, source)


def route_kernel(experts, ids, choice, choice_t, dispatch, first, second):
    tokens = choice.shape[0]
    parts, slots = dispatch.shape[0], dispatch.shape[1]
    capacity = slots * parts // experts
    wide = lax.broadcasted_iota(jnp.int32, (tokens, experts), 1)
    tall = lax.broadcasted_iota(jnp.int32, (experts, tokens), 0)
    c0, c1 = choice[:, 0:1], choice[:, 1:2]
    r0, r1 = choice_t[0:1, :], choice_t[1:2, :]
    named = ((wide == c0) | (wide == c1)).astype(BF16)
    named_t = ((tall == r0) | (tall == r1)).astype(BF16)
    i = lax.broadcasted_iota(jnp.int32, (tokens, tokens), 0)
    j = lax.broadcasted_iota(jnp.int32, (tokens, tokens), 1)
    rank = dot((j < i).astype(BF16), named).astype(jnp.int32)
    rank_t = dot(named_t, (i < j).astype(BF16)).astype(jnp.int32)
    place0 = c0 * capacity + jnp.sum(jnp.where(wide == c0, rank, 0), axis=1, keepdims=True)
    place1 = c1 * capacity + jnp.sum(jnp.where(wide == c1, rank, 0), axis=1, keepdims=True)
    across0 = r0 * capacity + jnp.sum(jnp.where(tall == r0, rank_t, 0), axis=0, keepdims=True)
    across1 = r1 * capacity + jnp.sum(jnp.where(tall == r1, rank_t, 0), axis=0, keepdims=True)
    lane = lax.broadcasted_iota(jnp.int32, (tokens, slots), 1)
    row = lax.broadcasted_iota(jnp.int32, (slots, tokens), 0)
    for k in range(parts):
        base = (ids[0] ^ k) * capacity if parts > 1 else 0
        dispatch[k] = ((row + base == across0) | (row + base == across1)).astype(BF16)
        first[k] = (lane + base == place0).astype(BF16)
        second[k] = (lane + base == place1).astype(BF16)


def route(ids, choice, experts, parts, capacity):
    tokens = choice.shape[0]
    slots = experts * capacity // parts
    return pl.pallas_call(
        functools.partial(route_kernel, experts),
        in_specs=[SCALARS, WHOLE, WHOLE],
        out_specs=[WHOLE] * 3,
        out_shape=[
            jax.ShapeDtypeStruct((parts, slots, tokens), BF16),
            jax.ShapeDtypeStruct((parts, tokens, slots), BF16),
            jax.ShapeDtypeStruct((parts, tokens, slots), BF16),
        ],
        compiler_params=PARAMS,
        name="route",
    )(ids, choice, choice.T)


def state_kernel(count, leave, *refs):
    ids, tokens, dispatch = refs[:3]
    contexts, weights = refs[3 : 3 + count], refs[3 + count : 3 + 2 * count]
    state = refs[3 + 2 * count]
    outs = refs[4 + 2 * count :]
    total = tokens[...].astype(F32)
    for context, weight in zip(contexts, weights):
        total += dot(context[...], weight[...])
    state[...] = total.astype(BF16)
    for out, (k, cuts) in zip(outs, leave):
        width = out.shape[1]
        at = (ids[1] & (cuts - 1)) * width
        out[...] = dot(dispatch[k], state[:, pl.ds(pl.multiple_of(at, width), width)]).astype(BF16)


def make_state(ids, tokens, dispatch, contexts, weights, leave):
    slots = dispatch.shape[1]
    features = tokens.shape[1]
    return pl.pallas_call(
        functools.partial(state_kernel, len(contexts), leave),
        in_specs=[SCALARS] + [WHOLE] * (2 + 2 * len(contexts)),
        out_specs=[WHOLE] * (1 + len(leave)),
        out_shape=[jax.ShapeDtypeStruct(tokens.shape, BF16)]
        + [jax.ShapeDtypeStruct((slots, features // cuts), BF16) for _, cuts in leave],
        compiler_params=PARAMS,
        name="state",
    )(ids, tokens, dispatch, *contexts, *weights)


def home_kernel(experts, ids, state, dispatch, router, choice, own_a, own_b, gates, columns):
    half = own_a.shape[1]
    core = ids[1] & 1
    own_a[...] = dot(dispatch[0], state[:, pl.ds(pl.multiple_of(core * half, half), half)]).astype(BF16)
    own_b[...] = dot(dispatch[0], state[:, pl.ds(pl.multiple_of((1 - core) * half, half), half)]).astype(BF16)
    logits = dot(state[...], router[...])
    wide = lax.broadcasted_iota(jnp.int32, logits.shape, 1)
    first = jnp.sum(jnp.where(wide == choice[:, 0:1], logits, 0.0), axis=1, keepdims=True)
    second = jnp.sum(jnp.where(wide == choice[:, 1:2], logits, 0.0), axis=1, keepdims=True)
    gates[:, 0:1] = jax.nn.sigmoid(first - second)
    gates[:, 1:2] = jax.nn.sigmoid(second - first)
    width = columns.shape[1]
    columns[...] = state[:, pl.ds(pl.multiple_of(ids[1] * width, width), width)].astype(F32)


def at_home(ids, state, dispatch, router, choice, experts, width):
    tokens, features = state.shape
    slots = dispatch.shape[1]
    return pl.pallas_call(
        functools.partial(home_kernel, experts),
        in_specs=[SCALARS] + [WHOLE] * 4,
        out_specs=[WHOLE] * 4,
        out_shape=[
            jax.ShapeDtypeStruct((slots, features // 2), BF16),
            jax.ShapeDtypeStruct((slots, features // 2), BF16),
            jax.ShapeDtypeStruct((tokens, 2), F32),
            jax.ShapeDtypeStruct((tokens, width), F32),
        ],
        compiler_params=PARAMS,
        name="home",
    )(ids, state, dispatch, router, choice)


def expert_kernel(order, *refs):
    ids, pieces = refs[0], refs[1 : 1 + len(order)]
    expand, shrink, keep, give, hidden = refs[1 + len(order) :]
    cuts = len(order)
    units = expand.shape[1]
    tile = min(TILE, units)
    for at in range(0, units, tile):
        total = jnp.zeros((hidden.shape[0], tile), F32)
        for index, piece in zip(order, pieces):
            width = piece.shape[1]
            rows = pl.ds(pl.multiple_of(((ids[1] & (cuts - 1)) ^ index) * width, width), width)
            total += dot(piece[...], expand[rows, at : at + tile])
        hidden[:, at : at + tile] = jnp.maximum(total, 0.0).astype(BF16)
    width = keep.shape[2]
    for j in range(keep.shape[0]):
        at = pl.multiple_of((ids[1] ^ (2 * j) ^ 1) * width, width)
        give[j] = dot(hidden[...], shrink[:, pl.ds(at, width)]).astype(BF16)
    for j in range(keep.shape[0]):
        at = pl.multiple_of((ids[1] ^ (2 * j)) * width, width)
        keep[j] = dot(hidden[...], shrink[:, pl.ds(at, width)])


def run_expert(ids, order, pieces, expand, shrink, parts):
    rows = pieces[0].shape[0]
    features, units = expand.shape
    width = features // (2 * parts)
    return pl.pallas_call(
        functools.partial(expert_kernel, tuple(order)),
        in_specs=[SCALARS] + [WHOLE] * (2 + len(pieces)),
        out_specs=[WHOLE] * 2,
        out_shape=[
            jax.ShapeDtypeStruct((parts, rows, width), F32),
            jax.ShapeDtypeStruct((parts, rows, width), BF16),
        ],
        scratch_shapes=[pltpu.VMEM((rows, units), BF16)],
        compiler_params=PARAMS,
        name="expert",
    )(ids, *pieces, expand, shrink)


def combine_kernel(count, gates, base, first, second, *refs):
    parts, out = refs[:count], refs[count]
    total = parts[0][...].astype(F32)
    for part in parts[1:]:
        total += part[...].astype(F32)
    total = total.astype(BF16)
    result = base[...] + gates[:, 0:1] * dot(first[...], total) + gates[:, 1:2] * dot(second[...], total)
    out[...] = result.astype(out.dtype)


def combine(gates, base, first, second, parts, dtype):
    return pl.pallas_call(
        functools.partial(combine_kernel, len(parts)),
        in_specs=[WHOLE] * (4 + len(parts)),
        out_specs=WHOLE,
        out_shape=jax.ShapeDtypeStruct(base.shape, dtype),
        compiler_params=PARAMS,
        name="combine",
    )(gates, base, first, second, *parts)


def local(
    tokens,
    encoder_states,
    source_owner,
    query_weight,
    output_weight,
    router_weight,
    expert_choice,
    expand_weight,
    shrink_weight,
):
    token_count, features = tokens.shape
    groups = lax.axis_size("expert")
    slices = lax.axis_size("mp")
    here, column = lax.axis_index("expert"), lax.axis_index("mp")
    ids = jnp.stack([here, column]).astype(jnp.int32)
    width = features // slices
    experts = expand_weight.shape[0] * groups
    capacity = max(2, 3 * token_count // experts)
    direct = groups <= DIRECT
    pairs = slices // 2

    def hop(value, along_expert, along_mp):
        if along_expert == 0 and along_mp == 0:
            return value
        moves = [
            (e * slices + m, (e ^ along_expert) * slices + (m ^ along_mp))
            for e in range(groups)
            for m in range(slices)
        ]
        return lax.ppermute(value, ("expert", "mp"), moves)

    def spread(value):
        parts = value.reshape(groups, -1, value.shape[-1])
        return lax.all_to_all(parts, "expert", 0, 0, tiled=True).reshape(value.shape)

    def after(value, other):
        return lax.optimization_barrier((value, other))[0]

    steps = range(groups) if direct else [0]
    dispatch, first, second = route(ids, expert_choice, experts, len(steps), capacity)

    queries = ask(tokens, query_weight)
    owner = source_owner[0]
    if direct:
        source = stage(after(encoder_states[0], queries))
        own = context = attend(queries, source, token_count)
        for k in reversed(range(1, groups)):
            asked = after(hop(queries, k, 0), own)
            back = hop(attend(asked, source, token_count), k, 0)
            context = jnp.where(owner == here ^ k, back, context)
    else:
        asked = lax.all_gather(queries, "expert", axis=0, tiled=True)
        back = spread(attend(asked, encoder_states[0], token_count))
        context = lax.dynamic_slice_in_dim(back, owner * token_count, token_count, 0)

    bits = []
    while 2 ** len(bits) < slices:
        bits.insert(0, 2 ** len(bits))
    weights, order = [after(output_weight, source if direct else queries)], [0]
    for bit in bits:
        if bit == 1:
            weights = [after(weight, context) for weight in weights]
        weights = weights + [hop(weight, 0, bit) for weight in weights]
        order = order + [index ^ bit for index in order]
    contexts = [hop(context, 0, index) for index in order]

    relayed = groups - 1 if direct and pairs > 1 and groups > 1 else -1
    leave = tuple((k, slices if k == relayed else 2) for k in reversed(range(1, groups))) if direct else ((0, 2),)
    state, *leaving = make_state(ids, tokens, dispatch, contexts, weights, leave)
    leaving = {k: rows for (k, _), rows in zip(leave, leaving)}
    own_a, own_b, gates, columns = at_home(ids, state, dispatch, router_weight, expert_choice, experts, width)

    results = columns
    turns = [0, *reversed(range(1, groups))] if direct else [0]
    for k in turns:
        if not direct:
            mine = spread(leaving[0])
            pieces, places = [mine, hop(mine, 0, 1)], [0, 1]
        elif k == 0:
            pieces, places = [own_a, own_b], [0, 1]
        elif k == relayed:
            pieces, places = [hop(leaving[k], k, 0)], [0]
            for bit in bits:
                pieces = pieces + [hop(piece, 0, bit) for piece in pieces]
                places = places + [index ^ bit for index in places]
        else:
            mine = hop(leaving[k], k, 0)
            pieces, places = [mine, hop(mine, 0, 1)], [0, 1]
        keep, give = run_expert(ids, places, pieces, expand_weight[0], shrink_weight[0], pairs)
        summed = keep + hop(give, 0, 1).astype(F32)
        if k == relayed:
            total = summed[0]
            for j in range(1, pairs):
                total += hop(summed[j].astype(BF16), 0, 2 * j).astype(F32)
            parts = [hop(total.astype(BF16), k, 0)]
        else:
            parts = []
            for j in range(pairs):
                part = summed[j].astype(BF16)
                parts.append(hop(part, k, 2 * j) if direct else hop(spread(part), 0, 2 * j))
        last = k == turns[-1]
        results = combine(gates, results, first[k], second[k], parts, BF16 if last else F32)
    return results


def solution(mesh):
    return jax.shard_map(
        local,
        mesh=mesh,
        in_specs=(
            P(("groups", "expert"), None),
            P(("groups", "expert"), None, None, "mp"),
            P(("groups", "expert")),
            P(None, "mp"),
            P("mp", None),
            P(),
            P(("groups", "expert"), None),
            P("expert", None, "mp"),
            P("expert", "mp", None),
        ),
        out_specs=P(("groups", "expert"), "mp"),
        check_vma=False,
    )
```

```python
import functools

import jax
import jax.numpy as jnp
from jax import lax
from jax.experimental import pallas as pl
from jax.experimental.pallas import tpu as pltpu
from jax.sharding import PartitionSpec as P

HEAD_DIM = 128
DIRECT = 8
CUTS = 4
TILE = 256
F32, BF16 = jnp.float32, jnp.bfloat16
PARAMS = pltpu.CompilerParams(vmem_limit_bytes=20 * 2**20)
CHEAP = pl.CostEstimate(flops=0, bytes_accessed=0, transcendentals=0)
SCALARS = pl.BlockSpec(memory_space=pltpu.SMEM)
WHOLE = pl.BlockSpec(memory_space=pltpu.VMEM)


def dot(a, b, dims=((1,), (0,))):
    return lax.dot_general(a, b, (dims, ((), ())), preferred_element_type=F32)


def in_hbm(value):
    return pltpu.with_memory_space_constraint(value, pltpu.HBM)


def query_kernel(tokens, weight, source, out, staged, tokens_here, weight_here, sems):
    features = tokens.shape[1]
    depth = features // CUTS
    copies, later = [], []
    for i in range(CUTS):
        part = pl.ds(i * depth, depth)
        copies.append(
            (
                pltpu.make_async_copy(tokens.at[:, part], tokens_here.at[:, part], sems.at[0, i]),
                pltpu.make_async_copy(weight.at[part, :], weight_here.at[part, :], sems.at[1, i]),
            )
        )
        rows = pl.ds(i * (source.shape[1] // CUTS), source.shape[1] // CUTS)
        later.append(pltpu.make_async_copy(source.at[:, rows], staged.at[:, rows], sems.at[2, i]))
    for pair in copies:
        for copy in pair:
            copy.start()
    for copy in later:
        copy.start()
    total = jnp.zeros(out.shape, F32)
    for i, pair in enumerate(copies):
        for copy in pair:
            copy.wait()
        part = slice(i * depth, (i + 1) * depth)
        total += dot(tokens_here[:, part], weight_here[part, :])
    out[...] = total.astype(BF16)
    for copy in later:
        copy.wait()


def ask(tokens, weight, source):
    return pl.pallas_call(
        query_kernel,
        in_specs=[pl.BlockSpec(memory_space=pltpu.HBM)] * 3,
        out_specs=[WHOLE] * 2,
        out_shape=[
            jax.ShapeDtypeStruct((tokens.shape[0], weight.shape[1]), BF16),
            jax.ShapeDtypeStruct(source.shape, BF16),
        ],
        scratch_shapes=[
            pltpu.VMEM(tokens.shape, BF16),
            pltpu.VMEM(weight.shape, BF16),
            pltpu.SemaphoreType.DMA((3, CUTS)),
        ],
        compiler_params=PARAMS,
        cost_estimate=CHEAP,
        name="query",
    )(in_hbm(tokens), in_hbm(weight), in_hbm(source))


def attend_kernel(queries, source, out):
    for head in range(queries.shape[1] // HEAD_DIM):
        part = slice(head * HEAD_DIM, (head + 1) * HEAD_DIM)
        scores = dot(queries[:, part], source[0, :, part], ((1,), (1,)))
        top = jnp.max(scores, axis=1, keepdims=True)
        weights = jnp.exp((scores - top) * HEAD_DIM**-0.5)
        total = jnp.sum(weights, axis=1, keepdims=True)
        context = dot(weights.astype(BF16), source[1, :, part])
        out[:, part] = (context / total).astype(BF16)


def attend(queries, source, block):
    rows, width = queries.shape
    if rows == block:
        return pl.pallas_call(
            attend_kernel,
            in_specs=[WHOLE] * 2,
            out_specs=WHOLE,
            out_shape=jax.ShapeDtypeStruct((rows, width), BF16),
            compiler_params=PARAMS,
        cost_estimate=CHEAP,
            name="attend",
        )(queries, source)
    return pl.pallas_call(
        attend_kernel,
        grid=(rows // block,),
        in_specs=[
            pl.BlockSpec((block, width), lambda i: (i, 0)),
            pl.BlockSpec(source.shape, lambda i: (0, 0, 0)),
        ],
        out_specs=pl.BlockSpec((block, width), lambda i: (i, 0)),
        out_shape=jax.ShapeDtypeStruct((rows, width), BF16),
        compiler_params=PARAMS,
        cost_estimate=CHEAP,
        name="attend",
    )(queries, source)


def route_kernel(experts, parts, ids, choice, choice_t, *outs):
    dispatch, first, second = outs[:parts], outs[parts : 2 * parts], outs[2 * parts :]
    tokens = choice.shape[0]
    slots = dispatch[0].shape[0]
    capacity = slots * parts // experts
    wide = lax.broadcasted_iota(jnp.int32, (tokens, experts), 1)
    tall = lax.broadcasted_iota(jnp.int32, (experts, tokens), 0)
    c0, c1 = choice[:, 0:1], choice[:, 1:2]
    r0, r1 = choice_t[0:1, :], choice_t[1:2, :]
    named = ((wide == c0) | (wide == c1)).astype(BF16)
    named_t = ((tall == r0) | (tall == r1)).astype(BF16)
    i = lax.broadcasted_iota(jnp.int32, (tokens, tokens), 0)
    j = lax.broadcasted_iota(jnp.int32, (tokens, tokens), 1)
    rank = dot((j < i).astype(BF16), named).astype(jnp.int32)
    rank_t = dot(named_t, (i < j).astype(BF16)).astype(jnp.int32)
    place0 = c0 * capacity + jnp.sum(jnp.where(wide == c0, rank, 0), axis=1, keepdims=True)
    place1 = c1 * capacity + jnp.sum(jnp.where(wide == c1, rank, 0), axis=1, keepdims=True)
    across0 = r0 * capacity + jnp.sum(jnp.where(tall == r0, rank_t, 0), axis=0, keepdims=True)
    across1 = r1 * capacity + jnp.sum(jnp.where(tall == r1, rank_t, 0), axis=0, keepdims=True)
    lane = lax.broadcasted_iota(jnp.int32, (tokens, slots), 1)
    row = lax.broadcasted_iota(jnp.int32, (slots, tokens), 0)
    for k in range(parts):
        base = (ids[0] ^ k) * capacity if parts > 1 else 0
        dispatch[k][...] = ((row + base == across0) | (row + base == across1)).astype(BF16)
        first[k][...] = (lane + base == place0).astype(BF16)
        second[k][...] = (lane + base == place1).astype(BF16)


def route(ids, choice, experts, parts, capacity):
    tokens = choice.shape[0]
    slots = experts * capacity // parts
    outs = pl.pallas_call(
        functools.partial(route_kernel, experts, parts),
        in_specs=[SCALARS, WHOLE, WHOLE],
        out_specs=[WHOLE] * (3 * parts),
        out_shape=[jax.ShapeDtypeStruct((slots, tokens), BF16)] * parts
        + [jax.ShapeDtypeStruct((tokens, slots), BF16)] * (2 * parts),
        compiler_params=PARAMS,
        cost_estimate=CHEAP,
        name="route",
    )(ids, choice, choice.T)
    return outs[:parts], outs[parts : 2 * parts], outs[2 * parts :]


def state_kernel(count, *refs):
    tokens, contexts, weights = refs[0], refs[1 : 1 + count], refs[1 + count : 1 + 2 * count]
    ids, dispatch, state, out = refs[1 + 2 * count :]
    total = tokens[...].astype(F32)
    for context, weight in zip(contexts, weights):
        total += dot(context[...], weight[...])
    state[...] = total.astype(BF16)
    leave_kernel(ids, dispatch, state, out)


def leave_kernel(ids, dispatch, state, out):
    width = out.shape[1]
    at = (ids[1] & (state.shape[1] // width - 1)) * width
    out[...] = dot(dispatch[...], state[:, pl.ds(pl.multiple_of(at, width), width)]).astype(BF16)


def make_state(ids, tokens, contexts, weights, dispatch, cuts):
    return pl.pallas_call(
        functools.partial(state_kernel, len(contexts)),
        in_specs=[WHOLE] * (1 + 2 * len(contexts)) + [SCALARS, WHOLE],
        out_specs=[WHOLE] * 2,
        out_shape=[
            jax.ShapeDtypeStruct(tokens.shape, BF16),
            jax.ShapeDtypeStruct((dispatch.shape[0], tokens.shape[1] // cuts), BF16),
        ],
        compiler_params=PARAMS,
        cost_estimate=CHEAP,
        name="state",
    )(tokens, *contexts, *weights, ids, dispatch)


def leave(ids, dispatch, state, cuts):
    return pl.pallas_call(
        leave_kernel,
        in_specs=[SCALARS, WHOLE, WHOLE],
        out_specs=WHOLE,
        out_shape=jax.ShapeDtypeStruct((dispatch.shape[0], state.shape[1] // cuts), BF16),
        compiler_params=PARAMS,
        cost_estimate=CHEAP,
        name="leave",
    )(ids, dispatch, state)


def home_kernel(experts, ids, state, dispatch, router, choice, own_a, own_b, gates, columns):
    half = own_a.shape[1]
    core = ids[1] & 1
    own_a[...] = dot(dispatch[...], state[:, pl.ds(pl.multiple_of(core * half, half), half)]).astype(BF16)
    own_b[...] = dot(dispatch[...], state[:, pl.ds(pl.multiple_of((1 - core) * half, half), half)]).astype(BF16)
    logits = dot(state[...], router[...])
    wide = lax.broadcasted_iota(jnp.int32, logits.shape, 1)
    first = jnp.sum(jnp.where(wide == choice[:, 0:1], logits, 0.0), axis=1, keepdims=True)
    second = jnp.sum(jnp.where(wide == choice[:, 1:2], logits, 0.0), axis=1, keepdims=True)
    gates[:, 0:1] = jax.nn.sigmoid(first - second)
    gates[:, 1:2] = jax.nn.sigmoid(second - first)
    width = columns.shape[1]
    columns[...] = state[:, pl.ds(pl.multiple_of(ids[1] * width, width), width)].astype(F32)


def at_home(ids, state, dispatch, router, choice, experts, width):
    tokens, features = state.shape
    slots = dispatch.shape[0]
    return pl.pallas_call(
        functools.partial(home_kernel, experts),
        in_specs=[SCALARS] + [WHOLE] * 4,
        out_specs=[WHOLE] * 4,
        out_shape=[
            jax.ShapeDtypeStruct((slots, features // 2), BF16),
            jax.ShapeDtypeStruct((slots, features // 2), BF16),
            jax.ShapeDtypeStruct((tokens, 2), F32),
            jax.ShapeDtypeStruct((tokens, width), F32),
        ],
        compiler_params=PARAMS,
        cost_estimate=CHEAP,
        name="home",
    )(ids, state, dispatch, router, choice)


def expert_kernel(order, *refs):
    ids, pieces = refs[0], refs[1 : 1 + len(order)]
    expand, shrink, keep, give, hidden = refs[1 + len(order) :]
    cuts = len(order)
    units = expand.shape[1]
    tile = min(TILE, units)
    for at in range(0, units, tile):
        total = jnp.zeros((hidden.shape[0], tile), F32)
        for index, piece in zip(order, pieces):
            width = piece.shape[1]
            rows = pl.ds(pl.multiple_of(((ids[1] & (cuts - 1)) ^ index) * width, width), width)
            total += dot(piece[...], expand[rows, at : at + tile])
        hidden[:, at : at + tile] = jnp.maximum(total, 0.0).astype(BF16)
    width = keep.shape[2]
    for j in range(keep.shape[0]):
        at = pl.multiple_of((ids[1] ^ (2 * j) ^ 1) * width, width)
        give[j] = dot(hidden[...], shrink[:, pl.ds(at, width)]).astype(BF16)
    for j in range(keep.shape[0]):
        at = pl.multiple_of((ids[1] ^ (2 * j)) * width, width)
        keep[j] = dot(hidden[...], shrink[:, pl.ds(at, width)])


def run_expert(ids, order, pieces, expand, shrink, parts):
    rows = pieces[0].shape[0]
    features, units = expand.shape
    width = features // (2 * parts)
    return pl.pallas_call(
        functools.partial(expert_kernel, tuple(order)),
        in_specs=[SCALARS] + [WHOLE] * (2 + len(pieces)),
        out_specs=[WHOLE] * 2,
        out_shape=[
            jax.ShapeDtypeStruct((parts, rows, width), F32),
            jax.ShapeDtypeStruct((parts, rows, width), BF16),
        ],
        scratch_shapes=[pltpu.VMEM((rows, units), BF16)],
        compiler_params=PARAMS,
        cost_estimate=CHEAP,
        name="expert",
    )(ids, *pieces, expand, shrink)


def combine_kernel(count, gates, base, first, second, *refs):
    parts, out = refs[:count], refs[count]
    total = parts[0][...].astype(F32)
    for part in parts[1:]:
        total += part[...].astype(F32)
    total = total.astype(BF16)
    result = base[...] + gates[:, 0:1] * dot(first[...], total) + gates[:, 1:2] * dot(second[...], total)
    out[...] = result.astype(out.dtype)


def combine(gates, base, first, second, parts, dtype):
    return pl.pallas_call(
        functools.partial(combine_kernel, len(parts)),
        in_specs=[WHOLE] * (4 + len(parts)),
        out_specs=WHOLE,
        out_shape=jax.ShapeDtypeStruct(base.shape, dtype),
        compiler_params=PARAMS,
        cost_estimate=CHEAP,
        name="combine",
    )(gates, base, first, second, *parts)


def bits_of(count):
    bits = []
    while 2 ** len(bits) < count:
        bits.insert(0, 2 ** len(bits))
    return bits


def local(
    tokens,
    encoder_states,
    source_owner,
    query_weight,
    output_weight,
    router_weight,
    expert_choice,
    expand_weight,
    shrink_weight,
):
    token_count, features = tokens.shape
    groups = lax.axis_size("expert")
    slices = lax.axis_size("mp")
    here, column = lax.axis_index("expert"), lax.axis_index("mp")
    ids = jnp.stack([here, column]).astype(jnp.int32)
    width = features // slices
    experts = expand_weight.shape[0] * groups
    capacity = max(2, 3 * token_count // experts)
    direct = groups <= DIRECT
    pairs = slices // 2

    def hop(value, along_expert, along_mp):
        if along_expert == 0 and along_mp == 0:
            return value
        moves = [
            (e * slices + m, (e ^ along_expert) * slices + (m ^ along_mp))
            for e in range(groups)
            for m in range(slices)
        ]
        return lax.ppermute(value, ("expert", "mp"), moves)

    def spread(value):
        parts = value.reshape(groups, -1, value.shape[-1])
        return lax.all_to_all(parts, "expert", 0, 0, tiled=True).reshape(value.shape)

    def after(value, other):
        return lax.optimization_barrier((value, other))[0]

    steps = range(groups) if direct else [0]

    queries, source = ask(tokens, query_weight, encoder_states[0])
    owner = source_owner[0]
    expert_bits = bits_of(groups)
    bits = bits_of(slices)
    if direct:
        own = context = attend(queries, source, token_count)
        asked, steps_of = [queries], [0]
        for bit in expert_bits:
            asked = asked + [hop(value if k == 0 else after(value, own), bit, 0) for k, value in zip(steps_of, asked)]
            steps_of = steps_of + [k ^ bit for k in steps_of]
        asked = dict(zip(steps_of, asked))
        previous, backs = own, {}
        for k in range(1, groups):
            answer = attend(after(asked[k], previous), source, token_count)
            backs[k] = hop(answer, k, 0)
            previous = answer
        for k in range(1, groups):
            context = jnp.where(owner == here ^ k, backs[k], context)
    else:
        asked = lax.all_gather(queries, "expert", axis=0, tiled=True)
        previous = attend(asked, source, token_count)
        context = lax.dynamic_slice_in_dim(spread(previous), owner * token_count, token_count, 0)

    weights, order = [output_weight], [0]
    for bit in bits:
        if bit == 1:
            weights = [after(weight, previous) for weight in weights]
        weights = weights + [hop(weight, 0, bit) for weight in weights]
        order = order + [index ^ bit for index in order]
    dispatch, first, second = route(ids, after(expert_choice, context), experts, len(steps), capacity)
    contexts = [context]
    for bit in bits:
        contexts = contexts + [hop(value if i == 0 else after(value, dispatch[0]), 0, bit) for i, value in enumerate(contexts)]

    relayed = groups // 2 if direct and pairs > 1 and groups > 1 else -1
    far = list(reversed(range(1, groups)))
    sends = ([relayed] if relayed >= 0 else []) + [k for k in far if k != relayed] if direct else [0]
    cuts = {k: slices if k == relayed else 2 for k in sends}
    leaving = {}
    for k in sends:
        if not leaving:
            state, leaving[k] = make_state(ids, tokens, contexts, weights, dispatch[k], cuts[k])
            waited = state
        else:
            waited = leaving[k] = leave(ids, dispatch[k], after(state, waited), cuts[k])
    own_a, own_b, gates, columns = at_home(
        ids, after(state, waited), dispatch[0], router_weight, expert_choice, experts, width
    )

    results = columns
    arrived = {k: hop(leaving[k], k, 0) for k in sends} if direct else {0: spread(leaving[0])}
    turns = far if direct else [0]
    inputs = {}
    if relayed >= 0:
        pieces, places = [arrived[relayed]], [0]
        for bit in bits:
            pieces = pieces + [hop(piece, 0, bit) for piece in pieces]
            places = places + [index ^ bit for index in places]
        inputs[relayed] = pieces, places

    def sum_cores(keep, give):
        return keep + hop(give, 0, 1).astype(F32)

    def send_home(k, summed):
        if k == relayed:
            total = summed[0]
            for j in range(1, pairs):
                total += hop(summed[j].astype(BF16), 0, 2 * j).astype(F32)
            return [hop(total.astype(BF16), k, 0)]
        parts = [summed[j].astype(BF16) for j in range(pairs)]
        return [hop(part, k, 2 * j) if direct else hop(spread(part), 0, 2 * j) for j, part in enumerate(parts)]

    home = {}
    turn_ids = ids
    if direct:
        keep, give = run_expert(ids, [0, 1], [own_a, own_b], expand_weight[0], shrink_weight[0], pairs)
        turn_ids = after(ids, give)
        home[0] = send_home(0, sum_cores(keep, after(give, arrived[sends[0]])))
    for k in turns:
        if k in inputs:
            pieces, places = inputs[k]
        else:
            pieces, places = [arrived[k], hop(arrived[k], 0, 1)], [0, 1]
        keep, give = run_expert(turn_ids, places, pieces, expand_weight[0], shrink_weight[0], pairs)
        summed = sum_cores(keep, give)
        home[k] = send_home(k, summed)
        turn_ids = after(ids, give)
    arrivals = ([0] if direct else []) + turns
    for k in arrivals:
        kind = BF16 if k == arrivals[-1] else F32
        results = combine(gates, results, first[k], second[k], home[k], kind)
    return results


def solution(mesh):
    return jax.shard_map(
        local,
        mesh=mesh,
        in_specs=(
            P(("groups", "expert"), None),
            P(("groups", "expert"), None, None, "mp"),
            P(("groups", "expert")),
            P(None, "mp"),
            P("mp", None),
            P(),
            P(("groups", "expert"), None),
            P("expert", None, "mp"),
            P("expert", "mp", None),
        ),
        out_specs=P(("groups", "expert"), "mp"),
        check_vma=False,
    )
```

```python
import functools

import jax
import jax.numpy as jnp
from jax import lax
from jax.experimental import pallas as pl
from jax.experimental.pallas import tpu as pltpu
from jax.sharding import PartitionSpec as P

HEAD_DIM = 128
DIRECT = 8
CUTS = 4
TILE = 256
F32, BF16 = jnp.float32, jnp.bfloat16
PARAMS = pltpu.CompilerParams(vmem_limit_bytes=20 * 2**20)
CHEAP = pl.CostEstimate(flops=0, bytes_accessed=0, transcendentals=0)
SCALARS = pl.BlockSpec(memory_space=pltpu.SMEM)
WHOLE = pl.BlockSpec(memory_space=pltpu.VMEM)


def dot(a, b, dims=((1,), (0,))):
    return lax.dot_general(a, b, (dims, ((), ())), preferred_element_type=F32)


def in_hbm(value):
    return pltpu.with_memory_space_constraint(value, pltpu.HBM)


def query_kernel(tokens, weight, source, out, staged, tokens_here, weight_here, sems):
    features = tokens.shape[1]
    depth = features // CUTS
    copies, later = [], []
    for i in range(CUTS):
        part = pl.ds(i * depth, depth)
        copies.append(
            (
                pltpu.make_async_copy(tokens.at[:, part], tokens_here.at[:, part], sems.at[0, i]),
                pltpu.make_async_copy(weight.at[part, :], weight_here.at[part, :], sems.at[1, i]),
            )
        )
        rows = pl.ds(i * (source.shape[1] // CUTS), source.shape[1] // CUTS)
        later.append(pltpu.make_async_copy(source.at[:, rows], staged.at[:, rows], sems.at[2, i]))
    for pair in copies:
        for copy in pair:
            copy.start()
    for copy in later:
        copy.start()
    total = jnp.zeros(out.shape, F32)
    for i, pair in enumerate(copies):
        for copy in pair:
            copy.wait()
        part = slice(i * depth, (i + 1) * depth)
        total += dot(tokens_here[:, part], weight_here[part, :])
    out[...] = total.astype(BF16)
    for copy in later:
        copy.wait()


def ask(tokens, weight, source):
    return pl.pallas_call(
        query_kernel,
        in_specs=[pl.BlockSpec(memory_space=pltpu.HBM)] * 3,
        out_specs=[WHOLE] * 2,
        out_shape=[
            jax.ShapeDtypeStruct((tokens.shape[0], weight.shape[1]), BF16),
            jax.ShapeDtypeStruct(source.shape, BF16),
        ],
        scratch_shapes=[
            pltpu.VMEM(tokens.shape, BF16),
            pltpu.VMEM(weight.shape, BF16),
            pltpu.SemaphoreType.DMA((3, CUTS)),
        ],
        compiler_params=PARAMS,
        cost_estimate=CHEAP,
        name="query",
    )(in_hbm(tokens), in_hbm(weight), in_hbm(source))


def attend_kernel(queries, source, out):
    for head in range(queries.shape[1] // HEAD_DIM):
        part = slice(head * HEAD_DIM, (head + 1) * HEAD_DIM)
        scores = dot(queries[:, part], source[0, :, part], ((1,), (1,)))
        top = jnp.max(scores, axis=1, keepdims=True)
        weights = jnp.exp((scores - top) * HEAD_DIM**-0.5)
        total = jnp.sum(weights, axis=1, keepdims=True)
        context = dot(weights.astype(BF16), source[1, :, part])
        out[:, part] = (context / total).astype(BF16)


def attend(queries, source, block):
    rows, width = queries.shape
    if rows == block:
        return pl.pallas_call(
            attend_kernel,
            in_specs=[WHOLE] * 2,
            out_specs=WHOLE,
            out_shape=jax.ShapeDtypeStruct((rows, width), BF16),
            compiler_params=PARAMS,
        cost_estimate=CHEAP,
            name="attend",
        )(queries, source)
    return pl.pallas_call(
        attend_kernel,
        grid=(rows // block,),
        in_specs=[
            pl.BlockSpec((block, width), lambda i: (i, 0)),
            pl.BlockSpec(source.shape, lambda i: (0, 0, 0)),
        ],
        out_specs=pl.BlockSpec((block, width), lambda i: (i, 0)),
        out_shape=jax.ShapeDtypeStruct((rows, width), BF16),
        compiler_params=PARAMS,
        cost_estimate=CHEAP,
        name="attend",
    )(queries, source)


def pick_kernel(ids, owner, *refs):
    backs, out = refs[:-1], refs[-1]
    for k, back in enumerate(backs):

        @pl.when(owner[0] == ids[0] ^ k)
        def _():
            out[...] = back[...]


def pick(ids, owner, backs):
    return pl.pallas_call(
        pick_kernel,
        in_specs=[SCALARS] * 2 + [WHOLE] * len(backs),
        out_specs=WHOLE,
        out_shape=jax.ShapeDtypeStruct(backs[0].shape, BF16),
        compiler_params=PARAMS,
        cost_estimate=CHEAP,
        name="pick",
    )(ids, owner, *backs)


def route_kernel(experts, parts, ids, choice_t, choice, *outs):
    dispatch, first, second = outs[:parts], outs[parts : 2 * parts], outs[2 * parts :]
    tokens = choice_t.shape[1]
    slots = dispatch[0].shape[0]
    capacity = slots * parts // experts
    wide = lax.broadcasted_iota(jnp.int32, (tokens, experts), 1)
    tall = lax.broadcasted_iota(jnp.int32, (experts, tokens), 0)
    i = lax.broadcasted_iota(jnp.int32, (tokens, tokens), 0)
    j = lax.broadcasted_iota(jnp.int32, (tokens, tokens), 1)
    r0, r1 = choice_t[0:1, :], choice_t[1:2, :]
    turned = dot((i == j).astype(BF16), choice_t[...].astype(F32).astype(BF16), ((1,), (1,))).astype(jnp.int32)
    choice[...] = turned
    c0, c1 = turned[:, 0:1], turned[:, 1:2]
    named = ((wide == c0) | (wide == c1)).astype(BF16)
    named_t = ((tall == r0) | (tall == r1)).astype(BF16)
    rank = dot((j < i).astype(BF16), named).astype(jnp.int32)
    rank_t = dot(named_t, (i < j).astype(BF16)).astype(jnp.int32)
    place0 = c0 * capacity + jnp.sum(jnp.where(wide == c0, rank, 0), axis=1, keepdims=True)
    place1 = c1 * capacity + jnp.sum(jnp.where(wide == c1, rank, 0), axis=1, keepdims=True)
    across0 = r0 * capacity + jnp.sum(jnp.where(tall == r0, rank_t, 0), axis=0, keepdims=True)
    across1 = r1 * capacity + jnp.sum(jnp.where(tall == r1, rank_t, 0), axis=0, keepdims=True)
    lane = lax.broadcasted_iota(jnp.int32, (tokens, slots), 1)
    row = lax.broadcasted_iota(jnp.int32, (slots, tokens), 0)
    for k in range(parts):
        base = (ids[0] ^ k) * capacity if parts > 1 else 0
        dispatch[k][...] = ((row + base == across0) | (row + base == across1)).astype(BF16)
        first[k][...] = (lane + base == place0).astype(BF16)
        second[k][...] = (lane + base == place1).astype(BF16)


def route(ids, choice, experts, parts, capacity):
    tokens = choice.shape[0]
    slots = experts * capacity // parts
    outs = pl.pallas_call(
        functools.partial(route_kernel, experts, parts),
        in_specs=[SCALARS, WHOLE],
        out_specs=[WHOLE] * (1 + 3 * parts),
        out_shape=[jax.ShapeDtypeStruct(choice.shape, jnp.int32)]
        + [jax.ShapeDtypeStruct((slots, tokens), BF16)] * parts
        + [jax.ShapeDtypeStruct((tokens, slots), BF16)] * (2 * parts),
        compiler_params=PARAMS,
        cost_estimate=CHEAP,
        name="route",
    )(ids, choice.T)
    return outs[0], outs[1 : 1 + parts], outs[1 + parts : 1 + 2 * parts], outs[1 + 2 * parts :]


def state_kernel(count, *refs):
    tokens, contexts, weights = refs[0], refs[1 : 1 + count], refs[1 + count : 1 + 2 * count]
    ids, dispatch, state, out = refs[1 + 2 * count :]
    total = tokens[...].astype(F32)
    for context, weight in zip(contexts, weights):
        total += dot(context[...], weight[...])
    state[...] = total.astype(BF16)
    leave_kernel(ids, dispatch, state, out)


def leave_kernel(ids, dispatch, state, out):
    width = out.shape[1]
    at = (ids[1] & (state.shape[1] // width - 1)) * width
    out[...] = dot(dispatch[...], state[:, pl.ds(pl.multiple_of(at, width), width)]).astype(BF16)


def make_state(ids, tokens, contexts, weights, dispatch, cuts):
    return pl.pallas_call(
        functools.partial(state_kernel, len(contexts)),
        in_specs=[WHOLE] * (1 + 2 * len(contexts)) + [SCALARS, WHOLE],
        out_specs=[WHOLE] * 2,
        out_shape=[
            jax.ShapeDtypeStruct(tokens.shape, BF16),
            jax.ShapeDtypeStruct((dispatch.shape[0], tokens.shape[1] // cuts), BF16),
        ],
        compiler_params=PARAMS,
        cost_estimate=CHEAP,
        name="state",
    )(tokens, *contexts, *weights, ids, dispatch)


def leave(ids, dispatch, state, cuts):
    return pl.pallas_call(
        leave_kernel,
        in_specs=[SCALARS, WHOLE, WHOLE],
        out_specs=WHOLE,
        out_shape=jax.ShapeDtypeStruct((dispatch.shape[0], state.shape[1] // cuts), BF16),
        compiler_params=PARAMS,
        cost_estimate=CHEAP,
        name="leave",
    )(ids, dispatch, state)


def home_kernel(experts, ids, state, dispatch, router, choice, own_a, own_b, gates, columns):
    half = own_a.shape[1]
    core = ids[1] & 1
    own_a[...] = dot(dispatch[...], state[:, pl.ds(pl.multiple_of(core * half, half), half)]).astype(BF16)
    own_b[...] = dot(dispatch[...], state[:, pl.ds(pl.multiple_of((1 - core) * half, half), half)]).astype(BF16)
    logits = dot(state[...], router[...], ((1,), (1,)))
    wide = lax.broadcasted_iota(jnp.int32, logits.shape, 1)
    first = jnp.sum(jnp.where(wide == choice[:, 0:1], logits, 0.0), axis=1, keepdims=True)
    second = jnp.sum(jnp.where(wide == choice[:, 1:2], logits, 0.0), axis=1, keepdims=True)
    gates[:, 0:1] = jax.nn.sigmoid(first - second)
    gates[:, 1:2] = jax.nn.sigmoid(second - first)
    width = columns.shape[1]
    columns[...] = state[:, pl.ds(pl.multiple_of(ids[1] * width, width), width)].astype(F32)


def at_home(ids, state, dispatch, router, choice, experts, width):
    tokens, features = state.shape
    slots = dispatch.shape[0]
    return pl.pallas_call(
        functools.partial(home_kernel, experts),
        in_specs=[SCALARS] + [WHOLE] * 4,
        out_specs=[WHOLE] * 4,
        out_shape=[
            jax.ShapeDtypeStruct((slots, features // 2), BF16),
            jax.ShapeDtypeStruct((slots, features // 2), BF16),
            jax.ShapeDtypeStruct((tokens, 2), F32),
            jax.ShapeDtypeStruct((tokens, width), F32),
        ],
        compiler_params=PARAMS,
        cost_estimate=CHEAP,
        name="home",
    )(ids, state, dispatch, router, choice)


def expert_kernel(order, *refs):
    ids, pieces = refs[0], refs[1 : 1 + len(order)]
    expand, shrink, keep, give, hidden = refs[1 + len(order) :]
    cuts = len(order)
    units = expand.shape[1]
    tile = min(TILE, units)
    for at in range(0, units, tile):
        total = jnp.zeros((hidden.shape[0], tile), F32)
        for index, piece in zip(order, pieces):
            width = piece.shape[1]
            rows = pl.ds(pl.multiple_of(((ids[1] & (cuts - 1)) ^ index) * width, width), width)
            total += dot(piece[...], expand[rows, at : at + tile])
        hidden[:, at : at + tile] = jnp.maximum(total, 0.0).astype(BF16)
    width = keep.shape[2]
    for j in range(keep.shape[0]):
        at = pl.multiple_of((ids[1] ^ (2 * j) ^ 1) * width, width)
        give[j] = dot(hidden[...], shrink[:, pl.ds(at, width)]).astype(BF16)
    for j in range(keep.shape[0]):
        at = pl.multiple_of((ids[1] ^ (2 * j)) * width, width)
        keep[j] = dot(hidden[...], shrink[:, pl.ds(at, width)])


def run_expert(ids, order, pieces, expand, shrink, parts):
    rows = pieces[0].shape[0]
    features, units = expand.shape
    width = features // (2 * parts)
    return pl.pallas_call(
        functools.partial(expert_kernel, tuple(order)),
        in_specs=[SCALARS] + [WHOLE] * (2 + len(pieces)),
        out_specs=[WHOLE] * 2,
        out_shape=[
            jax.ShapeDtypeStruct((parts, rows, width), F32),
            jax.ShapeDtypeStruct((parts, rows, width), BF16),
        ],
        scratch_shapes=[pltpu.VMEM((rows, units), BF16)],
        compiler_params=PARAMS,
        cost_estimate=CHEAP,
        name="expert",
    )(ids, *pieces, expand, shrink)


def combine_kernel(count, gates, base, first, second, *refs):
    parts, out = refs[:count], refs[count]
    total = parts[0][...].astype(F32)
    for part in parts[1:]:
        total += part[...].astype(F32)
    total = total.astype(BF16)
    result = base[...] + gates[:, 0:1] * dot(first[...], total) + gates[:, 1:2] * dot(second[...], total)
    out[...] = result.astype(out.dtype)


def combine(gates, base, first, second, parts, dtype):
    return pl.pallas_call(
        functools.partial(combine_kernel, len(parts)),
        in_specs=[WHOLE] * (4 + len(parts)),
        out_specs=WHOLE,
        out_shape=jax.ShapeDtypeStruct(base.shape, dtype),
        compiler_params=PARAMS,
        cost_estimate=CHEAP,
        name="combine",
    )(gates, base, first, second, *parts)


def bits_of(count):
    bits = []
    while 2 ** len(bits) < count:
        bits.insert(0, 2 ** len(bits))
    return bits


def local(
    tokens,
    encoder_states,
    source_owner,
    query_weight,
    output_weight,
    router_weight,
    expert_choice,
    expand_weight,
    shrink_weight,
):
    token_count, features = tokens.shape
    groups = lax.axis_size("expert")
    slices = lax.axis_size("mp")
    here, column = lax.axis_index("expert"), lax.axis_index("mp")
    ids = jnp.stack([here, column]).astype(jnp.int32)
    width = features // slices
    experts = expand_weight.shape[0] * groups
    capacity = max(2, 3 * token_count // experts)
    direct = groups <= DIRECT
    pairs = slices // 2

    def hop(value, along_expert, along_mp):
        if along_expert == 0 and along_mp == 0:
            return value
        moves = [
            (e * slices + m, (e ^ along_expert) * slices + (m ^ along_mp))
            for e in range(groups)
            for m in range(slices)
        ]
        return lax.ppermute(value, ("expert", "mp"), moves)

    def spread(value):
        parts = value.reshape(groups, -1, value.shape[-1])
        return lax.all_to_all(parts, "expert", 0, 0, tiled=True).reshape(value.shape)

    def after(value, other):
        return lax.optimization_barrier((value, other))[0]

    steps = range(groups) if direct else [0]

    queries, source = ask(after(tokens, ids), query_weight, encoder_states[0])
    expert_bits = bits_of(groups)
    bits = bits_of(slices)
    if direct:
        own = attend(queries, source, token_count)
        asked, steps_of = [queries], [0]
        for bit in expert_bits:
            asked = asked + [hop(value if k == 0 else after(value, own), bit, 0) for k, value in zip(steps_of, asked)]
            steps_of = steps_of + [k ^ bit for k in steps_of]
        asked = dict(zip(steps_of, asked))
        previous, backs = own, {}
        for k in range(1, groups):
            answer = attend(after(asked[k], previous), source, token_count)
            backs[k] = hop(answer, k, 0)
            previous = answer
        context = pick(ids, source_owner, [own] + [backs[k] for k in range(1, groups)])
    else:
        asked = lax.all_gather(queries, "expert", axis=0, tiled=True)
        previous = attend(asked, source, token_count)
        context = lax.dynamic_slice_in_dim(spread(previous), source_owner[0] * token_count, token_count, 0)

    choice, dispatch, first, second = route(ids, after(expert_choice, context), experts, len(steps), capacity)
    weights, order = [output_weight], [0]
    for bit in bits:
        if bit == 1:
            weights = [after(weight, dispatch[0]) for weight in weights]
        weights = weights + [hop(weight, 0, bit) for weight in weights]
        order = order + [index ^ bit for index in order]
    contexts = [context]
    for bit in bits:
        contexts = contexts + [hop(value if i == 0 else after(value, dispatch[0]), 0, bit) for i, value in enumerate(contexts)]

    relayed = groups // 2 if direct and pairs > 1 and groups > 1 else -1
    far = list(reversed(range(1, groups)))
    sends = ([relayed] if relayed >= 0 else []) + [k for k in far if k != relayed] if direct else [0]
    cuts = {k: slices if k == relayed else 2 for k in sends}
    leaving = {}
    for k in sends:
        if not leaving:
            state, leaving[k] = make_state(ids, tokens, contexts, weights, dispatch[k], cuts[k])
            waited = state
        else:
            waited = leaving[k] = leave(ids, dispatch[k], after(state, waited), cuts[k])
    own_a, own_b, gates, columns = at_home(
        ids, after(state, waited), dispatch[0], router_weight.T, choice, experts, width
    )

    results = columns
    arrived = {k: hop(leaving[k], k, 0) for k in sends} if direct else {0: spread(leaving[0])}
    turns = [k for k in far if k != relayed] + [k for k in far if k == relayed] if direct else [0]
    inputs = {}
    if relayed >= 0:
        pieces, places = [arrived[relayed]], [0]
        for bit in bits:
            pieces = pieces + [hop(piece, 0, bit) for piece in pieces]
            places = places + [index ^ bit for index in places]
        inputs[relayed] = pieces, places

    def sum_cores(keep, give):
        return keep + hop(give, 0, 1).astype(F32)

    def send_home(k, summed):
        if k == relayed:
            total = summed[0]
            for j in range(1, pairs):
                total += hop(summed[j].astype(BF16), 0, 2 * j).astype(F32)
            return [hop(total.astype(BF16), k, 0)]
        parts = [summed[j].astype(BF16) for j in range(pairs)]
        return [hop(part, k, 2 * j) if direct else hop(spread(part), 0, 2 * j) for j, part in enumerate(parts)]

    def gather(k, results, parts, dtype):
        return combine(gates, results, first[k], second[k], parts, dtype)

    turn_ids, home = ids, {}
    if direct:
        keep, give = run_expert(ids, [0, 1], [own_a, own_b], expand_weight[0], shrink_weight[0], pairs)
        parts = send_home(0, sum_cores(keep, after(give, arrived[sends[0]])))
        results = gather(0, results, parts, F32)
        turn_ids = after(ids, results)
    for k in turns:
        if k in inputs:
            pieces, places = inputs[k]
        else:
            pieces, places = [arrived[k], hop(arrived[k], 0, 1)], [0, 1]
        keep, give = run_expert(turn_ids, places, pieces, expand_weight[0], shrink_weight[0], pairs)
        turn_ids = after(ids, give)
        home[k] = send_home(k, sum_cores(keep, give))
    for k in turns:
        results = gather(k, results, home[k], BF16 if k == turns[-1] else F32)
    return results


def solution(mesh):
    return jax.shard_map(
        local,
        mesh=mesh,
        in_specs=(
            P(("groups", "expert"), None),
            P(("groups", "expert"), None, None, "mp"),
            P(("groups", "expert")),
            P(None, "mp"),
            P("mp", None),
            P(),
            P(("groups", "expert"), None),
            P("expert", None, "mp"),
            P("expert", "mp", None),
        ),
        out_specs=P(("groups", "expert"), "mp"),
        check_vma=False,
    )
```

```python
import functools

import jax
import jax.numpy as jnp
from jax import lax
from jax.experimental import pallas as pl
from jax.experimental.pallas import tpu as pltpu
from jax.sharding import PartitionSpec as P

HEAD_DIM = 128
DIRECT = 8
CUTS = 4
TILE = 256
F32, BF16 = jnp.float32, jnp.bfloat16
PARAMS = pltpu.CompilerParams(vmem_limit_bytes=20 * 2**20)
CHEAP = pl.CostEstimate(flops=0, bytes_accessed=0, transcendentals=0)
SCALARS = pl.BlockSpec(memory_space=pltpu.SMEM)
WHOLE = pl.BlockSpec(memory_space=pltpu.VMEM)


def dot(a, b, dims=((1,), (0,))):
    return lax.dot_general(a, b, (dims, ((), ())), preferred_element_type=F32)


def in_hbm(value):
    return pltpu.with_memory_space_constraint(value, pltpu.HBM)


def query_kernel(tokens, weight, source, out, staged, tokens_here, weight_here, sems):
    features = tokens.shape[1]
    depth = features // CUTS
    copies, later = [], []
    for i in range(CUTS):
        part = pl.ds(i * depth, depth)
        copies.append(
            (
                pltpu.make_async_copy(tokens.at[:, part], tokens_here.at[:, part], sems.at[0, i]),
                pltpu.make_async_copy(weight.at[part, :], weight_here.at[part, :], sems.at[1, i]),
            )
        )
        rows = pl.ds(i * (source.shape[1] // CUTS), source.shape[1] // CUTS)
        later.append(pltpu.make_async_copy(source.at[:, rows], staged.at[:, rows], sems.at[2, i]))
    for pair in copies:
        for copy in pair:
            copy.start()
    for copy in later:
        copy.start()
    total = jnp.zeros(out.shape, F32)
    for i, pair in enumerate(copies):
        for copy in pair:
            copy.wait()
        part = slice(i * depth, (i + 1) * depth)
        total += dot(tokens_here[:, part], weight_here[part, :])
    out[...] = total.astype(BF16)
    for copy in later:
        copy.wait()


def ask(tokens, weight, source):
    return pl.pallas_call(
        query_kernel,
        in_specs=[pl.BlockSpec(memory_space=pltpu.HBM)] * 3,
        out_specs=[WHOLE] * 2,
        out_shape=[
            jax.ShapeDtypeStruct((tokens.shape[0], weight.shape[1]), BF16),
            jax.ShapeDtypeStruct(source.shape, BF16),
        ],
        scratch_shapes=[
            pltpu.VMEM(tokens.shape, BF16),
            pltpu.VMEM(weight.shape, BF16),
            pltpu.SemaphoreType.DMA((3, CUTS)),
        ],
        compiler_params=PARAMS,
        cost_estimate=CHEAP,
        name="query",
    )(in_hbm(tokens), in_hbm(weight), in_hbm(source))


def attend_kernel(queries, source, out):
    for head in range(queries.shape[1] // HEAD_DIM):
        part = slice(head * HEAD_DIM, (head + 1) * HEAD_DIM)
        scores = dot(queries[:, part], source[0, :, part], ((1,), (1,)))
        top = jnp.max(scores, axis=1, keepdims=True)
        weights = jnp.exp((scores - top) * HEAD_DIM**-0.5)
        total = jnp.sum(weights, axis=1, keepdims=True)
        context = dot(weights.astype(BF16), source[1, :, part])
        out[:, part] = (context / total).astype(BF16)


def attend(queries, source, block):
    rows, width = queries.shape
    if rows == block:
        return pl.pallas_call(
            attend_kernel,
            in_specs=[WHOLE] * 2,
            out_specs=WHOLE,
            out_shape=jax.ShapeDtypeStruct((rows, width), BF16),
            compiler_params=PARAMS,
        cost_estimate=CHEAP,
            name="attend",
        )(queries, source)
    return pl.pallas_call(
        attend_kernel,
        grid=(rows // block,),
        in_specs=[
            pl.BlockSpec((block, width), lambda i: (i, 0)),
            pl.BlockSpec(source.shape, lambda i: (0, 0, 0)),
        ],
        out_specs=pl.BlockSpec((block, width), lambda i: (i, 0)),
        out_shape=jax.ShapeDtypeStruct((rows, width), BF16),
        compiler_params=PARAMS,
        cost_estimate=CHEAP,
        name="attend",
    )(queries, source)


def pick_kernel(ids, owner, *refs):
    backs, out = refs[:-1], refs[-1]
    for k, back in enumerate(backs):

        @pl.when(owner[0] == ids[0] ^ k)
        def _():
            out[...] = back[...]


def pick(ids, owner, backs):
    return pl.pallas_call(
        pick_kernel,
        in_specs=[SCALARS] * 2 + [WHOLE] * len(backs),
        out_specs=WHOLE,
        out_shape=jax.ShapeDtypeStruct(backs[0].shape, BF16),
        compiler_params=PARAMS,
        cost_estimate=CHEAP,
        name="pick",
    )(ids, owner, *backs)


def route_kernel(experts, parts, ids, choice_t, choice, *outs):
    dispatch, first, second = outs[:parts], outs[parts : 2 * parts], outs[2 * parts :]
    tokens = choice_t.shape[1]
    slots = dispatch[0].shape[0]
    capacity = slots * parts // experts
    wide = lax.broadcasted_iota(jnp.int32, (tokens, experts), 1)
    tall = lax.broadcasted_iota(jnp.int32, (experts, tokens), 0)
    i = lax.broadcasted_iota(jnp.int32, (tokens, tokens), 0)
    j = lax.broadcasted_iota(jnp.int32, (tokens, tokens), 1)
    r0, r1 = choice_t[0:1, :], choice_t[1:2, :]
    turned = dot((i == j).astype(BF16), choice_t[...].astype(F32).astype(BF16), ((1,), (1,))).astype(jnp.int32)
    choice[...] = turned
    c0, c1 = turned[:, 0:1], turned[:, 1:2]
    named = ((wide == c0) | (wide == c1)).astype(BF16)
    named_t = ((tall == r0) | (tall == r1)).astype(BF16)
    rank = dot((j < i).astype(BF16), named).astype(jnp.int32)
    rank_t = dot(named_t, (i < j).astype(BF16)).astype(jnp.int32)
    place0 = c0 * capacity + jnp.sum(jnp.where(wide == c0, rank, 0), axis=1, keepdims=True)
    place1 = c1 * capacity + jnp.sum(jnp.where(wide == c1, rank, 0), axis=1, keepdims=True)
    across0 = r0 * capacity + jnp.sum(jnp.where(tall == r0, rank_t, 0), axis=0, keepdims=True)
    across1 = r1 * capacity + jnp.sum(jnp.where(tall == r1, rank_t, 0), axis=0, keepdims=True)
    lane = lax.broadcasted_iota(jnp.int32, (tokens, slots), 1)
    row = lax.broadcasted_iota(jnp.int32, (slots, tokens), 0)
    for k in range(parts):
        base = (ids[0] ^ k) * capacity if parts > 1 else 0
        dispatch[k][...] = ((row + base == across0) | (row + base == across1)).astype(BF16)
        first[k][...] = (lane + base == place0).astype(BF16)
        second[k][...] = (lane + base == place1).astype(BF16)


def route(ids, choice, experts, parts, capacity):
    tokens = choice.shape[0]
    slots = experts * capacity // parts
    outs = pl.pallas_call(
        functools.partial(route_kernel, experts, parts),
        in_specs=[SCALARS, WHOLE],
        out_specs=[WHOLE] * (1 + 3 * parts),
        out_shape=[jax.ShapeDtypeStruct(choice.shape, jnp.int32)]
        + [jax.ShapeDtypeStruct((slots, tokens), BF16)] * parts
        + [jax.ShapeDtypeStruct((tokens, slots), BF16)] * (2 * parts),
        compiler_params=PARAMS,
        cost_estimate=CHEAP,
        name="route",
    )(ids, choice.T)
    return outs[0], outs[1 : 1 + parts], outs[1 + parts : 1 + 2 * parts], outs[1 + 2 * parts :]


def state_kernel(count, sends, *refs):
    ids, tokens = refs[:2]
    contexts, weights = refs[2 : 2 + count], refs[2 + count : 2 + 2 * count]
    dispatch = refs[2 + 2 * count : 2 + 2 * count + sends]
    state, outs = refs[2 + 2 * count + sends], refs[3 + 2 * count + sends :]
    total = tokens[...].astype(F32)
    for context, weight in zip(contexts, weights):
        total += dot(context[...], weight[...])
    state[...] = total.astype(BF16)
    for rows, out in zip(dispatch, outs):
        width = out.shape[1]
        at = (ids[1] & (state.shape[1] // width - 1)) * width
        out[...] = dot(rows[...], state[:, pl.ds(pl.multiple_of(at, width), width)]).astype(BF16)


def make_state(ids, tokens, contexts, weights, dispatch, cuts):
    return pl.pallas_call(
        functools.partial(state_kernel, len(contexts), len(dispatch)),
        in_specs=[SCALARS] + [WHOLE] * (1 + 2 * len(contexts) + len(dispatch)),
        out_specs=[WHOLE] * (1 + len(dispatch)),
        out_shape=[jax.ShapeDtypeStruct(tokens.shape, BF16)]
        + [jax.ShapeDtypeStruct((rows.shape[0], tokens.shape[1] // cut), BF16) for rows, cut in zip(dispatch, cuts)],
        compiler_params=PARAMS,
        cost_estimate=CHEAP,
        name="state",
    )(ids, tokens, *contexts, *weights, *dispatch)


def home_kernel(experts, ids, state, dispatch, router, choice, own_a, own_b, gates, columns):
    half = own_a.shape[1]
    core = ids[1] & 1
    own_a[...] = dot(dispatch[...], state[:, pl.ds(pl.multiple_of(core * half, half), half)]).astype(BF16)
    own_b[...] = dot(dispatch[...], state[:, pl.ds(pl.multiple_of((1 - core) * half, half), half)]).astype(BF16)
    logits = dot(state[...], router[...], ((1,), (1,)))
    wide = lax.broadcasted_iota(jnp.int32, logits.shape, 1)
    first = jnp.sum(jnp.where(wide == choice[:, 0:1], logits, 0.0), axis=1, keepdims=True)
    second = jnp.sum(jnp.where(wide == choice[:, 1:2], logits, 0.0), axis=1, keepdims=True)
    gates[:, 0:1] = jax.nn.sigmoid(first - second)
    gates[:, 1:2] = jax.nn.sigmoid(second - first)
    width = columns.shape[1]
    columns[...] = state[:, pl.ds(pl.multiple_of(ids[1] * width, width), width)].astype(F32)


def at_home(ids, state, dispatch, router, choice, experts, width):
    tokens, features = state.shape
    slots = dispatch.shape[0]
    return pl.pallas_call(
        functools.partial(home_kernel, experts),
        in_specs=[SCALARS] + [WHOLE] * 4,
        out_specs=[WHOLE] * 4,
        out_shape=[
            jax.ShapeDtypeStruct((slots, features // 2), BF16),
            jax.ShapeDtypeStruct((slots, features // 2), BF16),
            jax.ShapeDtypeStruct((tokens, 2), F32),
            jax.ShapeDtypeStruct((tokens, width), F32),
        ],
        compiler_params=PARAMS,
        cost_estimate=CHEAP,
        name="home",
    )(ids, state, dispatch, router, choice)


def expert_kernel(order, blocks, *refs):
    cuts = len(order)
    ids, pieces = refs[0], refs[1 : 1 + blocks * cuts]
    expand, shrink, keep, give, rows_here, hidden = refs[1 + blocks * cuts :]
    count, width = pieces[0].shape
    for block in range(blocks):
        for i in range(cuts):
            rows_here[i, block * count : (block + 1) * count] = pieces[block * cuts + i][...]
    units = expand.shape[1]
    tile = min(TILE, units)
    for at in range(0, units, tile):
        total = jnp.zeros((hidden.shape[0], tile), F32)
        for i, index in enumerate(order):
            part = pl.ds(pl.multiple_of(((ids[1] & (cuts - 1)) ^ index) * width, width), width)
            total += dot(rows_here[i], expand[part, at : at + tile])
        hidden[:, at : at + tile] = jnp.maximum(total, 0.0).astype(BF16)
    width = keep.shape[2]
    for j in range(keep.shape[0]):
        at = pl.multiple_of((ids[1] ^ (2 * j) ^ 1) * width, width)
        give[j] = dot(hidden[...], shrink[:, pl.ds(at, width)]).astype(BF16)
    for j in range(keep.shape[0]):
        at = pl.multiple_of((ids[1] ^ (2 * j)) * width, width)
        keep[j] = dot(hidden[...], shrink[:, pl.ds(at, width)])


def run_expert(ids, order, blocks, expand, shrink, parts):
    pieces = [piece for block in blocks for piece in block]
    count, piece_width = pieces[0].shape
    rows = count * len(blocks)
    features, units = expand.shape
    width = features // (2 * parts)
    return pl.pallas_call(
        functools.partial(expert_kernel, tuple(order), len(blocks)),
        in_specs=[SCALARS] + [WHOLE] * (2 + len(pieces)),
        out_specs=[WHOLE] * 2,
        out_shape=[
            jax.ShapeDtypeStruct((parts, rows, width), F32),
            jax.ShapeDtypeStruct((parts, rows, width), BF16),
        ],
        scratch_shapes=[pltpu.VMEM((len(order), rows, piece_width), BF16), pltpu.VMEM((rows, units), BF16)],
        compiler_params=PARAMS,
        cost_estimate=CHEAP,
        name="expert",
    )(ids, *pieces, expand, shrink)


def combine_kernel(count, gates, base, first, second, *refs):
    parts, out = refs[:count], refs[count]
    total = parts[0][...].astype(F32)
    for part in parts[1:]:
        total += part[...].astype(F32)
    total = total.astype(BF16)
    result = base[...] + gates[:, 0:1] * dot(first[...], total) + gates[:, 1:2] * dot(second[...], total)
    out[...] = result.astype(out.dtype)


def combine(gates, base, first, second, parts, dtype):
    return pl.pallas_call(
        functools.partial(combine_kernel, len(parts)),
        in_specs=[WHOLE] * (4 + len(parts)),
        out_specs=WHOLE,
        out_shape=jax.ShapeDtypeStruct(base.shape, dtype),
        compiler_params=PARAMS,
        cost_estimate=CHEAP,
        name="combine",
    )(gates, base, first, second, *parts)


def bits_of(count):
    bits = []
    while 2 ** len(bits) < count:
        bits.insert(0, 2 ** len(bits))
    return bits


def local(
    tokens,
    encoder_states,
    source_owner,
    query_weight,
    output_weight,
    router_weight,
    expert_choice,
    expand_weight,
    shrink_weight,
):
    token_count, features = tokens.shape
    groups = lax.axis_size("expert")
    slices = lax.axis_size("mp")
    here, column = lax.axis_index("expert"), lax.axis_index("mp")
    ids = jnp.stack([here, column]).astype(jnp.int32)
    width = features // slices
    experts = expand_weight.shape[0] * groups
    capacity = max(2, 3 * token_count // experts)
    direct = groups <= DIRECT
    pairs = slices // 2
    slots = capacity if direct else experts * capacity

    def hop(value, along_expert, along_mp):
        if along_expert == 0 and along_mp == 0:
            return value
        moves = [
            (e * slices + m, (e ^ along_expert) * slices + (m ^ along_mp))
            for e in range(groups)
            for m in range(slices)
        ]
        return lax.ppermute(value, ("expert", "mp"), moves)

    def spread(value):
        parts = value.reshape(groups, -1, value.shape[-1])
        return lax.all_to_all(parts, "expert", 0, 0, tiled=True).reshape(value.shape)

    def after(value, other):
        return lax.optimization_barrier((value, other))[0]

    steps = range(groups) if direct else [0]

    queries, source = ask(after(tokens, ids), query_weight, encoder_states[0])
    expert_bits = bits_of(groups)
    bits = bits_of(slices)
    if direct:
        own = attend(queries, source, token_count)
        asked, steps_of = [queries], [0]
        for bit in expert_bits:
            asked = asked + [hop(value if k == 0 else after(value, own), bit, 0) for k, value in zip(steps_of, asked)]
            steps_of = steps_of + [k ^ bit for k in steps_of]
        asked = dict(zip(steps_of, asked))
        previous, backs = own, {}
        for k in range(1, groups):
            answer = attend(after(asked[k], previous), source, token_count)
            backs[k] = hop(answer, k, 0)
            previous = answer
        context = pick(ids, source_owner, [own] + [backs[k] for k in range(1, groups)])
    else:
        asked = lax.all_gather(queries, "expert", axis=0, tiled=True)
        previous = attend(asked, source, token_count)
        context = lax.dynamic_slice_in_dim(spread(previous), source_owner[0] * token_count, token_count, 0)

    choice, dispatch, first, second = route(ids, after(expert_choice, previous), experts, len(steps), capacity)
    weights, order = [output_weight], [0]
    for bit in bits:
        if bit == 1:
            weights = [after(weight, context) for weight in weights]
        weights = weights + [hop(weight, 0, bit) for weight in weights]
        order = order + [index ^ bit for index in order]
    contexts = [context]
    for bit in bits:
        contexts = contexts + [hop(value if i == 0 else after(value, dispatch[0]), 0, bit) for i, value in enumerate(contexts)]

    relayed = groups // 2 if direct and pairs > 1 and groups > 1 else -1
    rest = [k for k in reversed(range(1, groups)) if k != relayed]
    sends = ([relayed] if relayed >= 0 else []) + rest if direct else [0]
    cuts = [slices if k == relayed else 2 for k in sends]
    state, *leaving = make_state(ids, tokens, contexts, weights, [dispatch[k] for k in sends], cuts)
    own_a, own_b, gates, columns = at_home(
        ids, state, dispatch[0], router_weight.T, choice, experts, width
    )
    expert = functools.partial(run_expert, expand=expand_weight[0], shrink=shrink_weight[0], parts=pairs)

    def sum_cores(keep, give):
        return keep + hop(give, 0, 1).astype(F32)

    def send_home(k, summed):
        if k == relayed:
            total = summed[0]
            for j in range(1, pairs):
                total += hop(summed[j].astype(BF16), 0, 2 * j).astype(F32)
            return [hop(total.astype(BF16), k, 0)]
        parts = [summed[j].astype(BF16) for j in range(pairs)]
        return [hop(part, k, 2 * j) if direct else hop(spread(part), 0, 2 * j) for j, part in enumerate(parts)]

    home = {}
    if direct:
        arrived = {k: hop(rows, k, 0) for k, rows in zip(sends, leaving)}
        keep, give = expert(ids, [0, 1], [[own_a, own_b]])
        if sends:
            give = after(give, arrived[sends[0]])
        home[0] = send_home(0, sum_cores(keep, give))
        turn_ids = after(ids, give)
        if rest:
            mine = [arrived[k] for k in rest]
            keep, give = expert(turn_ids, [0, 1], [[rows, hop(rows, 0, 1)] for rows in mine])
            turn_ids = after(ids, give)
            summed = sum_cores(keep, give)
            for i, k in enumerate(rest):
                home[k] = send_home(k, summed[:, i * slots : (i + 1) * slots])
        if relayed >= 0:
            pieces, places = [arrived[relayed]], [0]
            for bit in bits:
                pieces = pieces + [hop(piece, 0, bit) for piece in pieces]
                places = places + [index ^ bit for index in places]
            keep, give = expert(turn_ids, places, [pieces])
            home[relayed] = send_home(relayed, sum_cores(keep, give))
        order = [0] + rest + ([relayed] if relayed >= 0 else [])
    else:
        mine = spread(leaving[0])
        keep, give = expert(ids, [0, 1], [[mine, hop(mine, 0, 1)]])
        home[0] = send_home(0, sum_cores(keep, give))
        order = [0]
    results = columns
    for k in order:
        results = combine(gates, results, first[k], second[k], home[k], BF16 if k == order[-1] else F32)
    return results


def solution(mesh):
    return jax.shard_map(
        local,
        mesh=mesh,
        in_specs=(
            P(("groups", "expert"), None),
            P(("groups", "expert"), None, None, "mp"),
            P(("groups", "expert")),
            P(None, "mp"),
            P("mp", None),
            P(),
            P(("groups", "expert"), None),
            P("expert", None, "mp"),
            P("expert", "mp", None),
        ),
        out_specs=P(("groups", "expert"), "mp"),
        check_vma=False,
    )
```

```python
import functools

import jax
import jax.numpy as jnp
from jax import lax
from jax.experimental import pallas as pl
from jax.experimental.pallas import tpu as pltpu
from jax.sharding import PartitionSpec as P

HEAD_DIM = 128
DIRECT = 8
CUTS = 4
TILE = 256
F32, BF16 = jnp.float32, jnp.bfloat16
PARAMS = pltpu.CompilerParams(vmem_limit_bytes=20 * 2**20)
CHEAP = pl.CostEstimate(flops=0, bytes_accessed=0, transcendentals=0)
SCALARS = pl.BlockSpec(memory_space=pltpu.SMEM)
WHOLE = pl.BlockSpec(memory_space=pltpu.VMEM)


def dot(a, b, dims=((1,), (0,))):
    return lax.dot_general(a, b, (dims, ((), ())), preferred_element_type=F32)


def in_hbm(value):
    return pltpu.with_memory_space_constraint(value, pltpu.HBM)


def query_kernel(tokens, weight, source, out, staged, tokens_here, weight_here, sems):
    features = tokens.shape[1]
    depth = features // CUTS
    copies, later = [], []
    for i in range(CUTS):
        part = pl.ds(i * depth, depth)
        copies.append(
            (
                pltpu.make_async_copy(tokens.at[:, part], tokens_here.at[:, part], sems.at[0, i]),
                pltpu.make_async_copy(weight.at[part, :], weight_here.at[part, :], sems.at[1, i]),
            )
        )
        rows = pl.ds(i * (source.shape[1] // CUTS), source.shape[1] // CUTS)
        later.append(pltpu.make_async_copy(source.at[:, rows], staged.at[:, rows], sems.at[2, i]))
    for pair in copies:
        for copy in pair:
            copy.start()
    for copy in later:
        copy.start()
    total = jnp.zeros(out.shape, F32)
    for i, pair in enumerate(copies):
        for copy in pair:
            copy.wait()
        part = slice(i * depth, (i + 1) * depth)
        total += dot(tokens_here[:, part], weight_here[part, :])
    out[...] = total.astype(BF16)
    for copy in later:
        copy.wait()


def ask(tokens, weight, source):
    return pl.pallas_call(
        query_kernel,
        in_specs=[pl.BlockSpec(memory_space=pltpu.HBM)] * 3,
        out_specs=[WHOLE] * 2,
        out_shape=[
            jax.ShapeDtypeStruct((tokens.shape[0], weight.shape[1]), BF16),
            jax.ShapeDtypeStruct(source.shape, BF16),
        ],
        scratch_shapes=[
            pltpu.VMEM(tokens.shape, BF16),
            pltpu.VMEM(weight.shape, BF16),
            pltpu.SemaphoreType.DMA((3, CUTS)),
        ],
        compiler_params=PARAMS,
        cost_estimate=CHEAP,
        name="query",
    )(in_hbm(tokens), in_hbm(weight), in_hbm(source))


def attend_kernel(queries, source, out):
    for head in range(queries.shape[1] // HEAD_DIM):
        part = slice(head * HEAD_DIM, (head + 1) * HEAD_DIM)
        scores = dot(queries[:, part], source[0, :, part], ((1,), (1,)))
        top = jnp.max(scores, axis=1, keepdims=True)
        weights = jnp.exp((scores - top) * HEAD_DIM**-0.5)
        total = jnp.sum(weights, axis=1, keepdims=True)
        context = dot(weights.astype(BF16), source[1, :, part])
        out[:, part] = (context / total).astype(BF16)


def attend(queries, source, block):
    rows, width = queries.shape
    if rows == block:
        return pl.pallas_call(
            attend_kernel,
            in_specs=[WHOLE] * 2,
            out_specs=WHOLE,
            out_shape=jax.ShapeDtypeStruct((rows, width), BF16),
            compiler_params=PARAMS,
        cost_estimate=CHEAP,
            name="attend",
        )(queries, source)
    return pl.pallas_call(
        attend_kernel,
        grid=(rows // block,),
        in_specs=[
            pl.BlockSpec((block, width), lambda i: (i, 0)),
            pl.BlockSpec(source.shape, lambda i: (0, 0, 0)),
        ],
        out_specs=pl.BlockSpec((block, width), lambda i: (i, 0)),
        out_shape=jax.ShapeDtypeStruct((rows, width), BF16),
        compiler_params=PARAMS,
        cost_estimate=CHEAP,
        name="attend",
    )(queries, source)


def pick_kernel(ids, owner, *refs):
    backs, out = refs[:-1], refs[-1]
    for k, back in enumerate(backs):

        @pl.when(owner[0] == ids[0] ^ k)
        def _():
            out[...] = back[...]


def pick(ids, owner, backs):
    return pl.pallas_call(
        pick_kernel,
        in_specs=[SCALARS] * 2 + [WHOLE] * len(backs),
        out_specs=WHOLE,
        out_shape=jax.ShapeDtypeStruct(backs[0].shape, BF16),
        compiler_params=PARAMS,
        cost_estimate=CHEAP,
        name="pick",
    )(ids, owner, *backs)


def route_kernel(experts, parts, ids, choice_t, choice, *outs):
    dispatch, first, second = outs[:parts], outs[parts : 2 * parts], outs[2 * parts :]
    tokens = choice_t.shape[1]
    slots = dispatch[0].shape[0]
    capacity = slots * parts // experts
    wide = lax.broadcasted_iota(jnp.int32, (tokens, experts), 1)
    tall = lax.broadcasted_iota(jnp.int32, (experts, tokens), 0)
    i = lax.broadcasted_iota(jnp.int32, (tokens, tokens), 0)
    j = lax.broadcasted_iota(jnp.int32, (tokens, tokens), 1)
    r0, r1 = choice_t[0:1, :], choice_t[1:2, :]
    turned = dot((i == j).astype(BF16), choice_t[...].astype(F32).astype(BF16), ((1,), (1,))).astype(jnp.int32)
    choice[...] = turned
    c0, c1 = turned[:, 0:1], turned[:, 1:2]
    named = ((wide == c0) | (wide == c1)).astype(BF16)
    named_t = ((tall == r0) | (tall == r1)).astype(BF16)
    rank = dot((j < i).astype(BF16), named).astype(jnp.int32)
    rank_t = dot(named_t, (i < j).astype(BF16)).astype(jnp.int32)
    place0 = c0 * capacity + jnp.sum(jnp.where(wide == c0, rank, 0), axis=1, keepdims=True)
    place1 = c1 * capacity + jnp.sum(jnp.where(wide == c1, rank, 0), axis=1, keepdims=True)
    across0 = r0 * capacity + jnp.sum(jnp.where(tall == r0, rank_t, 0), axis=0, keepdims=True)
    across1 = r1 * capacity + jnp.sum(jnp.where(tall == r1, rank_t, 0), axis=0, keepdims=True)
    lane = lax.broadcasted_iota(jnp.int32, (tokens, slots), 1)
    row = lax.broadcasted_iota(jnp.int32, (slots, tokens), 0)
    for k in range(parts):
        base = (ids[0] ^ k) * capacity if parts > 1 else 0
        dispatch[k][...] = ((row + base == across0) | (row + base == across1)).astype(BF16)
        first[k][...] = (lane + base == place0).astype(BF16)
        second[k][...] = (lane + base == place1).astype(BF16)


def route(ids, choice, experts, parts, capacity):
    tokens = choice.shape[0]
    slots = experts * capacity // parts
    outs = pl.pallas_call(
        functools.partial(route_kernel, experts, parts),
        in_specs=[SCALARS, WHOLE],
        out_specs=[WHOLE] * (1 + 3 * parts),
        out_shape=[jax.ShapeDtypeStruct(choice.shape, jnp.int32)]
        + [jax.ShapeDtypeStruct((slots, tokens), BF16)] * parts
        + [jax.ShapeDtypeStruct((tokens, slots), BF16)] * (2 * parts),
        compiler_params=PARAMS,
        cost_estimate=CHEAP,
        name="route",
    )(ids, choice.T)
    return outs[0], outs[1 : 1 + parts], outs[1 + parts : 1 + 2 * parts], outs[1 + 2 * parts :]


def state_kernel(count, sends, *refs):
    ids, tokens = refs[:2]
    contexts, weights = refs[2 : 2 + count], refs[2 + count : 2 + 2 * count]
    dispatch = refs[2 + 2 * count : 2 + 2 * count + sends]
    state, outs = refs[2 + 2 * count + sends], refs[3 + 2 * count + sends :]
    total = tokens[...].astype(F32)
    for context, weight in zip(contexts, weights):
        total += dot(context[...], weight[...])
    state[...] = total.astype(BF16)
    for rows, out in zip(dispatch, outs):
        width = out.shape[1]
        at = (ids[1] & (state.shape[1] // width - 1)) * width
        out[...] = dot(rows[...], state[:, pl.ds(pl.multiple_of(at, width), width)]).astype(BF16)


def make_state(ids, tokens, contexts, weights, dispatch, cuts):
    return pl.pallas_call(
        functools.partial(state_kernel, len(contexts), len(dispatch)),
        in_specs=[SCALARS] + [WHOLE] * (1 + 2 * len(contexts) + len(dispatch)),
        out_specs=[WHOLE] * (1 + len(dispatch)),
        out_shape=[jax.ShapeDtypeStruct(tokens.shape, BF16)]
        + [jax.ShapeDtypeStruct((rows.shape[0], tokens.shape[1] // cut), BF16) for rows, cut in zip(dispatch, cuts)],
        compiler_params=PARAMS,
        cost_estimate=CHEAP,
        name="state",
    )(ids, tokens, *contexts, *weights, *dispatch)


def home_kernel(experts, ids, state, dispatch, router, choice, own_a, own_b, gates, columns):
    half = own_a.shape[1]
    core = ids[1] & 1
    own_a[...] = dot(dispatch[...], state[:, pl.ds(pl.multiple_of(core * half, half), half)]).astype(BF16)
    own_b[...] = dot(dispatch[...], state[:, pl.ds(pl.multiple_of((1 - core) * half, half), half)]).astype(BF16)
    logits = dot(state[...], router[...], ((1,), (1,)))
    wide = lax.broadcasted_iota(jnp.int32, logits.shape, 1)
    first = jnp.sum(jnp.where(wide == choice[:, 0:1], logits, 0.0), axis=1, keepdims=True)
    second = jnp.sum(jnp.where(wide == choice[:, 1:2], logits, 0.0), axis=1, keepdims=True)
    gates[:, 0:1] = jax.nn.sigmoid(first - second)
    gates[:, 1:2] = jax.nn.sigmoid(second - first)
    width = columns.shape[1]
    columns[...] = state[:, pl.ds(pl.multiple_of(ids[1] * width, width), width)].astype(F32)


def at_home(ids, state, dispatch, router, choice, experts, width):
    tokens, features = state.shape
    slots = dispatch.shape[0]
    return pl.pallas_call(
        functools.partial(home_kernel, experts),
        in_specs=[SCALARS] + [WHOLE] * 4,
        out_specs=[WHOLE] * 4,
        out_shape=[
            jax.ShapeDtypeStruct((slots, features // 2), BF16),
            jax.ShapeDtypeStruct((slots, features // 2), BF16),
            jax.ShapeDtypeStruct((tokens, 2), F32),
            jax.ShapeDtypeStruct((tokens, width), F32),
        ],
        compiler_params=PARAMS,
        cost_estimate=CHEAP,
        name="home",
    )(ids, state, dispatch, router, choice)


def expert_kernel(orders, *refs):
    blocks, at = [], 1
    for order in orders:
        blocks.append(refs[at : at + len(order)])
        at += len(order)
    ids = refs[0]
    expand, shrink, keep, give, rows_here, hidden = refs[at:]
    count = blocks[0][0].shape[0]
    for block, (order, pieces) in enumerate(zip(orders, blocks)):
        for index, piece in zip(order, pieces):
            width = piece.shape[1]
            part = pl.ds(pl.multiple_of(((ids[1] & (len(order) - 1)) ^ index) * width, width), width)
            rows_here[block * count : (block + 1) * count, part] = piece[...]
    units = expand.shape[1]
    tile = min(TILE, units)
    for at in range(0, units, tile):
        total = dot(rows_here[...], expand[:, at : at + tile])
        hidden[:, at : at + tile] = jnp.maximum(total, 0.0).astype(BF16)
    width = keep.shape[2]
    for j in range(keep.shape[0]):
        at = pl.multiple_of((ids[1] ^ (2 * j) ^ 1) * width, width)
        give[j] = dot(hidden[...], shrink[:, pl.ds(at, width)]).astype(BF16)
    for j in range(keep.shape[0]):
        at = pl.multiple_of((ids[1] ^ (2 * j)) * width, width)
        keep[j] = dot(hidden[...], shrink[:, pl.ds(at, width)])


def run_expert(ids, orders, blocks, expand, shrink, parts):
    pieces = [piece for block in blocks for piece in block]
    rows = pieces[0].shape[0] * len(blocks)
    features, units = expand.shape
    width = features // (2 * parts)
    return pl.pallas_call(
        functools.partial(expert_kernel, tuple(map(tuple, orders))),
        in_specs=[SCALARS] + [WHOLE] * (2 + len(pieces)),
        out_specs=[WHOLE] * 2,
        out_shape=[
            jax.ShapeDtypeStruct((parts, rows, width), F32),
            jax.ShapeDtypeStruct((parts, rows, width), BF16),
        ],
        scratch_shapes=[pltpu.VMEM((rows, features), BF16), pltpu.VMEM((rows, units), BF16)],
        compiler_params=PARAMS,
        cost_estimate=CHEAP,
        name="expert",
    )(ids, *pieces, expand, shrink)


def combine_kernel(count, gates, base, first, second, *refs):
    parts, out = refs[:count], refs[count]
    total = parts[0][...].astype(F32)
    for part in parts[1:]:
        total += part[...].astype(F32)
    total = total.astype(BF16)
    result = base[...] + gates[:, 0:1] * dot(first[...], total) + gates[:, 1:2] * dot(second[...], total)
    out[...] = result.astype(out.dtype)


def combine(gates, base, first, second, parts, dtype):
    return pl.pallas_call(
        functools.partial(combine_kernel, len(parts)),
        in_specs=[WHOLE] * (4 + len(parts)),
        out_specs=WHOLE,
        out_shape=jax.ShapeDtypeStruct(base.shape, dtype),
        compiler_params=PARAMS,
        cost_estimate=CHEAP,
        name="combine",
    )(gates, base, first, second, *parts)


def bits_of(count):
    bits = []
    while 2 ** len(bits) < count:
        bits.insert(0, 2 ** len(bits))
    return bits


def local(
    tokens,
    encoder_states,
    source_owner,
    query_weight,
    output_weight,
    router_weight,
    expert_choice,
    expand_weight,
    shrink_weight,
):
    token_count, features = tokens.shape
    groups = lax.axis_size("expert")
    slices = lax.axis_size("mp")
    here, column = lax.axis_index("expert"), lax.axis_index("mp")
    ids = jnp.stack([here, column]).astype(jnp.int32)
    width = features // slices
    experts = expand_weight.shape[0] * groups
    capacity = max(2, 3 * token_count // experts)
    direct = groups <= DIRECT
    pairs = slices // 2
    slots = capacity if direct else experts * capacity

    def hop(value, along_expert, along_mp):
        if along_expert == 0 and along_mp == 0:
            return value
        moves = [
            (e * slices + m, (e ^ along_expert) * slices + (m ^ along_mp))
            for e in range(groups)
            for m in range(slices)
        ]
        return lax.ppermute(value, ("expert", "mp"), moves)

    def spread(value):
        parts = value.reshape(groups, -1, value.shape[-1])
        return lax.all_to_all(parts, "expert", 0, 0, tiled=True).reshape(value.shape)

    def after(value, other):
        return lax.optimization_barrier((value, other))[0]

    steps = range(groups) if direct else [0]

    queries, source = ask(after(tokens, ids), query_weight, encoder_states[0])
    expert_bits = bits_of(groups)
    bits = bits_of(slices)
    if direct:
        own = attend(queries, source, token_count)
        asked, steps_of = [queries], [0]
        for bit in expert_bits:
            asked = asked + [hop(value if k == 0 else after(value, own), bit, 0) for k, value in zip(steps_of, asked)]
            steps_of = steps_of + [k ^ bit for k in steps_of]
        asked = dict(zip(steps_of, asked))
        previous, backs = own, {}
        for k in range(1, groups):
            answer = attend(after(asked[k], previous), source, token_count)
            backs[k] = hop(answer, k, 0)
            previous = answer
        swap_after = backs.get(1, own)
        context = pick(ids, source_owner, [own] + [backs[k] for k in range(1, groups)])
    else:
        asked = lax.all_gather(queries, "expert", axis=0, tiled=True)
        previous = attend(asked, source, token_count)
        swap_after = previous
        context = lax.dynamic_slice_in_dim(spread(previous), source_owner[0] * token_count, token_count, 0)

    choice, dispatch, first, second = route(ids, after(expert_choice, previous), experts, len(steps), capacity)
    weights, order = [output_weight], [0]
    for bit in bits:
        if bit == 1:
            weights = [after(weight, swap_after) for weight in weights]
        weights = weights + [hop(weight, 0, bit) for weight in weights]
        order = order + [index ^ bit for index in order]
    contexts = [context]
    for bit in bits:
        contexts = contexts + [hop(value if i == 0 else after(value, dispatch[0]), 0, bit) for i, value in enumerate(contexts)]

    relayed = groups // 2 if direct and pairs > 1 and groups > 1 else -1
    rest = [k for k in reversed(range(1, groups)) if k != relayed]
    sends = ([relayed] if relayed >= 0 else []) + rest if direct else [0]
    cuts = [slices if k == relayed else 2 for k in sends]
    state, *leaving = make_state(ids, tokens, contexts, weights, [dispatch[k] for k in sends], cuts)
    own_a, own_b, gates, columns = at_home(
        ids, state, dispatch[0], router_weight.T, choice, experts, width
    )
    expert = functools.partial(run_expert, expand=expand_weight[0], shrink=shrink_weight[0], parts=pairs)

    def sum_cores(keep, give):
        return keep + hop(give, 0, 1).astype(F32)

    def send_home(k, summed, earlier=None):
        if k > 1:
            total = summed[0]
            for j in range(1, pairs):
                other = hop(summed[j].astype(BF16), 0, 2 * j)
                total += (other if earlier is None else after(other, earlier)).astype(F32)
            return [total.astype(BF16)]
        parts = [summed[j].astype(BF16) for j in range(pairs)]
        return [hop(part, k, 2 * j) if direct else hop(spread(part), 0, 2 * j) for j, part in enumerate(parts)]

    home = {}
    if direct:
        arrived = {k: hop(rows, k, 0) for k, rows in zip(sends, leaving)}
        keep, give = expert(ids, [[0, 1]], [[own_a, own_b]])
        turn_ids = after(ids, give)
        used = {k: after(rows, give) for k, rows in arrived.items()}
        if sends:
            give = after(give, arrived[sends[0]])
        home[0] = send_home(0, sum_cores(keep, give))
        order = [*rest, relayed] if relayed >= 0 else rest
        blocks, orders = [], []
        for k in order:
            pieces, places = [used[k]], [0]
            for bit in bits if k == relayed else [1]:
                pieces = pieces + [hop(piece, 0, bit) for piece in pieces]
                places = places + [index ^ bit for index in places]
            blocks.append(pieces)
            orders.append(places)
        if order:
            summed = sum_cores(*expert(turn_ids, orders, blocks))
            earlier = None
            for k in sorted(order, reverse=True):
                i = order.index(k)
                home[k] = send_home(k, summed[:, i * slots : (i + 1) * slots], earlier)
                if k > 1:
                    earlier = home[k][0]
                    home[k] = [hop(earlier, k, 0)]
        order = [0] + sorted(order, key=lambda k: (k > 1, -k))
    else:
        mine = spread(leaving[0])
        home[0] = send_home(0, sum_cores(*expert(ids, [[0, 1]], [[mine, hop(mine, 0, 1)]])))
        order = [0]
    results = columns
    for k in order:
        results = combine(gates, results, first[k], second[k], home[k], BF16 if k == order[-1] else F32)
    return results


def solution(mesh):
    return jax.shard_map(
        local,
        mesh=mesh,
        in_specs=(
            P(("groups", "expert"), None),
            P(("groups", "expert"), None, None, "mp"),
            P(("groups", "expert")),
            P(None, "mp"),
            P("mp", None),
            P(),
            P(("groups", "expert"), None),
            P("expert", None, "mp"),
            P("expert", "mp", None),
        ),
        out_specs=P(("groups", "expert"), "mp"),
        check_vma=False,
    )
```

```python
import functools

import jax
import jax.numpy as jnp
from jax import lax
from jax.experimental import pallas as pl
from jax.experimental.pallas import tpu as pltpu
from jax.sharding import PartitionSpec as P

HEAD_DIM = 128
DIRECT = 8
CUTS = 4
TILE = 256
F32, BF16 = jnp.float32, jnp.bfloat16
PARAMS = pltpu.CompilerParams(vmem_limit_bytes=20 * 2**20)
CHEAP = pl.CostEstimate(flops=0, bytes_accessed=0, transcendentals=0)
SCALARS = pl.BlockSpec(memory_space=pltpu.SMEM)
WHOLE = pl.BlockSpec(memory_space=pltpu.VMEM)


def dot(a, b, dims=((1,), (0,))):
    return lax.dot_general(a, b, (dims, ((), ())), preferred_element_type=F32)


def in_hbm(value):
    return pltpu.with_memory_space_constraint(value, pltpu.HBM)


def query_kernel(tokens, weight, source, out, staged, tokens_here, weight_here, sems):
    features = tokens.shape[1]
    depth = features // CUTS
    copies, later = [], []
    for i in range(CUTS):
        part = pl.ds(i * depth, depth)
        copies.append(
            (
                pltpu.make_async_copy(tokens.at[:, part], tokens_here.at[:, part], sems.at[0, i]),
                pltpu.make_async_copy(weight.at[part, :], weight_here.at[part, :], sems.at[1, i]),
            )
        )
        rows = pl.ds(i * (source.shape[1] // CUTS), source.shape[1] // CUTS)
        later.append(pltpu.make_async_copy(source.at[:, rows], staged.at[:, rows], sems.at[2, i]))
    for pair in copies:
        for copy in pair:
            copy.start()
    for copy in later:
        copy.start()
    total = jnp.zeros(out.shape, F32)
    for i, pair in enumerate(copies):
        for copy in pair:
            copy.wait()
        part = slice(i * depth, (i + 1) * depth)
        total += dot(tokens_here[:, part], weight_here[part, :])
    out[...] = total.astype(BF16)
    for copy in later:
        copy.wait()


def ask(tokens, weight, source):
    return pl.pallas_call(
        query_kernel,
        in_specs=[pl.BlockSpec(memory_space=pltpu.HBM)] * 3,
        out_specs=[WHOLE] * 2,
        out_shape=[
            jax.ShapeDtypeStruct((tokens.shape[0], weight.shape[1]), BF16),
            jax.ShapeDtypeStruct(source.shape, BF16),
        ],
        scratch_shapes=[
            pltpu.VMEM(tokens.shape, BF16),
            pltpu.VMEM(weight.shape, BF16),
            pltpu.SemaphoreType.DMA((3, CUTS)),
        ],
        compiler_params=PARAMS,
        cost_estimate=CHEAP,
        name="query",
    )(in_hbm(tokens), in_hbm(weight), in_hbm(source))


def attend_kernel(queries, source, out):
    for head in range(queries.shape[1] // HEAD_DIM):
        part = slice(head * HEAD_DIM, (head + 1) * HEAD_DIM)
        scores = dot(queries[:, part], source[0, :, part], ((1,), (1,)))
        top = jnp.max(scores, axis=1, keepdims=True)
        weights = jnp.exp((scores - top) * HEAD_DIM**-0.5)
        total = jnp.sum(weights, axis=1, keepdims=True)
        context = dot(weights.astype(BF16), source[1, :, part])
        out[:, part] = (context / total).astype(BF16)


def attend(queries, source, block):
    rows, width = queries.shape
    if rows == block:
        return pl.pallas_call(
            attend_kernel,
            in_specs=[WHOLE] * 2,
            out_specs=WHOLE,
            out_shape=jax.ShapeDtypeStruct((rows, width), BF16),
            compiler_params=PARAMS,
        cost_estimate=CHEAP,
            name="attend",
        )(queries, source)
    return pl.pallas_call(
        attend_kernel,
        grid=(rows // block,),
        in_specs=[
            pl.BlockSpec((block, width), lambda i: (i, 0)),
            pl.BlockSpec(source.shape, lambda i: (0, 0, 0)),
        ],
        out_specs=pl.BlockSpec((block, width), lambda i: (i, 0)),
        out_shape=jax.ShapeDtypeStruct((rows, width), BF16),
        compiler_params=PARAMS,
        cost_estimate=CHEAP,
        name="attend",
    )(queries, source)


def pick_kernel(ids, owner, *refs):
    backs, out = refs[:-1], refs[-1]
    for k, back in enumerate(backs):

        @pl.when(owner[0] == ids[0] ^ k)
        def _():
            out[...] = back[...]


def pick(ids, owner, backs):
    return pl.pallas_call(
        pick_kernel,
        in_specs=[SCALARS] * 2 + [WHOLE] * len(backs),
        out_specs=WHOLE,
        out_shape=jax.ShapeDtypeStruct(backs[0].shape, BF16),
        compiler_params=PARAMS,
        cost_estimate=CHEAP,
        name="pick",
    )(ids, owner, *backs)


def route_kernel(experts, parts, ids, choice_t, choice, *outs):
    dispatch, first, second = outs[:parts], outs[parts : 2 * parts], outs[2 * parts :]
    tokens = choice_t.shape[1]
    slots = dispatch[0].shape[0]
    capacity = slots * parts // experts
    wide = lax.broadcasted_iota(jnp.int32, (tokens, experts), 1)
    tall = lax.broadcasted_iota(jnp.int32, (experts, tokens), 0)
    i = lax.broadcasted_iota(jnp.int32, (tokens, tokens), 0)
    j = lax.broadcasted_iota(jnp.int32, (tokens, tokens), 1)
    r0, r1 = choice_t[0:1, :], choice_t[1:2, :]
    turned = dot((i == j).astype(BF16), choice_t[...].astype(F32).astype(BF16), ((1,), (1,))).astype(jnp.int32)
    choice[...] = turned
    c0, c1 = turned[:, 0:1], turned[:, 1:2]
    named = ((wide == c0) | (wide == c1)).astype(BF16)
    named_t = ((tall == r0) | (tall == r1)).astype(BF16)
    rank = dot((j < i).astype(BF16), named).astype(jnp.int32)
    rank_t = dot(named_t, (i < j).astype(BF16)).astype(jnp.int32)
    place0 = c0 * capacity + jnp.sum(jnp.where(wide == c0, rank, 0), axis=1, keepdims=True)
    place1 = c1 * capacity + jnp.sum(jnp.where(wide == c1, rank, 0), axis=1, keepdims=True)
    across0 = r0 * capacity + jnp.sum(jnp.where(tall == r0, rank_t, 0), axis=0, keepdims=True)
    across1 = r1 * capacity + jnp.sum(jnp.where(tall == r1, rank_t, 0), axis=0, keepdims=True)
    lane = lax.broadcasted_iota(jnp.int32, (tokens, slots), 1)
    row = lax.broadcasted_iota(jnp.int32, (slots, tokens), 0)
    for k in range(parts):
        base = (ids[0] ^ k) * capacity if parts > 1 else 0
        dispatch[k][...] = ((row + base == across0) | (row + base == across1)).astype(BF16)
        first[k][...] = (lane + base == place0).astype(BF16)
        second[k][...] = (lane + base == place1).astype(BF16)


def route(ids, choice, experts, parts, capacity):
    tokens = choice.shape[0]
    slots = experts * capacity // parts
    outs = pl.pallas_call(
        functools.partial(route_kernel, experts, parts),
        in_specs=[SCALARS, WHOLE],
        out_specs=[WHOLE] * (1 + 3 * parts),
        out_shape=[jax.ShapeDtypeStruct(choice.shape, jnp.int32)]
        + [jax.ShapeDtypeStruct((slots, tokens), BF16)] * parts
        + [jax.ShapeDtypeStruct((tokens, slots), BF16)] * (2 * parts),
        compiler_params=PARAMS,
        cost_estimate=CHEAP,
        name="route",
    )(ids, choice.T)
    return outs[0], outs[1 : 1 + parts], outs[1 + parts : 1 + 2 * parts], outs[1 + 2 * parts :]


def state_kernel(count, sends, *refs):
    ids, tokens = refs[:2]
    contexts, weights = refs[2 : 2 + count], refs[2 + count : 2 + 2 * count]
    dispatch = refs[2 + 2 * count : 2 + 2 * count + sends]
    state, outs = refs[2 + 2 * count + sends], refs[3 + 2 * count + sends :]
    total = tokens[...].astype(F32)
    for context, weight in zip(contexts, weights):
        total += dot(context[...], weight[...])
    state[...] = total.astype(BF16)
    for rows, out in zip(dispatch, outs):
        width = out.shape[1]
        at = (ids[1] & (state.shape[1] // width - 1)) * width
        out[...] = dot(rows[...], state[:, pl.ds(pl.multiple_of(at, width), width)]).astype(BF16)


def make_state(ids, tokens, contexts, weights, dispatch, cuts):
    return pl.pallas_call(
        functools.partial(state_kernel, len(contexts), len(dispatch)),
        in_specs=[SCALARS] + [WHOLE] * (1 + 2 * len(contexts) + len(dispatch)),
        out_specs=[WHOLE] * (1 + len(dispatch)),
        out_shape=[jax.ShapeDtypeStruct(tokens.shape, BF16)]
        + [jax.ShapeDtypeStruct((rows.shape[0], tokens.shape[1] // cut), BF16) for rows, cut in zip(dispatch, cuts)],
        compiler_params=PARAMS,
        cost_estimate=CHEAP,
        name="state",
    )(ids, tokens, *contexts, *weights, *dispatch)


def home_kernel(experts, ids, state, dispatch, router, choice, own_a, own_b, gates, columns):
    half = own_a.shape[1]
    core = ids[1] & 1
    own_a[...] = dot(dispatch[...], state[:, pl.ds(pl.multiple_of(core * half, half), half)]).astype(BF16)
    own_b[...] = dot(dispatch[...], state[:, pl.ds(pl.multiple_of((1 - core) * half, half), half)]).astype(BF16)
    logits = dot(state[...], router[...], ((1,), (1,)))
    wide = lax.broadcasted_iota(jnp.int32, logits.shape, 1)
    first = jnp.sum(jnp.where(wide == choice[:, 0:1], logits, 0.0), axis=1, keepdims=True)
    second = jnp.sum(jnp.where(wide == choice[:, 1:2], logits, 0.0), axis=1, keepdims=True)
    gates[:, 0:1] = jax.nn.sigmoid(first - second)
    gates[:, 1:2] = jax.nn.sigmoid(second - first)
    width = columns.shape[1]
    columns[...] = state[:, pl.ds(pl.multiple_of(ids[1] * width, width), width)].astype(F32)


def at_home(ids, state, dispatch, router, choice, experts, width):
    tokens, features = state.shape
    slots = dispatch.shape[0]
    return pl.pallas_call(
        functools.partial(home_kernel, experts),
        in_specs=[SCALARS] + [WHOLE] * 4,
        out_specs=[WHOLE] * 4,
        out_shape=[
            jax.ShapeDtypeStruct((slots, features // 2), BF16),
            jax.ShapeDtypeStruct((slots, features // 2), BF16),
            jax.ShapeDtypeStruct((tokens, 2), F32),
            jax.ShapeDtypeStruct((tokens, width), F32),
        ],
        compiler_params=PARAMS,
        cost_estimate=CHEAP,
        name="home",
    )(ids, state, dispatch, router, choice)


def expert_kernel(order, blocks, *refs):
    cuts = len(order)
    ids, pieces = refs[0], refs[1 : 1 + blocks * cuts]
    expand, shrink, keep, give, rows_here, hidden = refs[1 + blocks * cuts :]
    count, width = pieces[0].shape
    for block in range(blocks):
        for i in range(cuts):
            rows_here[i, block * count : (block + 1) * count] = pieces[block * cuts + i][...]
    units = expand.shape[1]
    tile = min(TILE, units)
    for at in range(0, units, tile):
        total = jnp.zeros((hidden.shape[0], tile), F32)
        for i, index in enumerate(order):
            part = pl.ds(pl.multiple_of(((ids[1] & (cuts - 1)) ^ index) * width, width), width)
            total += dot(rows_here[i], expand[part, at : at + tile])
        hidden[:, at : at + tile] = jnp.maximum(total, 0.0).astype(BF16)
    width = keep.shape[2]
    for j in range(keep.shape[0]):
        at = pl.multiple_of((ids[1] ^ (2 * j) ^ 1) * width, width)
        give[j] = dot(hidden[...], shrink[:, pl.ds(at, width)]).astype(BF16)
    for j in range(keep.shape[0]):
        at = pl.multiple_of((ids[1] ^ (2 * j)) * width, width)
        keep[j] = dot(hidden[...], shrink[:, pl.ds(at, width)])


def run_expert(ids, order, blocks, expand, shrink, parts):
    pieces = [piece for block in blocks for piece in block]
    count, piece_width = pieces[0].shape
    rows = count * len(blocks)
    features, units = expand.shape
    width = features // (2 * parts)
    return pl.pallas_call(
        functools.partial(expert_kernel, tuple(order), len(blocks)),
        in_specs=[SCALARS] + [WHOLE] * (2 + len(pieces)),
        out_specs=[WHOLE] * 2,
        out_shape=[
            jax.ShapeDtypeStruct((parts, rows, width), F32),
            jax.ShapeDtypeStruct((parts, rows, width), BF16),
        ],
        scratch_shapes=[pltpu.VMEM((len(order), rows, piece_width), BF16), pltpu.VMEM((rows, units), BF16)],
        compiler_params=PARAMS,
        cost_estimate=CHEAP,
        name="expert",
    )(ids, *pieces, expand, shrink)


def combine_kernel(count, gates, base, first, second, *refs):
    parts, out = refs[:count], refs[count]
    total = parts[0][...].astype(F32)
    for part in parts[1:]:
        total += part[...].astype(F32)
    total = total.astype(BF16)
    result = base[...] + gates[:, 0:1] * dot(first[...], total) + gates[:, 1:2] * dot(second[...], total)
    out[...] = result.astype(out.dtype)


def combine(gates, base, first, second, parts, dtype):
    return pl.pallas_call(
        functools.partial(combine_kernel, len(parts)),
        in_specs=[WHOLE] * (4 + len(parts)),
        out_specs=WHOLE,
        out_shape=jax.ShapeDtypeStruct(base.shape, dtype),
        compiler_params=PARAMS,
        cost_estimate=CHEAP,
        name="combine",
    )(gates, base, first, second, *parts)


def bits_of(count):
    bits = []
    while 2 ** len(bits) < count:
        bits.insert(0, 2 ** len(bits))
    return bits


def local(
    tokens,
    encoder_states,
    source_owner,
    query_weight,
    output_weight,
    router_weight,
    expert_choice,
    expand_weight,
    shrink_weight,
):
    token_count, features = tokens.shape
    groups = lax.axis_size("expert")
    slices = lax.axis_size("mp")
    here, column = lax.axis_index("expert"), lax.axis_index("mp")
    ids = jnp.stack([here, column]).astype(jnp.int32)
    width = features // slices
    experts = expand_weight.shape[0] * groups
    capacity = max(2, 3 * token_count // experts)
    direct = groups <= DIRECT
    pairs = slices // 2
    slots = capacity if direct else experts * capacity

    def hop(value, along_expert, along_mp):
        if along_expert == 0 and along_mp == 0:
            return value
        moves = [
            (e * slices + m, (e ^ along_expert) * slices + (m ^ along_mp))
            for e in range(groups)
            for m in range(slices)
        ]
        return lax.ppermute(value, ("expert", "mp"), moves)

    def spread(value):
        parts = value.reshape(groups, -1, value.shape[-1])
        return lax.all_to_all(parts, "expert", 0, 0, tiled=True).reshape(value.shape)

    def after(value, other):
        return lax.optimization_barrier((value, other))[0]

    steps = range(groups) if direct else [0]

    queries, source = ask(after(tokens, ids), query_weight, encoder_states[0])
    expert_bits = bits_of(groups)
    bits = bits_of(slices)
    if direct:
        own = attend(queries, source, token_count)
        asked, steps_of = [queries], [0]
        for bit in expert_bits:
            asked = asked + [hop(value if k == 0 else after(value, own), bit, 0) for k, value in zip(steps_of, asked)]
            steps_of = steps_of + [k ^ bit for k in steps_of]
        asked = dict(zip(steps_of, asked))
        previous, backs = own, {}
        for k in sorted(range(1, groups), key=lambda k: (k & (k - 1) != 0, -k)):
            answer = previous = attend(after(asked[k], previous), source, token_count)
            backs[k] = hop(answer, k, 0)
        context = pick(ids, source_owner, [own] + [backs[k] for k in range(1, groups)])
    else:
        asked = lax.all_gather(queries, "expert", axis=0, tiled=True)
        previous = attend(asked, source, token_count)
        context = lax.dynamic_slice_in_dim(spread(previous), source_owner[0] * token_count, token_count, 0)

    choice, dispatch, first, second = route(ids, after(expert_choice, previous), experts, len(steps), capacity)
    weights, order = [output_weight], [0]
    for bit in bits:
        if bit == 1:
            weights = [after(weight, context) for weight in weights]
        weights = weights + [hop(weight, 0, bit) for weight in weights]
        order = order + [index ^ bit for index in order]
    contexts = [context]
    for bit in bits:
        contexts = contexts + [hop(value if i == 0 else after(value, dispatch[0]), 0, bit) for i, value in enumerate(contexts)]

    relayed = groups // 2 if direct and pairs > 1 and groups > 1 else -1
    rest = [k for k in reversed(range(1, groups)) if k != relayed]
    sends = ([relayed] if relayed >= 0 else []) + rest if direct else [0]
    cuts = [slices if k == relayed else 2 for k in sends]
    state, *leaving = make_state(ids, tokens, contexts, weights, [dispatch[k] for k in sends], cuts)
    own_a, own_b, gates, columns = at_home(
        ids, state, dispatch[0], router_weight.T, choice, experts, width
    )
    expert = functools.partial(run_expert, expand=expand_weight[0], shrink=shrink_weight[0], parts=pairs)

    def sum_cores(keep, give):
        return keep + hop(give, 0, 1).astype(F32)

    def send_home(k, summed):
        if k == relayed:
            total = summed[0]
            for j in range(1, pairs):
                total += hop(summed[j].astype(BF16), 0, 2 * j).astype(F32)
            return [hop(total.astype(BF16), k, 0)]
        parts = [summed[j].astype(BF16) for j in range(pairs)]
        return [hop(part, k, 2 * j) if direct else hop(spread(part), 0, 2 * j) for j, part in enumerate(parts)]

    home = {}
    if direct:
        arrived = {k: hop(rows, k, 0) for k, rows in zip(sends, leaving)}
        keep, give = expert(ids, [0, 1], [[own_a, own_b]])
        if sends:
            give = after(give, arrived[sends[0]])
        home[0] = send_home(0, sum_cores(keep, give))
        turn_ids = after(ids, give)
        if rest:
            mine = [arrived[k] for k in rest]
            keep, give = expert(turn_ids, [0, 1], [[rows, hop(rows, 0, 1)] for rows in mine])
            turn_ids = after(ids, give)
            summed = sum_cores(keep, give)
            for i, k in enumerate(rest):
                home[k] = send_home(k, summed[:, i * slots : (i + 1) * slots])
        if relayed >= 0:
            pieces, places = [arrived[relayed]], [0]
            for bit in bits:
                pieces = pieces + [hop(piece, 0, bit) for piece in pieces]
                places = places + [index ^ bit for index in places]
            keep, give = expert(turn_ids, places, [pieces])
            home[relayed] = send_home(relayed, sum_cores(keep, give))
        order = [0] + rest[::-1] + ([relayed] if relayed >= 0 else [])
    else:
        mine = spread(leaving[0])
        keep, give = expert(ids, [0, 1], [[mine, hop(mine, 0, 1)]])
        home[0] = send_home(0, sum_cores(keep, give))
        order = [0]
    results = columns
    for k in order:
        results = combine(gates, results, first[k], second[k], home[k], BF16 if k == order[-1] else F32)
    return results


def solution(mesh):
    return jax.shard_map(
        local,
        mesh=mesh,
        in_specs=(
            P(("groups", "expert"), None),
            P(("groups", "expert"), None, None, "mp"),
            P(("groups", "expert")),
            P(None, "mp"),
            P("mp", None),
            P(),
            P(("groups", "expert"), None),
            P("expert", None, "mp"),
            P("expert", "mp", None),
        ),
        out_specs=P(("groups", "expert"), "mp"),
        check_vma=False,
    )
```

```python
import functools

import jax
import jax.numpy as jnp
from jax import lax
from jax.experimental import pallas as pl
from jax.experimental.pallas import tpu as pltpu
from jax.sharding import PartitionSpec as P

HEAD_DIM = 128
DIRECT = 8
CUTS = 4
TILE = 256
F32, BF16 = jnp.float32, jnp.bfloat16
PARAMS = pltpu.CompilerParams(vmem_limit_bytes=20 * 2**20)
CHEAP = pl.CostEstimate(flops=0, bytes_accessed=0, transcendentals=0)
SCALARS = pl.BlockSpec(memory_space=pltpu.SMEM)
WHOLE = pl.BlockSpec(memory_space=pltpu.VMEM)


def dot(a, b, dims=((1,), (0,))):
    return lax.dot_general(a, b, (dims, ((), ())), preferred_element_type=F32)


def in_hbm(value):
    return pltpu.with_memory_space_constraint(value, pltpu.HBM)


def query_kernel(tokens, weight, source, out, staged, tokens_here, weight_here, sems):
    features = tokens.shape[1]
    depth = features // CUTS
    copies, later = [], []
    for i in range(CUTS):
        part = pl.ds(i * depth, depth)
        copies.append(
            (
                pltpu.make_async_copy(tokens.at[:, part], tokens_here.at[:, part], sems.at[0, i]),
                pltpu.make_async_copy(weight.at[part, :], weight_here.at[part, :], sems.at[1, i]),
            )
        )
        rows = pl.ds(i * (source.shape[1] // CUTS), source.shape[1] // CUTS)
        later.append(pltpu.make_async_copy(source.at[:, rows], staged.at[:, rows], sems.at[2, i]))
    for pair in copies:
        for copy in pair:
            copy.start()
    for copy in later:
        copy.start()
    total = jnp.zeros(out.shape, F32)
    for i, pair in enumerate(copies):
        for copy in pair:
            copy.wait()
        part = slice(i * depth, (i + 1) * depth)
        total += dot(tokens_here[:, part], weight_here[part, :])
    out[...] = total.astype(BF16)
    for copy in later:
        copy.wait()


def ask(tokens, weight, source):
    return pl.pallas_call(
        query_kernel,
        in_specs=[pl.BlockSpec(memory_space=pltpu.HBM)] * 3,
        out_specs=[WHOLE] * 2,
        out_shape=[
            jax.ShapeDtypeStruct((tokens.shape[0], weight.shape[1]), BF16),
            jax.ShapeDtypeStruct(source.shape, BF16),
        ],
        scratch_shapes=[
            pltpu.VMEM(tokens.shape, BF16),
            pltpu.VMEM(weight.shape, BF16),
            pltpu.SemaphoreType.DMA((3, CUTS)),
        ],
        compiler_params=PARAMS,
        cost_estimate=CHEAP,
        name="query",
    )(in_hbm(tokens), in_hbm(weight), in_hbm(source))


def attend_kernel(queries, source, out):
    for head in range(queries.shape[1] // HEAD_DIM):
        part = slice(head * HEAD_DIM, (head + 1) * HEAD_DIM)
        scores = dot(queries[:, part], source[0, :, part], ((1,), (1,)))
        top = jnp.max(scores, axis=1, keepdims=True)
        weights = jnp.exp((scores - top) * HEAD_DIM**-0.5)
        total = jnp.sum(weights, axis=1, keepdims=True)
        context = dot(weights.astype(BF16), source[1, :, part])
        out[:, part] = (context / total).astype(BF16)


def attend(queries, source, block):
    rows, width = queries.shape
    if rows == block:
        return pl.pallas_call(
            attend_kernel,
            in_specs=[WHOLE] * 2,
            out_specs=WHOLE,
            out_shape=jax.ShapeDtypeStruct((rows, width), BF16),
            compiler_params=PARAMS,
        cost_estimate=CHEAP,
            name="attend",
        )(queries, source)
    return pl.pallas_call(
        attend_kernel,
        grid=(rows // block,),
        in_specs=[
            pl.BlockSpec((block, width), lambda i: (i, 0)),
            pl.BlockSpec(source.shape, lambda i: (0, 0, 0)),
        ],
        out_specs=pl.BlockSpec((block, width), lambda i: (i, 0)),
        out_shape=jax.ShapeDtypeStruct((rows, width), BF16),
        compiler_params=PARAMS,
        cost_estimate=CHEAP,
        name="attend",
    )(queries, source)


def pick_kernel(ids, owner, *refs):
    backs, out = refs[:-1], refs[-1]
    for k, back in enumerate(backs):

        @pl.when(owner[0] == ids[0] ^ k)
        def _():
            out[...] = back[...]


def pick(ids, owner, backs):
    return pl.pallas_call(
        pick_kernel,
        in_specs=[SCALARS] * 2 + [WHOLE] * len(backs),
        out_specs=WHOLE,
        out_shape=jax.ShapeDtypeStruct(backs[0].shape, BF16),
        compiler_params=PARAMS,
        cost_estimate=CHEAP,
        name="pick",
    )(ids, owner, *backs)


def route_kernel(experts, parts, ids, choice_t, choice, *outs):
    dispatch, first, second = outs[:parts], outs[parts : 2 * parts], outs[2 * parts :]
    tokens = choice_t.shape[1]
    slots = dispatch[0].shape[0]
    capacity = slots * parts // experts
    wide = lax.broadcasted_iota(jnp.int32, (tokens, experts), 1)
    tall = lax.broadcasted_iota(jnp.int32, (experts, tokens), 0)
    i = lax.broadcasted_iota(jnp.int32, (tokens, tokens), 0)
    j = lax.broadcasted_iota(jnp.int32, (tokens, tokens), 1)
    r0, r1 = choice_t[0:1, :], choice_t[1:2, :]
    turned = dot((i == j).astype(BF16), choice_t[...].astype(F32).astype(BF16), ((1,), (1,))).astype(jnp.int32)
    choice[...] = turned
    c0, c1 = turned[:, 0:1], turned[:, 1:2]
    named = ((wide == c0) | (wide == c1)).astype(BF16)
    named_t = ((tall == r0) | (tall == r1)).astype(BF16)
    rank = dot((j < i).astype(BF16), named).astype(jnp.int32)
    rank_t = dot(named_t, (i < j).astype(BF16)).astype(jnp.int32)
    place0 = c0 * capacity + jnp.sum(jnp.where(wide == c0, rank, 0), axis=1, keepdims=True)
    place1 = c1 * capacity + jnp.sum(jnp.where(wide == c1, rank, 0), axis=1, keepdims=True)
    across0 = r0 * capacity + jnp.sum(jnp.where(tall == r0, rank_t, 0), axis=0, keepdims=True)
    across1 = r1 * capacity + jnp.sum(jnp.where(tall == r1, rank_t, 0), axis=0, keepdims=True)
    lane = lax.broadcasted_iota(jnp.int32, (tokens, slots), 1)
    row = lax.broadcasted_iota(jnp.int32, (slots, tokens), 0)
    for k in range(parts):
        base = (ids[0] ^ k) * capacity if parts > 1 else 0
        dispatch[k][...] = ((row + base == across0) | (row + base == across1)).astype(BF16)
        first[k][...] = (lane + base == place0).astype(BF16)
        second[k][...] = (lane + base == place1).astype(BF16)


def route(ids, choice, experts, parts, capacity):
    tokens = choice.shape[0]
    slots = experts * capacity // parts
    outs = pl.pallas_call(
        functools.partial(route_kernel, experts, parts),
        in_specs=[SCALARS, WHOLE],
        out_specs=[WHOLE] * (1 + 3 * parts),
        out_shape=[jax.ShapeDtypeStruct(choice.shape, jnp.int32)]
        + [jax.ShapeDtypeStruct((slots, tokens), BF16)] * parts
        + [jax.ShapeDtypeStruct((tokens, slots), BF16)] * (2 * parts),
        compiler_params=PARAMS,
        cost_estimate=CHEAP,
        name="route",
    )(ids, choice.T)
    return outs[0], outs[1 : 1 + parts], outs[1 + parts : 1 + 2 * parts], outs[1 + 2 * parts :]


def state_kernel(count, sends, *refs):
    ids, tokens = refs[:2]
    contexts, weights = refs[2 : 2 + count], refs[2 + count : 2 + 2 * count]
    dispatch = refs[2 + 2 * count : 2 + 2 * count + sends]
    state, outs = refs[2 + 2 * count + sends], refs[3 + 2 * count + sends :]
    total = tokens[...].astype(F32)
    for context, weight in zip(contexts, weights):
        total += dot(context[...], weight[...])
    state[...] = total.astype(BF16)
    for rows, out in zip(dispatch, outs):
        width = out.shape[1]
        at = (ids[1] & (state.shape[1] // width - 1)) * width
        out[...] = dot(rows[...], state[:, pl.ds(pl.multiple_of(at, width), width)]).astype(BF16)


def make_state(ids, tokens, contexts, weights, dispatch, cuts):
    return pl.pallas_call(
        functools.partial(state_kernel, len(contexts), len(dispatch)),
        in_specs=[SCALARS] + [WHOLE] * (1 + 2 * len(contexts) + len(dispatch)),
        out_specs=[WHOLE] * (1 + len(dispatch)),
        out_shape=[jax.ShapeDtypeStruct(tokens.shape, BF16)]
        + [jax.ShapeDtypeStruct((rows.shape[0], tokens.shape[1] // cut), BF16) for rows, cut in zip(dispatch, cuts)],
        compiler_params=PARAMS,
        cost_estimate=CHEAP,
        name="state",
    )(ids, tokens, *contexts, *weights, *dispatch)


def home_kernel(experts, ids, state, dispatch, router, choice, own_a, own_b, gates, columns):
    half = own_a.shape[1]
    core = ids[1] & 1
    own_a[...] = dot(dispatch[...], state[:, pl.ds(pl.multiple_of(core * half, half), half)]).astype(BF16)
    own_b[...] = dot(dispatch[...], state[:, pl.ds(pl.multiple_of((1 - core) * half, half), half)]).astype(BF16)
    logits = dot(state[...], router[...], ((1,), (1,)))
    wide = lax.broadcasted_iota(jnp.int32, logits.shape, 1)
    first = jnp.sum(jnp.where(wide == choice[:, 0:1], logits, 0.0), axis=1, keepdims=True)
    second = jnp.sum(jnp.where(wide == choice[:, 1:2], logits, 0.0), axis=1, keepdims=True)
    gates[:, 0:1] = jax.nn.sigmoid(first - second)
    gates[:, 1:2] = jax.nn.sigmoid(second - first)
    width = columns.shape[1]
    columns[...] = state[:, pl.ds(pl.multiple_of(ids[1] * width, width), width)].astype(F32)


def at_home(ids, state, dispatch, router, choice, experts, width):
    tokens, features = state.shape
    slots = dispatch.shape[0]
    return pl.pallas_call(
        functools.partial(home_kernel, experts),
        in_specs=[SCALARS] + [WHOLE] * 4,
        out_specs=[WHOLE] * 4,
        out_shape=[
            jax.ShapeDtypeStruct((slots, features // 2), BF16),
            jax.ShapeDtypeStruct((slots, features // 2), BF16),
            jax.ShapeDtypeStruct((tokens, 2), F32),
            jax.ShapeDtypeStruct((tokens, width), F32),
        ],
        compiler_params=PARAMS,
        cost_estimate=CHEAP,
        name="home",
    )(ids, state, dispatch, router, choice)


def expert_kernel(orders, *refs):
    blocks, at = [], 1
    for order in orders:
        blocks.append(refs[at : at + len(order)])
        at += len(order)
    ids = refs[0]
    expand, shrink, keep, give, rows_here, hidden = refs[at:]
    count = blocks[0][0].shape[0]
    for block, (order, pieces) in enumerate(zip(orders, blocks)):
        for index, piece in zip(order, pieces):
            width = piece.shape[1]
            part = pl.ds(pl.multiple_of(((ids[1] & (len(order) - 1)) ^ index) * width, width), width)
            rows_here[block * count : (block + 1) * count, part] = piece[...]
    units = expand.shape[1]
    tile = min(TILE, units)
    for at in range(0, units, tile):
        total = dot(rows_here[...], expand[:, at : at + tile])
        hidden[:, at : at + tile] = jnp.maximum(total, 0.0).astype(BF16)
    width = keep.shape[2]
    for j in range(keep.shape[0]):
        at = pl.multiple_of((ids[1] ^ (2 * j) ^ 1) * width, width)
        give[j] = dot(hidden[...], shrink[:, pl.ds(at, width)]).astype(BF16)
    for j in range(keep.shape[0]):
        at = pl.multiple_of((ids[1] ^ (2 * j)) * width, width)
        keep[j] = dot(hidden[...], shrink[:, pl.ds(at, width)])


def run_expert(ids, orders, blocks, expand, shrink, parts):
    pieces = [piece for block in blocks for piece in block]
    rows = pieces[0].shape[0] * len(blocks)
    features, units = expand.shape
    width = features // (2 * parts)
    return pl.pallas_call(
        functools.partial(expert_kernel, tuple(map(tuple, orders))),
        in_specs=[SCALARS] + [WHOLE] * (2 + len(pieces)),
        out_specs=[WHOLE] * 2,
        out_shape=[
            jax.ShapeDtypeStruct((parts, rows, width), F32),
            jax.ShapeDtypeStruct((parts, rows, width), BF16),
        ],
        scratch_shapes=[pltpu.VMEM((rows, features), BF16), pltpu.VMEM((rows, units), BF16)],
        compiler_params=PARAMS,
        cost_estimate=CHEAP,
        name="expert",
    )(ids, *pieces, expand, shrink)


def combine_kernel(count, gates, base, first, second, *refs):
    parts, out = refs[:count], refs[count]
    total = parts[0][...].astype(F32)
    for part in parts[1:]:
        total += part[...].astype(F32)
    total = total.astype(BF16)
    result = base[...] + gates[:, 0:1] * dot(first[...], total) + gates[:, 1:2] * dot(second[...], total)
    out[...] = result.astype(out.dtype)


def combine(gates, base, first, second, parts, dtype):
    return pl.pallas_call(
        functools.partial(combine_kernel, len(parts)),
        in_specs=[WHOLE] * (4 + len(parts)),
        out_specs=WHOLE,
        out_shape=jax.ShapeDtypeStruct(base.shape, dtype),
        compiler_params=PARAMS,
        cost_estimate=CHEAP,
        name="combine",
    )(gates, base, first, second, *parts)


def bits_of(count):
    bits = []
    while 2 ** len(bits) < count:
        bits.insert(0, 2 ** len(bits))
    return bits


def local(
    tokens,
    encoder_states,
    source_owner,
    query_weight,
    output_weight,
    router_weight,
    expert_choice,
    expand_weight,
    shrink_weight,
):
    token_count, features = tokens.shape
    groups = lax.axis_size("expert")
    slices = lax.axis_size("mp")
    here, column = lax.axis_index("expert"), lax.axis_index("mp")
    ids = jnp.stack([here, column]).astype(jnp.int32)
    width = features // slices
    experts = expand_weight.shape[0] * groups
    capacity = max(2, 3 * token_count // experts)
    direct = groups <= DIRECT
    pairs = slices // 2
    slots = capacity if direct else experts * capacity

    def hop(value, along_expert, along_mp):
        if along_expert == 0 and along_mp == 0:
            return value
        moves = [
            (e * slices + m, (e ^ along_expert) * slices + (m ^ along_mp))
            for e in range(groups)
            for m in range(slices)
        ]
        return lax.ppermute(value, ("expert", "mp"), moves)

    def spread(value):
        parts = value.reshape(groups, -1, value.shape[-1])
        return lax.all_to_all(parts, "expert", 0, 0, tiled=True).reshape(value.shape)

    def after(value, other):
        return lax.optimization_barrier((value, other))[0]

    steps = range(groups) if direct else [0]

    queries, source = ask(after(tokens, ids), query_weight, encoder_states[0])
    expert_bits = bits_of(groups)
    bits = bits_of(slices)
    if direct:
        own = attend(queries, source, token_count)
        asked, steps_of = [queries], [0]
        for bit in expert_bits:
            asked = asked + [hop(value if k == 0 else after(value, own), bit, 0) for k, value in zip(steps_of, asked)]
            steps_of = steps_of + [k ^ bit for k in steps_of]
        asked = dict(zip(steps_of, asked))
        previous, backs = own, {}
        for k in sorted(range(1, groups), key=lambda k: (k & (k - 1) != 0, -k)):
            answer = previous = attend(after(asked[k], previous), source, token_count)
            backs[k] = hop(answer, k, 0)
        context = pick(ids, source_owner, [own] + [backs[k] for k in range(1, groups)])
    else:
        asked = lax.all_gather(queries, "expert", axis=0, tiled=True)
        previous = attend(asked, source, token_count)
        context = lax.dynamic_slice_in_dim(spread(previous), source_owner[0] * token_count, token_count, 0)

    choice, dispatch, first, second = route(ids, after(expert_choice, previous), experts, len(steps), capacity)
    weights, order = [output_weight], [0]
    for bit in bits:
        if bit == 1:
            weights = [after(weight, context) for weight in weights]
        weights = weights + [hop(weight, 0, bit) for weight in weights]
        order = order + [index ^ bit for index in order]
    contexts = [context]
    for bit in bits:
        contexts = contexts + [hop(value if i == 0 else after(value, dispatch[0]), 0, bit) for i, value in enumerate(contexts)]

    far = set(range(2, groups)) if direct and pairs > 1 else set()
    sends = [k for k in range(2, groups)] + ([1] if groups > 1 else []) if direct else [0]
    cuts = [slices if k in far else 2 for k in sends]
    state, *leaving = make_state(ids, tokens, contexts, weights, [dispatch[k] for k in sends], cuts)
    own_a, own_b, gates, columns = at_home(
        ids, state, dispatch[0], router_weight.T, choice, experts, width
    )
    expert = functools.partial(run_expert, expand=expand_weight[0], shrink=shrink_weight[0], parts=pairs)

    def sum_cores(keep, give):
        return keep + hop(give, 0, 1).astype(F32)

    def send_home(k, summed):
        if k in far:
            total = summed[0]
            for j in range(1, pairs):
                total += hop(summed[j].astype(BF16), 0, 2 * j).astype(F32)
            return [hop(total.astype(BF16), k, 0)]
        parts = [summed[j].astype(BF16) for j in range(pairs)]
        return [hop(part, k, 2 * j) if direct else hop(spread(part), 0, 2 * j) for j, part in enumerate(parts)]

    home, order = {}, [0]
    if direct:
        arrived = {k: hop(rows, k, 0) for k, rows in zip(sends, leaving)}
        keep, give = expert(ids, [[0, 1]], [[own_a, own_b]])
        turn_ids = after(ids, give)
        if sends:
            give = after(give, arrived[sends[0]])
        home[0] = send_home(0, sum_cores(keep, give))
        turns = [[k for k in sends if k < groups - 1], [groups - 1]] if groups > 2 else [sends]
        for turn in turns:
            blocks, orders = [], []
            for k in turn:
                pieces, places = [arrived[k]], [0]
                for bit in bits if k in far else [1]:
                    pieces = pieces + [hop(piece, 0, bit) for piece in pieces]
                    places = places + [index ^ bit for index in places]
                blocks.append(pieces)
                orders.append(places)
            if turn:
                keep, give = expert(turn_ids, orders, blocks)
                turn_ids = after(ids, give)
                summed = sum_cores(keep, give)
                for i, k in enumerate(turn):
                    home[k] = send_home(k, summed[:, i * slots : (i + 1) * slots])
        order = [0] + sorted(sends)
    else:
        mine = spread(leaving[0])
        home[0] = send_home(0, sum_cores(*expert(ids, [[0, 1]], [[mine, hop(mine, 0, 1)]])))
    results = columns
    for k in order:
        results = combine(gates, results, first[k], second[k], home[k], BF16 if k == order[-1] else F32)
    return results


def solution(mesh):
    return jax.shard_map(
        local,
        mesh=mesh,
        in_specs=(
            P(("groups", "expert"), None),
            P(("groups", "expert"), None, None, "mp"),
            P(("groups", "expert")),
            P(None, "mp"),
            P("mp", None),
            P(),
            P(("groups", "expert"), None),
            P("expert", None, "mp"),
            P("expert", "mp", None),
        ),
        out_specs=P(("groups", "expert"), "mp"),
        check_vma=False,
    )
```

```python
import functools

import jax
import jax.numpy as jnp
from jax import lax
from jax.experimental import pallas as pl
from jax.experimental.pallas import tpu as pltpu
from jax.sharding import PartitionSpec as P

HEAD_DIM = 128
DIRECT = 8
CUTS = 4
TILE = 256
F32, BF16 = jnp.float32, jnp.bfloat16
PARAMS = pltpu.CompilerParams(vmem_limit_bytes=20 * 2**20)
CHEAP = pl.CostEstimate(flops=0, bytes_accessed=0, transcendentals=0)
SCALARS = pl.BlockSpec(memory_space=pltpu.SMEM)
WHOLE = pl.BlockSpec(memory_space=pltpu.VMEM)


def dot(a, b, dims=((1,), (0,))):
    return lax.dot_general(a, b, (dims, ((), ())), preferred_element_type=F32)


def in_hbm(value):
    return pltpu.with_memory_space_constraint(value, pltpu.HBM)


def query_kernel(tokens, weight, source, out, staged, tokens_here, weight_here, sems):
    features = tokens.shape[1]
    depth = features // CUTS
    copies, later = [], []
    for i in range(CUTS):
        part = pl.ds(i * depth, depth)
        copies.append(
            (
                pltpu.make_async_copy(tokens.at[:, part], tokens_here.at[:, part], sems.at[0, i]),
                pltpu.make_async_copy(weight.at[part, :], weight_here.at[part, :], sems.at[1, i]),
            )
        )
        rows = pl.ds(i * (source.shape[1] // CUTS), source.shape[1] // CUTS)
        later.append(pltpu.make_async_copy(source.at[:, rows], staged.at[:, rows], sems.at[2, i]))
    for pair in copies:
        for copy in pair:
            copy.start()
    for copy in later:
        copy.start()
    total = jnp.zeros(out.shape, F32)
    for i, pair in enumerate(copies):
        for copy in pair:
            copy.wait()
        part = slice(i * depth, (i + 1) * depth)
        total += dot(tokens_here[:, part], weight_here[part, :])
    out[...] = total.astype(BF16)
    for copy in later:
        copy.wait()


def ask(tokens, weight, source):
    return pl.pallas_call(
        query_kernel,
        in_specs=[pl.BlockSpec(memory_space=pltpu.HBM)] * 3,
        out_specs=[WHOLE] * 2,
        out_shape=[
            jax.ShapeDtypeStruct((tokens.shape[0], weight.shape[1]), BF16),
            jax.ShapeDtypeStruct(source.shape, BF16),
        ],
        scratch_shapes=[
            pltpu.VMEM(tokens.shape, BF16),
            pltpu.VMEM(weight.shape, BF16),
            pltpu.SemaphoreType.DMA((3, CUTS)),
        ],
        compiler_params=PARAMS,
        cost_estimate=CHEAP,
        name="query",
    )(in_hbm(tokens), in_hbm(weight), in_hbm(source))


def attend_kernel(queries, source, out):
    for head in range(queries.shape[1] // HEAD_DIM):
        part = slice(head * HEAD_DIM, (head + 1) * HEAD_DIM)
        scores = dot(queries[:, part], source[0, :, part], ((1,), (1,)))
        top = jnp.max(scores, axis=1, keepdims=True)
        weights = jnp.exp((scores - top) * HEAD_DIM**-0.5)
        total = jnp.sum(weights, axis=1, keepdims=True)
        context = dot(weights.astype(BF16), source[1, :, part])
        out[:, part] = (context / total).astype(BF16)


def attend(queries, source, block):
    rows, width = queries.shape
    if rows == block:
        return pl.pallas_call(
            attend_kernel,
            in_specs=[WHOLE] * 2,
            out_specs=WHOLE,
            out_shape=jax.ShapeDtypeStruct((rows, width), BF16),
            compiler_params=PARAMS,
        cost_estimate=CHEAP,
            name="attend",
        )(queries, source)
    return pl.pallas_call(
        attend_kernel,
        grid=(rows // block,),
        in_specs=[
            pl.BlockSpec((block, width), lambda i: (i, 0)),
            pl.BlockSpec(source.shape, lambda i: (0, 0, 0)),
        ],
        out_specs=pl.BlockSpec((block, width), lambda i: (i, 0)),
        out_shape=jax.ShapeDtypeStruct((rows, width), BF16),
        compiler_params=PARAMS,
        cost_estimate=CHEAP,
        name="attend",
    )(queries, source)


def pick_kernel(ids, owner, *refs):
    backs, out = refs[:-1], refs[-1]
    for k, back in enumerate(backs):

        @pl.when(owner[0] == ids[0] ^ k)
        def _():
            out[...] = back[...]


def pick(ids, owner, backs):
    return pl.pallas_call(
        pick_kernel,
        in_specs=[SCALARS] * 2 + [WHOLE] * len(backs),
        out_specs=WHOLE,
        out_shape=jax.ShapeDtypeStruct(backs[0].shape, BF16),
        compiler_params=PARAMS,
        cost_estimate=CHEAP,
        name="pick",
    )(ids, owner, *backs)


def route_kernel(experts, parts, ids, choice_t, choice, *outs):
    dispatch, first, second = outs[:parts], outs[parts : 2 * parts], outs[2 * parts :]
    tokens = choice_t.shape[1]
    slots = dispatch[0].shape[0]
    capacity = slots * parts // experts
    wide = lax.broadcasted_iota(jnp.int32, (tokens, experts), 1)
    tall = lax.broadcasted_iota(jnp.int32, (experts, tokens), 0)
    i = lax.broadcasted_iota(jnp.int32, (tokens, tokens), 0)
    j = lax.broadcasted_iota(jnp.int32, (tokens, tokens), 1)
    r0, r1 = choice_t[0:1, :], choice_t[1:2, :]
    turned = dot((i == j).astype(BF16), choice_t[...].astype(F32).astype(BF16), ((1,), (1,))).astype(jnp.int32)
    choice[...] = turned
    c0, c1 = turned[:, 0:1], turned[:, 1:2]
    named = ((wide == c0) | (wide == c1)).astype(BF16)
    named_t = ((tall == r0) | (tall == r1)).astype(BF16)
    rank = dot((j < i).astype(BF16), named).astype(jnp.int32)
    rank_t = dot(named_t, (i < j).astype(BF16)).astype(jnp.int32)
    place0 = c0 * capacity + jnp.sum(jnp.where(wide == c0, rank, 0), axis=1, keepdims=True)
    place1 = c1 * capacity + jnp.sum(jnp.where(wide == c1, rank, 0), axis=1, keepdims=True)
    across0 = r0 * capacity + jnp.sum(jnp.where(tall == r0, rank_t, 0), axis=0, keepdims=True)
    across1 = r1 * capacity + jnp.sum(jnp.where(tall == r1, rank_t, 0), axis=0, keepdims=True)
    lane = lax.broadcasted_iota(jnp.int32, (tokens, slots), 1)
    row = lax.broadcasted_iota(jnp.int32, (slots, tokens), 0)
    for k in range(parts):
        base = (ids[0] ^ k) * capacity if parts > 1 else 0
        dispatch[k][...] = ((row + base == across0) | (row + base == across1)).astype(BF16)
        first[k][...] = (lane + base == place0).astype(BF16)
        second[k][...] = (lane + base == place1).astype(BF16)


def route(ids, choice, experts, parts, capacity):
    tokens = choice.shape[0]
    slots = experts * capacity // parts
    outs = pl.pallas_call(
        functools.partial(route_kernel, experts, parts),
        in_specs=[SCALARS, WHOLE],
        out_specs=[WHOLE] * (1 + 3 * parts),
        out_shape=[jax.ShapeDtypeStruct(choice.shape, jnp.int32)]
        + [jax.ShapeDtypeStruct((slots, tokens), BF16)] * parts
        + [jax.ShapeDtypeStruct((tokens, slots), BF16)] * (2 * parts),
        compiler_params=PARAMS,
        cost_estimate=CHEAP,
        name="route",
    )(ids, choice.T)
    return outs[0], outs[1 : 1 + parts], outs[1 + parts : 1 + 2 * parts], outs[1 + 2 * parts :]


def state_kernel(count, sends, *refs):
    ids, tokens = refs[:2]
    contexts, weights = refs[2 : 2 + count], refs[2 + count : 2 + 2 * count]
    dispatch = refs[2 + 2 * count : 2 + 2 * count + sends]
    state, outs = refs[2 + 2 * count + sends], refs[3 + 2 * count + sends :]
    total = tokens[...].astype(F32)
    for context, weight in zip(contexts, weights):
        total += dot(context[...], weight[...])
    state[...] = total.astype(BF16)
    for rows, out in zip(dispatch, outs):
        width = out.shape[1]
        at = (ids[1] & (state.shape[1] // width - 1)) * width
        out[...] = dot(rows[...], state[:, pl.ds(pl.multiple_of(at, width), width)]).astype(BF16)


def make_state(ids, tokens, contexts, weights, dispatch, cuts):
    return pl.pallas_call(
        functools.partial(state_kernel, len(contexts), len(dispatch)),
        in_specs=[SCALARS] + [WHOLE] * (1 + 2 * len(contexts) + len(dispatch)),
        out_specs=[WHOLE] * (1 + len(dispatch)),
        out_shape=[jax.ShapeDtypeStruct(tokens.shape, BF16)]
        + [jax.ShapeDtypeStruct((rows.shape[0], tokens.shape[1] // cut), BF16) for rows, cut in zip(dispatch, cuts)],
        compiler_params=PARAMS,
        cost_estimate=CHEAP,
        name="state",
    )(ids, tokens, *contexts, *weights, *dispatch)


def home_kernel(experts, ids, state, dispatch, router, choice, own_a, own_b, gates, columns):
    half = own_a.shape[1]
    core = ids[1] & 1
    own_a[...] = dot(dispatch[...], state[:, pl.ds(pl.multiple_of(core * half, half), half)]).astype(BF16)
    own_b[...] = dot(dispatch[...], state[:, pl.ds(pl.multiple_of((1 - core) * half, half), half)]).astype(BF16)
    logits = dot(state[...], router[...], ((1,), (1,)))
    wide = lax.broadcasted_iota(jnp.int32, logits.shape, 1)
    first = jnp.sum(jnp.where(wide == choice[:, 0:1], logits, 0.0), axis=1, keepdims=True)
    second = jnp.sum(jnp.where(wide == choice[:, 1:2], logits, 0.0), axis=1, keepdims=True)
    gates[:, 0:1] = jax.nn.sigmoid(first - second)
    gates[:, 1:2] = jax.nn.sigmoid(second - first)
    width = columns.shape[1]
    columns[...] = state[:, pl.ds(pl.multiple_of(ids[1] * width, width), width)].astype(F32)


def at_home(ids, state, dispatch, router, choice, experts, width):
    tokens, features = state.shape
    slots = dispatch.shape[0]
    return pl.pallas_call(
        functools.partial(home_kernel, experts),
        in_specs=[SCALARS] + [WHOLE] * 4,
        out_specs=[WHOLE] * 4,
        out_shape=[
            jax.ShapeDtypeStruct((slots, features // 2), BF16),
            jax.ShapeDtypeStruct((slots, features // 2), BF16),
            jax.ShapeDtypeStruct((tokens, 2), F32),
            jax.ShapeDtypeStruct((tokens, width), F32),
        ],
        compiler_params=PARAMS,
        cost_estimate=CHEAP,
        name="home",
    )(ids, state, dispatch, router, choice)


def expert_kernel(orders, *refs):
    blocks, at = [], 1
    for order in orders:
        blocks.append(refs[at : at + len(order)])
        at += len(order)
    ids = refs[0]
    expand, shrink, keep, give, rows_here, hidden = refs[at:]
    count = blocks[0][0].shape[0]
    for block, (order, pieces) in enumerate(zip(orders, blocks)):
        for index, piece in zip(order, pieces):
            width = piece.shape[1]
            part = pl.ds(pl.multiple_of(((ids[1] & (len(order) - 1)) ^ index) * width, width), width)
            rows_here[block * count : (block + 1) * count, part] = piece[...]
    units = expand.shape[1]
    tile = min(TILE, units)
    for at in range(0, units, tile):
        total = dot(rows_here[...], expand[:, at : at + tile])
        hidden[:, at : at + tile] = jnp.maximum(total, 0.0).astype(BF16)
    width = keep.shape[2]
    for j in range(keep.shape[0]):
        at = pl.multiple_of((ids[1] ^ (2 * j) ^ 1) * width, width)
        give[j] = dot(hidden[...], shrink[:, pl.ds(at, width)]).astype(BF16)
    for j in range(keep.shape[0]):
        at = pl.multiple_of((ids[1] ^ (2 * j)) * width, width)
        keep[j] = dot(hidden[...], shrink[:, pl.ds(at, width)])


def run_expert(ids, orders, blocks, expand, shrink, parts):
    pieces = [piece for block in blocks for piece in block]
    rows = pieces[0].shape[0] * len(blocks)
    features, units = expand.shape
    width = features // (2 * parts)
    return pl.pallas_call(
        functools.partial(expert_kernel, tuple(map(tuple, orders))),
        in_specs=[SCALARS] + [WHOLE] * (2 + len(pieces)),
        out_specs=[WHOLE] * 2,
        out_shape=[
            jax.ShapeDtypeStruct((parts, rows, width), F32),
            jax.ShapeDtypeStruct((parts, rows, width), BF16),
        ],
        scratch_shapes=[pltpu.VMEM((rows, features), BF16), pltpu.VMEM((rows, units), BF16)],
        compiler_params=PARAMS,
        cost_estimate=CHEAP,
        name="expert",
    )(ids, *pieces, expand, shrink)


def combine_kernel(count, gates, base, first, second, *refs):
    parts, out = refs[:count], refs[count]
    total = parts[0][...].astype(F32)
    for part in parts[1:]:
        total += part[...].astype(F32)
    total = total.astype(BF16)
    result = base[...] + gates[:, 0:1] * dot(first[...], total) + gates[:, 1:2] * dot(second[...], total)
    out[...] = result.astype(out.dtype)


def combine(gates, base, first, second, parts, dtype):
    return pl.pallas_call(
        functools.partial(combine_kernel, len(parts)),
        in_specs=[WHOLE] * (4 + len(parts)),
        out_specs=WHOLE,
        out_shape=jax.ShapeDtypeStruct(base.shape, dtype),
        compiler_params=PARAMS,
        cost_estimate=CHEAP,
        name="combine",
    )(gates, base, first, second, *parts)


def bits_of(count):
    bits = []
    while 2 ** len(bits) < count:
        bits.insert(0, 2 ** len(bits))
    return bits


def local(
    tokens,
    encoder_states,
    source_owner,
    query_weight,
    output_weight,
    router_weight,
    expert_choice,
    expand_weight,
    shrink_weight,
):
    token_count, features = tokens.shape
    groups = lax.axis_size("expert")
    slices = lax.axis_size("mp")
    here, column = lax.axis_index("expert"), lax.axis_index("mp")
    ids = jnp.stack([here, column]).astype(jnp.int32)
    width = features // slices
    experts = expand_weight.shape[0] * groups
    capacity = max(2, 3 * token_count // experts)
    direct = groups <= DIRECT
    pairs = slices // 2
    slots = capacity if direct else experts * capacity

    def hop(value, along_expert, along_mp):
        if along_expert == 0 and along_mp == 0:
            return value
        moves = [
            (e * slices + m, (e ^ along_expert) * slices + (m ^ along_mp))
            for e in range(groups)
            for m in range(slices)
        ]
        return lax.ppermute(value, ("expert", "mp"), moves)

    def spread(value):
        parts = value.reshape(groups, -1, value.shape[-1])
        return lax.all_to_all(parts, "expert", 0, 0, tiled=True).reshape(value.shape)

    def after(value, other):
        return lax.optimization_barrier((value, other))[0]

    steps = range(groups) if direct else [0]

    queries, source = ask(after(tokens, ids), query_weight, encoder_states[0])
    expert_bits = bits_of(groups)
    bits = bits_of(slices)
    if direct:
        own = attend(queries, source, token_count)
        asked, steps_of = [queries], [0]
        for bit in expert_bits:
            asked = asked + [hop(value if k == 0 else after(value, own), bit, 0) for k, value in zip(steps_of, asked)]
            steps_of = steps_of + [k ^ bit for k in steps_of]
        asked = dict(zip(steps_of, asked))
        previous, backs = own, {}
        for k in sorted(range(1, groups), key=lambda k: (k & (k - 1) != 0, -k)):
            answer = previous = attend(after(asked[k], previous), source, token_count)
            backs[k] = hop(answer, k, 0)
        context = pick(ids, source_owner, [own] + [backs[k] for k in range(1, groups)])
    else:
        asked = lax.all_gather(queries, "expert", axis=0, tiled=True)
        previous = attend(asked, source, token_count)
        context = lax.dynamic_slice_in_dim(spread(previous), source_owner[0] * token_count, token_count, 0)

    choice, dispatch, first, second = route(ids, after(expert_choice, previous), experts, len(steps), capacity)
    weights, order = [output_weight], [0]
    for bit in bits:
        if bit == 1:
            weights = [after(weight, context) for weight in weights]
        weights = weights + [hop(weight, 0, bit) for weight in weights]
        order = order + [index ^ bit for index in order]
    contexts = [context]
    for bit in bits:
        contexts = contexts + [hop(value if i == 0 else after(value, dispatch[0]), 0, bit) for i, value in enumerate(contexts)]

    far = set(range(2, groups)) if direct and pairs > 1 else set()
    sends = [k for k in range(2, groups)] + ([1] if groups > 1 else []) if direct else [0]
    cuts = [slices if k in far else 2 for k in sends]
    state, *leaving = make_state(ids, tokens, contexts, weights, [dispatch[k] for k in sends], cuts)
    own_a, own_b, gates, columns = at_home(
        ids, state, dispatch[0], router_weight.T, choice, experts, width
    )
    expert = functools.partial(run_expert, expand=expand_weight[0], shrink=shrink_weight[0], parts=pairs)

    def sum_cores(keep, give):
        return keep + hop(give, 0, 1).astype(F32)

    def sum_slices(summed):
        total = summed[0]
        for j in range(1, pairs):
            total += hop(summed[j].astype(BF16), 0, 2 * j).astype(F32)
        return total.astype(BF16)

    def send_home(k, summed, wait=None):
        parts = [summed[j].astype(BF16) for j in range(pairs)]
        if wait is not None:
            parts = parts[:1] + [after(part, wait) for part in parts[1:]]
        return [hop(part, k, 2 * j) if direct else hop(spread(part), 0, 2 * j) for j, part in enumerate(parts)]

    home, order = {}, [0]
    if direct:
        arrived = {k: hop(rows, k, 0) for k, rows in zip(sends, leaving)}
        keep, give = expert(ids, [[0, 1]], [[own_a, own_b]])
        turn_ids = after(ids, give)
        if sends:
            give = after(give, arrived[sends[0]])
        own_sum, wait = sum_cores(keep, give), None
        turn_ids = after(ids, own_sum)
        turns = [[k for k in sends if k < groups - 1], [groups - 1]] if groups > 2 else [sends]
        for turn in turns:
            blocks, orders = [], []
            for k in turn:
                pieces, places = [arrived[k]], [0]
                for bit in bits if k in far else [1]:
                    pieces = pieces + [hop(piece, 0, bit) for piece in pieces]
                    places = places + [index ^ bit for index in places]
                blocks.append(pieces)
                orders.append(places)
            if turn:
                keep, give = expert(turn_ids, orders, blocks)
                turn_ids = after(ids, give)
                summed = sum_cores(keep, give)
                for i, k in enumerate(turn):
                    rows = summed[:, i * slots : (i + 1) * slots]
                    if k in far:
                        total = sum_slices(rows)
                        wait = total if wait is None else wait
                        home[k] = [hop(total, k, 0)]
                    else:
                        home[k] = send_home(k, rows)
        home[0] = send_home(0, own_sum, wait)
        order = [0] + sorted(sends)
    else:
        mine = spread(leaving[0])
        home[0] = send_home(0, sum_cores(*expert(ids, [[0, 1]], [[mine, hop(mine, 0, 1)]])))
    results = columns
    for k in order:
        results = combine(gates, results, first[k], second[k], home[k], BF16 if k == order[-1] else F32)
    return results


def solution(mesh):
    return jax.shard_map(
        local,
        mesh=mesh,
        in_specs=(
            P(("groups", "expert"), None),
            P(("groups", "expert"), None, None, "mp"),
            P(("groups", "expert")),
            P(None, "mp"),
            P("mp", None),
            P(),
            P(("groups", "expert"), None),
            P("expert", None, "mp"),
            P("expert", "mp", None),
        ),
        out_specs=P(("groups", "expert"), "mp"),
        check_vma=False,
    )
```

```python
import functools

import jax
import jax.numpy as jnp
from jax import lax
from jax.experimental import pallas as pl
from jax.experimental.pallas import tpu as pltpu
from jax.sharding import PartitionSpec as P

HEAD_DIM = 128
DIRECT = 8
CUTS = 4
TILE = 256
F32, BF16 = jnp.float32, jnp.bfloat16
PARAMS = pltpu.CompilerParams(vmem_limit_bytes=20 * 2**20)
CHEAP = pl.CostEstimate(flops=0, bytes_accessed=0, transcendentals=0)
WHOLE = pl.BlockSpec(memory_space=pltpu.VMEM)


def dot(a, b, dims=((1,), (0,))):
    return lax.dot_general(a, b, (dims, ((), ())), preferred_element_type=F32)


def in_hbm(value):
    return pltpu.with_memory_space_constraint(value, pltpu.HBM)


def position():
    return lax.axis_index("expert"), lax.axis_index("mp")


def query_kernel(tokens, weight, source, out, staged, tokens_here, weight_here, sems):
    features = tokens.shape[1]
    depth = features // CUTS
    copies, later = [], []
    for i in range(CUTS):
        part = pl.ds(i * depth, depth)
        copies.append(
            (
                pltpu.make_async_copy(tokens.at[:, part], tokens_here.at[:, part], sems.at[0, i]),
                pltpu.make_async_copy(weight.at[part, :], weight_here.at[part, :], sems.at[1, i]),
            )
        )
        rows = pl.ds(i * (source.shape[1] // CUTS), source.shape[1] // CUTS)
        later.append(pltpu.make_async_copy(source.at[:, rows], staged.at[:, rows], sems.at[2, i]))
    for pair in copies:
        for copy in pair:
            copy.start()
    for copy in later:
        copy.start()
    total = jnp.zeros(out.shape, F32)
    for i, pair in enumerate(copies):
        for copy in pair:
            copy.wait()
        part = slice(i * depth, (i + 1) * depth)
        total += dot(tokens_here[:, part], weight_here[part, :])
    out[...] = total.astype(BF16)
    for copy in later:
        copy.wait()


def ask(tokens, weight, source):
    return pl.pallas_call(
        query_kernel,
        in_specs=[pl.BlockSpec(memory_space=pltpu.HBM)] * 3,
        out_specs=[WHOLE] * 2,
        out_shape=[
            jax.ShapeDtypeStruct((tokens.shape[0], weight.shape[1]), BF16),
            jax.ShapeDtypeStruct(source.shape, BF16),
        ],
        scratch_shapes=[
            pltpu.VMEM(tokens.shape, BF16),
            pltpu.VMEM(weight.shape, BF16),
            pltpu.SemaphoreType.DMA((3, CUTS)),
        ],
        compiler_params=PARAMS,
        cost_estimate=CHEAP,
        name="query",
    )(in_hbm(tokens), in_hbm(weight), in_hbm(source))


def attend_kernel(queries, source, out):
    for head in range(queries.shape[1] // HEAD_DIM):
        part = slice(head * HEAD_DIM, (head + 1) * HEAD_DIM)
        scores = dot(queries[:, part], source[0, :, part], ((1,), (1,)))
        top = jnp.max(scores, axis=1, keepdims=True)
        weights = jnp.exp((scores - top) * HEAD_DIM**-0.5)
        total = jnp.sum(weights, axis=1, keepdims=True)
        context = dot(weights.astype(BF16), source[1, :, part])
        out[:, part] = (context / total).astype(BF16)


def attend(queries, source, block):
    rows, width = queries.shape
    if rows == block:
        return pl.pallas_call(
            attend_kernel,
            in_specs=[WHOLE] * 2,
            out_specs=WHOLE,
            out_shape=jax.ShapeDtypeStruct((rows, width), BF16),
            compiler_params=PARAMS,
        cost_estimate=CHEAP,
            name="attend",
        )(queries, source)
    return pl.pallas_call(
        attend_kernel,
        grid=(rows // block,),
        in_specs=[
            pl.BlockSpec((block, width), lambda i: (i, 0)),
            pl.BlockSpec(source.shape, lambda i: (0, 0, 0)),
        ],
        out_specs=pl.BlockSpec((block, width), lambda i: (i, 0)),
        out_shape=jax.ShapeDtypeStruct((rows, width), BF16),
        compiler_params=PARAMS,
        cost_estimate=CHEAP,
        name="attend",
    )(queries, source)


def pick_kernel(owner, *refs):
    backs, out = refs[:-1], refs[-1]
    here, _ = position()
    names = jnp.broadcast_to(owner[0:1, 0:1], out.shape)
    total = backs[0][...].astype(F32)
    for k in range(1, len(backs)):
        total = jnp.where(names == here ^ k, backs[k][...].astype(F32), total)
    out[...] = total.astype(BF16)


def pick(owner, backs):
    return pl.pallas_call(
        pick_kernel,
        in_specs=[WHOLE] * (1 + len(backs)),
        out_specs=WHOLE,
        out_shape=jax.ShapeDtypeStruct(backs[0].shape, BF16),
        compiler_params=PARAMS,
        cost_estimate=CHEAP,
        name="pick",
    )(owner, *backs)


def route_kernel(experts, parts, choice_t, choice, *outs):
    dispatch, first, second = outs[:parts], outs[parts : 2 * parts], outs[2 * parts :]
    tokens = choice_t.shape[1]
    slots = dispatch[0].shape[0]
    capacity = slots * parts // experts
    wide = lax.broadcasted_iota(jnp.int32, (tokens, experts), 1)
    tall = lax.broadcasted_iota(jnp.int32, (experts, tokens), 0)
    i = lax.broadcasted_iota(jnp.int32, (tokens, tokens), 0)
    j = lax.broadcasted_iota(jnp.int32, (tokens, tokens), 1)
    r0, r1 = choice_t[0:1, :], choice_t[1:2, :]
    turned = dot((i == j).astype(BF16), choice_t[...].astype(F32).astype(BF16), ((1,), (1,))).astype(jnp.int32)
    choice[...] = turned
    c0, c1 = turned[:, 0:1], turned[:, 1:2]
    named = ((wide == c0) | (wide == c1)).astype(BF16)
    named_t = ((tall == r0) | (tall == r1)).astype(BF16)
    rank = dot((j < i).astype(BF16), named).astype(jnp.int32)
    rank_t = dot(named_t, (i < j).astype(BF16)).astype(jnp.int32)
    place0 = c0 * capacity + jnp.sum(jnp.where(wide == c0, rank, 0), axis=1, keepdims=True)
    place1 = c1 * capacity + jnp.sum(jnp.where(wide == c1, rank, 0), axis=1, keepdims=True)
    across0 = r0 * capacity + jnp.sum(jnp.where(tall == r0, rank_t, 0), axis=0, keepdims=True)
    across1 = r1 * capacity + jnp.sum(jnp.where(tall == r1, rank_t, 0), axis=0, keepdims=True)
    lane = lax.broadcasted_iota(jnp.int32, (tokens, slots), 1)
    row = lax.broadcasted_iota(jnp.int32, (slots, tokens), 0)
    for k in range(parts):
        base = (position()[0] ^ k) * capacity if parts > 1 else 0
        dispatch[k][...] = ((row + base == across0) | (row + base == across1)).astype(BF16)
        first[k][...] = (lane + base == place0).astype(BF16)
        second[k][...] = (lane + base == place1).astype(BF16)


def route(choice, experts, parts, capacity):
    tokens = choice.shape[0]
    slots = experts * capacity // parts
    outs = pl.pallas_call(
        functools.partial(route_kernel, experts, parts),
        in_specs=[WHOLE],
        out_specs=[WHOLE] * (1 + 3 * parts),
        out_shape=[jax.ShapeDtypeStruct(choice.shape, jnp.int32)]
        + [jax.ShapeDtypeStruct((slots, tokens), BF16)] * parts
        + [jax.ShapeDtypeStruct((tokens, slots), BF16)] * (2 * parts),
        compiler_params=PARAMS,
        cost_estimate=CHEAP,
        name="route",
    )(choice.T)
    return outs[0], outs[1 : 1 + parts], outs[1 + parts : 1 + 2 * parts], outs[1 + 2 * parts :]


def state_kernel(count, sends, *refs):
    tokens = refs[0]
    contexts, weights = refs[1 : 1 + count], refs[1 + count : 1 + 2 * count]
    dispatch = refs[1 + 2 * count : 1 + 2 * count + sends]
    state, outs = refs[1 + 2 * count + sends], refs[2 + 2 * count + sends :]
    tile = min(TILE, state.shape[1])
    for at in range(0, state.shape[1], tile):
        part = slice(at, at + tile)
        total = tokens[:, part].astype(F32)
        for context, weight in zip(contexts, weights):
            total += dot(context[...], weight[:, part])
        state[:, part] = total.astype(BF16)
    for rows, out in zip(dispatch, outs):
        width = out.shape[1]
        at = (position()[1] & (state.shape[1] // width - 1)) * width
        out[...] = dot(rows[...], state[:, pl.ds(pl.multiple_of(at, width), width)]).astype(BF16)


def make_state(tokens, contexts, weights, dispatch, cuts):
    return pl.pallas_call(
        functools.partial(state_kernel, len(contexts), len(dispatch)),
        in_specs=[WHOLE] * (1 + 2 * len(contexts) + len(dispatch)),
        out_specs=[WHOLE] * (1 + len(dispatch)),
        out_shape=[jax.ShapeDtypeStruct(tokens.shape, BF16)]
        + [jax.ShapeDtypeStruct((rows.shape[0], tokens.shape[1] // cut), BF16) for rows, cut in zip(dispatch, cuts)],
        compiler_params=PARAMS,
        cost_estimate=CHEAP,
        name="state",
    )(tokens, *contexts, *weights, *dispatch)


def home_kernel(experts, state, dispatch, router, choice, own_a, own_b, gates, columns):
    half = own_a.shape[1]
    column = position()[1]
    core = column & 1
    own_a[...] = dot(dispatch[...], state[:, pl.ds(pl.multiple_of(core * half, half), half)]).astype(BF16)
    own_b[...] = dot(dispatch[...], state[:, pl.ds(pl.multiple_of((1 - core) * half, half), half)]).astype(BF16)
    logits = dot(state[...], router[...], ((1,), (1,)))
    wide = lax.broadcasted_iota(jnp.int32, logits.shape, 1)
    first = jnp.sum(jnp.where(wide == choice[:, 0:1], logits, 0.0), axis=1, keepdims=True)
    second = jnp.sum(jnp.where(wide == choice[:, 1:2], logits, 0.0), axis=1, keepdims=True)
    gates[:, 0:1] = jax.nn.sigmoid(first - second)
    gates[:, 1:2] = jax.nn.sigmoid(second - first)
    width = columns.shape[1]
    columns[...] = state[:, pl.ds(pl.multiple_of(column * width, width), width)].astype(F32)


def at_home(state, dispatch, router, choice, experts, width):
    tokens, features = state.shape
    slots = dispatch.shape[0]
    return pl.pallas_call(
        functools.partial(home_kernel, experts),
        in_specs=[WHOLE] * 4,
        out_specs=[WHOLE] * 4,
        out_shape=[
            jax.ShapeDtypeStruct((slots, features // 2), BF16),
            jax.ShapeDtypeStruct((slots, features // 2), BF16),
            jax.ShapeDtypeStruct((tokens, 2), F32),
            jax.ShapeDtypeStruct((tokens, width), F32),
        ],
        compiler_params=PARAMS,
        cost_estimate=CHEAP,
        name="home",
    )(state, dispatch, router, choice)


def expert_kernel(orders, *refs):
    blocks, at = [], 0
    for order in orders:
        blocks.append(refs[at : at + len(order)])
        at += len(order)
    column = position()[1]
    expand, shrink, keep, give, rows_here, hidden = refs[at:]
    count = blocks[0][0].shape[0]
    for block, (order, pieces) in enumerate(zip(orders, blocks)):
        for index, piece in zip(order, pieces):
            width = piece.shape[1]
            part = pl.ds(pl.multiple_of(((column & (len(order) - 1)) ^ index) * width, width), width)
            rows_here[block * count : (block + 1) * count, part] = piece[...]
    units = expand.shape[1]
    tile = min(TILE, units)
    for at in range(0, units, tile):
        total = dot(rows_here[...], expand[:, at : at + tile])
        hidden[:, at : at + tile] = jnp.maximum(total, 0.0).astype(BF16)
    width = keep.shape[2]
    for j in range(keep.shape[0]):
        at = pl.multiple_of((column ^ (2 * j) ^ 1) * width, width)
        give[j] = dot(hidden[...], shrink[:, pl.ds(at, width)]).astype(BF16)
    for j in range(keep.shape[0]):
        at = pl.multiple_of((column ^ (2 * j)) * width, width)
        keep[j] = dot(hidden[...], shrink[:, pl.ds(at, width)])


def run_expert(orders, blocks, expand, shrink, parts):
    pieces = [piece for block in blocks for piece in block]
    rows = pieces[0].shape[0] * len(blocks)
    features, units = expand.shape
    width = features // (2 * parts)
    return pl.pallas_call(
        functools.partial(expert_kernel, tuple(map(tuple, orders))),
        in_specs=[WHOLE] * (2 + len(pieces)),
        out_specs=[WHOLE] * 2,
        out_shape=[
            jax.ShapeDtypeStruct((parts, rows, width), F32),
            jax.ShapeDtypeStruct((parts, rows, width), BF16),
        ],
        scratch_shapes=[pltpu.VMEM((rows, features), BF16), pltpu.VMEM((rows, units), BF16)],
        compiler_params=PARAMS,
        cost_estimate=CHEAP,
        name="expert",
    )(*pieces, expand, shrink)


def combine_kernel(count, gates, base, first, second, *refs):
    parts, out = refs[:count], refs[count]
    total = parts[0][...].astype(F32)
    for part in parts[1:]:
        total += part[...].astype(F32)
    total = total.astype(BF16)
    result = base[...] + gates[:, 0:1] * dot(first[...], total) + gates[:, 1:2] * dot(second[...], total)
    out[...] = result.astype(out.dtype)


def combine(gates, base, first, second, parts, dtype):
    return pl.pallas_call(
        functools.partial(combine_kernel, len(parts)),
        in_specs=[WHOLE] * (4 + len(parts)),
        out_specs=WHOLE,
        out_shape=jax.ShapeDtypeStruct(base.shape, dtype),
        compiler_params=PARAMS,
        cost_estimate=CHEAP,
        name="combine",
    )(gates, base, first, second, *parts)


def bits_of(count):
    bits = []
    while 2 ** len(bits) < count:
        bits.insert(0, 2 ** len(bits))
    return bits


def local(
    tokens,
    encoder_states,
    source_owner,
    query_weight,
    output_weight,
    router_weight,
    expert_choice,
    expand_weight,
    shrink_weight,
):
    token_count, features = tokens.shape
    groups = lax.axis_size("expert")
    slices = lax.axis_size("mp")
    here, column = lax.axis_index("expert"), lax.axis_index("mp")
    owner_rows = jnp.broadcast_to(source_owner[:, None], (8, 128))
    width = features // slices
    experts = expand_weight.shape[0] * groups
    capacity = max(2, 3 * token_count // experts)
    direct = groups <= DIRECT
    pairs = slices // 2
    slots = capacity if direct else experts * capacity

    def hop(value, along_expert, along_mp):
        if along_expert == 0 and along_mp == 0:
            return value
        moves = [
            (e * slices + m, (e ^ along_expert) * slices + (m ^ along_mp))
            for e in range(groups)
            for m in range(slices)
        ]
        return lax.ppermute(value, ("expert", "mp"), moves)

    def spread(value):
        parts = value.reshape(groups, -1, value.shape[-1])
        return lax.all_to_all(parts, "expert", 0, 0, tiled=True).reshape(value.shape)

    def after(value, other):
        return lax.optimization_barrier((value, other))[0]

    steps = range(groups) if direct else [0]

    queries, source = ask(after(tokens, owner_rows), query_weight, encoder_states[0])
    expert_bits = bits_of(groups)
    bits = bits_of(slices)
    if direct:
        own = attend(queries, source, token_count)
        asked, steps_of = [queries], [0]
        for bit in expert_bits:
            asked = asked + [hop(value if k == 0 else after(value, own), bit, 0) for k, value in zip(steps_of, asked)]
            steps_of = steps_of + [k ^ bit for k in steps_of]
        asked = dict(zip(steps_of, asked))
        previous, backs = own, {}
        for k in sorted(range(1, groups), key=lambda k: (k & (k - 1) != 0, -k)):
            answer = previous = attend(after(asked[k], previous), source, token_count)
            backs[k] = hop(answer, k, 0)
        context = pick(owner_rows, [own] + [backs[k] for k in range(1, groups)])
    else:
        asked = lax.all_gather(queries, "expert", axis=0, tiled=True)
        previous = attend(asked, source, token_count)
        context = lax.dynamic_slice_in_dim(spread(previous), source_owner[0] * token_count, token_count, 0)

    choice, dispatch, first, second = route(after(expert_choice, previous), experts, len(steps), capacity)
    weights, order = [output_weight], [0]
    for bit in bits:
        if bit == 1:
            weights = [after(weight, context) for weight in weights]
        weights = weights + [hop(weight, 0, bit) for weight in weights]
        order = order + [index ^ bit for index in order]
    contexts = [context]
    for bit in bits:
        contexts = contexts + [hop(value if i == 0 else after(value, dispatch[0]), 0, bit) for i, value in enumerate(contexts)]

    far = set(range(2, groups)) if direct and pairs > 1 else set()
    sends = [k for k in range(2, groups)] + ([1] if groups > 1 else []) if direct else [0]
    cuts = [slices if k in far else 2 for k in sends]
    state, *leaving = make_state(tokens, contexts, weights, [dispatch[k] for k in sends], cuts)
    own_a, own_b, gates, columns = at_home(
        state, dispatch[0], router_weight.T, choice, experts, width
    )
    expert = functools.partial(run_expert, expand=expand_weight[0], shrink=shrink_weight[0], parts=pairs)

    def sum_cores(keep, give):
        return keep + hop(give, 0, 1).astype(F32)

    def sum_slices(summed):
        total = summed[0]
        for j in range(1, pairs):
            total += hop(summed[j].astype(BF16), 0, 2 * j).astype(F32)
        return total.astype(BF16)

    def send_home(k, summed, wait=None):
        parts = [summed[j].astype(BF16) for j in range(pairs)]
        if wait is not None:
            parts = parts[:1] + [after(part, wait) for part in parts[1:]]
        return [hop(part, k, 2 * j) if direct else hop(spread(part), 0, 2 * j) for j, part in enumerate(parts)]

    home, order = {}, [0]
    if direct:
        arrived = {k: hop(rows, k, 0) for k, rows in zip(sends, leaving)}
        keep, give = expert([[0, 1]], [[own_a, own_b]])
        if sends:
            give = after(give, arrived[sends[0]])
        own_sum, wait = sum_cores(keep, give), None
        earlier = own_sum
        turns = [[k for k in sends if k < groups - 1], [groups - 1]] if groups > 2 else [sends]
        for turn in turns:
            blocks, orders = [], []
            for k in turn:
                pieces, places = [arrived[k]], [0]
                for bit in bits if k in far else [1]:
                    pieces = pieces + [hop(piece, 0, bit) for piece in pieces]
                    places = places + [index ^ bit for index in places]
                blocks.append(pieces)
                orders.append(places)
            if turn:
                blocks[0][0] = after(blocks[0][0], earlier)
                keep, give = expert(orders, blocks)
                earlier = give
                summed = sum_cores(keep, give)
                for i, k in enumerate(turn):
                    rows = summed[:, i * slots : (i + 1) * slots]
                    if k in far:
                        total = sum_slices(rows)
                        wait = total if wait is None else wait
                        home[k] = [hop(total, k, 0)]
                    else:
                        home[k] = send_home(k, rows)
        home[0] = send_home(0, own_sum, wait)
        order = [0] + sorted(sends)
    else:
        mine = spread(leaving[0])
        home[0] = send_home(0, sum_cores(*expert([[0, 1]], [[mine, hop(mine, 0, 1)]])))
    results = columns
    for k in order:
        results = combine(gates, results, first[k], second[k], home[k], BF16 if k == order[-1] else F32)
    return results


def solution(mesh):
    return jax.shard_map(
        local,
        mesh=mesh,
        in_specs=(
            P(("groups", "expert"), None),
            P(("groups", "expert"), None, None, "mp"),
            P(("groups", "expert")),
            P(None, "mp"),
            P("mp", None),
            P(),
            P(("groups", "expert"), None),
            P("expert", None, "mp"),
            P("expert", "mp", None),
        ),
        out_specs=P(("groups", "expert"), "mp"),
        check_vma=False,
    )
```

```python
import functools

import jax
import jax.numpy as jnp
from jax import lax
from jax.experimental import pallas as pl
from jax.experimental.pallas import tpu as pltpu
from jax.sharding import PartitionSpec as P

HEAD_DIM = 128
DIRECT = 8
CUTS = 4
TILE = 256
F32, BF16 = jnp.float32, jnp.bfloat16
PARAMS = pltpu.CompilerParams(vmem_limit_bytes=20 * 2**20)
CHEAP = pl.CostEstimate(flops=0, bytes_accessed=0, transcendentals=0)
WHOLE = pl.BlockSpec(memory_space=pltpu.VMEM)


def dot(a, b, dims=((1,), (0,))):
    return lax.dot_general(a, b, (dims, ((), ())), preferred_element_type=F32)


def in_hbm(value):
    return pltpu.with_memory_space_constraint(value, pltpu.HBM)


def position():
    return lax.axis_index("expert"), lax.axis_index("mp")


def query_kernel(tokens, weight, source, out, staged, tokens_here, weight_here, sems):
    features = tokens.shape[1]
    depth = features // CUTS
    copies, later = [], []
    for i in range(CUTS):
        part = pl.ds(i * depth, depth)
        copies.append(
            (
                pltpu.make_async_copy(tokens.at[:, part], tokens_here.at[:, part], sems.at[0, i]),
                pltpu.make_async_copy(weight.at[part, :], weight_here.at[part, :], sems.at[1, i]),
            )
        )
        rows = pl.ds(i * (source.shape[1] // CUTS), source.shape[1] // CUTS)
        later.append(pltpu.make_async_copy(source.at[:, rows], staged.at[:, rows], sems.at[2, i]))
    for pair in copies:
        for copy in pair:
            copy.start()
    for copy in later:
        copy.start()
    total = jnp.zeros(out.shape, F32)
    for i, pair in enumerate(copies):
        for copy in pair:
            copy.wait()
        part = slice(i * depth, (i + 1) * depth)
        total += dot(tokens_here[:, part], weight_here[part, :])
    out[...] = total.astype(BF16)
    for copy in later:
        copy.wait()


def ask(tokens, weight, source):
    return pl.pallas_call(
        query_kernel,
        in_specs=[pl.BlockSpec(memory_space=pltpu.HBM)] * 3,
        out_specs=[WHOLE] * 2,
        out_shape=[
            jax.ShapeDtypeStruct((tokens.shape[0], weight.shape[1]), BF16),
            jax.ShapeDtypeStruct(source.shape, BF16),
        ],
        scratch_shapes=[
            pltpu.VMEM(tokens.shape, BF16),
            pltpu.VMEM(weight.shape, BF16),
            pltpu.SemaphoreType.DMA((3, CUTS)),
        ],
        compiler_params=PARAMS,
        cost_estimate=CHEAP,
        name="query",
    )(in_hbm(tokens), in_hbm(weight), in_hbm(source))


def attend_kernel(queries, source, out):
    for head in range(queries.shape[1] // HEAD_DIM):
        part = slice(head * HEAD_DIM, (head + 1) * HEAD_DIM)
        scores = dot(queries[:, part], source[0, :, part], ((1,), (1,)))
        top = jnp.max(scores, axis=1, keepdims=True)
        weights = jnp.exp((scores - top) * HEAD_DIM**-0.5)
        total = jnp.sum(weights, axis=1, keepdims=True)
        context = dot(weights.astype(BF16), source[1, :, part])
        out[:, part] = (context / total).astype(BF16)


def attend(queries, source, block):
    rows, width = queries.shape
    if rows == block:
        return pl.pallas_call(
            attend_kernel,
            in_specs=[WHOLE] * 2,
            out_specs=WHOLE,
            out_shape=jax.ShapeDtypeStruct((rows, width), BF16),
            compiler_params=PARAMS,
        cost_estimate=CHEAP,
            name="attend",
        )(queries, source)
    return pl.pallas_call(
        attend_kernel,
        grid=(rows // block,),
        in_specs=[
            pl.BlockSpec((block, width), lambda i: (i, 0)),
            pl.BlockSpec(source.shape, lambda i: (0, 0, 0)),
        ],
        out_specs=pl.BlockSpec((block, width), lambda i: (i, 0)),
        out_shape=jax.ShapeDtypeStruct((rows, width), BF16),
        compiler_params=PARAMS,
        cost_estimate=CHEAP,
        name="attend",
    )(queries, source)


def pick_kernel(owner, *refs):
    backs, out = refs[:-1], refs[-1]
    here, _ = position()
    names = jnp.broadcast_to(owner[0:1, 0:1], out.shape)
    total = backs[0][...].astype(F32)
    for k in range(1, len(backs)):
        total = jnp.where(names == here ^ k, backs[k][...].astype(F32), total)
    out[...] = total.astype(BF16)


def pick(owner, backs):
    return pl.pallas_call(
        pick_kernel,
        in_specs=[WHOLE] * (1 + len(backs)),
        out_specs=WHOLE,
        out_shape=jax.ShapeDtypeStruct(backs[0].shape, BF16),
        compiler_params=PARAMS,
        cost_estimate=CHEAP,
        name="pick",
    )(owner, *backs)


def route_kernel(experts, parts, choice_t, choice, *outs):
    dispatch, first, second = outs[:parts], outs[parts : 2 * parts], outs[2 * parts :]
    tokens = choice_t.shape[1]
    slots = dispatch[0].shape[0]
    capacity = slots * parts // experts
    wide = lax.broadcasted_iota(jnp.int32, (tokens, experts), 1)
    tall = lax.broadcasted_iota(jnp.int32, (experts, tokens), 0)
    i = lax.broadcasted_iota(jnp.int32, (tokens, tokens), 0)
    j = lax.broadcasted_iota(jnp.int32, (tokens, tokens), 1)
    r0, r1 = choice_t[0:1, :], choice_t[1:2, :]
    turned = dot((i == j).astype(BF16), choice_t[...].astype(F32).astype(BF16), ((1,), (1,))).astype(jnp.int32)
    choice[...] = turned
    c0, c1 = turned[:, 0:1], turned[:, 1:2]
    named = ((wide == c0) | (wide == c1)).astype(BF16)
    named_t = ((tall == r0) | (tall == r1)).astype(BF16)
    rank = dot((j < i).astype(BF16), named).astype(jnp.int32)
    rank_t = dot(named_t, (i < j).astype(BF16)).astype(jnp.int32)
    place0 = c0 * capacity + jnp.sum(jnp.where(wide == c0, rank, 0), axis=1, keepdims=True)
    place1 = c1 * capacity + jnp.sum(jnp.where(wide == c1, rank, 0), axis=1, keepdims=True)
    across0 = r0 * capacity + jnp.sum(jnp.where(tall == r0, rank_t, 0), axis=0, keepdims=True)
    across1 = r1 * capacity + jnp.sum(jnp.where(tall == r1, rank_t, 0), axis=0, keepdims=True)
    lane = lax.broadcasted_iota(jnp.int32, (tokens, slots), 1)
    row = lax.broadcasted_iota(jnp.int32, (slots, tokens), 0)
    for k in range(parts):
        base = (position()[0] ^ k) * capacity if parts > 1 else 0
        dispatch[k][...] = ((row + base == across0) | (row + base == across1)).astype(BF16)
        first[k][...] = (lane + base == place0).astype(BF16)
        second[k][...] = (lane + base == place1).astype(BF16)


def route(choice, experts, parts, capacity):
    tokens = choice.shape[0]
    slots = experts * capacity // parts
    outs = pl.pallas_call(
        functools.partial(route_kernel, experts, parts),
        in_specs=[WHOLE],
        out_specs=[WHOLE] * (1 + 3 * parts),
        out_shape=[jax.ShapeDtypeStruct(choice.shape, jnp.int32)]
        + [jax.ShapeDtypeStruct((slots, tokens), BF16)] * parts
        + [jax.ShapeDtypeStruct((tokens, slots), BF16)] * (2 * parts),
        compiler_params=PARAMS,
        cost_estimate=CHEAP,
        name="route",
    )(choice.T)
    return outs[0], outs[1 : 1 + parts], outs[1 + parts : 1 + 2 * parts], outs[1 + 2 * parts :]


def state_kernel(count, sends, *refs):
    tokens = refs[0]
    contexts, weights = refs[1 : 1 + count], refs[1 + count : 1 + 2 * count]
    dispatch = refs[1 + 2 * count : 1 + 2 * count + sends]
    state, outs = refs[1 + 2 * count + sends], refs[2 + 2 * count + sends :]
    tile = min(TILE, state.shape[1])
    for at in range(0, state.shape[1], tile):
        part = slice(at, at + tile)
        total = tokens[:, part].astype(F32)
        for context, weight in zip(contexts, weights):
            total += dot(context[...], weight[:, part])
        state[:, part] = total.astype(BF16)
    for rows, out in zip(dispatch, outs):
        width = out.shape[1]
        at = (position()[1] & (state.shape[1] // width - 1)) * width
        out[...] = dot(rows[...], state[:, pl.ds(pl.multiple_of(at, width), width)]).astype(BF16)


def make_state(tokens, contexts, weights, dispatch, cuts):
    return pl.pallas_call(
        functools.partial(state_kernel, len(contexts), len(dispatch)),
        in_specs=[WHOLE] * (1 + 2 * len(contexts) + len(dispatch)),
        out_specs=[WHOLE] * (1 + len(dispatch)),
        out_shape=[jax.ShapeDtypeStruct(tokens.shape, BF16)]
        + [jax.ShapeDtypeStruct((rows.shape[0], tokens.shape[1] // cut), BF16) for rows, cut in zip(dispatch, cuts)],
        compiler_params=PARAMS,
        cost_estimate=CHEAP,
        name="state",
    )(tokens, *contexts, *weights, *dispatch)


def home_kernel(experts, state, dispatch, router, choice, own_a, own_b, gates, columns):
    half = own_a.shape[1]
    column = position()[1]
    core = column & 1
    own_a[...] = dot(dispatch[...], state[:, pl.ds(pl.multiple_of(core * half, half), half)]).astype(BF16)
    own_b[...] = dot(dispatch[...], state[:, pl.ds(pl.multiple_of((1 - core) * half, half), half)]).astype(BF16)
    logits = dot(state[...], router[...], ((1,), (1,)))
    wide = lax.broadcasted_iota(jnp.int32, logits.shape, 1)
    first = jnp.sum(jnp.where(wide == choice[:, 0:1], logits, 0.0), axis=1, keepdims=True)
    second = jnp.sum(jnp.where(wide == choice[:, 1:2], logits, 0.0), axis=1, keepdims=True)
    gates[:, 0:1] = jax.nn.sigmoid(first - second)
    gates[:, 1:2] = jax.nn.sigmoid(second - first)
    width = columns.shape[1]
    columns[...] = state[:, pl.ds(pl.multiple_of(column * width, width), width)].astype(F32)


def at_home(state, dispatch, router, choice, experts, width):
    tokens, features = state.shape
    slots = dispatch.shape[0]
    return pl.pallas_call(
        functools.partial(home_kernel, experts),
        in_specs=[WHOLE] * 4,
        out_specs=[WHOLE] * 4,
        out_shape=[
            jax.ShapeDtypeStruct((slots, features // 2), BF16),
            jax.ShapeDtypeStruct((slots, features // 2), BF16),
            jax.ShapeDtypeStruct((tokens, 2), F32),
            jax.ShapeDtypeStruct((tokens, width), F32),
        ],
        compiler_params=PARAMS,
        cost_estimate=CHEAP,
        name="home",
    )(state, dispatch, router, choice)


def expert_kernel(orders, *refs):
    blocks, at = [], 0
    for order in orders:
        blocks.append(refs[at : at + len(order)])
        at += len(order)
    column = position()[1]
    expand, shrink, keep, give, rows_here, hidden = refs[at:]
    count = blocks[0][0].shape[0]
    for block, (order, pieces) in enumerate(zip(orders, blocks)):
        for index, piece in zip(order, pieces):
            width = piece.shape[1]
            part = pl.ds(pl.multiple_of(((column & (len(order) - 1)) ^ index) * width, width), width)
            rows_here[block * count : (block + 1) * count, part] = piece[...]
    units = expand.shape[1]
    tile = min(TILE, units)
    for at in range(0, units, tile):
        total = dot(rows_here[...], expand[:, at : at + tile])
        hidden[:, at : at + tile] = jnp.maximum(total, 0.0).astype(BF16)
    width = keep.shape[2]
    for j in range(keep.shape[0]):
        at = pl.multiple_of((column ^ (2 * j) ^ 1) * width, width)
        give[j] = dot(hidden[...], shrink[:, pl.ds(at, width)]).astype(BF16)
    for j in range(keep.shape[0]):
        at = pl.multiple_of((column ^ (2 * j)) * width, width)
        keep[j] = dot(hidden[...], shrink[:, pl.ds(at, width)])


def run_expert(orders, blocks, expand, shrink, parts):
    pieces = [piece for block in blocks for piece in block]
    rows = pieces[0].shape[0] * len(blocks)
    features, units = expand.shape
    width = features // (2 * parts)
    return pl.pallas_call(
        functools.partial(expert_kernel, tuple(map(tuple, orders))),
        in_specs=[WHOLE] * (2 + len(pieces)),
        out_specs=[WHOLE] * 2,
        out_shape=[
            jax.ShapeDtypeStruct((parts, rows, width), F32),
            jax.ShapeDtypeStruct((parts, rows, width), BF16),
        ],
        scratch_shapes=[pltpu.VMEM((rows, features), BF16), pltpu.VMEM((rows, units), BF16)],
        compiler_params=PARAMS,
        cost_estimate=CHEAP,
        name="expert",
    )(*pieces, expand, shrink)


def combine_kernel(count, gates, base, first, second, *refs):
    parts, out = refs[:count], refs[count]
    total = parts[0][...].astype(F32)
    for part in parts[1:]:
        total += part[...].astype(F32)
    total = total.astype(BF16)
    result = base[...] + gates[:, 0:1] * dot(first[...], total) + gates[:, 1:2] * dot(second[...], total)
    out[...] = result.astype(out.dtype)


def combine(gates, base, first, second, parts, dtype):
    return pl.pallas_call(
        functools.partial(combine_kernel, len(parts)),
        in_specs=[WHOLE] * (4 + len(parts)),
        out_specs=WHOLE,
        out_shape=jax.ShapeDtypeStruct(base.shape, dtype),
        compiler_params=PARAMS,
        cost_estimate=CHEAP,
        name="combine",
    )(gates, base, first, second, *parts)


def bits_of(count):
    bits = []
    while 2 ** len(bits) < count:
        bits.insert(0, 2 ** len(bits))
    return bits


def local(
    tokens,
    encoder_states,
    source_owner,
    query_weight,
    output_weight,
    router_weight,
    expert_choice,
    expand_weight,
    shrink_weight,
):
    token_count, features = tokens.shape
    groups = lax.axis_size("expert")
    slices = lax.axis_size("mp")
    here, column = lax.axis_index("expert"), lax.axis_index("mp")
    width = features // slices
    experts = expand_weight.shape[0] * groups
    capacity = max(2, 3 * token_count // experts)
    direct = groups <= DIRECT
    pairs = slices // 2
    slots = capacity if direct else experts * capacity

    def hop(value, along_expert, along_mp):
        if along_expert == 0 and along_mp == 0:
            return value
        moves = [
            (e * slices + m, (e ^ along_expert) * slices + (m ^ along_mp))
            for e in range(groups)
            for m in range(slices)
        ]
        return lax.ppermute(value, ("expert", "mp"), moves)

    def spread(value):
        parts = value.reshape(groups, -1, value.shape[-1])
        return lax.all_to_all(parts, "expert", 0, 0, tiled=True).reshape(value.shape)

    def after(value, other):
        return lax.optimization_barrier((value, other))[0]

    steps = range(groups) if direct else [0]

    queries, source = ask(tokens, query_weight, encoder_states[0])
    expert_bits = bits_of(groups)
    bits = bits_of(slices)
    if direct:
        own = attend(queries, source, token_count)
        asked, steps_of = [queries], [0]
        for bit in expert_bits:
            asked = asked + [hop(value if k == 0 else after(value, own), bit, 0) for k, value in zip(steps_of, asked)]
            steps_of = steps_of + [k ^ bit for k in steps_of]
        asked = dict(zip(steps_of, asked))
        previous, backs = own, {}
        for k in sorted(range(1, groups), key=lambda k: (k & (k - 1) != 0, -k)):
            answer = previous = attend(after(asked[k], previous), source, token_count)
            backs[k] = hop(answer, k, 0)
        context = pick(source_owner.reshape(1, 1), [own] + [backs[k] for k in range(1, groups)])
    else:
        asked = lax.all_gather(queries, "expert", axis=0, tiled=True)
        previous = attend(asked, source, token_count)
        context = lax.dynamic_slice_in_dim(spread(previous), source_owner[0] * token_count, token_count, 0)

    choice, dispatch, first, second = route(after(expert_choice, previous), experts, len(steps), capacity)
    weights, order = [output_weight], [0]
    for bit in bits:
        if bit == 1:
            weights = [after(weight, context) for weight in weights]
        weights = weights + [hop(weight, 0, bit) for weight in weights]
        order = order + [index ^ bit for index in order]
    contexts = [context]
    for bit in bits:
        contexts = contexts + [hop(value if i == 0 else after(value, dispatch[0]), 0, bit) for i, value in enumerate(contexts)]

    far = set(range(2, groups)) if direct and pairs > 1 else set()
    sends = [k for k in range(2, groups)] + ([1] if groups > 1 else []) if direct else [0]
    cuts = [slices if k in far else 2 for k in sends]
    state, *leaving = make_state(tokens, contexts, weights, [dispatch[k] for k in sends], cuts)
    own_a, own_b, gates, columns = at_home(
        state, dispatch[0], router_weight.T, choice, experts, width
    )
    expert = functools.partial(run_expert, expand=expand_weight[0], shrink=shrink_weight[0], parts=pairs)

    def sum_cores(keep, give):
        return keep + hop(give, 0, 1).astype(F32)

    def sum_slices(summed, wait):
        total = summed[0]
        for j in range(1, pairs):
            part = summed[j].astype(BF16)
            total += hop(part if wait is None else after(part, wait), 0, 2 * j).astype(F32)
        return total.astype(BF16)

    def send_home(k, summed, wait=None):
        parts = [summed[j].astype(BF16) for j in range(pairs)]
        if wait is not None:
            parts = parts[:1] + [after(part, wait) for part in parts[1:]]
        return [hop(part, k, 2 * j) if direct else hop(spread(part), 0, 2 * j) for j, part in enumerate(parts)]

    home, order = {}, [0]
    if direct:
        arrived = {k: hop(rows, k, 0) for k, rows in zip(sends, leaving)}
        keep, give = expert([[0, 1]], [[own_a, own_b]])
        if sends:
            give = after(give, arrived[sends[0]])
        own_sum, wait = sum_cores(keep, give), None
        earlier = own_sum
        turns = [[k for k in sends if k < groups - 1], [groups - 1]] if groups > 2 else [sends]
        give, relay = None, None
        for turn in turns:
            blocks, orders = [], []
            for k in turn:
                pieces, places = [arrived[k]], [0]
                for bit in bits if k in far else [1]:
                    pieces = pieces + [hop(piece, 0, bit) for piece in pieces]
                    places = places + [index ^ bit for index in places]
                    if bit > 1:
                        relay = pieces[-1]
                blocks.append(pieces)
                orders.append(places)
            if turn:
                blocks[0][0] = after(blocks[0][0], earlier)
                keep, give = expert(orders, blocks)
                earlier = give
                summed = sum_cores(keep, give)
                for i, k in enumerate(turn):
                    rows = summed[:, i * slots : (i + 1) * slots]
                    if k in far:
                        wait = sum_slices(rows, wait)
                        home[k] = [hop(wait, k, 0)]
                    else:
                        near = k, rows
        if sends and 1 not in far:
            home[near[0]] = send_home(*near, wait)
        home[0] = send_home(0, own_sum, wait)
        order = sorted(sends, key=lambda k: (k == 1, k)) + [0]
    else:
        mine = spread(leaving[0])
        home[0] = send_home(0, sum_cores(*expert([[0, 1]], [[mine, hop(mine, 0, 1)]])))
    results = columns
    for k in order:
        results = combine(gates, results, first[k], second[k], home[k], BF16 if k == order[-1] else F32)
    return results


def solution(mesh):
    return jax.shard_map(
        local,
        mesh=mesh,
        in_specs=(
            P(("groups", "expert"), None),
            P(("groups", "expert"), None, None, "mp"),
            P(("groups", "expert")),
            P(None, "mp"),
            P("mp", None),
            P(),
            P(("groups", "expert"), None),
            P("expert", None, "mp"),
            P("expert", "mp", None),
        ),
        out_specs=P(("groups", "expert"), "mp"),
        check_vma=False,
    )
```

```python
import functools
import math

import jax
import jax.numpy as jnp
from jax import lax
from jax.experimental import pallas as pl
from jax.experimental.pallas import tpu as pltpu
from jax.sharding import PartitionSpec as P

HEAD_DIM = 128
SHARPNESS = HEAD_DIM**-0.5 * math.log2(math.e)
DIRECT = 8
CUTS = 4
TILE = 256
F32, BF16 = jnp.float32, jnp.bfloat16
PARAMS = pltpu.CompilerParams(vmem_limit_bytes=20 * 2**20)
CHEAP = pl.CostEstimate(flops=0, bytes_accessed=0, transcendentals=0)
WHOLE = pl.BlockSpec(memory_space=pltpu.VMEM)


def dot(a, b, dims=((1,), (0,))):
    return lax.dot_general(a, b, (dims, ((), ())), preferred_element_type=F32)


def in_hbm(value):
    return pltpu.with_memory_space_constraint(value, pltpu.HBM)


def position():
    return lax.axis_index("expert"), lax.axis_index("mp")


def query_kernel(tokens, weight, source, out, staged, tokens_here, weight_here, sems):
    features = tokens.shape[1]
    depth = features // CUTS
    copies, later = [], []
    for i in range(CUTS):
        part = pl.ds(i * depth, depth)
        copies.append(
            (
                pltpu.make_async_copy(tokens.at[:, part], tokens_here.at[:, part], sems.at[0, i]),
                pltpu.make_async_copy(weight.at[part, :], weight_here.at[part, :], sems.at[1, i]),
            )
        )
        rows = pl.ds(i * (source.shape[1] // CUTS), source.shape[1] // CUTS)
        later.append(pltpu.make_async_copy(source.at[:, rows], staged.at[:, rows], sems.at[2, i]))
    for pair in copies:
        for copy in pair:
            copy.start()
    for copy in later:
        copy.start()
    total = jnp.zeros(out.shape, F32)
    for i, pair in enumerate(copies):
        for copy in pair:
            copy.wait()
        part = slice(i * depth, (i + 1) * depth)
        total += dot(tokens_here[:, part], weight_here[part, :])
    out[...] = total.astype(BF16)
    for copy in later:
        copy.wait()


def ask(tokens, weight, source):
    return pl.pallas_call(
        query_kernel,
        in_specs=[pl.BlockSpec(memory_space=pltpu.HBM)] * 3,
        out_specs=[WHOLE] * 2,
        out_shape=[
            jax.ShapeDtypeStruct((tokens.shape[0], weight.shape[1]), BF16),
            jax.ShapeDtypeStruct(source.shape, BF16),
        ],
        scratch_shapes=[
            pltpu.VMEM(tokens.shape, BF16),
            pltpu.VMEM(weight.shape, BF16),
            pltpu.SemaphoreType.DMA((3, CUTS)),
        ],
        compiler_params=PARAMS,
        cost_estimate=CHEAP,
        name="query",
    )(in_hbm(tokens), in_hbm(weight), in_hbm(source))


def attend_kernel(queries, source, out):
    for head in range(queries.shape[1] // HEAD_DIM):
        part = slice(head * HEAD_DIM, (head + 1) * HEAD_DIM)
        scores = dot(queries[:, part], source[0, :, part], ((1,), (1,)))
        top = jnp.max(scores, axis=1, keepdims=True)
        weights = jnp.exp2((scores - top) * SHARPNESS).astype(BF16)
        values = jnp.concatenate([source[1, :, part], jnp.ones((source.shape[1], HEAD_DIM), BF16)], axis=1)
        summed = dot(weights, values)
        out[:, part] = (summed[:, :HEAD_DIM] / summed[:, HEAD_DIM:]).astype(BF16)


def attend(queries, source, block):
    rows, width = queries.shape
    if rows == block:
        return pl.pallas_call(
            attend_kernel,
            in_specs=[WHOLE] * 2,
            out_specs=WHOLE,
            out_shape=jax.ShapeDtypeStruct((rows, width), BF16),
            compiler_params=PARAMS,
        cost_estimate=CHEAP,
            name="attend",
        )(queries, source)
    return pl.pallas_call(
        attend_kernel,
        grid=(rows // block,),
        in_specs=[
            pl.BlockSpec((block, width), lambda i: (i, 0)),
            pl.BlockSpec(source.shape, lambda i: (0, 0, 0)),
        ],
        out_specs=pl.BlockSpec((block, width), lambda i: (i, 0)),
        out_shape=jax.ShapeDtypeStruct((rows, width), BF16),
        compiler_params=PARAMS,
        cost_estimate=CHEAP,
        name="attend",
    )(queries, source)


def pick_kernel(owner, *refs):
    backs, out = refs[:-1], refs[-1]
    here, _ = position()
    names = jnp.broadcast_to(owner[0:1, 0:1], out.shape)
    total = backs[0][...].astype(F32)
    for k in range(1, len(backs)):
        total = jnp.where(names == here ^ k, backs[k][...].astype(F32), total)
    out[...] = total.astype(BF16)


def pick(owner, backs):
    return pl.pallas_call(
        pick_kernel,
        in_specs=[WHOLE] * (1 + len(backs)),
        out_specs=WHOLE,
        out_shape=jax.ShapeDtypeStruct(backs[0].shape, BF16),
        compiler_params=PARAMS,
        cost_estimate=CHEAP,
        name="pick",
    )(owner, *backs)


def route_kernel(experts, parts, choice_t, choice, *outs):
    dispatch, first, second = outs[:parts], outs[parts : 2 * parts], outs[2 * parts :]
    tokens = choice_t.shape[1]
    slots = dispatch[0].shape[0]
    capacity = slots * parts // experts
    wide = lax.broadcasted_iota(jnp.int32, (tokens, experts), 1)
    tall = lax.broadcasted_iota(jnp.int32, (experts, tokens), 0)
    i = lax.broadcasted_iota(jnp.int32, (tokens, tokens), 0)
    j = lax.broadcasted_iota(jnp.int32, (tokens, tokens), 1)
    r0, r1 = choice_t[0:1, :], choice_t[1:2, :]
    turned = dot((i == j).astype(BF16), choice_t[...].astype(F32).astype(BF16), ((1,), (1,))).astype(jnp.int32)
    choice[...] = turned
    c0, c1 = turned[:, 0:1], turned[:, 1:2]
    named = ((wide == c0) | (wide == c1)).astype(BF16)
    named_t = ((tall == r0) | (tall == r1)).astype(BF16)
    rank = dot((j < i).astype(BF16), named).astype(jnp.int32)
    rank_t = dot(named_t, (i < j).astype(BF16)).astype(jnp.int32)
    place0 = c0 * capacity + jnp.sum(jnp.where(wide == c0, rank, 0), axis=1, keepdims=True)
    place1 = c1 * capacity + jnp.sum(jnp.where(wide == c1, rank, 0), axis=1, keepdims=True)
    across0 = r0 * capacity + jnp.sum(jnp.where(tall == r0, rank_t, 0), axis=0, keepdims=True)
    across1 = r1 * capacity + jnp.sum(jnp.where(tall == r1, rank_t, 0), axis=0, keepdims=True)
    lane = lax.broadcasted_iota(jnp.int32, (tokens, slots), 1)
    row = lax.broadcasted_iota(jnp.int32, (slots, tokens), 0)
    for k in range(parts):
        base = (position()[0] ^ k) * capacity if parts > 1 else 0
        dispatch[k][...] = ((row + base == across0) | (row + base == across1)).astype(BF16)
        first[k][...] = (lane + base == place0).astype(BF16)
        second[k][...] = (lane + base == place1).astype(BF16)


def route(choice, experts, parts, capacity):
    tokens = choice.shape[0]
    slots = experts * capacity // parts
    outs = pl.pallas_call(
        functools.partial(route_kernel, experts, parts),
        in_specs=[WHOLE],
        out_specs=[WHOLE] * (1 + 3 * parts),
        out_shape=[jax.ShapeDtypeStruct(choice.shape, jnp.int32)]
        + [jax.ShapeDtypeStruct((slots, tokens), BF16)] * parts
        + [jax.ShapeDtypeStruct((tokens, slots), BF16)] * (2 * parts),
        compiler_params=PARAMS,
        cost_estimate=CHEAP,
        name="route",
    )(choice.T)
    return outs[0], outs[1 : 1 + parts], outs[1 + parts : 1 + 2 * parts], outs[1 + 2 * parts :]


def state_kernel(count, sends, *refs):
    tokens = refs[0]
    contexts, weights = refs[1 : 1 + count], refs[1 + count : 1 + 2 * count]
    dispatch = refs[1 + 2 * count : 1 + 2 * count + sends]
    state, outs = refs[1 + 2 * count + sends], refs[2 + 2 * count + sends :]
    tile = min(TILE, state.shape[1])
    for at in range(0, state.shape[1], tile):
        part = slice(at, at + tile)
        total = tokens[:, part].astype(F32)
        for context, weight in zip(contexts, weights):
            total += dot(context[...], weight[:, part])
        state[:, part] = total.astype(BF16)
    for rows, out in zip(dispatch, outs):
        width = out.shape[1]
        at = (position()[1] & (state.shape[1] // width - 1)) * width
        out[...] = dot(rows[...], state[:, pl.ds(pl.multiple_of(at, width), width)]).astype(BF16)


def make_state(tokens, contexts, weights, dispatch, cuts):
    return pl.pallas_call(
        functools.partial(state_kernel, len(contexts), len(dispatch)),
        in_specs=[WHOLE] * (1 + 2 * len(contexts) + len(dispatch)),
        out_specs=[WHOLE] * (1 + len(dispatch)),
        out_shape=[jax.ShapeDtypeStruct(tokens.shape, BF16)]
        + [jax.ShapeDtypeStruct((rows.shape[0], tokens.shape[1] // cut), BF16) for rows, cut in zip(dispatch, cuts)],
        compiler_params=PARAMS,
        cost_estimate=CHEAP,
        name="state",
    )(tokens, *contexts, *weights, *dispatch)


def home_kernel(experts, state, dispatch, router, choice, own_a, own_b, gates, columns):
    half = own_a.shape[1]
    column = position()[1]
    core = column & 1
    own_a[...] = dot(dispatch[...], state[:, pl.ds(pl.multiple_of(core * half, half), half)]).astype(BF16)
    own_b[...] = dot(dispatch[...], state[:, pl.ds(pl.multiple_of((1 - core) * half, half), half)]).astype(BF16)
    logits = dot(state[...], router[...], ((1,), (1,)))
    wide = lax.broadcasted_iota(jnp.int32, logits.shape, 1)
    first = jnp.sum(jnp.where(wide == choice[:, 0:1], logits, 0.0), axis=1, keepdims=True)
    second = jnp.sum(jnp.where(wide == choice[:, 1:2], logits, 0.0), axis=1, keepdims=True)
    gates[:, 0:1] = jax.nn.sigmoid(first - second)
    gates[:, 1:2] = jax.nn.sigmoid(second - first)
    width = columns.shape[1]
    columns[...] = state[:, pl.ds(pl.multiple_of(column * width, width), width)].astype(F32)


def at_home(state, dispatch, router, choice, experts, width):
    tokens, features = state.shape
    slots = dispatch.shape[0]
    return pl.pallas_call(
        functools.partial(home_kernel, experts),
        in_specs=[WHOLE] * 4,
        out_specs=[WHOLE] * 4,
        out_shape=[
            jax.ShapeDtypeStruct((slots, features // 2), BF16),
            jax.ShapeDtypeStruct((slots, features // 2), BF16),
            jax.ShapeDtypeStruct((tokens, 2), F32),
            jax.ShapeDtypeStruct((tokens, width), F32),
        ],
        compiler_params=PARAMS,
        cost_estimate=CHEAP,
        name="home",
    )(state, dispatch, router, choice)


def expert_kernel(orders, *refs):
    blocks, at = [], 0
    for order in orders:
        blocks.append(refs[at : at + len(order)])
        at += len(order)
    column = position()[1]
    expand, shrink, keep, give, rows_here, hidden = refs[at:]
    count = blocks[0][0].shape[0]
    for block, (order, pieces) in enumerate(zip(orders, blocks)):
        for index, piece in zip(order, pieces):
            width = piece.shape[1]
            part = pl.ds(pl.multiple_of(((column & (len(order) - 1)) ^ index) * width, width), width)
            rows_here[block * count : (block + 1) * count, part] = piece[...]
    units = expand.shape[1]
    tile = min(TILE, units)
    for at in range(0, units, tile):
        total = dot(rows_here[...], expand[:, at : at + tile])
        hidden[:, at : at + tile] = jnp.maximum(total, 0.0).astype(BF16)
    width = keep.shape[2]
    for j in range(keep.shape[0]):
        at = pl.multiple_of((column ^ (2 * j) ^ 1) * width, width)
        give[j] = dot(hidden[...], shrink[:, pl.ds(at, width)]).astype(BF16)
    for j in range(keep.shape[0]):
        at = pl.multiple_of((column ^ (2 * j)) * width, width)
        keep[j] = dot(hidden[...], shrink[:, pl.ds(at, width)])


def run_expert(orders, blocks, expand, shrink, parts):
    pieces = [piece for block in blocks for piece in block]
    rows = pieces[0].shape[0] * len(blocks)
    features, units = expand.shape
    width = features // (2 * parts)
    return pl.pallas_call(
        functools.partial(expert_kernel, tuple(map(tuple, orders))),
        in_specs=[WHOLE] * (2 + len(pieces)),
        out_specs=[WHOLE] * 2,
        out_shape=[
            jax.ShapeDtypeStruct((parts, rows, width), F32),
            jax.ShapeDtypeStruct((parts, rows, width), BF16),
        ],
        scratch_shapes=[pltpu.VMEM((rows, features), BF16), pltpu.VMEM((rows, units), BF16)],
        compiler_params=PARAMS,
        cost_estimate=CHEAP,
        name="expert",
    )(*pieces, expand, shrink)


def combine_kernel(count, gates, base, first, second, *refs):
    parts, out = refs[:count], refs[count]
    total = parts[0][...].astype(F32)
    for part in parts[1:]:
        total += part[...].astype(F32)
    total = total.astype(BF16)
    result = base[...] + gates[:, 0:1] * dot(first[...], total) + gates[:, 1:2] * dot(second[...], total)
    out[...] = result.astype(out.dtype)


def combine(gates, base, first, second, parts, dtype):
    return pl.pallas_call(
        functools.partial(combine_kernel, len(parts)),
        in_specs=[WHOLE] * (4 + len(parts)),
        out_specs=WHOLE,
        out_shape=jax.ShapeDtypeStruct(base.shape, dtype),
        compiler_params=PARAMS,
        cost_estimate=CHEAP,
        name="combine",
    )(gates, base, first, second, *parts)


def bits_of(count):
    bits = []
    while 2 ** len(bits) < count:
        bits.insert(0, 2 ** len(bits))
    return bits


def local(
    tokens,
    encoder_states,
    source_owner,
    query_weight,
    output_weight,
    router_weight,
    expert_choice,
    expand_weight,
    shrink_weight,
):
    token_count, features = tokens.shape
    groups = lax.axis_size("expert")
    slices = lax.axis_size("mp")
    here, column = lax.axis_index("expert"), lax.axis_index("mp")
    width = features // slices
    experts = expand_weight.shape[0] * groups
    capacity = max(2, 3 * token_count // experts)
    direct = groups <= DIRECT
    pairs = slices // 2
    slots = capacity if direct else experts * capacity

    def hop(value, along_expert, along_mp):
        if along_expert == 0 and along_mp == 0:
            return value
        moves = [
            (e * slices + m, (e ^ along_expert) * slices + (m ^ along_mp))
            for e in range(groups)
            for m in range(slices)
        ]
        return lax.ppermute(value, ("expert", "mp"), moves)

    def spread(value):
        parts = value.reshape(groups, -1, value.shape[-1])
        return lax.all_to_all(parts, "expert", 0, 0, tiled=True).reshape(value.shape)

    def after(value, other):
        return lax.optimization_barrier((value, other))[0]

    steps = range(groups) if direct else [0]

    queries, source = ask(tokens, query_weight, encoder_states[0])
    expert_bits = bits_of(groups)
    bits = bits_of(slices)
    if direct:
        own = attend(queries, source, token_count)
        asked, steps_of = [queries], [0]
        for bit in expert_bits:
            asked = asked + [hop(value if k == 0 else after(value, own), bit, 0) for k, value in zip(steps_of, asked)]
            steps_of = steps_of + [k ^ bit for k in steps_of]
        asked = dict(zip(steps_of, asked))
        previous, backs = own, {}
        for k in sorted(range(1, groups), key=lambda k: (k & (k - 1) != 0, -k)):
            answer = previous = attend(after(asked[k], previous), source, token_count)
            backs[k] = hop(answer, k, 0)
        context = pick(source_owner.reshape(1, 1), [own] + [backs[k] for k in range(1, groups)])
    else:
        asked = lax.all_gather(queries, "expert", axis=0, tiled=True)
        previous = attend(asked, source, token_count)
        context = lax.dynamic_slice_in_dim(spread(previous), source_owner[0] * token_count, token_count, 0)

    choice, dispatch, first, second = route(after(expert_choice, previous), experts, len(steps), capacity)
    weights, order = [output_weight], [0]
    for bit in bits:
        if bit == 1:
            weights = [after(weight, context) for weight in weights]
        weights = weights + [hop(weight, 0, bit) for weight in weights]
        order = order + [index ^ bit for index in order]
    contexts = [context]
    for bit in bits:
        contexts = contexts + [hop(value if i == 0 else after(value, dispatch[0]), 0, bit) for i, value in enumerate(contexts)]

    far = set(range(2, groups)) if direct and pairs > 1 else set()
    sends = [k for k in range(2, groups)] + ([1] if groups > 1 else []) if direct else [0]
    cuts = [slices if k in far else 2 for k in sends]
    state, *leaving = make_state(tokens, contexts, weights, [dispatch[k] for k in sends], cuts)
    own_a, own_b, gates, columns = at_home(
        state, dispatch[0], router_weight.T, choice, experts, width
    )
    expert = functools.partial(run_expert, expand=expand_weight[0], shrink=shrink_weight[0], parts=pairs)

    def sum_cores(keep, give):
        return keep + hop(give, 0, 1).astype(F32)

    def sum_slices(summed):
        total = summed[0]
        for j in range(1, pairs):
            total += hop(summed[j].astype(BF16), 0, 2 * j).astype(F32)
        return total.astype(BF16)

    def send_home(k, summed, wait=None):
        parts = [summed[j].astype(BF16) for j in range(pairs)]
        if wait is not None:
            parts = parts[:1] + [after(part, wait) for part in parts[1:]]
        return [hop(part, k, 2 * j) if direct else hop(spread(part), 0, 2 * j) for j, part in enumerate(parts)]

    home, order = {}, [0]
    if direct:
        arrived = {k: hop(rows, k, 0) for k, rows in zip(sends, leaving)}
        keep, give = expert([[0, 1]], [[own_a, own_b]])
        if sends:
            give = after(give, arrived[groups - 1])
        own_sum, wait = sum_cores(keep, give), None
        earlier = own_sum
        turns = [[k for k in sends if k < groups - 1], [groups - 1]] if groups > 2 else [sends]
        for turn in turns:
            blocks, orders = [], []
            for k in turn:
                pieces, places = [arrived[k]], [0]
                for bit in bits if k in far else [1]:
                    if bit == 1 and wait is not None:
                        pieces = [after(piece, earlier) for piece in pieces]
                    pieces = pieces + [hop(piece, 0, bit) for piece in pieces]
                    places = places + [index ^ bit for index in places]
                blocks.append(pieces)
                orders.append(places)
            if turn:
                blocks[0][0] = after(blocks[0][0], earlier)
                keep, give = expert(orders, blocks)
                earlier = give
                summed = sum_cores(keep, give)
                for i, k in enumerate(turn):
                    rows = summed[:, i * slots : (i + 1) * slots]
                    if k in far:
                        total = sum_slices(rows)
                        wait = total if wait is None else wait
                        home[k] = [hop(total, k, 0)]
                    else:
                        home[k] = send_home(k, rows)
        home[0] = send_home(0, own_sum, wait)
        order = [0] + sorted(sends)
    else:
        mine = spread(leaving[0])
        home[0] = send_home(0, sum_cores(*expert([[0, 1]], [[mine, hop(mine, 0, 1)]])))
    results = columns
    for k in order:
        results = combine(gates, results, first[k], second[k], home[k], BF16 if k == order[-1] else F32)
    return results


def solution(mesh):
    return jax.shard_map(
        local,
        mesh=mesh,
        in_specs=(
            P(("groups", "expert"), None),
            P(("groups", "expert"), None, None, "mp"),
            P(("groups", "expert")),
            P(None, "mp"),
            P("mp", None),
            P(),
            P(("groups", "expert"), None),
            P("expert", None, "mp"),
            P("expert", "mp", None),
        ),
        out_specs=P(("groups", "expert"), "mp"),
        check_vma=False,
    )
```

```python
import functools
import math

import jax
import jax.numpy as jnp
from jax import lax
from jax.experimental import pallas as pl
from jax.experimental.pallas import tpu as pltpu
from jax.sharding import PartitionSpec as P

HEAD_DIM = 128
SHARPNESS = HEAD_DIM**-0.5 * math.log2(math.e)
DIRECT = 8
CUTS = 4
TILE = 256
F32, BF16 = jnp.float32, jnp.bfloat16
PARAMS = pltpu.CompilerParams(vmem_limit_bytes=20 * 2**20)
CHEAP = pl.CostEstimate(flops=0, bytes_accessed=0, transcendentals=0)
WHOLE = pl.BlockSpec(memory_space=pltpu.VMEM)


def dot(a, b, dims=((1,), (0,))):
    return lax.dot_general(a, b, (dims, ((), ())), preferred_element_type=F32)


def in_hbm(value):
    return pltpu.with_memory_space_constraint(value, pltpu.HBM)


def position():
    return lax.axis_index("expert"), lax.axis_index("mp")


def query_kernel(tokens, weight, source, out, staged, tokens_here, weight_here, sems):
    features = tokens.shape[1]
    depth = features // CUTS
    copies, later = [], []
    for i in range(CUTS):
        part = pl.ds(i * depth, depth)
        copies.append(
            (
                pltpu.make_async_copy(tokens.at[:, part], tokens_here.at[:, part], sems.at[0, i]),
                pltpu.make_async_copy(weight.at[part, :], weight_here.at[part, :], sems.at[1, i]),
            )
        )
        rows = pl.ds(i * (source.shape[1] // CUTS), source.shape[1] // CUTS)
        later.append(pltpu.make_async_copy(source.at[:, rows], staged.at[:, rows], sems.at[2, i]))
    for pair in copies:
        for copy in pair:
            copy.start()
    for copy in later:
        copy.start()
    total = jnp.zeros(out.shape, F32)
    for i, pair in enumerate(copies):
        for copy in pair:
            copy.wait()
        part = slice(i * depth, (i + 1) * depth)
        total += dot(tokens_here[:, part], weight_here[part, :])
    out[...] = total.astype(BF16)
    for copy in later:
        copy.wait()


def ask(tokens, weight, source):
    return pl.pallas_call(
        query_kernel,
        in_specs=[pl.BlockSpec(memory_space=pltpu.HBM)] * 3,
        out_specs=[WHOLE] * 2,
        out_shape=[
            jax.ShapeDtypeStruct((tokens.shape[0], weight.shape[1]), BF16),
            jax.ShapeDtypeStruct(source.shape, BF16),
        ],
        scratch_shapes=[
            pltpu.VMEM(tokens.shape, BF16),
            pltpu.VMEM(weight.shape, BF16),
            pltpu.SemaphoreType.DMA((3, CUTS)),
        ],
        compiler_params=PARAMS,
        cost_estimate=CHEAP,
        name="query",
    )(in_hbm(tokens), in_hbm(weight), in_hbm(source))


def attend_kernel(queries, source, out):
    for head in range(queries.shape[1] // HEAD_DIM):
        part = slice(head * HEAD_DIM, (head + 1) * HEAD_DIM)
        scores = dot(queries[:, part], source[0, :, part], ((1,), (1,)))
        top = jnp.max(scores, axis=1, keepdims=True)
        weights = jnp.exp2((scores - top) * SHARPNESS).astype(BF16)
        values = jnp.concatenate([source[1, :, part], jnp.ones((source.shape[1], HEAD_DIM), BF16)], axis=1)
        summed = dot(weights, values)
        out[:, part] = (summed[:, :HEAD_DIM] / summed[:, HEAD_DIM:]).astype(BF16)


def attend(queries, source, block):
    rows, width = queries.shape
    if rows == block:
        return pl.pallas_call(
            attend_kernel,
            in_specs=[WHOLE] * 2,
            out_specs=WHOLE,
            out_shape=jax.ShapeDtypeStruct((rows, width), BF16),
            compiler_params=PARAMS,
        cost_estimate=CHEAP,
            name="attend",
        )(queries, source)
    return pl.pallas_call(
        attend_kernel,
        grid=(rows // block,),
        in_specs=[
            pl.BlockSpec((block, width), lambda i: (i, 0)),
            pl.BlockSpec(source.shape, lambda i: (0, 0, 0)),
        ],
        out_specs=pl.BlockSpec((block, width), lambda i: (i, 0)),
        out_shape=jax.ShapeDtypeStruct((rows, width), BF16),
        compiler_params=PARAMS,
        cost_estimate=CHEAP,
        name="attend",
    )(queries, source)


def pick_kernel(owner, *refs):
    backs, out = refs[:-1], refs[-1]
    here, _ = position()
    names = jnp.broadcast_to(owner[0:1, 0:1], out.shape)
    total = backs[0][...].astype(F32)
    for k in range(1, len(backs)):
        total = jnp.where(names == here ^ k, backs[k][...].astype(F32), total)
    out[...] = total.astype(BF16)


def pick(owner, backs):
    return pl.pallas_call(
        pick_kernel,
        in_specs=[WHOLE] * (1 + len(backs)),
        out_specs=WHOLE,
        out_shape=jax.ShapeDtypeStruct(backs[0].shape, BF16),
        compiler_params=PARAMS,
        cost_estimate=CHEAP,
        name="pick",
    )(owner, *backs)


def route_kernel(experts, parts, choice_t, choice, *outs):
    dispatch, first, second = outs[:parts], outs[parts : 2 * parts], outs[2 * parts :]
    tokens = choice_t.shape[1]
    slots = dispatch[0].shape[0]
    capacity = slots * parts // experts
    wide = lax.broadcasted_iota(jnp.int32, (tokens, experts), 1)
    tall = lax.broadcasted_iota(jnp.int32, (experts, tokens), 0)
    i = lax.broadcasted_iota(jnp.int32, (tokens, tokens), 0)
    j = lax.broadcasted_iota(jnp.int32, (tokens, tokens), 1)
    r0, r1 = choice_t[0:1, :], choice_t[1:2, :]
    turned = dot((i == j).astype(BF16), choice_t[...].astype(F32).astype(BF16), ((1,), (1,))).astype(jnp.int32)
    choice[...] = turned
    c0, c1 = turned[:, 0:1], turned[:, 1:2]
    named = ((wide == c0) | (wide == c1)).astype(BF16)
    named_t = ((tall == r0) | (tall == r1)).astype(BF16)
    rank = dot((j < i).astype(BF16), named).astype(jnp.int32)
    rank_t = dot(named_t, (i < j).astype(BF16)).astype(jnp.int32)
    place0 = c0 * capacity + jnp.sum(jnp.where(wide == c0, rank, 0), axis=1, keepdims=True)
    place1 = c1 * capacity + jnp.sum(jnp.where(wide == c1, rank, 0), axis=1, keepdims=True)
    across0 = r0 * capacity + jnp.sum(jnp.where(tall == r0, rank_t, 0), axis=0, keepdims=True)
    across1 = r1 * capacity + jnp.sum(jnp.where(tall == r1, rank_t, 0), axis=0, keepdims=True)
    lane = lax.broadcasted_iota(jnp.int32, (tokens, slots), 1)
    row = lax.broadcasted_iota(jnp.int32, (slots, tokens), 0)
    for k in range(parts):
        base = (position()[0] ^ k) * capacity if parts > 1 else 0
        dispatch[k][...] = ((row + base == across0) | (row + base == across1)).astype(BF16)
        first[k][...] = (lane + base == place0).astype(BF16)
        second[k][...] = (lane + base == place1).astype(BF16)


def route(choice, experts, parts, capacity):
    tokens = choice.shape[0]
    slots = experts * capacity // parts
    outs = pl.pallas_call(
        functools.partial(route_kernel, experts, parts),
        in_specs=[WHOLE],
        out_specs=[WHOLE] * (1 + 3 * parts),
        out_shape=[jax.ShapeDtypeStruct(choice.shape, jnp.int32)]
        + [jax.ShapeDtypeStruct((slots, tokens), BF16)] * parts
        + [jax.ShapeDtypeStruct((tokens, slots), BF16)] * (2 * parts),
        compiler_params=PARAMS,
        cost_estimate=CHEAP,
        name="route",
    )(choice.T)
    return outs[0], outs[1 : 1 + parts], outs[1 + parts : 1 + 2 * parts], outs[1 + 2 * parts :]


def state_kernel(count, sends, *refs):
    tokens = refs[0]
    contexts, weights = refs[1 : 1 + count], refs[1 + count : 1 + 2 * count]
    dispatch = refs[1 + 2 * count : 1 + 2 * count + sends]
    state, outs = refs[1 + 2 * count + sends], refs[2 + 2 * count + sends :]
    tile = min(TILE, state.shape[1])
    for at in range(0, state.shape[1], tile):
        part = slice(at, at + tile)
        total = tokens[:, part].astype(F32)
        for context, weight in zip(contexts, weights):
            total += dot(context[...], weight[:, part])
        state[:, part] = total.astype(BF16)
    for rows, out in zip(dispatch, outs):
        width = out.shape[1]
        at = (position()[1] & (state.shape[1] // width - 1)) * width
        out[...] = dot(rows[...], state[:, pl.ds(pl.multiple_of(at, width), width)]).astype(BF16)


def make_state(tokens, contexts, weights, dispatch, cuts):
    return pl.pallas_call(
        functools.partial(state_kernel, len(contexts), len(dispatch)),
        in_specs=[WHOLE] * (1 + 2 * len(contexts) + len(dispatch)),
        out_specs=[WHOLE] * (1 + len(dispatch)),
        out_shape=[jax.ShapeDtypeStruct(tokens.shape, BF16)]
        + [jax.ShapeDtypeStruct((rows.shape[0], tokens.shape[1] // cut), BF16) for rows, cut in zip(dispatch, cuts)],
        compiler_params=PARAMS,
        cost_estimate=CHEAP,
        name="state",
    )(tokens, *contexts, *weights, *dispatch)


def home_kernel(experts, state, dispatch, router, choice, own_a, own_b, gates, columns):
    half = own_a.shape[1]
    column = position()[1]
    core = column & 1
    own_a[...] = dot(dispatch[...], state[:, pl.ds(pl.multiple_of(core * half, half), half)]).astype(BF16)
    own_b[...] = dot(dispatch[...], state[:, pl.ds(pl.multiple_of((1 - core) * half, half), half)]).astype(BF16)
    logits = dot(state[...], router[...], ((1,), (1,)))
    wide = lax.broadcasted_iota(jnp.int32, logits.shape, 1)
    first = jnp.sum(jnp.where(wide == choice[:, 0:1], logits, 0.0), axis=1, keepdims=True)
    second = jnp.sum(jnp.where(wide == choice[:, 1:2], logits, 0.0), axis=1, keepdims=True)
    gates[:, 0:1] = jax.nn.sigmoid(first - second)
    gates[:, 1:2] = jax.nn.sigmoid(second - first)
    width = columns.shape[1]
    columns[...] = state[:, pl.ds(pl.multiple_of(column * width, width), width)].astype(F32)


def at_home(state, dispatch, router, choice, experts, width):
    tokens, features = state.shape
    slots = dispatch.shape[0]
    return pl.pallas_call(
        functools.partial(home_kernel, experts),
        in_specs=[WHOLE] * 4,
        out_specs=[WHOLE] * 4,
        out_shape=[
            jax.ShapeDtypeStruct((slots, features // 2), BF16),
            jax.ShapeDtypeStruct((slots, features // 2), BF16),
            jax.ShapeDtypeStruct((tokens, 2), F32),
            jax.ShapeDtypeStruct((tokens, width), F32),
        ],
        compiler_params=PARAMS,
        cost_estimate=CHEAP,
        name="home",
    )(state, dispatch, router, choice)


def expert_kernel(orders, *refs):
    blocks, at = [], 0
    for order in orders:
        blocks.append(refs[at : at + len(order)])
        at += len(order)
    column = position()[1]
    expand, shrink, keep, give, rows_here, hidden = refs[at:]
    count = blocks[0][0].shape[0]
    for block, (order, pieces) in enumerate(zip(orders, blocks)):
        for index, piece in zip(order, pieces):
            width = piece.shape[1]
            part = pl.ds(pl.multiple_of(((column & (len(order) - 1)) ^ index) * width, width), width)
            rows_here[block * count : (block + 1) * count, part] = piece[...]
    units = expand.shape[1]
    tile = min(TILE, units)
    for at in range(0, units, tile):
        total = dot(rows_here[...], expand[:, at : at + tile])
        hidden[:, at : at + tile] = jnp.maximum(total, 0.0).astype(BF16)
    width = keep.shape[2]
    for j in range(keep.shape[0]):
        at = pl.multiple_of((column ^ (2 * j) ^ 1) * width, width)
        give[j] = dot(hidden[...], shrink[:, pl.ds(at, width)]).astype(BF16)
    for j in range(keep.shape[0]):
        at = pl.multiple_of((column ^ (2 * j)) * width, width)
        keep[j] = dot(hidden[...], shrink[:, pl.ds(at, width)])


def run_expert(orders, blocks, expand, shrink, parts):
    pieces = [piece for block in blocks for piece in block]
    rows = pieces[0].shape[0] * len(blocks)
    features, units = expand.shape
    width = features // (2 * parts)
    return pl.pallas_call(
        functools.partial(expert_kernel, tuple(map(tuple, orders))),
        in_specs=[WHOLE] * (2 + len(pieces)),
        out_specs=[WHOLE] * 2,
        out_shape=[
            jax.ShapeDtypeStruct((parts, rows, width), F32),
            jax.ShapeDtypeStruct((parts, rows, width), BF16),
        ],
        scratch_shapes=[pltpu.VMEM((rows, features), BF16), pltpu.VMEM((rows, units), BF16)],
        compiler_params=PARAMS,
        cost_estimate=CHEAP,
        name="expert",
    )(*pieces, expand, shrink)


def combine_kernel(count, gates, base, first, second, *refs):
    parts, out = refs[:count], refs[count]
    total = parts[0][...].astype(F32)
    for part in parts[1:]:
        total += part[...].astype(F32)
    total = total.astype(BF16)
    result = base[...] + gates[:, 0:1] * dot(first[...], total) + gates[:, 1:2] * dot(second[...], total)
    out[...] = result.astype(out.dtype)


def combine(gates, base, first, second, parts, dtype):
    return pl.pallas_call(
        functools.partial(combine_kernel, len(parts)),
        in_specs=[WHOLE] * (4 + len(parts)),
        out_specs=WHOLE,
        out_shape=jax.ShapeDtypeStruct(base.shape, dtype),
        compiler_params=PARAMS,
        cost_estimate=CHEAP,
        name="combine",
    )(gates, base, first, second, *parts)


def bits_of(count):
    bits = []
    while 2 ** len(bits) < count:
        bits.insert(0, 2 ** len(bits))
    return bits


def local(
    tokens,
    encoder_states,
    source_owner,
    query_weight,
    output_weight,
    router_weight,
    expert_choice,
    expand_weight,
    shrink_weight,
):
    token_count, features = tokens.shape
    groups = lax.axis_size("expert")
    slices = lax.axis_size("mp")
    here, column = lax.axis_index("expert"), lax.axis_index("mp")
    width = features // slices
    experts = expand_weight.shape[0] * groups
    capacity = max(2, 3 * token_count // experts)
    direct = groups <= DIRECT
    pairs = slices // 2
    slots = capacity if direct else experts * capacity

    def hop(value, along_expert, along_mp):
        if along_expert == 0 and along_mp == 0:
            return value
        moves = [
            (e * slices + m, (e ^ along_expert) * slices + (m ^ along_mp))
            for e in range(groups)
            for m in range(slices)
        ]
        return lax.ppermute(value, ("expert", "mp"), moves)

    def spread(value):
        parts = value.reshape(groups, -1, value.shape[-1])
        return lax.all_to_all(parts, "expert", 0, 0, tiled=True).reshape(value.shape)

    def after(value, other):
        return lax.optimization_barrier((value, other))[0]

    steps = range(groups) if direct else [0]

    queries, source = ask(tokens, query_weight, encoder_states[0])
    expert_bits = bits_of(groups)
    bits = bits_of(slices)
    if direct:
        own = attend(queries, source, token_count)
        asked, steps_of = [queries], [0]
        for bit in expert_bits:
            asked = asked + [hop(value if k == 0 else after(value, own), bit, 0) for k, value in zip(steps_of, asked)]
            steps_of = steps_of + [k ^ bit for k in steps_of]
        asked = dict(zip(steps_of, asked))
        previous, backs = own, {}
        for k in sorted(range(1, groups), key=lambda k: (k & (k - 1) != 0, -k)):
            answer = previous = attend(after(asked[k], previous), source, token_count)
            backs[k] = hop(answer, k, 0)
        context = pick(source_owner.reshape(1, 1), [own] + [backs[k] for k in range(1, groups)])
    else:
        asked = lax.all_gather(queries, "expert", axis=0, tiled=True)
        previous = attend(asked, source, token_count)
        context = lax.dynamic_slice_in_dim(spread(previous), source_owner[0] * token_count, token_count, 0)

    choice, dispatch, first, second = route(after(expert_choice, previous), experts, len(steps), capacity)
    weights, order = [output_weight], [0]
    for bit in bits:
        if bit == 1:
            weights = [after(weight, context) for weight in weights]
        weights = weights + [hop(weight, 0, bit) for weight in weights]
        order = order + [index ^ bit for index in order]
    contexts = [context]
    for bit in bits:
        contexts = contexts + [hop(value if i == 0 else after(value, dispatch[0]), 0, bit) for i, value in enumerate(contexts)]

    far = set(range(2, groups)) if direct and pairs > 1 else set()
    sends = [k for k in range(2, groups)] + ([1] if groups > 1 else []) if direct else [0]
    cuts = [slices if k in far else 2 for k in sends]
    state, *leaving = make_state(tokens, contexts, weights, [dispatch[k] for k in sends], cuts)
    own_a, own_b, gates, columns = at_home(
        state, dispatch[0], router_weight.T, choice, experts, width
    )
    expert = functools.partial(run_expert, expand=expand_weight[0], shrink=shrink_weight[0], parts=pairs)

    def sum_cores(keep, give):
        return keep + hop(give, 0, 1).astype(F32)

    def send_home(k, summed, wait=None):
        parts = [summed[j].astype(BF16) for j in range(pairs)]
        if wait is not None:
            parts = parts[:1] + [after(part, wait) for part in parts[1:]]
        return [hop(part, k, 2 * j) if direct else hop(spread(part), 0, 2 * j) for j, part in enumerate(parts)]

    home, order = {}, [0]
    if direct:
        arrived = {k: hop(rows, k, 0) for k, rows in zip(sends, leaving)}
        keep, give = expert([[0, 1]], [[own_a, own_b]])
        if sends:
            give = after(give, arrived[groups - 1])
        own_sum, wait = sum_cores(keep, give), None
        earlier = [own_sum]
        crossing, started, relays = {}, None, {}
        for k in sends:
            pieces, places = [arrived[k]], [0]
            for bit in bits[:-1] if k in far else []:
                pieces = pieces + [hop(piece, 0, bit) for piece in pieces]
                places = places + [index ^ bit for index in places]
            relays[k] = pieces, places
            if k in far:
                earlier.append(pieces[-1])
        turns = [[k for k in sends if k < groups - 1], [groups - 1]] if groups > 2 else [sends]
        for turn in turns:
            blocks, orders = [], []
            for k in turn:
                pieces, places = relays[k]
                if started is not None:
                    pieces = [after(piece, started) for piece in pieces]
                pieces = pieces + [hop(piece, 0, 1) for piece in pieces]
                places = places + [index ^ 1 for index in places]
                blocks.append(pieces)
                orders.append(places)
            if turn:
                for value in earlier:
                    blocks[0][0] = after(blocks[0][0], value)
                keep, give = expert(orders, blocks)
                summed = sum_cores(keep, give)
                earlier, started = [summed], give
                for i, k in enumerate(turn):
                    rows = summed[:, i * slots : (i + 1) * slots]
                    if k in far:
                        crossed = [hop(rows[j].astype(BF16), 0, 2 * j) for j in range(1, pairs)]
                        crossing[k] = [rows[0]] + crossed
                    else:
                        near = k, rows
        for k, (total, *crossed) in crossing.items():
            for part in crossed:
                total += (part if k == groups - 1 else after(part, summed)).astype(F32)
            total = total.astype(BF16)
            wait = total if wait is None else wait
            home[k] = [hop(total, k, 0)]
        if sends:
            home[near[0]] = send_home(near[0], after(near[1], give))
        home[0] = send_home(0, own_sum, wait)
        order = [0] + sorted(sends)
    else:
        mine = spread(leaving[0])
        home[0] = send_home(0, sum_cores(*expert([[0, 1]], [[mine, hop(mine, 0, 1)]])))
    results = columns
    for k in order:
        results = combine(gates, results, first[k], second[k], home[k], BF16 if k == order[-1] else F32)
    return results


def solution(mesh):
    return jax.shard_map(
        local,
        mesh=mesh,
        in_specs=(
            P(("groups", "expert"), None),
            P(("groups", "expert"), None, None, "mp"),
            P(("groups", "expert")),
            P(None, "mp"),
            P("mp", None),
            P(),
            P(("groups", "expert"), None),
            P("expert", None, "mp"),
            P("expert", "mp", None),
        ),
        out_specs=P(("groups", "expert"), "mp"),
        check_vma=False,
    )
```

```python
import functools
import math

import jax
import jax.numpy as jnp
from jax import lax
from jax.experimental import pallas as pl
from jax.experimental.pallas import tpu as pltpu
from jax.sharding import PartitionSpec as P

HEAD_DIM = 128
SHARPNESS = HEAD_DIM**-0.5 * math.log2(math.e)
DIRECT = 8
CUTS = 4
TILE = 256
F32, BF16 = jnp.float32, jnp.bfloat16
PARAMS = pltpu.CompilerParams(vmem_limit_bytes=20 * 2**20)
CHEAP = pl.CostEstimate(flops=0, bytes_accessed=0, transcendentals=0)
WHOLE = pl.BlockSpec(memory_space=pltpu.VMEM)


def dot(a, b, dims=((1,), (0,))):
    return lax.dot_general(a, b, (dims, ((), ())), preferred_element_type=F32)


def in_hbm(value):
    return pltpu.with_memory_space_constraint(value, pltpu.HBM)


def position():
    return lax.axis_index("expert"), lax.axis_index("mp")


def query_kernel(tokens, weight, source, out, staged, tokens_here, weight_here, sems):
    features = tokens.shape[1]
    depth = features // CUTS
    copies, later = [], []
    for i in range(CUTS):
        part = pl.ds(i * depth, depth)
        copies.append(
            (
                pltpu.make_async_copy(tokens.at[:, part], tokens_here.at[:, part], sems.at[0, i]),
                pltpu.make_async_copy(weight.at[part, :], weight_here.at[part, :], sems.at[1, i]),
            )
        )
        rows = pl.ds(i * (source.shape[1] // CUTS), source.shape[1] // CUTS)
        later.append(pltpu.make_async_copy(source.at[:, rows], staged.at[:, rows], sems.at[2, i]))
    for pair in copies:
        for copy in pair:
            copy.start()
    for copy in later:
        copy.start()
    total = jnp.zeros(out.shape, F32)
    for i, pair in enumerate(copies):
        for copy in pair:
            copy.wait()
        part = slice(i * depth, (i + 1) * depth)
        total += dot(tokens_here[:, part], weight_here[part, :])
    out[...] = total.astype(BF16)
    for copy in later:
        copy.wait()


def ask(tokens, weight, source):
    return pl.pallas_call(
        query_kernel,
        in_specs=[pl.BlockSpec(memory_space=pltpu.HBM)] * 3,
        out_specs=[WHOLE] * 2,
        out_shape=[
            jax.ShapeDtypeStruct((tokens.shape[0], weight.shape[1]), BF16),
            jax.ShapeDtypeStruct(source.shape, BF16),
        ],
        scratch_shapes=[
            pltpu.VMEM(tokens.shape, BF16),
            pltpu.VMEM(weight.shape, BF16),
            pltpu.SemaphoreType.DMA((3, CUTS)),
        ],
        compiler_params=PARAMS,
        cost_estimate=CHEAP,
        name="query",
    )(in_hbm(tokens), in_hbm(weight), in_hbm(source))


def attend_kernel(queries, source, out):
    for head in range(queries.shape[1] // HEAD_DIM):
        part = slice(head * HEAD_DIM, (head + 1) * HEAD_DIM)
        scores = dot(queries[:, part], source[0, :, part], ((1,), (1,)))
        top = jnp.max(scores, axis=1, keepdims=True)
        weights = jnp.exp2((scores - top) * SHARPNESS).astype(BF16)
        values = jnp.concatenate([source[1, :, part], jnp.ones((source.shape[1], HEAD_DIM), BF16)], axis=1)
        summed = dot(weights, values)
        out[:, part] = (summed[:, :HEAD_DIM] / summed[:, HEAD_DIM:]).astype(BF16)


def attend(queries, source, block):
    rows, width = queries.shape
    if rows == block:
        return pl.pallas_call(
            attend_kernel,
            in_specs=[WHOLE] * 2,
            out_specs=WHOLE,
            out_shape=jax.ShapeDtypeStruct((rows, width), BF16),
            compiler_params=PARAMS,
        cost_estimate=CHEAP,
            name="attend",
        )(queries, source)
    return pl.pallas_call(
        attend_kernel,
        grid=(rows // block,),
        in_specs=[
            pl.BlockSpec((block, width), lambda i: (i, 0)),
            pl.BlockSpec(source.shape, lambda i: (0, 0, 0)),
        ],
        out_specs=pl.BlockSpec((block, width), lambda i: (i, 0)),
        out_shape=jax.ShapeDtypeStruct((rows, width), BF16),
        compiler_params=PARAMS,
        cost_estimate=CHEAP,
        name="attend",
    )(queries, source)


def pick_kernel(owner, *refs):
    backs, out = refs[:-1], refs[-1]
    here, _ = position()
    names = jnp.broadcast_to(owner[0:1, 0:1], out.shape)
    total = backs[0][...].astype(F32)
    for k in range(1, len(backs)):
        total = jnp.where(names == here ^ k, backs[k][...].astype(F32), total)
    out[...] = total.astype(BF16)


def pick(owner, backs):
    return pl.pallas_call(
        pick_kernel,
        in_specs=[WHOLE] * (1 + len(backs)),
        out_specs=WHOLE,
        out_shape=jax.ShapeDtypeStruct(backs[0].shape, BF16),
        compiler_params=PARAMS,
        cost_estimate=CHEAP,
        name="pick",
    )(owner, *backs)


def route_kernel(experts, parts, choice_t, choice, *outs):
    dispatch, first, second = outs[:parts], outs[parts : 2 * parts], outs[2 * parts :]
    tokens = choice_t.shape[1]
    slots = dispatch[0].shape[0]
    capacity = slots * parts // experts
    wide = lax.broadcasted_iota(jnp.int32, (tokens, experts), 1)
    tall = lax.broadcasted_iota(jnp.int32, (experts, tokens), 0)
    i = lax.broadcasted_iota(jnp.int32, (tokens, tokens), 0)
    j = lax.broadcasted_iota(jnp.int32, (tokens, tokens), 1)
    r0, r1 = choice_t[0:1, :], choice_t[1:2, :]
    turned = dot((i == j).astype(BF16), choice_t[...].astype(F32).astype(BF16), ((1,), (1,))).astype(jnp.int32)
    choice[...] = turned
    c0, c1 = turned[:, 0:1], turned[:, 1:2]
    named = ((wide == c0) | (wide == c1)).astype(BF16)
    named_t = ((tall == r0) | (tall == r1)).astype(BF16)
    rank = dot((j < i).astype(BF16), named).astype(jnp.int32)
    rank_t = dot(named_t, (i < j).astype(BF16)).astype(jnp.int32)
    place0 = c0 * capacity + jnp.sum(jnp.where(wide == c0, rank, 0), axis=1, keepdims=True)
    place1 = c1 * capacity + jnp.sum(jnp.where(wide == c1, rank, 0), axis=1, keepdims=True)
    across0 = r0 * capacity + jnp.sum(jnp.where(tall == r0, rank_t, 0), axis=0, keepdims=True)
    across1 = r1 * capacity + jnp.sum(jnp.where(tall == r1, rank_t, 0), axis=0, keepdims=True)
    lane = lax.broadcasted_iota(jnp.int32, (tokens, slots), 1)
    row = lax.broadcasted_iota(jnp.int32, (slots, tokens), 0)
    for k in range(parts):
        base = (position()[0] ^ k) * capacity if parts > 1 else 0
        dispatch[k][...] = ((row + base == across0) | (row + base == across1)).astype(BF16)
        first[k][...] = (lane + base == place0).astype(BF16)
        second[k][...] = (lane + base == place1).astype(BF16)


def route(choice, experts, parts, capacity):
    tokens = choice.shape[0]
    slots = experts * capacity // parts
    outs = pl.pallas_call(
        functools.partial(route_kernel, experts, parts),
        in_specs=[WHOLE],
        out_specs=[WHOLE] * (1 + 3 * parts),
        out_shape=[jax.ShapeDtypeStruct(choice.shape, jnp.int32)]
        + [jax.ShapeDtypeStruct((slots, tokens), BF16)] * parts
        + [jax.ShapeDtypeStruct((tokens, slots), BF16)] * (2 * parts),
        compiler_params=PARAMS,
        cost_estimate=CHEAP,
        name="route",
    )(choice.T)
    return outs[0], outs[1 : 1 + parts], outs[1 + parts : 1 + 2 * parts], outs[1 + 2 * parts :]


def state_kernel(count, sends, *refs):
    tokens = refs[0]
    contexts, weights = refs[1 : 1 + count], refs[1 + count : 1 + 2 * count]
    dispatch = refs[1 + 2 * count : 1 + 2 * count + sends]
    state, outs = refs[1 + 2 * count + sends], refs[2 + 2 * count + sends :]
    tile = min(TILE, state.shape[1])
    for at in range(0, state.shape[1], tile):
        part = slice(at, at + tile)
        total = tokens[:, part].astype(F32)
        for context, weight in zip(contexts, weights):
            total += dot(context[...], weight[:, part])
        state[:, part] = total.astype(BF16)
    for rows, out in zip(dispatch, outs):
        width = out.shape[1]
        at = (position()[1] & (state.shape[1] // width - 1)) * width
        out[...] = dot(rows[...], state[:, pl.ds(pl.multiple_of(at, width), width)]).astype(BF16)


def make_state(tokens, contexts, weights, dispatch, cuts):
    return pl.pallas_call(
        functools.partial(state_kernel, len(contexts), len(dispatch)),
        in_specs=[WHOLE] * (1 + 2 * len(contexts) + len(dispatch)),
        out_specs=[WHOLE] * (1 + len(dispatch)),
        out_shape=[jax.ShapeDtypeStruct(tokens.shape, BF16)]
        + [jax.ShapeDtypeStruct((rows.shape[0], tokens.shape[1] // cut), BF16) for rows, cut in zip(dispatch, cuts)],
        compiler_params=PARAMS,
        cost_estimate=CHEAP,
        name="state",
    )(tokens, *contexts, *weights, *dispatch)


def home_kernel(experts, state, dispatch, router, choice, own_a, own_b, gates, columns):
    half = own_a.shape[1]
    column = position()[1]
    core = column & 1
    own_a[...] = dot(dispatch[...], state[:, pl.ds(pl.multiple_of(core * half, half), half)]).astype(BF16)
    own_b[...] = dot(dispatch[...], state[:, pl.ds(pl.multiple_of((1 - core) * half, half), half)]).astype(BF16)
    logits = dot(state[...], router[...], ((1,), (1,)))
    wide = lax.broadcasted_iota(jnp.int32, logits.shape, 1)
    first = jnp.sum(jnp.where(wide == choice[:, 0:1], logits, 0.0), axis=1, keepdims=True)
    second = jnp.sum(jnp.where(wide == choice[:, 1:2], logits, 0.0), axis=1, keepdims=True)
    gates[:, 0:1] = jax.nn.sigmoid(first - second)
    gates[:, 1:2] = jax.nn.sigmoid(second - first)
    width = columns.shape[1]
    columns[...] = state[:, pl.ds(pl.multiple_of(column * width, width), width)].astype(F32)


def at_home(state, dispatch, router, choice, experts, width):
    tokens, features = state.shape
    slots = dispatch.shape[0]
    return pl.pallas_call(
        functools.partial(home_kernel, experts),
        in_specs=[WHOLE] * 4,
        out_specs=[WHOLE] * 4,
        out_shape=[
            jax.ShapeDtypeStruct((slots, features // 2), BF16),
            jax.ShapeDtypeStruct((slots, features // 2), BF16),
            jax.ShapeDtypeStruct((tokens, 2), F32),
            jax.ShapeDtypeStruct((tokens, width), F32),
        ],
        compiler_params=PARAMS,
        cost_estimate=CHEAP,
        name="home",
    )(state, dispatch, router, choice)


def expert_kernel(orders, *refs):
    blocks, at = [], 0
    for order in orders:
        blocks.append(refs[at : at + len(order)])
        at += len(order)
    column = position()[1]
    expand, shrink, keep, give, rows_here, hidden = refs[at:]
    count = blocks[0][0].shape[0]
    for block, (order, pieces) in enumerate(zip(orders, blocks)):
        for index, piece in zip(order, pieces):
            width = piece.shape[1]
            part = pl.ds(pl.multiple_of(((column & (len(order) - 1)) ^ index) * width, width), width)
            rows_here[block * count : (block + 1) * count, part] = piece[...]
    units = expand.shape[1]
    tile = min(TILE, units)
    for at in range(0, units, tile):
        total = dot(rows_here[...], expand[:, at : at + tile])
        hidden[:, at : at + tile] = jnp.maximum(total, 0.0).astype(BF16)
    width = keep.shape[2]
    for j in range(keep.shape[0]):
        at = pl.multiple_of((column ^ (2 * j) ^ 1) * width, width)
        give[j] = dot(hidden[...], shrink[:, pl.ds(at, width)]).astype(BF16)
    for j in range(keep.shape[0]):
        at = pl.multiple_of((column ^ (2 * j)) * width, width)
        keep[j] = dot(hidden[...], shrink[:, pl.ds(at, width)])


def run_expert(orders, blocks, expand, shrink, parts):
    pieces = [piece for block in blocks for piece in block]
    rows = pieces[0].shape[0] * len(blocks)
    features, units = expand.shape
    width = features // (2 * parts)
    return pl.pallas_call(
        functools.partial(expert_kernel, tuple(map(tuple, orders))),
        in_specs=[WHOLE] * (2 + len(pieces)),
        out_specs=[WHOLE] * 2,
        out_shape=[
            jax.ShapeDtypeStruct((parts, rows, width), F32),
            jax.ShapeDtypeStruct((parts, rows, width), BF16),
        ],
        scratch_shapes=[pltpu.VMEM((rows, features), BF16), pltpu.VMEM((rows, units), BF16)],
        compiler_params=PARAMS,
        cost_estimate=CHEAP,
        name="expert",
    )(*pieces, expand, shrink)


def combine_kernel(count, gates, base, first, second, *refs):
    parts, out = refs[:count], refs[count]
    total = parts[0][...].astype(F32)
    for part in parts[1:]:
        total += part[...].astype(F32)
    total = total.astype(BF16)
    result = base[...] + gates[:, 0:1] * dot(first[...], total) + gates[:, 1:2] * dot(second[...], total)
    out[...] = result.astype(out.dtype)


def combine(gates, base, first, second, parts, dtype):
    return pl.pallas_call(
        functools.partial(combine_kernel, len(parts)),
        in_specs=[WHOLE] * (4 + len(parts)),
        out_specs=WHOLE,
        out_shape=jax.ShapeDtypeStruct(base.shape, dtype),
        compiler_params=PARAMS,
        cost_estimate=CHEAP,
        name="combine",
    )(gates, base, first, second, *parts)


def bits_of(count):
    bits = []
    while 2 ** len(bits) < count:
        bits.insert(0, 2 ** len(bits))
    return bits


def local(
    tokens,
    encoder_states,
    source_owner,
    query_weight,
    output_weight,
    router_weight,
    expert_choice,
    expand_weight,
    shrink_weight,
):
    token_count, features = tokens.shape
    groups = lax.axis_size("expert")
    slices = lax.axis_size("mp")
    here, column = lax.axis_index("expert"), lax.axis_index("mp")
    width = features // slices
    experts = expand_weight.shape[0] * groups
    capacity = max(2, 3 * token_count // experts)
    direct = groups <= DIRECT
    pairs = slices // 2
    slots = capacity if direct else experts * capacity

    def hop(value, along_expert, along_mp):
        if along_expert == 0 and along_mp == 0:
            return value
        moves = [
            (e * slices + m, (e ^ along_expert) * slices + (m ^ along_mp))
            for e in range(groups)
            for m in range(slices)
        ]
        return lax.ppermute(value, ("expert", "mp"), moves)

    def spread(value):
        parts = value.reshape(groups, -1, value.shape[-1])
        return lax.all_to_all(parts, "expert", 0, 0, tiled=True).reshape(value.shape)

    def after(value, other):
        return lax.optimization_barrier((value, other))[0]

    steps = range(groups) if direct else [0]

    queries, source = ask(tokens, query_weight, encoder_states[0])
    expert_bits = bits_of(groups)
    bits = bits_of(slices)
    if direct:
        own = attend(queries, source, token_count)
        asked, steps_of = [queries], [0]
        for bit in expert_bits:
            asked = asked + [hop(value if k == 0 else after(value, own), bit, 0) for k, value in zip(steps_of, asked)]
            steps_of = steps_of + [k ^ bit for k in steps_of]
        asked = dict(zip(steps_of, asked))
        previous, backs = own, {}
        for k in sorted(range(1, groups), key=lambda k: (k & (k - 1) != 0, -k)):
            answer = previous = attend(after(asked[k], previous), source, token_count)
            backs[k] = hop(answer, k, 0)
        context = pick(source_owner.reshape(1, 1), [own] + [backs[k] for k in range(1, groups)])
    else:
        asked = lax.all_gather(queries, "expert", axis=0, tiled=True)
        previous = attend(asked, source, token_count)
        context = lax.dynamic_slice_in_dim(spread(previous), source_owner[0] * token_count, token_count, 0)

    choice, dispatch, first, second = route(after(expert_choice, previous), experts, len(steps), capacity)
    weights, order = [output_weight], [0]
    for bit in bits:
        if bit == 1:
            weights = [after(weight, context) for weight in weights]
        weights = weights + [hop(weight, 0, bit) for weight in weights]
        order = order + [index ^ bit for index in order]
    contexts = [context]
    for bit in bits:
        contexts = contexts + [hop(value if i == 0 else after(value, dispatch[0]), 0, bit) for i, value in enumerate(contexts)]

    far = set(range(2, groups)) if direct and pairs > 1 else set()
    sends = [k for k in range(2, groups)] + ([1] if groups > 1 else []) if direct else [0]
    cuts = [slices if k in far else 2 for k in sends]
    state, *leaving = make_state(tokens, contexts, weights, [dispatch[k] for k in sends], cuts)
    own_a, own_b, gates, columns = at_home(
        state, dispatch[0], router_weight.T, choice, experts, width
    )
    expert = functools.partial(run_expert, expand=expand_weight[0], shrink=shrink_weight[0], parts=pairs)

    def sum_cores(keep, give):
        return keep + hop(give, 0, 1).astype(F32)

    def send_home(k, summed, wait=None):
        parts = [summed[j].astype(BF16) for j in range(pairs)]
        if wait is not None:
            parts = parts[:1] + [after(part, wait) for part in parts[1:]]
        return [hop(part, k, 2 * j) if direct else hop(spread(part), 0, 2 * j) for j, part in enumerate(parts)]

    home, order = {}, [0]
    if direct:
        arrived = {k: hop(rows, k, 0) for k, rows in zip(sends, leaving)}
        keep, give = expert([[0, 1]], [[own_a, own_b]])
        if sends:
            give = after(give, arrived[groups - 1])
        own_sum, wait = sum_cores(keep, give), None
        earlier = [own_sum]
        crossing, started, relays = {}, None, {}
        for k in sends:
            pieces, places = [arrived[k]], [0]
            for bit in bits[:-1] if k in far else []:
                pieces = pieces + [hop(piece, 0, bit) for piece in pieces]
                places = places + [index ^ bit for index in places]
            relays[k] = pieces, places
            if k in far:
                earlier.append(pieces[-1])
                wait = pieces[-1]
        home[0] = send_home(0, own_sum, wait)
        turns = [[k for k in sends if k < groups - 1], [groups - 1]] if groups > 2 else [sends]
        for turn in turns:
            blocks, orders = [], []
            for k in turn:
                pieces, places = relays[k]
                if started is not None:
                    pieces = [after(piece, started) for piece in pieces]
                pieces = pieces + [hop(piece, 0, 1) for piece in pieces]
                places = places + [index ^ 1 for index in places]
                blocks.append(pieces)
                orders.append(places)
            if turn:
                for value in earlier:
                    blocks[0][0] = after(blocks[0][0], value)
                keep, give = expert(orders, blocks)
                summed = sum_cores(keep, give)
                earlier, started = [summed], give
                for i, k in enumerate(turn):
                    rows = summed[:, i * slots : (i + 1) * slots]
                    if k in far:
                        crossed = [hop(rows[j].astype(BF16), 0, 2 * j) for j in range(1, pairs)]
                        crossing[k] = [rows[0]] + crossed
                    else:
                        near = k, rows
        for k, (total, *crossed) in crossing.items():
            for part in crossed:
                total += (part if k == groups - 1 else after(part, summed)).astype(F32)
            total = total.astype(BF16)
            home[k] = [hop(total, k, 0)]
        if sends:
            home[near[0]] = send_home(near[0], after(near[1], give))
        order = [0] + sorted(sends)
    else:
        mine = spread(leaving[0])
        home[0] = send_home(0, sum_cores(*expert([[0, 1]], [[mine, hop(mine, 0, 1)]])))
    results = columns
    for k in order:
        results = combine(gates, results, first[k], second[k], home[k], BF16 if k == order[-1] else F32)
    return results


def solution(mesh):
    return jax.shard_map(
        local,
        mesh=mesh,
        in_specs=(
            P(("groups", "expert"), None),
            P(("groups", "expert"), None, None, "mp"),
            P(("groups", "expert")),
            P(None, "mp"),
            P("mp", None),
            P(),
            P(("groups", "expert"), None),
            P("expert", None, "mp"),
            P("expert", "mp", None),
        ),
        out_specs=P(("groups", "expert"), "mp"),
        check_vma=False,
    )
```

```python
import functools
import math

import jax
import jax.numpy as jnp
from jax import lax
from jax.experimental import pallas as pl
from jax.experimental.pallas import tpu as pltpu
from jax.sharding import PartitionSpec as P

HEAD_DIM = 128
SHARPNESS = HEAD_DIM**-0.5 * math.log2(math.e)
DIRECT = 8
CUTS = 4
TILE = 256
F32, BF16 = jnp.float32, jnp.bfloat16
PARAMS = pltpu.CompilerParams(vmem_limit_bytes=20 * 2**20)
CHEAP = pl.CostEstimate(flops=0, bytes_accessed=0, transcendentals=0)
WHOLE = pl.BlockSpec(memory_space=pltpu.VMEM)


def dot(a, b, dims=((1,), (0,))):
    return lax.dot_general(a, b, (dims, ((), ())), preferred_element_type=F32)


def in_hbm(value):
    return pltpu.with_memory_space_constraint(value, pltpu.HBM)


def position():
    return lax.axis_index("expert"), lax.axis_index("mp")


def query_kernel(tokens, weight, source, out, staged, tokens_here, weight_here, sems):
    features = tokens.shape[1]
    depth = features // CUTS
    copies, later = [], []
    for i in range(CUTS):
        part = pl.ds(i * depth, depth)
        copies.append(
            (
                pltpu.make_async_copy(tokens.at[:, part], tokens_here.at[:, part], sems.at[0, i]),
                pltpu.make_async_copy(weight.at[part, :], weight_here.at[part, :], sems.at[1, i]),
            )
        )
        rows = pl.ds(i * (source.shape[1] // CUTS), source.shape[1] // CUTS)
        later.append(pltpu.make_async_copy(source.at[:, rows], staged.at[:, rows], sems.at[2, i]))
    for pair in copies:
        for copy in pair:
            copy.start()
    for copy in later:
        copy.start()
    total = jnp.zeros(out.shape, F32)
    for i, pair in enumerate(copies):
        for copy in pair:
            copy.wait()
        part = slice(i * depth, (i + 1) * depth)
        total += dot(tokens_here[:, part], weight_here[part, :])
    out[...] = total.astype(BF16)
    for copy in later:
        copy.wait()


def ask(tokens, weight, source):
    return pl.pallas_call(
        query_kernel,
        in_specs=[pl.BlockSpec(memory_space=pltpu.HBM)] * 3,
        out_specs=[WHOLE] * 2,
        out_shape=[
            jax.ShapeDtypeStruct((tokens.shape[0], weight.shape[1]), BF16),
            jax.ShapeDtypeStruct(source.shape, BF16),
        ],
        scratch_shapes=[
            pltpu.VMEM(tokens.shape, BF16),
            pltpu.VMEM(weight.shape, BF16),
            pltpu.SemaphoreType.DMA((3, CUTS)),
        ],
        compiler_params=PARAMS,
        cost_estimate=CHEAP,
        name="query",
    )(in_hbm(tokens), in_hbm(weight), in_hbm(source))


def attend_kernel(queries, source, out):
    for head in range(queries.shape[1] // HEAD_DIM):
        part = slice(head * HEAD_DIM, (head + 1) * HEAD_DIM)
        scores = dot(queries[:, part], source[0, :, part], ((1,), (1,)))
        top = jnp.max(scores, axis=1, keepdims=True)
        weights = jnp.exp2((scores - top) * SHARPNESS).astype(BF16)
        values = jnp.concatenate([source[1, :, part], jnp.ones((source.shape[1], HEAD_DIM), BF16)], axis=1)
        summed = dot(weights, values)
        out[:, part] = (summed[:, :HEAD_DIM] / summed[:, HEAD_DIM:]).astype(BF16)


def attend(queries, source, block):
    rows, width = queries.shape
    if rows == block:
        return pl.pallas_call(
            attend_kernel,
            in_specs=[WHOLE] * 2,
            out_specs=WHOLE,
            out_shape=jax.ShapeDtypeStruct((rows, width), BF16),
            compiler_params=PARAMS,
        cost_estimate=CHEAP,
            name="attend",
        )(queries, source)
    return pl.pallas_call(
        attend_kernel,
        grid=(rows // block,),
        in_specs=[
            pl.BlockSpec((block, width), lambda i: (i, 0)),
            pl.BlockSpec(source.shape, lambda i: (0, 0, 0)),
        ],
        out_specs=pl.BlockSpec((block, width), lambda i: (i, 0)),
        out_shape=jax.ShapeDtypeStruct((rows, width), BF16),
        compiler_params=PARAMS,
        cost_estimate=CHEAP,
        name="attend",
    )(queries, source)


def pick_kernel(owner, *refs):
    backs, out = refs[:-1], refs[-1]
    here, _ = position()
    names = jnp.broadcast_to(owner[0:1, 0:1], out.shape)
    total = backs[0][...].astype(F32)
    for k in range(1, len(backs)):
        total = jnp.where(names == here ^ k, backs[k][...].astype(F32), total)
    out[...] = total.astype(BF16)


def pick(owner, backs):
    return pl.pallas_call(
        pick_kernel,
        in_specs=[WHOLE] * (1 + len(backs)),
        out_specs=WHOLE,
        out_shape=jax.ShapeDtypeStruct(backs[0].shape, BF16),
        compiler_params=PARAMS,
        cost_estimate=CHEAP,
        name="pick",
    )(owner, *backs)


def route_kernel(experts, parts, choice_t, choice, *outs):
    dispatch, first, second = outs[:parts], outs[parts : 2 * parts], outs[2 * parts :]
    tokens = choice_t.shape[1]
    slots = dispatch[0].shape[0]
    capacity = slots * parts // experts
    wide = lax.broadcasted_iota(jnp.int32, (tokens, experts), 1)
    tall = lax.broadcasted_iota(jnp.int32, (experts, tokens), 0)
    i = lax.broadcasted_iota(jnp.int32, (tokens, tokens), 0)
    j = lax.broadcasted_iota(jnp.int32, (tokens, tokens), 1)
    r0, r1 = choice_t[0:1, :], choice_t[1:2, :]
    turned = dot((i == j).astype(BF16), choice_t[...].astype(F32).astype(BF16), ((1,), (1,))).astype(jnp.int32)
    choice[...] = turned
    c0, c1 = turned[:, 0:1], turned[:, 1:2]
    named = ((wide == c0) | (wide == c1)).astype(BF16)
    named_t = ((tall == r0) | (tall == r1)).astype(BF16)
    rank = dot((j < i).astype(BF16), named).astype(jnp.int32)
    rank_t = dot(named_t, (i < j).astype(BF16)).astype(jnp.int32)
    place0 = c0 * capacity + jnp.sum(jnp.where(wide == c0, rank, 0), axis=1, keepdims=True)
    place1 = c1 * capacity + jnp.sum(jnp.where(wide == c1, rank, 0), axis=1, keepdims=True)
    across0 = r0 * capacity + jnp.sum(jnp.where(tall == r0, rank_t, 0), axis=0, keepdims=True)
    across1 = r1 * capacity + jnp.sum(jnp.where(tall == r1, rank_t, 0), axis=0, keepdims=True)
    lane = lax.broadcasted_iota(jnp.int32, (tokens, slots), 1)
    row = lax.broadcasted_iota(jnp.int32, (slots, tokens), 0)
    for k in range(parts):
        base = (position()[0] ^ k) * capacity if parts > 1 else 0
        dispatch[k][...] = ((row + base == across0) | (row + base == across1)).astype(BF16)
        first[k][...] = (lane + base == place0).astype(BF16)
        second[k][...] = (lane + base == place1).astype(BF16)


def route(choice, experts, parts, capacity):
    tokens = choice.shape[0]
    slots = experts * capacity // parts
    outs = pl.pallas_call(
        functools.partial(route_kernel, experts, parts),
        in_specs=[WHOLE],
        out_specs=[WHOLE] * (1 + 3 * parts),
        out_shape=[jax.ShapeDtypeStruct(choice.shape, jnp.int32)]
        + [jax.ShapeDtypeStruct((slots, tokens), BF16)] * parts
        + [jax.ShapeDtypeStruct((tokens, slots), BF16)] * (2 * parts),
        compiler_params=PARAMS,
        cost_estimate=CHEAP,
        name="route",
    )(choice.T)
    return outs[0], outs[1 : 1 + parts], outs[1 + parts : 1 + 2 * parts], outs[1 + 2 * parts :]


def state_kernel(count, sends, *refs):
    tokens = refs[0]
    contexts, weights = refs[1 : 1 + count], refs[1 + count : 1 + 2 * count]
    dispatch = refs[1 + 2 * count : 1 + 2 * count + sends]
    state, outs = refs[1 + 2 * count + sends], refs[2 + 2 * count + sends :]
    tile = min(TILE, state.shape[1])
    for at in range(0, state.shape[1], tile):
        part = slice(at, at + tile)
        total = tokens[:, part].astype(F32)
        for context, weight in zip(contexts, weights):
            total += dot(context[...], weight[:, part])
        state[:, part] = total.astype(BF16)
    for rows, out in zip(dispatch, outs):
        width = out.shape[1]
        at = (position()[1] & (state.shape[1] // width - 1)) * width
        out[...] = dot(rows[...], state[:, pl.ds(pl.multiple_of(at, width), width)]).astype(BF16)


def make_state(tokens, contexts, weights, dispatch, cuts):
    return pl.pallas_call(
        functools.partial(state_kernel, len(contexts), len(dispatch)),
        in_specs=[WHOLE] * (1 + 2 * len(contexts) + len(dispatch)),
        out_specs=[WHOLE] * (1 + len(dispatch)),
        out_shape=[jax.ShapeDtypeStruct(tokens.shape, BF16)]
        + [jax.ShapeDtypeStruct((rows.shape[0], tokens.shape[1] // cut), BF16) for rows, cut in zip(dispatch, cuts)],
        compiler_params=PARAMS,
        cost_estimate=CHEAP,
        name="state",
    )(tokens, *contexts, *weights, *dispatch)


def home_kernel(experts, state, dispatch, router, choice, own_a, own_b, gates, columns):
    half = own_a.shape[1]
    column = position()[1]
    core = column & 1
    own_a[...] = dot(dispatch[...], state[:, pl.ds(pl.multiple_of(core * half, half), half)]).astype(BF16)
    own_b[...] = dot(dispatch[...], state[:, pl.ds(pl.multiple_of((1 - core) * half, half), half)]).astype(BF16)
    logits = dot(state[...], router[...], ((1,), (1,)))
    wide = lax.broadcasted_iota(jnp.int32, logits.shape, 1)
    first = jnp.sum(jnp.where(wide == choice[:, 0:1], logits, 0.0), axis=1, keepdims=True)
    second = jnp.sum(jnp.where(wide == choice[:, 1:2], logits, 0.0), axis=1, keepdims=True)
    gates[:, 0:1] = jax.nn.sigmoid(first - second)
    gates[:, 1:2] = jax.nn.sigmoid(second - first)
    width = columns.shape[1]
    columns[...] = state[:, pl.ds(pl.multiple_of(column * width, width), width)].astype(F32)


def at_home(state, dispatch, router, choice, experts, width):
    tokens, features = state.shape
    slots = dispatch.shape[0]
    return pl.pallas_call(
        functools.partial(home_kernel, experts),
        in_specs=[WHOLE] * 4,
        out_specs=[WHOLE] * 4,
        out_shape=[
            jax.ShapeDtypeStruct((slots, features // 2), BF16),
            jax.ShapeDtypeStruct((slots, features // 2), BF16),
            jax.ShapeDtypeStruct((tokens, 2), F32),
            jax.ShapeDtypeStruct((tokens, width), F32),
        ],
        compiler_params=PARAMS,
        cost_estimate=CHEAP,
        name="home",
    )(state, dispatch, router, choice)


def expert_kernel(orders, *refs):
    blocks, at = [], 0
    for order in orders:
        blocks.append(refs[at : at + len(order)])
        at += len(order)
    column = position()[1]
    expand, shrink, keep, give, rows_here, hidden = refs[at:]
    count = blocks[0][0].shape[0]
    for block, (order, pieces) in enumerate(zip(orders, blocks)):
        for index, piece in zip(order, pieces):
            width = piece.shape[1]
            part = pl.ds(pl.multiple_of(((column & (len(order) - 1)) ^ index) * width, width), width)
            rows_here[block * count : (block + 1) * count, part] = piece[...]
    units = expand.shape[1]
    tile = min(TILE, units)
    for at in range(0, units, tile):
        total = dot(rows_here[...], expand[:, at : at + tile])
        hidden[:, at : at + tile] = jnp.maximum(total, 0.0).astype(BF16)
    width = keep.shape[2]
    for j in range(keep.shape[0]):
        at = pl.multiple_of((column ^ (2 * j) ^ 1) * width, width)
        give[j] = dot(hidden[...], shrink[:, pl.ds(at, width)]).astype(BF16)
    for j in range(keep.shape[0]):
        at = pl.multiple_of((column ^ (2 * j)) * width, width)
        keep[j] = dot(hidden[...], shrink[:, pl.ds(at, width)])


def run_expert(orders, blocks, expand, shrink, parts):
    pieces = [piece for block in blocks for piece in block]
    rows = pieces[0].shape[0] * len(blocks)
    features, units = expand.shape
    width = features // (2 * parts)
    return pl.pallas_call(
        functools.partial(expert_kernel, tuple(map(tuple, orders))),
        in_specs=[WHOLE] * (2 + len(pieces)),
        out_specs=[WHOLE] * 2,
        out_shape=[
            jax.ShapeDtypeStruct((parts, rows, width), F32),
            jax.ShapeDtypeStruct((parts, rows, width), BF16),
        ],
        scratch_shapes=[pltpu.VMEM((rows, features), BF16), pltpu.VMEM((rows, units), BF16)],
        compiler_params=PARAMS,
        cost_estimate=CHEAP,
        name="expert",
    )(*pieces, expand, shrink)


def combine_kernel(count, gates, base, first, second, *refs):
    parts, out = refs[:count], refs[count]
    total = parts[0][...].astype(F32)
    for part in parts[1:]:
        total += part[...].astype(F32)
    total = total.astype(BF16)
    result = base[...] + gates[:, 0:1] * dot(first[...], total) + gates[:, 1:2] * dot(second[...], total)
    out[...] = result.astype(out.dtype)


def combine(gates, base, first, second, parts, dtype):
    return pl.pallas_call(
        functools.partial(combine_kernel, len(parts)),
        in_specs=[WHOLE] * (4 + len(parts)),
        out_specs=WHOLE,
        out_shape=jax.ShapeDtypeStruct(base.shape, dtype),
        compiler_params=PARAMS,
        cost_estimate=CHEAP,
        name="combine",
    )(gates, base, first, second, *parts)


def bits_of(count):
    bits = []
    while 2 ** len(bits) < count:
        bits.insert(0, 2 ** len(bits))
    return bits


def local(
    tokens,
    encoder_states,
    source_owner,
    query_weight,
    output_weight,
    router_weight,
    expert_choice,
    expand_weight,
    shrink_weight,
):
    token_count, features = tokens.shape
    groups = lax.axis_size("expert")
    slices = lax.axis_size("mp")
    here, column = lax.axis_index("expert"), lax.axis_index("mp")
    width = features // slices
    experts = expand_weight.shape[0] * groups
    capacity = max(2, 3 * token_count // experts)
    direct = groups <= DIRECT
    pairs = slices // 2
    slots = capacity if direct else experts * capacity

    def hop(value, along_expert, along_mp):
        if along_expert == 0 and along_mp == 0:
            return value
        moves = [
            (e * slices + m, (e ^ along_expert) * slices + (m ^ along_mp))
            for e in range(groups)
            for m in range(slices)
        ]
        return lax.ppermute(value, ("expert", "mp"), moves)

    def spread(value):
        parts = value.reshape(groups, -1, value.shape[-1])
        return lax.all_to_all(parts, "expert", 0, 0, tiled=True).reshape(value.shape)

    def after(value, other):
        return lax.optimization_barrier((value, other))[0]

    steps = range(groups) if direct else [0]

    queries, source = ask(tokens, query_weight, encoder_states[0])
    expert_bits = bits_of(groups)
    bits = bits_of(slices)
    if direct:
        own = attend(queries, source, token_count)
        asked, steps_of = [queries], [0]
        for bit in expert_bits:
            asked = asked + [hop(value if k == 0 else after(value, own), bit, 0) for k, value in zip(steps_of, asked)]
            steps_of = steps_of + [k ^ bit for k in steps_of]
        asked = dict(zip(steps_of, asked))
        previous, backs = own, {}
        for k in sorted(range(1, groups), key=lambda k: (k & (k - 1) != 0, -k)):
            answer = previous = attend(after(asked[k], previous), source, token_count)
            backs[k] = hop(answer, k, 0)
        context = pick(source_owner.reshape(1, 1), [own] + [backs[k] for k in range(1, groups)])
    else:
        asked = lax.all_gather(queries, "expert", axis=0, tiled=True)
        previous = attend(asked, source, token_count)
        context = lax.dynamic_slice_in_dim(spread(previous), source_owner[0] * token_count, token_count, 0)

    choice, dispatch, first, second = route(after(expert_choice, previous), experts, len(steps), capacity)
    weights, order = [output_weight], [0]
    for bit in bits:
        if bit == 1:
            weights = [after(weight, context) for weight in weights]
        weights = weights + [hop(weight, 0, bit) for weight in weights]
        order = order + [index ^ bit for index in order]
    contexts = [context]
    for bit in bits:
        contexts = contexts + [hop(value if i == 0 else after(value, dispatch[0]), 0, bit) for i, value in enumerate(contexts)]

    far = set(range(2, groups)) if direct and pairs > 1 else set()
    sends = [k for k in range(2, groups)] + ([1] if groups > 1 else []) if direct else [0]
    relayed = {groups - 1} & far
    cuts = [slices if k in relayed else 2 for k in sends]
    state, *leaving = make_state(tokens, contexts, weights, [dispatch[k] for k in sends], cuts)
    own_a, own_b, gates, columns = at_home(
        state, dispatch[0], router_weight.T, choice, experts, width
    )
    expert = functools.partial(run_expert, expand=expand_weight[0], shrink=shrink_weight[0], parts=pairs)

    def sum_cores(keep, give):
        return keep + hop(give, 0, 1).astype(F32)

    def send_home(k, summed, wait=None):
        parts = [summed[j].astype(BF16) for j in range(pairs)]
        if wait is not None:
            parts = parts[:1] + [after(part, wait) for part in parts[1:]]
        return [hop(part, k, 2 * j) if direct else hop(spread(part), 0, 2 * j) for j, part in enumerate(parts)]

    home, order = {}, [0]
    if direct:
        arrived = {k: hop(rows, k, 0) for k, rows in zip(sends, leaving)}
        keep, give = expert([[0, 1]], [[own_a, own_b]])
        if sends:
            give = after(give, arrived[groups - 1])
        own_sum, wait = sum_cores(keep, give), None
        earlier = [own_sum]
        crossing, started, relays = {}, None, {}
        for k in sends:
            pieces, places = [arrived[k]], [0]
            for bit in bits[:-1] if k in relayed else []:
                pieces = pieces + [hop(piece, 0, bit) for piece in pieces]
                places = places + [index ^ bit for index in places]
            relays[k] = pieces, places
            if k in relayed:
                earlier.append(pieces[-1])
                wait = pieces[-1]
        home[0] = send_home(0, own_sum, wait)
        turns = [[k for k in sends if k < groups - 1], [groups - 1]] if groups > 2 else [sends]
        for turn in turns:
            blocks, orders = [], []
            for k in turn:
                pieces, places = relays[k]
                if started is not None:
                    pieces = [after(piece, started) for piece in pieces]
                pieces = pieces + [hop(piece, 0, 1) for piece in pieces]
                places = places + [index ^ 1 for index in places]
                blocks.append(pieces)
                orders.append(places)
            if turn:
                for value in earlier:
                    blocks[0][0] = after(blocks[0][0], value)
                keep, give = expert(orders, blocks)
                summed = sum_cores(keep, give)
                earlier, started = [summed], give
                for i, k in enumerate(turn):
                    rows = summed[:, i * slots : (i + 1) * slots]
                    if k in far:
                        crossed = [hop(rows[j].astype(BF16), 0, 2 * j) for j in range(1, pairs)]
                        crossing[k] = [rows[0]] + crossed
                    else:
                        near = k, rows
        for k, (total, *crossed) in crossing.items():
            for part in crossed:
                total += (part if k == groups - 1 else after(part, summed)).astype(F32)
            total = total.astype(BF16)
            home[k] = [hop(total, k, 0)]
        if sends:
            home[near[0]] = send_home(near[0], after(near[1], give))
        order = [0] + sorted(sends)
    else:
        mine = spread(leaving[0])
        home[0] = send_home(0, sum_cores(*expert([[0, 1]], [[mine, hop(mine, 0, 1)]])))
    results = columns
    for k in order:
        results = combine(gates, results, first[k], second[k], home[k], BF16 if k == order[-1] else F32)
    return results


def solution(mesh):
    return jax.shard_map(
        local,
        mesh=mesh,
        in_specs=(
            P(("groups", "expert"), None),
            P(("groups", "expert"), None, None, "mp"),
            P(("groups", "expert")),
            P(None, "mp"),
            P("mp", None),
            P(),
            P(("groups", "expert"), None),
            P("expert", None, "mp"),
            P("expert", "mp", None),
        ),
        out_specs=P(("groups", "expert"), "mp"),
        check_vma=False,
    )
```

```python
import functools
import math

import jax
import jax.numpy as jnp
from jax import lax
from jax.experimental import pallas as pl
from jax.experimental.pallas import tpu as pltpu
from jax.sharding import PartitionSpec as P

HEAD_DIM = 128
SHARPNESS = HEAD_DIM**-0.5 * math.log2(math.e)
DIRECT = 8
CUTS = 4
TILE = 256
F32, BF16 = jnp.float32, jnp.bfloat16
PARAMS = pltpu.CompilerParams(vmem_limit_bytes=20 * 2**20)
CHEAP = pl.CostEstimate(flops=0, bytes_accessed=0, transcendentals=0)
WHOLE = pl.BlockSpec(memory_space=pltpu.VMEM)


def dot(a, b, dims=((1,), (0,))):
    return lax.dot_general(a, b, (dims, ((), ())), preferred_element_type=F32)


def in_hbm(value):
    return pltpu.with_memory_space_constraint(value, pltpu.HBM)


def position():
    return lax.axis_index("expert"), lax.axis_index("mp")


def query_kernel(tokens, weight, source, out, staged, tokens_here, weight_here, sems):
    features = tokens.shape[1]
    depth = features // CUTS
    copies, later = [], []
    for i in range(CUTS):
        part = pl.ds(i * depth, depth)
        copies.append(
            (
                pltpu.make_async_copy(tokens.at[:, part], tokens_here.at[:, part], sems.at[0, i]),
                pltpu.make_async_copy(weight.at[part, :], weight_here.at[part, :], sems.at[1, i]),
            )
        )
        rows = pl.ds(i * (source.shape[1] // CUTS), source.shape[1] // CUTS)
        later.append(pltpu.make_async_copy(source.at[:, rows], staged.at[:, rows], sems.at[2, i]))
    for pair in copies:
        for copy in pair:
            copy.start()
    for copy in later:
        copy.start()
    total = jnp.zeros(out.shape, F32)
    for i, pair in enumerate(copies):
        for copy in pair:
            copy.wait()
        part = slice(i * depth, (i + 1) * depth)
        total += dot(tokens_here[:, part], weight_here[part, :])
    out[...] = total.astype(BF16)
    for copy in later:
        copy.wait()


def ask(tokens, weight, source):
    return pl.pallas_call(
        query_kernel,
        in_specs=[pl.BlockSpec(memory_space=pltpu.HBM)] * 3,
        out_specs=[WHOLE] * 2,
        out_shape=[
            jax.ShapeDtypeStruct((tokens.shape[0], weight.shape[1]), BF16),
            jax.ShapeDtypeStruct(source.shape, BF16),
        ],
        scratch_shapes=[
            pltpu.VMEM(tokens.shape, BF16),
            pltpu.VMEM(weight.shape, BF16),
            pltpu.SemaphoreType.DMA((3, CUTS)),
        ],
        compiler_params=PARAMS,
        cost_estimate=CHEAP,
        name="query",
    )(in_hbm(tokens), in_hbm(weight), in_hbm(source))


def attend_kernel(queries, source, out):
    for head in range(queries.shape[1] // HEAD_DIM):
        part = slice(head * HEAD_DIM, (head + 1) * HEAD_DIM)
        scores = dot(queries[:, part], source[0, :, part], ((1,), (1,)))
        top = jnp.max(scores, axis=1, keepdims=True)
        weights = jnp.exp2((scores - top) * SHARPNESS).astype(BF16)
        values = jnp.concatenate([source[1, :, part], jnp.ones((source.shape[1], HEAD_DIM), BF16)], axis=1)
        summed = dot(weights, values)
        out[:, part] = (summed[:, :HEAD_DIM] / summed[:, HEAD_DIM:]).astype(BF16)


def attend(queries, source, block):
    rows, width = queries.shape
    if rows == block:
        return pl.pallas_call(
            attend_kernel,
            in_specs=[WHOLE] * 2,
            out_specs=WHOLE,
            out_shape=jax.ShapeDtypeStruct((rows, width), BF16),
            compiler_params=PARAMS,
        cost_estimate=CHEAP,
            name="attend",
        )(queries, source)
    return pl.pallas_call(
        attend_kernel,
        grid=(rows // block,),
        in_specs=[
            pl.BlockSpec((block, width), lambda i: (i, 0)),
            pl.BlockSpec(source.shape, lambda i: (0, 0, 0)),
        ],
        out_specs=pl.BlockSpec((block, width), lambda i: (i, 0)),
        out_shape=jax.ShapeDtypeStruct((rows, width), BF16),
        compiler_params=PARAMS,
        cost_estimate=CHEAP,
        name="attend",
    )(queries, source)


def pick_kernel(owner, *refs):
    backs, out = refs[:-1], refs[-1]
    here, _ = position()
    names = jnp.broadcast_to(owner[0:1, 0:1], out.shape)
    total = backs[0][...].astype(F32)
    for k in range(1, len(backs)):
        total = jnp.where(names == here ^ k, backs[k][...].astype(F32), total)
    out[...] = total.astype(BF16)


def pick(owner, backs):
    return pl.pallas_call(
        pick_kernel,
        in_specs=[WHOLE] * (1 + len(backs)),
        out_specs=WHOLE,
        out_shape=jax.ShapeDtypeStruct(backs[0].shape, BF16),
        compiler_params=PARAMS,
        cost_estimate=CHEAP,
        name="pick",
    )(owner, *backs)


def route_kernel(experts, parts, choice_t, choice, *outs):
    dispatch, first, second = outs[:parts], outs[parts : 2 * parts], outs[2 * parts :]
    tokens = choice_t.shape[1]
    slots = dispatch[0].shape[0]
    capacity = slots * parts // experts
    wide = lax.broadcasted_iota(jnp.int32, (tokens, experts), 1)
    tall = lax.broadcasted_iota(jnp.int32, (experts, tokens), 0)
    i = lax.broadcasted_iota(jnp.int32, (tokens, tokens), 0)
    j = lax.broadcasted_iota(jnp.int32, (tokens, tokens), 1)
    r0, r1 = choice_t[0:1, :], choice_t[1:2, :]
    turned = dot((i == j).astype(BF16), choice_t[...].astype(F32).astype(BF16), ((1,), (1,))).astype(jnp.int32)
    choice[...] = turned
    c0, c1 = turned[:, 0:1], turned[:, 1:2]
    named = ((wide == c0) | (wide == c1)).astype(BF16)
    named_t = ((tall == r0) | (tall == r1)).astype(BF16)
    rank = dot((j < i).astype(BF16), named).astype(jnp.int32)
    rank_t = dot(named_t, (i < j).astype(BF16)).astype(jnp.int32)
    place0 = c0 * capacity + jnp.sum(jnp.where(wide == c0, rank, 0), axis=1, keepdims=True)
    place1 = c1 * capacity + jnp.sum(jnp.where(wide == c1, rank, 0), axis=1, keepdims=True)
    across0 = r0 * capacity + jnp.sum(jnp.where(tall == r0, rank_t, 0), axis=0, keepdims=True)
    across1 = r1 * capacity + jnp.sum(jnp.where(tall == r1, rank_t, 0), axis=0, keepdims=True)
    lane = lax.broadcasted_iota(jnp.int32, (tokens, slots), 1)
    row = lax.broadcasted_iota(jnp.int32, (slots, tokens), 0)
    for k in range(parts):
        base = (position()[0] ^ k) * capacity if parts > 1 else 0
        dispatch[k][...] = ((row + base == across0) | (row + base == across1)).astype(BF16)
        first[k][...] = (lane + base == place0).astype(BF16)
        second[k][...] = (lane + base == place1).astype(BF16)


def route(choice, experts, parts, capacity):
    tokens = choice.shape[0]
    slots = experts * capacity // parts
    outs = pl.pallas_call(
        functools.partial(route_kernel, experts, parts),
        in_specs=[WHOLE],
        out_specs=[WHOLE] * (1 + 3 * parts),
        out_shape=[jax.ShapeDtypeStruct(choice.shape, jnp.int32)]
        + [jax.ShapeDtypeStruct((slots, tokens), BF16)] * parts
        + [jax.ShapeDtypeStruct((tokens, slots), BF16)] * (2 * parts),
        compiler_params=PARAMS,
        cost_estimate=CHEAP,
        name="route",
    )(choice.T)
    return outs[0], outs[1 : 1 + parts], outs[1 + parts : 1 + 2 * parts], outs[1 + 2 * parts :]


def state_kernel(count, sends, *refs):
    tokens = refs[0]
    contexts, weights = refs[1 : 1 + count], refs[1 + count : 1 + 2 * count]
    dispatch = refs[1 + 2 * count : 1 + 2 * count + sends]
    state, outs = refs[1 + 2 * count + sends], refs[2 + 2 * count + sends :]
    tile = min(TILE, state.shape[1])
    for at in range(0, state.shape[1], tile):
        part = slice(at, at + tile)
        total = tokens[:, part].astype(F32)
        for context, weight in zip(contexts, weights):
            total += dot(context[...], weight[:, part])
        state[:, part] = total.astype(BF16)
    for rows, out in zip(dispatch, outs):
        width = out.shape[1]
        at = (position()[1] & (state.shape[1] // width - 1)) * width
        out[...] = dot(rows[...], state[:, pl.ds(pl.multiple_of(at, width), width)]).astype(BF16)


def make_state(tokens, contexts, weights, dispatch, cuts):
    return pl.pallas_call(
        functools.partial(state_kernel, len(contexts), len(dispatch)),
        in_specs=[WHOLE] * (1 + 2 * len(contexts) + len(dispatch)),
        out_specs=[WHOLE] * (1 + len(dispatch)),
        out_shape=[jax.ShapeDtypeStruct(tokens.shape, BF16)]
        + [jax.ShapeDtypeStruct((rows.shape[0], tokens.shape[1] // cut), BF16) for rows, cut in zip(dispatch, cuts)],
        compiler_params=PARAMS,
        cost_estimate=CHEAP,
        name="state",
    )(tokens, *contexts, *weights, *dispatch)


def home_kernel(experts, state, dispatch, router, choice, own_a, own_b, gates, columns):
    half = own_a.shape[1]
    column = position()[1]
    core = column & 1
    own_a[...] = dot(dispatch[...], state[:, pl.ds(pl.multiple_of(core * half, half), half)]).astype(BF16)
    own_b[...] = dot(dispatch[...], state[:, pl.ds(pl.multiple_of((1 - core) * half, half), half)]).astype(BF16)
    logits = dot(state[...], router[...], ((1,), (1,)))
    wide = lax.broadcasted_iota(jnp.int32, logits.shape, 1)
    first = jnp.sum(jnp.where(wide == choice[:, 0:1], logits, 0.0), axis=1, keepdims=True)
    second = jnp.sum(jnp.where(wide == choice[:, 1:2], logits, 0.0), axis=1, keepdims=True)
    gates[:, 0:1] = jax.nn.sigmoid(first - second)
    gates[:, 1:2] = jax.nn.sigmoid(second - first)
    width = columns.shape[1]
    columns[...] = state[:, pl.ds(pl.multiple_of(column * width, width), width)].astype(F32)


def at_home(state, dispatch, router, choice, experts, width):
    tokens, features = state.shape
    slots = dispatch.shape[0]
    return pl.pallas_call(
        functools.partial(home_kernel, experts),
        in_specs=[WHOLE] * 4,
        out_specs=[WHOLE] * 4,
        out_shape=[
            jax.ShapeDtypeStruct((slots, features // 2), BF16),
            jax.ShapeDtypeStruct((slots, features // 2), BF16),
            jax.ShapeDtypeStruct((tokens, 2), F32),
            jax.ShapeDtypeStruct((tokens, width), F32),
        ],
        compiler_params=PARAMS,
        cost_estimate=CHEAP,
        name="home",
    )(state, dispatch, router, choice)


def expert_kernel(orders, *refs):
    blocks, at = [], 0
    for order in orders:
        blocks.append(refs[at : at + len(order)])
        at += len(order)
    column = position()[1]
    expand, shrink, keep, give, rows_here, hidden = refs[at:]
    count = blocks[0][0].shape[0]
    for block, (order, pieces) in enumerate(zip(orders, blocks)):
        for index, piece in zip(order, pieces):
            width = piece.shape[1]
            part = pl.ds(pl.multiple_of(((column & (len(order) - 1)) ^ index) * width, width), width)
            rows_here[block * count : (block + 1) * count, part] = piece[...]
    units = expand.shape[1]
    tile = min(TILE, units)
    for at in range(0, units, tile):
        total = dot(rows_here[...], expand[:, at : at + tile])
        hidden[:, at : at + tile] = jnp.maximum(total, 0.0).astype(BF16)
    width = keep.shape[2]
    for j in range(keep.shape[0]):
        at = pl.multiple_of((column ^ (2 * j) ^ 1) * width, width)
        give[j] = dot(hidden[...], shrink[:, pl.ds(at, width)]).astype(BF16)
    for j in range(keep.shape[0]):
        at = pl.multiple_of((column ^ (2 * j)) * width, width)
        keep[j] = dot(hidden[...], shrink[:, pl.ds(at, width)])


def run_expert(orders, blocks, expand, shrink, parts):
    pieces = [piece for block in blocks for piece in block]
    rows = pieces[0].shape[0] * len(blocks)
    features, units = expand.shape
    width = features // (2 * parts)
    return pl.pallas_call(
        functools.partial(expert_kernel, tuple(map(tuple, orders))),
        in_specs=[WHOLE] * (2 + len(pieces)),
        out_specs=[WHOLE] * 2,
        out_shape=[
            jax.ShapeDtypeStruct((parts, rows, width), F32),
            jax.ShapeDtypeStruct((parts, rows, width), BF16),
        ],
        scratch_shapes=[pltpu.VMEM((rows, features), BF16), pltpu.VMEM((rows, units), BF16)],
        compiler_params=PARAMS,
        cost_estimate=CHEAP,
        name="expert",
    )(*pieces, expand, shrink)


def combine_kernel(count, gates, base, first, second, *refs):
    parts, out = refs[:count], refs[count]
    total = parts[0][...].astype(F32)
    for part in parts[1:]:
        total += part[...].astype(F32)
    total = total.astype(BF16)
    result = base[...] + gates[:, 0:1] * dot(first[...], total) + gates[:, 1:2] * dot(second[...], total)
    out[...] = result.astype(out.dtype)


def combine(gates, base, first, second, parts, dtype):
    return pl.pallas_call(
        functools.partial(combine_kernel, len(parts)),
        in_specs=[WHOLE] * (4 + len(parts)),
        out_specs=WHOLE,
        out_shape=jax.ShapeDtypeStruct(base.shape, dtype),
        compiler_params=PARAMS,
        cost_estimate=CHEAP,
        name="combine",
    )(gates, base, first, second, *parts)


def bits_of(count):
    bits = []
    while 2 ** len(bits) < count:
        bits.insert(0, 2 ** len(bits))
    return bits


def local(
    tokens,
    encoder_states,
    source_owner,
    query_weight,
    output_weight,
    router_weight,
    expert_choice,
    expand_weight,
    shrink_weight,
):
    token_count, features = tokens.shape
    groups = lax.axis_size("expert")
    slices = lax.axis_size("mp")
    here, column = lax.axis_index("expert"), lax.axis_index("mp")
    width = features // slices
    experts = expand_weight.shape[0] * groups
    capacity = max(2, 3 * token_count // experts)
    direct = groups <= DIRECT
    pairs = slices // 2
    slots = capacity if direct else experts * capacity

    def hop(value, along_expert, along_mp):
        if along_expert == 0 and along_mp == 0:
            return value
        moves = [
            (e * slices + m, (e ^ along_expert) * slices + (m ^ along_mp))
            for e in range(groups)
            for m in range(slices)
        ]
        return lax.ppermute(value, ("expert", "mp"), moves)

    def spread(value):
        parts = value.reshape(groups, -1, value.shape[-1])
        return lax.all_to_all(parts, "expert", 0, 0, tiled=True).reshape(value.shape)

    def after(value, other):
        return lax.optimization_barrier((value, other))[0]

    steps = range(groups) if direct else [0]

    queries, source = ask(tokens, query_weight, encoder_states[0])
    expert_bits = bits_of(groups)
    bits = bits_of(slices)
    if direct:
        own = attend(queries, source, token_count)
        asked, steps_of = [queries], [0]
        for bit in expert_bits:
            asked = asked + [hop(value if k == 0 else after(value, own), bit, 0) for k, value in zip(steps_of, asked)]
            steps_of = steps_of + [k ^ bit for k in steps_of]
        asked = dict(zip(steps_of, asked))
        previous, backs = own, {}
        for k in sorted(range(1, groups), key=lambda k: (k & (k - 1) != 0, -k)):
            answer = previous = attend(after(asked[k], previous), source, token_count)
            backs[k] = hop(answer, k, 0)
        context = pick(source_owner.reshape(1, 1), [own] + [backs[k] for k in range(1, groups)])
    else:
        asked = lax.all_gather(queries, "expert", axis=0, tiled=True)
        previous = attend(asked, source, token_count)
        context = lax.dynamic_slice_in_dim(spread(previous), source_owner[0] * token_count, token_count, 0)

    choice, dispatch, first, second = route(after(expert_choice, previous), experts, len(steps), capacity)
    weights, order = [output_weight], [0]
    for bit in bits:
        if bit == 1:
            weights = [after(weight, context) for weight in weights]
        weights = weights + [hop(weight, 0, bit) for weight in weights]
        order = order + [index ^ bit for index in order]
    contexts = [context]
    for bit in bits:
        contexts = contexts + [hop(value if i == 0 else after(value, dispatch[0]), 0, bit) for i, value in enumerate(contexts)]

    far = set(range(2, groups)) if direct and pairs > 1 else set()
    sends = [k for k in range(2, groups)] + ([1] if groups > 1 else []) if direct else [0]
    relayed = {groups - 1} & far
    cuts = [slices if k in relayed else 2 for k in sends]
    state, *leaving = make_state(tokens, contexts, weights, [dispatch[k] for k in sends], cuts)
    own_a, own_b, gates, columns = at_home(
        state, dispatch[0], router_weight.T, choice, experts, width
    )
    expert = functools.partial(run_expert, expand=expand_weight[0], shrink=shrink_weight[0], parts=pairs)

    def sum_cores(keep, give):
        return keep + hop(give, 0, 1).astype(F32)

    def send_home(k, summed, wait=None):
        parts = [summed[j].astype(BF16) for j in range(pairs)]
        if wait is not None:
            parts = parts[:1] + [after(part, wait) for part in parts[1:]]
        return [hop(part, k, 2 * j) if direct else hop(spread(part), 0, 2 * j) for j, part in enumerate(parts)]

    home, order = {}, [0]
    if direct:
        arrived = {k: hop(rows, k, 0) for k, rows in zip(sends, leaving)}
        keep, give = expert([[0, 1]], [[own_a, own_b]])
        if sends:
            give = after(give, arrived[groups - 1])
        own_sum, wait = sum_cores(keep, give), None
        earlier = [own_sum]
        crossing, started, relays = {}, None, {}
        for k in sends:
            pieces, places = [arrived[k]], [0]
            for bit in bits[:-1] if k in relayed else []:
                pieces = pieces + [hop(piece, 0, bit) for piece in pieces]
                places = places + [index ^ bit for index in places]
            relays[k] = pieces, places
            if k in relayed:
                earlier.append(pieces[-1])
                wait = pieces[-1]
        home[0] = send_home(0, own_sum, wait)
        turns = [[groups - 1], [k for k in sends if k < groups - 1]] if groups > 2 else [sends]
        for turn in turns:
            blocks, orders = [], []
            for k in turn:
                pieces, places = relays[k]
                if started is None and len(turns) > 1:
                    pieces = [after(piece, arrived[turns[1][0]]) for piece in pieces]
                pieces = pieces + [hop(piece, 0, 1) for piece in pieces]
                places = places + [index ^ 1 for index in places]
                blocks.append(pieces)
                orders.append(places)
            if turn:
                for value in earlier:
                    blocks[0][0] = after(blocks[0][0], value)
                keep, give = expert(orders, blocks)
                summed = sum_cores(keep, give)
                earlier, started = [summed], give
                for i, k in enumerate(turn):
                    rows = summed[:, i * slots : (i + 1) * slots]
                    if k in far:
                        leaves = [rows[j].astype(BF16) for j in range(1, pairs)]
                        earlier = earlier + leaves
                        crossing[k] = [rows[0]] + [hop(part, 0, 2 * j) for j, part in enumerate(leaves, 1)]
                    else:
                        near = k, rows
        for k, (total, *crossed) in crossing.items():
            for part in crossed:
                total += (after(part, summed) if k == groups - 1 else part).astype(F32)
            total = total.astype(BF16)
            home[k] = [hop(total, k, 0)]
        if sends:
            home[near[0]] = send_home(near[0], after(near[1], give))
        order = sorted(sends, key=lambda k: (k == 1, -k)) + [0]
    else:
        mine = spread(leaving[0])
        home[0] = send_home(0, sum_cores(*expert([[0, 1]], [[mine, hop(mine, 0, 1)]])))
    results = columns
    for k in order:
        results = combine(gates, results, first[k], second[k], home[k], BF16 if k == order[-1] else F32)
    return results


def solution(mesh):
    return jax.shard_map(
        local,
        mesh=mesh,
        in_specs=(
            P(("groups", "expert"), None),
            P(("groups", "expert"), None, None, "mp"),
            P(("groups", "expert")),
            P(None, "mp"),
            P("mp", None),
            P(),
            P(("groups", "expert"), None),
            P("expert", None, "mp"),
            P("expert", "mp", None),
        ),
        out_specs=P(("groups", "expert"), "mp"),
        check_vma=False,
    )
```

```python
import functools
import math

import jax
import jax.numpy as jnp
from jax import lax
from jax.experimental import pallas as pl
from jax.experimental.pallas import tpu as pltpu
from jax.sharding import PartitionSpec as P

HEAD_DIM = 128
SHARPNESS = HEAD_DIM**-0.5 * math.log2(math.e)
DIRECT = 8
CUTS = 1
TILE = 256
F32, BF16 = jnp.float32, jnp.bfloat16
PARAMS = pltpu.CompilerParams(vmem_limit_bytes=20 * 2**20)
CHEAP = pl.CostEstimate(flops=0, bytes_accessed=0, transcendentals=0)
WHOLE = pl.BlockSpec(memory_space=pltpu.VMEM)


def dot(a, b, dims=((1,), (0,))):
    return lax.dot_general(a, b, (dims, ((), ())), preferred_element_type=F32)


def in_hbm(value):
    return pltpu.with_memory_space_constraint(value, pltpu.HBM)


def position():
    return lax.axis_index("expert"), lax.axis_index("mp")


def query_kernel(tokens, weight, source, out, staged, tokens_here, weight_here, sems):
    features = tokens.shape[1]
    depth = features // CUTS
    copies, later = [], []
    for i in range(CUTS):
        part = pl.ds(i * depth, depth)
        copies.append(
            (
                pltpu.make_async_copy(tokens.at[:, part], tokens_here.at[:, part], sems.at[0, i]),
                pltpu.make_async_copy(weight.at[part, :], weight_here.at[part, :], sems.at[1, i]),
            )
        )
        rows = pl.ds(i * (source.shape[1] // CUTS), source.shape[1] // CUTS)
        later.append(pltpu.make_async_copy(source.at[:, rows], staged.at[:, rows], sems.at[2, i]))
    for pair in copies:
        for copy in pair:
            copy.start()
    for copy in later:
        copy.start()
    total = jnp.zeros(out.shape, F32)
    for i, pair in enumerate(copies):
        for copy in pair:
            copy.wait()
        part = slice(i * depth, (i + 1) * depth)
        total += dot(tokens_here[:, part], weight_here[part, :])
    out[...] = total.astype(BF16)
    for copy in later:
        copy.wait()


def ask(tokens, weight, source):
    return pl.pallas_call(
        query_kernel,
        in_specs=[pl.BlockSpec(memory_space=pltpu.HBM)] * 3,
        out_specs=[WHOLE] * 2,
        out_shape=[
            jax.ShapeDtypeStruct((tokens.shape[0], weight.shape[1]), BF16),
            jax.ShapeDtypeStruct(source.shape, BF16),
        ],
        scratch_shapes=[
            pltpu.VMEM(tokens.shape, BF16),
            pltpu.VMEM(weight.shape, BF16),
            pltpu.SemaphoreType.DMA((3, CUTS)),
        ],
        compiler_params=PARAMS,
        cost_estimate=CHEAP,
        name="query",
    )(in_hbm(tokens), in_hbm(weight), in_hbm(source))


def attend_kernel(queries, source, out):
    for head in range(queries.shape[1] // HEAD_DIM):
        part = slice(head * HEAD_DIM, (head + 1) * HEAD_DIM)
        scores = dot(queries[:, part], source[0, :, part], ((1,), (1,)))
        top = jnp.max(scores, axis=1, keepdims=True)
        weights = jnp.exp2((scores - top) * SHARPNESS).astype(BF16)
        values = jnp.concatenate([source[1, :, part], jnp.ones((source.shape[1], HEAD_DIM), BF16)], axis=1)
        summed = dot(weights, values)
        out[:, part] = (summed[:, :HEAD_DIM] / summed[:, HEAD_DIM:]).astype(BF16)


def attend(queries, source, block):
    rows, width = queries.shape
    if rows == block:
        return pl.pallas_call(
            attend_kernel,
            in_specs=[WHOLE] * 2,
            out_specs=WHOLE,
            out_shape=jax.ShapeDtypeStruct((rows, width), BF16),
            compiler_params=PARAMS,
        cost_estimate=CHEAP,
            name="attend",
        )(queries, source)
    return pl.pallas_call(
        attend_kernel,
        grid=(rows // block,),
        in_specs=[
            pl.BlockSpec((block, width), lambda i: (i, 0)),
            pl.BlockSpec(source.shape, lambda i: (0, 0, 0)),
        ],
        out_specs=pl.BlockSpec((block, width), lambda i: (i, 0)),
        out_shape=jax.ShapeDtypeStruct((rows, width), BF16),
        compiler_params=PARAMS,
        cost_estimate=CHEAP,
        name="attend",
    )(queries, source)


def pick_kernel(owner, *refs):
    backs, out = refs[:-1], refs[-1]
    here, _ = position()
    names = jnp.broadcast_to(owner[0:1, 0:1], out.shape)
    total = backs[0][...].astype(F32)
    for k in range(1, len(backs)):
        total = jnp.where(names == here ^ k, backs[k][...].astype(F32), total)
    out[...] = total.astype(BF16)


def pick(owner, backs):
    return pl.pallas_call(
        pick_kernel,
        in_specs=[WHOLE] * (1 + len(backs)),
        out_specs=WHOLE,
        out_shape=jax.ShapeDtypeStruct(backs[0].shape, BF16),
        compiler_params=PARAMS,
        cost_estimate=CHEAP,
        name="pick",
    )(owner, *backs)


def route_kernel(experts, parts, choice_t, choice, *outs):
    dispatch, first, second = outs[:parts], outs[parts : 2 * parts], outs[2 * parts :]
    tokens = choice_t.shape[1]
    slots = dispatch[0].shape[0]
    capacity = slots * parts // experts
    wide = lax.broadcasted_iota(jnp.int32, (tokens, experts), 1)
    tall = lax.broadcasted_iota(jnp.int32, (experts, tokens), 0)
    i = lax.broadcasted_iota(jnp.int32, (tokens, tokens), 0)
    j = lax.broadcasted_iota(jnp.int32, (tokens, tokens), 1)
    r0, r1 = choice_t[0:1, :], choice_t[1:2, :]
    turned = dot((i == j).astype(BF16), choice_t[...].astype(F32).astype(BF16), ((1,), (1,))).astype(jnp.int32)
    choice[...] = turned
    c0, c1 = turned[:, 0:1], turned[:, 1:2]
    named = ((wide == c0) | (wide == c1)).astype(BF16)
    named_t = ((tall == r0) | (tall == r1)).astype(BF16)
    rank = dot((j < i).astype(BF16), named).astype(jnp.int32)
    rank_t = dot(named_t, (i < j).astype(BF16)).astype(jnp.int32)
    place0 = c0 * capacity + jnp.sum(jnp.where(wide == c0, rank, 0), axis=1, keepdims=True)
    place1 = c1 * capacity + jnp.sum(jnp.where(wide == c1, rank, 0), axis=1, keepdims=True)
    across0 = r0 * capacity + jnp.sum(jnp.where(tall == r0, rank_t, 0), axis=0, keepdims=True)
    across1 = r1 * capacity + jnp.sum(jnp.where(tall == r1, rank_t, 0), axis=0, keepdims=True)
    lane = lax.broadcasted_iota(jnp.int32, (tokens, slots), 1)
    row = lax.broadcasted_iota(jnp.int32, (slots, tokens), 0)
    for k in range(parts):
        base = (position()[0] ^ k) * capacity if parts > 1 else 0
        dispatch[k][...] = ((row + base == across0) | (row + base == across1)).astype(BF16)
        first[k][...] = (lane + base == place0).astype(BF16)
        second[k][...] = (lane + base == place1).astype(BF16)


def route(choice, experts, parts, capacity):
    tokens = choice.shape[0]
    slots = experts * capacity // parts
    outs = pl.pallas_call(
        functools.partial(route_kernel, experts, parts),
        in_specs=[WHOLE],
        out_specs=[WHOLE] * (1 + 3 * parts),
        out_shape=[jax.ShapeDtypeStruct(choice.shape, jnp.int32)]
        + [jax.ShapeDtypeStruct((slots, tokens), BF16)] * parts
        + [jax.ShapeDtypeStruct((tokens, slots), BF16)] * (2 * parts),
        compiler_params=PARAMS,
        cost_estimate=CHEAP,
        name="route",
    )(choice.T)
    return outs[0], outs[1 : 1 + parts], outs[1 + parts : 1 + 2 * parts], outs[1 + 2 * parts :]


def state_kernel(count, sends, *refs):
    tokens = refs[0]
    contexts, weights = refs[1 : 1 + count], refs[1 + count : 1 + 2 * count]
    dispatch = refs[1 + 2 * count : 1 + 2 * count + sends]
    state, outs = refs[1 + 2 * count + sends], refs[2 + 2 * count + sends :]
    tile = min(TILE, state.shape[1])
    for at in range(0, state.shape[1], tile):
        part = slice(at, at + tile)
        total = tokens[:, part].astype(F32)
        for context, weight in zip(contexts, weights):
            total += dot(context[...], weight[:, part])
        state[:, part] = total.astype(BF16)
    for rows, out in zip(dispatch, outs):
        width = out.shape[1]
        at = (position()[1] & (state.shape[1] // width - 1)) * width
        out[...] = dot(rows[...], state[:, pl.ds(pl.multiple_of(at, width), width)]).astype(BF16)


def make_state(tokens, contexts, weights, dispatch, cuts):
    return pl.pallas_call(
        functools.partial(state_kernel, len(contexts), len(dispatch)),
        in_specs=[WHOLE] * (1 + 2 * len(contexts) + len(dispatch)),
        out_specs=[WHOLE] * (1 + len(dispatch)),
        out_shape=[jax.ShapeDtypeStruct(tokens.shape, BF16)]
        + [jax.ShapeDtypeStruct((rows.shape[0], tokens.shape[1] // cut), BF16) for rows, cut in zip(dispatch, cuts)],
        compiler_params=PARAMS,
        cost_estimate=CHEAP,
        name="state",
    )(tokens, *contexts, *weights, *dispatch)


def home_kernel(experts, state, dispatch, router, choice, own_a, own_b, gates, columns):
    half = own_a.shape[1]
    column = position()[1]
    core = column & 1
    own_a[...] = dot(dispatch[...], state[:, pl.ds(pl.multiple_of(core * half, half), half)]).astype(BF16)
    own_b[...] = dot(dispatch[...], state[:, pl.ds(pl.multiple_of((1 - core) * half, half), half)]).astype(BF16)
    logits = dot(state[...], router[...], ((1,), (1,)))
    wide = lax.broadcasted_iota(jnp.int32, logits.shape, 1)
    first = jnp.sum(jnp.where(wide == choice[:, 0:1], logits, 0.0), axis=1, keepdims=True)
    second = jnp.sum(jnp.where(wide == choice[:, 1:2], logits, 0.0), axis=1, keepdims=True)
    gates[:, 0:1] = jax.nn.sigmoid(first - second)
    gates[:, 1:2] = jax.nn.sigmoid(second - first)
    width = columns.shape[1]
    columns[...] = state[:, pl.ds(pl.multiple_of(column * width, width), width)].astype(F32)


def at_home(state, dispatch, router, choice, experts, width):
    tokens, features = state.shape
    slots = dispatch.shape[0]
    return pl.pallas_call(
        functools.partial(home_kernel, experts),
        in_specs=[WHOLE] * 4,
        out_specs=[WHOLE] * 4,
        out_shape=[
            jax.ShapeDtypeStruct((slots, features // 2), BF16),
            jax.ShapeDtypeStruct((slots, features // 2), BF16),
            jax.ShapeDtypeStruct((tokens, 2), F32),
            jax.ShapeDtypeStruct((tokens, width), F32),
        ],
        compiler_params=PARAMS,
        cost_estimate=CHEAP,
        name="home",
    )(state, dispatch, router, choice)


def expert_kernel(orders, *refs):
    blocks, at = [], 0
    for order in orders:
        blocks.append(refs[at : at + len(order)])
        at += len(order)
    column = position()[1]
    expand, shrink, keep, give, rows_here, hidden = refs[at:]
    count = blocks[0][0].shape[0]
    for block, (order, pieces) in enumerate(zip(orders, blocks)):
        for index, piece in zip(order, pieces):
            width = piece.shape[1]
            part = pl.ds(pl.multiple_of(((column & (len(order) - 1)) ^ index) * width, width), width)
            rows_here[block * count : (block + 1) * count, part] = piece[...]
    units = expand.shape[1]
    tile = min(TILE, units)
    for at in range(0, units, tile):
        total = dot(rows_here[...], expand[:, at : at + tile])
        hidden[:, at : at + tile] = jnp.maximum(total, 0.0).astype(BF16)
    width = keep.shape[2]
    for j in range(keep.shape[0]):
        at = pl.multiple_of((column ^ (2 * j) ^ 1) * width, width)
        give[j] = dot(hidden[...], shrink[:, pl.ds(at, width)]).astype(BF16)
    for j in range(keep.shape[0]):
        at = pl.multiple_of((column ^ (2 * j)) * width, width)
        keep[j] = dot(hidden[...], shrink[:, pl.ds(at, width)])


def run_expert(orders, blocks, expand, shrink, parts):
    pieces = [piece for block in blocks for piece in block]
    rows = pieces[0].shape[0] * len(blocks)
    features, units = expand.shape
    width = features // (2 * parts)
    return pl.pallas_call(
        functools.partial(expert_kernel, tuple(map(tuple, orders))),
        in_specs=[WHOLE] * (2 + len(pieces)),
        out_specs=[WHOLE] * 2,
        out_shape=[
            jax.ShapeDtypeStruct((parts, rows, width), F32),
            jax.ShapeDtypeStruct((parts, rows, width), BF16),
        ],
        scratch_shapes=[pltpu.VMEM((rows, features), BF16), pltpu.VMEM((rows, units), BF16)],
        compiler_params=PARAMS,
        cost_estimate=CHEAP,
        name="expert",
    )(*pieces, expand, shrink)


def combine_kernel(count, gates, base, first, second, *refs):
    parts, out = refs[:count], refs[count]
    total = parts[0][...].astype(F32)
    for part in parts[1:]:
        total += part[...].astype(F32)
    total = total.astype(BF16)
    result = base[...] + gates[:, 0:1] * dot(first[...], total) + gates[:, 1:2] * dot(second[...], total)
    out[...] = result.astype(out.dtype)


def combine(gates, base, first, second, parts, dtype):
    return pl.pallas_call(
        functools.partial(combine_kernel, len(parts)),
        in_specs=[WHOLE] * (4 + len(parts)),
        out_specs=WHOLE,
        out_shape=jax.ShapeDtypeStruct(base.shape, dtype),
        compiler_params=PARAMS,
        cost_estimate=CHEAP,
        name="combine",
    )(gates, base, first, second, *parts)


def bits_of(count):
    bits = []
    while 2 ** len(bits) < count:
        bits.insert(0, 2 ** len(bits))
    return bits


def local(
    tokens,
    encoder_states,
    source_owner,
    query_weight,
    output_weight,
    router_weight,
    expert_choice,
    expand_weight,
    shrink_weight,
):
    token_count, features = tokens.shape
    groups = lax.axis_size("expert")
    slices = lax.axis_size("mp")
    here, column = lax.axis_index("expert"), lax.axis_index("mp")
    width = features // slices
    experts = expand_weight.shape[0] * groups
    capacity = max(2, 3 * token_count // experts)
    direct = groups <= DIRECT
    pairs = slices // 2
    slots = capacity if direct else experts * capacity

    def hop(value, along_expert, along_mp):
        if along_expert == 0 and along_mp == 0:
            return value
        moves = [
            (e * slices + m, (e ^ along_expert) * slices + (m ^ along_mp))
            for e in range(groups)
            for m in range(slices)
        ]
        return lax.ppermute(value, ("expert", "mp"), moves)

    def spread(value):
        parts = value.reshape(groups, -1, value.shape[-1])
        return lax.all_to_all(parts, "expert", 0, 0, tiled=True).reshape(value.shape)

    def after(value, other):
        return lax.optimization_barrier((value, other))[0]

    steps = range(groups) if direct else [0]

    queries, source = ask(tokens, query_weight, encoder_states[0])
    expert_bits = bits_of(groups)
    bits = bits_of(slices)
    if direct:
        own = attend(queries, source, token_count)
        asked, steps_of = [queries], [0]
        for bit in expert_bits:
            asked = asked + [hop(value if k == 0 else after(value, own), bit, 0) for k, value in zip(steps_of, asked)]
            steps_of = steps_of + [k ^ bit for k in steps_of]
        asked = dict(zip(steps_of, asked))
        previous, backs = own, {}
        for k in sorted(range(1, groups), key=lambda k: (k & (k - 1) != 0, -k)):
            answer = previous = attend(after(asked[k], previous), source, token_count)
            backs[k] = hop(answer, k, 0)
        context = pick(source_owner.reshape(1, 1), [own] + [backs[k] for k in range(1, groups)])
    else:
        asked = lax.all_gather(queries, "expert", axis=0, tiled=True)
        previous = attend(asked, source, token_count)
        context = lax.dynamic_slice_in_dim(spread(previous), source_owner[0] * token_count, token_count, 0)

    choice, dispatch, first, second = route(after(expert_choice, previous), experts, len(steps), capacity)
    weights, order = [output_weight], [0]
    for bit in bits:
        if bit == 1:
            weights = [after(weight, context) for weight in weights]
        weights = weights + [hop(weight, 0, bit) for weight in weights]
        order = order + [index ^ bit for index in order]
    contexts = [context]
    for bit in bits:
        contexts = contexts + [hop(value if i == 0 else after(value, dispatch[0]), 0, bit) for i, value in enumerate(contexts)]

    far = set(range(2, groups)) if direct and pairs > 1 else set()
    sends = [k for k in range(2, groups)] + ([1] if groups > 1 else []) if direct else [0]
    relayed = {groups - 1} & far
    cuts = [slices if k in relayed else 2 for k in sends]
    state, *leaving = make_state(tokens, contexts, weights, [dispatch[k] for k in sends], cuts)
    own_a, own_b, gates, columns = at_home(
        state, dispatch[0], router_weight.T, choice, experts, width
    )
    expert = functools.partial(run_expert, expand=expand_weight[0], shrink=shrink_weight[0], parts=pairs)

    def sum_cores(keep, give):
        return keep + hop(give, 0, 1).astype(F32)

    def send_home(k, summed, wait=None):
        parts = [summed[j].astype(BF16) for j in range(pairs)]
        if wait is not None:
            parts = parts[:1] + [after(part, wait) for part in parts[1:]]
        return [hop(part, k, 2 * j) if direct else hop(spread(part), 0, 2 * j) for j, part in enumerate(parts)]

    home, order = {}, [0]
    if direct:
        arrived = {k: hop(rows, k, 0) for k, rows in zip(sends, leaving)}
        keep, give = expert([[0, 1]], [[own_a, own_b]])
        if sends:
            give = after(give, arrived[groups - 1])
        own_sum, wait = sum_cores(keep, give), None
        earlier = [own_sum]
        crossing, started, relays = {}, None, {}
        for k in sends:
            pieces, places = [arrived[k]], [0]
            for bit in bits[:-1] if k in relayed else []:
                pieces = pieces + [hop(piece, 0, bit) for piece in pieces]
                places = places + [index ^ bit for index in places]
            relays[k] = pieces, places
            if k in relayed:
                earlier.append(pieces[-1])
                wait = pieces[-1]
        home[0] = send_home(0, own_sum, wait)
        turns = [[k for k in sends if k < groups - 1], [groups - 1]] if groups > 2 else [sends]
        for turn in turns:
            blocks, orders = [], []
            for k in turn:
                pieces, places = relays[k]
                if started is not None:
                    pieces = [after(piece, started) for piece in pieces]
                pieces = pieces + [hop(piece, 0, 1) for piece in pieces]
                places = places + [index ^ 1 for index in places]
                blocks.append(pieces)
                orders.append(places)
            if turn:
                for value in earlier:
                    blocks[0][0] = after(blocks[0][0], value)
                keep, give = expert(orders, blocks)
                summed = sum_cores(keep, give)
                earlier, started = [summed], give
                for i, k in enumerate(turn):
                    rows = summed[:, i * slots : (i + 1) * slots]
                    if k in far:
                        crossed = [hop(rows[j].astype(BF16), 0, 2 * j) for j in range(1, pairs)]
                        crossing[k] = [rows[0]] + crossed
                    else:
                        near = k, rows
        for k, (total, *crossed) in crossing.items():
            for part in crossed:
                total += (part if k == groups - 1 else after(part, summed)).astype(F32)
            total = total.astype(BF16)
            home[k] = [hop(total, k, 0)]
        if sends:
            home[near[0]] = send_home(near[0], after(near[1], give))
        order = [0] + sorted(sends)
    else:
        mine = spread(leaving[0])
        home[0] = send_home(0, sum_cores(*expert([[0, 1]], [[mine, hop(mine, 0, 1)]])))
    results = columns
    for k in order:
        results = combine(gates, results, first[k], second[k], home[k], BF16 if k == order[-1] else F32)
    return results


def solution(mesh):
    return jax.shard_map(
        local,
        mesh=mesh,
        in_specs=(
            P(("groups", "expert"), None),
            P(("groups", "expert"), None, None, "mp"),
            P(("groups", "expert")),
            P(None, "mp"),
            P("mp", None),
            P(),
            P(("groups", "expert"), None),
            P("expert", None, "mp"),
            P("expert", "mp", None),
        ),
        out_specs=P(("groups", "expert"), "mp"),
        check_vma=False,
    )
```

```python
import functools
import math

import jax
import jax.numpy as jnp
from jax import lax
from jax.experimental import pallas as pl
from jax.experimental.pallas import tpu as pltpu
from jax.sharding import PartitionSpec as P

HEAD_DIM = 128
SHARPNESS = HEAD_DIM**-0.5 * math.log2(math.e)
DIRECT = 8
TILE = 256
F32, BF16 = jnp.float32, jnp.bfloat16
PARAMS = pltpu.CompilerParams(vmem_limit_bytes=20 * 2**20)
CHEAP = pl.CostEstimate(flops=0, bytes_accessed=0, transcendentals=0)
WHOLE = pl.BlockSpec(memory_space=pltpu.VMEM)


def dot(a, b, dims=((1,), (0,))):
    return lax.dot_general(a, b, (dims, ((), ())), preferred_element_type=F32)


def in_hbm(value):
    return pltpu.with_memory_space_constraint(value, pltpu.HBM)


def position():
    return lax.axis_index("expert"), lax.axis_index("mp")


def query_kernel(tokens, weight, out, tokens_here, weight_here, sems):
    copies = [
        pltpu.make_async_copy(tokens, tokens_here, sems.at[0]),
        pltpu.make_async_copy(weight, weight_here, sems.at[1]),
    ]
    for copy in copies:
        copy.start()
    for copy in copies:
        copy.wait()
    out[...] = dot(tokens_here[...], weight_here[...]).astype(BF16)


def ask(tokens, weight):
    return pl.pallas_call(
        query_kernel,
        in_specs=[pl.BlockSpec(memory_space=pltpu.HBM)] * 2,
        out_specs=WHOLE,
        out_shape=jax.ShapeDtypeStruct((tokens.shape[0], weight.shape[1]), BF16),
        scratch_shapes=[
            pltpu.VMEM(tokens.shape, BF16),
            pltpu.VMEM(weight.shape, BF16),
            pltpu.SemaphoreType.DMA((2,)),
        ],
        compiler_params=PARAMS,
        cost_estimate=CHEAP,
        name="query",
    )(in_hbm(tokens), in_hbm(weight))


def stage_kernel(source, out, sem):
    copy = pltpu.make_async_copy(source, out, sem)
    copy.start()
    copy.wait()


def stage(source):
    return pl.pallas_call(
        stage_kernel,
        in_specs=[pl.BlockSpec(memory_space=pltpu.HBM)],
        out_specs=WHOLE,
        out_shape=jax.ShapeDtypeStruct(source.shape, BF16),
        scratch_shapes=[pltpu.SemaphoreType.DMA],
        compiler_params=PARAMS,
        cost_estimate=CHEAP,
        name="stage",
    )(in_hbm(source))


def attend_kernel(queries, source, out):
    for head in range(queries.shape[1] // HEAD_DIM):
        part = slice(head * HEAD_DIM, (head + 1) * HEAD_DIM)
        scores = dot(queries[:, part], source[0, :, part], ((1,), (1,)))
        top = jnp.max(scores, axis=1, keepdims=True)
        weights = jnp.exp2((scores - top) * SHARPNESS).astype(BF16)
        values = jnp.concatenate([source[1, :, part], jnp.ones((source.shape[1], HEAD_DIM), BF16)], axis=1)
        summed = dot(weights, values)
        out[:, part] = (summed[:, :HEAD_DIM] / summed[:, HEAD_DIM:]).astype(BF16)


def attend(queries, source, block):
    rows, width = queries.shape
    if rows == block:
        return pl.pallas_call(
            attend_kernel,
            in_specs=[WHOLE] * 2,
            out_specs=WHOLE,
            out_shape=jax.ShapeDtypeStruct((rows, width), BF16),
            compiler_params=PARAMS,
        cost_estimate=CHEAP,
            name="attend",
        )(queries, source)
    return pl.pallas_call(
        attend_kernel,
        grid=(rows // block,),
        in_specs=[
            pl.BlockSpec((block, width), lambda i: (i, 0)),
            pl.BlockSpec(source.shape, lambda i: (0, 0, 0)),
        ],
        out_specs=pl.BlockSpec((block, width), lambda i: (i, 0)),
        out_shape=jax.ShapeDtypeStruct((rows, width), BF16),
        compiler_params=PARAMS,
        cost_estimate=CHEAP,
        name="attend",
    )(queries, source)


def pick_kernel(owner, *refs):
    backs, out = refs[:-1], refs[-1]
    here, _ = position()
    names = jnp.broadcast_to(owner[0:1, 0:1], out.shape)
    total = backs[0][...].astype(F32)
    for k in range(1, len(backs)):
        total = jnp.where(names == here ^ k, backs[k][...].astype(F32), total)
    out[...] = total.astype(BF16)


def pick(owner, backs):
    return pl.pallas_call(
        pick_kernel,
        in_specs=[WHOLE] * (1 + len(backs)),
        out_specs=WHOLE,
        out_shape=jax.ShapeDtypeStruct(backs[0].shape, BF16),
        compiler_params=PARAMS,
        cost_estimate=CHEAP,
        name="pick",
    )(owner, *backs)


def route_kernel(experts, parts, choice_t, choice, *outs):
    dispatch, first, second = outs[:parts], outs[parts : 2 * parts], outs[2 * parts :]
    tokens = choice_t.shape[1]
    slots = dispatch[0].shape[0]
    capacity = slots * parts // experts
    wide = lax.broadcasted_iota(jnp.int32, (tokens, experts), 1)
    tall = lax.broadcasted_iota(jnp.int32, (experts, tokens), 0)
    i = lax.broadcasted_iota(jnp.int32, (tokens, tokens), 0)
    j = lax.broadcasted_iota(jnp.int32, (tokens, tokens), 1)
    r0, r1 = choice_t[0:1, :], choice_t[1:2, :]
    turned = dot((i == j).astype(BF16), choice_t[...].astype(F32).astype(BF16), ((1,), (1,))).astype(jnp.int32)
    choice[...] = turned
    c0, c1 = turned[:, 0:1], turned[:, 1:2]
    named = ((wide == c0) | (wide == c1)).astype(BF16)
    named_t = ((tall == r0) | (tall == r1)).astype(BF16)
    rank = dot((j < i).astype(BF16), named).astype(jnp.int32)
    rank_t = dot(named_t, (i < j).astype(BF16)).astype(jnp.int32)
    place0 = c0 * capacity + jnp.sum(jnp.where(wide == c0, rank, 0), axis=1, keepdims=True)
    place1 = c1 * capacity + jnp.sum(jnp.where(wide == c1, rank, 0), axis=1, keepdims=True)
    across0 = r0 * capacity + jnp.sum(jnp.where(tall == r0, rank_t, 0), axis=0, keepdims=True)
    across1 = r1 * capacity + jnp.sum(jnp.where(tall == r1, rank_t, 0), axis=0, keepdims=True)
    lane = lax.broadcasted_iota(jnp.int32, (tokens, slots), 1)
    row = lax.broadcasted_iota(jnp.int32, (slots, tokens), 0)
    for k in range(parts):
        base = (position()[0] ^ k) * capacity if parts > 1 else 0
        dispatch[k][...] = ((row + base == across0) | (row + base == across1)).astype(BF16)
        first[k][...] = (lane + base == place0).astype(BF16)
        second[k][...] = (lane + base == place1).astype(BF16)


def route(choice, experts, parts, capacity):
    tokens = choice.shape[0]
    slots = experts * capacity // parts
    outs = pl.pallas_call(
        functools.partial(route_kernel, experts, parts),
        in_specs=[WHOLE],
        out_specs=[WHOLE] * (1 + 3 * parts),
        out_shape=[jax.ShapeDtypeStruct(choice.shape, jnp.int32)]
        + [jax.ShapeDtypeStruct((slots, tokens), BF16)] * parts
        + [jax.ShapeDtypeStruct((tokens, slots), BF16)] * (2 * parts),
        compiler_params=PARAMS,
        cost_estimate=CHEAP,
        name="route",
    )(choice.T)
    return outs[0], outs[1 : 1 + parts], outs[1 + parts : 1 + 2 * parts], outs[1 + 2 * parts :]


def state_kernel(count, sends, *refs):
    tokens = refs[0]
    contexts, weights = refs[1 : 1 + count], refs[1 + count : 1 + 2 * count]
    dispatch = refs[1 + 2 * count : 1 + 2 * count + sends]
    state, outs = refs[1 + 2 * count + sends], refs[2 + 2 * count + sends :]
    tile = min(TILE, state.shape[1])
    for at in range(0, state.shape[1], tile):
        part = slice(at, at + tile)
        total = tokens[:, part].astype(F32)
        for context, weight in zip(contexts, weights):
            total += dot(context[...], weight[:, part])
        state[:, part] = total.astype(BF16)
    for rows, out in zip(dispatch, outs):
        width = out.shape[1]
        at = (position()[1] & (state.shape[1] // width - 1)) * width
        out[...] = dot(rows[...], state[:, pl.ds(pl.multiple_of(at, width), width)]).astype(BF16)


def make_state(tokens, contexts, weights, dispatch, cuts):
    return pl.pallas_call(
        functools.partial(state_kernel, len(contexts), len(dispatch)),
        in_specs=[WHOLE] * (1 + 2 * len(contexts) + len(dispatch)),
        out_specs=[WHOLE] * (1 + len(dispatch)),
        out_shape=[jax.ShapeDtypeStruct(tokens.shape, BF16)]
        + [jax.ShapeDtypeStruct((rows.shape[0], tokens.shape[1] // cut), BF16) for rows, cut in zip(dispatch, cuts)],
        compiler_params=PARAMS,
        cost_estimate=CHEAP,
        name="state",
    )(tokens, *contexts, *weights, *dispatch)


def home_kernel(experts, state, dispatch, router, choice, own_a, own_b, gates, columns):
    half = own_a.shape[1]
    column = position()[1]
    core = column & 1
    own_a[...] = dot(dispatch[...], state[:, pl.ds(pl.multiple_of(core * half, half), half)]).astype(BF16)
    own_b[...] = dot(dispatch[...], state[:, pl.ds(pl.multiple_of((1 - core) * half, half), half)]).astype(BF16)
    logits = dot(state[...], router[...], ((1,), (1,)))
    wide = lax.broadcasted_iota(jnp.int32, logits.shape, 1)
    first = jnp.sum(jnp.where(wide == choice[:, 0:1], logits, 0.0), axis=1, keepdims=True)
    second = jnp.sum(jnp.where(wide == choice[:, 1:2], logits, 0.0), axis=1, keepdims=True)
    gates[:, 0:1] = jax.nn.sigmoid(first - second)
    gates[:, 1:2] = jax.nn.sigmoid(second - first)
    width = columns.shape[1]
    columns[...] = state[:, pl.ds(pl.multiple_of(column * width, width), width)].astype(F32)


def at_home(state, dispatch, router, choice, experts, width):
    tokens, features = state.shape
    slots = dispatch.shape[0]
    return pl.pallas_call(
        functools.partial(home_kernel, experts),
        in_specs=[WHOLE] * 4,
        out_specs=[WHOLE] * 4,
        out_shape=[
            jax.ShapeDtypeStruct((slots, features // 2), BF16),
            jax.ShapeDtypeStruct((slots, features // 2), BF16),
            jax.ShapeDtypeStruct((tokens, 2), F32),
            jax.ShapeDtypeStruct((tokens, width), F32),
        ],
        compiler_params=PARAMS,
        cost_estimate=CHEAP,
        name="home",
    )(state, dispatch, router, choice)


def expert_kernel(orders, *refs):
    blocks, at = [], 0
    for order in orders:
        blocks.append(refs[at : at + len(order)])
        at += len(order)
    column = position()[1]
    expand, shrink, keep, give, rows_here, hidden = refs[at:]
    count = blocks[0][0].shape[0]
    for block, (order, pieces) in enumerate(zip(orders, blocks)):
        for index, piece in zip(order, pieces):
            width = piece.shape[1]
            part = pl.ds(pl.multiple_of(((column & (len(order) - 1)) ^ index) * width, width), width)
            rows_here[block * count : (block + 1) * count, part] = piece[...]
    units = expand.shape[1]
    tile = min(TILE, units)
    for at in range(0, units, tile):
        total = dot(rows_here[...], expand[:, at : at + tile])
        hidden[:, at : at + tile] = jnp.maximum(total, 0.0).astype(BF16)
    width = keep.shape[2]
    for j in range(keep.shape[0]):
        at = pl.multiple_of((column ^ (2 * j) ^ 1) * width, width)
        give[j] = dot(hidden[...], shrink[:, pl.ds(at, width)]).astype(BF16)
    for j in range(keep.shape[0]):
        at = pl.multiple_of((column ^ (2 * j)) * width, width)
        keep[j] = dot(hidden[...], shrink[:, pl.ds(at, width)])


def run_expert(orders, blocks, expand, shrink, parts):
    pieces = [piece for block in blocks for piece in block]
    rows = pieces[0].shape[0] * len(blocks)
    features, units = expand.shape
    width = features // (2 * parts)
    return pl.pallas_call(
        functools.partial(expert_kernel, tuple(map(tuple, orders))),
        in_specs=[WHOLE] * (2 + len(pieces)),
        out_specs=[WHOLE] * 2,
        out_shape=[
            jax.ShapeDtypeStruct((parts, rows, width), F32),
            jax.ShapeDtypeStruct((parts, rows, width), BF16),
        ],
        scratch_shapes=[pltpu.VMEM((rows, features), BF16), pltpu.VMEM((rows, units), BF16)],
        compiler_params=PARAMS,
        cost_estimate=CHEAP,
        name="expert",
    )(*pieces, expand, shrink)


def combine_kernel(count, gates, base, first, second, *refs):
    parts, out = refs[:count], refs[count]
    total = parts[0][...].astype(F32)
    for part in parts[1:]:
        total += part[...].astype(F32)
    total = total.astype(BF16)
    result = base[...] + gates[:, 0:1] * dot(first[...], total) + gates[:, 1:2] * dot(second[...], total)
    out[...] = result.astype(out.dtype)


def combine(gates, base, first, second, parts, dtype):
    return pl.pallas_call(
        functools.partial(combine_kernel, len(parts)),
        in_specs=[WHOLE] * (4 + len(parts)),
        out_specs=WHOLE,
        out_shape=jax.ShapeDtypeStruct(base.shape, dtype),
        compiler_params=PARAMS,
        cost_estimate=CHEAP,
        name="combine",
    )(gates, base, first, second, *parts)


def bits_of(count):
    bits = []
    while 2 ** len(bits) < count:
        bits.insert(0, 2 ** len(bits))
    return bits


def local(
    tokens,
    encoder_states,
    source_owner,
    query_weight,
    output_weight,
    router_weight,
    expert_choice,
    expand_weight,
    shrink_weight,
):
    token_count, features = tokens.shape
    groups = lax.axis_size("expert")
    slices = lax.axis_size("mp")
    here, column = lax.axis_index("expert"), lax.axis_index("mp")
    width = features // slices
    experts = expand_weight.shape[0] * groups
    capacity = max(2, 3 * token_count // experts)
    direct = groups <= DIRECT
    pairs = slices // 2
    slots = capacity if direct else experts * capacity

    def hop(value, along_expert, along_mp):
        if along_expert == 0 and along_mp == 0:
            return value
        moves = [
            (e * slices + m, (e ^ along_expert) * slices + (m ^ along_mp))
            for e in range(groups)
            for m in range(slices)
        ]
        return lax.ppermute(value, ("expert", "mp"), moves)

    def spread(value):
        parts = value.reshape(groups, -1, value.shape[-1])
        return lax.all_to_all(parts, "expert", 0, 0, tiled=True).reshape(value.shape)

    def after(value, other):
        return lax.optimization_barrier((value, other))[0]

    steps = range(groups) if direct else [0]

    queries = ask(tokens, query_weight)
    source = stage(after(encoder_states[0], queries))
    expert_bits = bits_of(groups)
    bits = bits_of(slices)
    if direct:
        own = attend(queries, source, token_count)
        asked, steps_of = [queries], [0]
        for bit in expert_bits:
            asked = asked + [hop(value if k == 0 else after(value, own), bit, 0) for k, value in zip(steps_of, asked)]
            steps_of = steps_of + [k ^ bit for k in steps_of]
        asked = dict(zip(steps_of, asked))
        previous, backs = own, {}
        for k in sorted(range(1, groups), key=lambda k: (k & (k - 1) != 0, -k)):
            answer = previous = attend(after(asked[k], previous), source, token_count)
            backs[k] = hop(answer, k, 0)
        context = pick(source_owner.reshape(1, 1), [own] + [backs[k] for k in range(1, groups)])
    else:
        asked = lax.all_gather(queries, "expert", axis=0, tiled=True)
        previous = attend(asked, source, token_count)
        context = lax.dynamic_slice_in_dim(spread(previous), source_owner[0] * token_count, token_count, 0)

    choice, dispatch, first, second = route(after(expert_choice, previous), experts, len(steps), capacity)
    weights, order = [output_weight], [0]
    for bit in bits:
        if bit == 1:
            weights = [after(weight, context) for weight in weights]
        weights = weights + [hop(weight, 0, bit) for weight in weights]
        order = order + [index ^ bit for index in order]
    contexts = [context]
    for bit in bits:
        contexts = contexts + [hop(value if i == 0 else after(value, dispatch[0]), 0, bit) for i, value in enumerate(contexts)]

    far = set(range(2, groups)) if direct and pairs > 1 else set()
    sends = [k for k in range(2, groups)] + ([1] if groups > 1 else []) if direct else [0]
    relayed = {groups - 1} & far
    cuts = [slices if k in relayed else 2 for k in sends]
    state, *leaving = make_state(tokens, contexts, weights, [dispatch[k] for k in sends], cuts)
    own_a, own_b, gates, columns = at_home(
        state, dispatch[0], router_weight.T, choice, experts, width
    )
    expert = functools.partial(run_expert, expand=expand_weight[0], shrink=shrink_weight[0], parts=pairs)

    def sum_cores(keep, give):
        return keep + hop(give, 0, 1).astype(F32)

    def send_home(k, summed, wait=None):
        parts = [summed[j].astype(BF16) for j in range(pairs)]
        if wait is not None:
            parts = parts[:1] + [after(part, wait) for part in parts[1:]]
        return [hop(part, k, 2 * j) if direct else hop(spread(part), 0, 2 * j) for j, part in enumerate(parts)]

    home, order = {}, [0]
    if direct:
        arrived = {k: hop(rows, k, 0) for k, rows in zip(sends, leaving)}
        keep, give = expert([[0, 1]], [[own_a, own_b]])
        if sends:
            give = after(give, arrived[groups - 1])
        own_sum, wait = sum_cores(keep, give), None
        earlier = [own_sum]
        crossing, started, relays = {}, None, {}
        for k in sends:
            pieces, places = [arrived[k]], [0]
            for bit in bits[:-1] if k in relayed else []:
                pieces = pieces + [hop(piece, 0, bit) for piece in pieces]
                places = places + [index ^ bit for index in places]
            relays[k] = pieces, places
            if k in relayed:
                earlier.append(pieces[-1])
                wait = pieces[-1]
        home[0] = send_home(0, own_sum, wait)
        turns = [[k for k in sends if k < groups - 1], [groups - 1]] if groups > 2 else [sends]
        for turn in turns:
            blocks, orders = [], []
            for k in turn:
                pieces, places = relays[k]
                if started is not None:
                    pieces = [after(piece, started) for piece in pieces]
                pieces = pieces + [hop(piece, 0, 1) for piece in pieces]
                places = places + [index ^ 1 for index in places]
                blocks.append(pieces)
                orders.append(places)
            if turn:
                for value in earlier:
                    blocks[0][0] = after(blocks[0][0], value)
                keep, give = expert(orders, blocks)
                summed = sum_cores(keep, give)
                earlier, started = [summed], give
                for i, k in enumerate(turn):
                    rows = summed[:, i * slots : (i + 1) * slots]
                    if k in far:
                        crossed = [hop(rows[j].astype(BF16), 0, 2 * j) for j in range(1, pairs)]
                        crossing[k] = [rows[0]] + crossed
                    else:
                        near = k, rows
        for k, (total, *crossed) in crossing.items():
            for part in crossed:
                total += (part if k == groups - 1 else after(part, summed)).astype(F32)
            total = total.astype(BF16)
            home[k] = [hop(total, k, 0)]
        if sends:
            home[near[0]] = send_home(near[0], after(near[1], give))
        order = [0] + sorted(sends)
    else:
        mine = spread(leaving[0])
        home[0] = send_home(0, sum_cores(*expert([[0, 1]], [[mine, hop(mine, 0, 1)]])))
    results = columns
    for k in order:
        results = combine(gates, results, first[k], second[k], home[k], BF16 if k == order[-1] else F32)
    return results


def solution(mesh):
    return jax.shard_map(
        local,
        mesh=mesh,
        in_specs=(
            P(("groups", "expert"), None),
            P(("groups", "expert"), None, None, "mp"),
            P(("groups", "expert")),
            P(None, "mp"),
            P("mp", None),
            P(),
            P(("groups", "expert"), None),
            P("expert", None, "mp"),
            P("expert", "mp", None),
        ),
        out_specs=P(("groups", "expert"), "mp"),
        check_vma=False,
    )
```

```python
import functools
import math

import jax
import jax.numpy as jnp
from jax import lax
from jax.experimental import pallas as pl
from jax.experimental.pallas import tpu as pltpu
from jax.sharding import PartitionSpec as P

HEAD_DIM = 128
SHARPNESS = HEAD_DIM**-0.5 * math.log2(math.e)
DIRECT = 8
CUTS = 1
TILE = 512
F32, BF16 = jnp.float32, jnp.bfloat16
PARAMS = pltpu.CompilerParams(vmem_limit_bytes=20 * 2**20)
CHEAP = pl.CostEstimate(flops=0, bytes_accessed=0, transcendentals=0)
WHOLE = pl.BlockSpec(memory_space=pltpu.VMEM)


def dot(a, b, dims=((1,), (0,))):
    return lax.dot_general(a, b, (dims, ((), ())), preferred_element_type=F32)


def in_hbm(value):
    return pltpu.with_memory_space_constraint(value, pltpu.HBM)


def position():
    return lax.axis_index("expert"), lax.axis_index("mp")


def query_kernel(tokens, weight, source, out, staged, tokens_here, weight_here, sems):
    features = tokens.shape[1]
    depth = features // CUTS
    copies, later = [], []
    for i in range(CUTS):
        part = pl.ds(i * depth, depth)
        copies.append(
            (
                pltpu.make_async_copy(tokens.at[:, part], tokens_here.at[:, part], sems.at[0, i]),
                pltpu.make_async_copy(weight.at[part, :], weight_here.at[part, :], sems.at[1, i]),
            )
        )
        rows = pl.ds(i * (source.shape[1] // CUTS), source.shape[1] // CUTS)
        later.append(pltpu.make_async_copy(source.at[:, rows], staged.at[:, rows], sems.at[2, i]))
    for pair in copies:
        for copy in pair:
            copy.start()
    for copy in later:
        copy.start()
    total = jnp.zeros(out.shape, F32)
    for i, pair in enumerate(copies):
        for copy in pair:
            copy.wait()
        part = slice(i * depth, (i + 1) * depth)
        total += dot(tokens_here[:, part], weight_here[part, :])
    out[...] = total.astype(BF16)
    for copy in later:
        copy.wait()


def ask(tokens, weight, source):
    return pl.pallas_call(
        query_kernel,
        in_specs=[pl.BlockSpec(memory_space=pltpu.HBM)] * 3,
        out_specs=[WHOLE] * 2,
        out_shape=[
            jax.ShapeDtypeStruct((tokens.shape[0], weight.shape[1]), BF16),
            jax.ShapeDtypeStruct(source.shape, BF16),
        ],
        scratch_shapes=[
            pltpu.VMEM(tokens.shape, BF16),
            pltpu.VMEM(weight.shape, BF16),
            pltpu.SemaphoreType.DMA((3, CUTS)),
        ],
        compiler_params=PARAMS,
        cost_estimate=CHEAP,
        name="query",
    )(in_hbm(tokens), in_hbm(weight), in_hbm(source))


def attend_kernel(queries, source, out):
    for head in range(queries.shape[1] // HEAD_DIM):
        part = slice(head * HEAD_DIM, (head + 1) * HEAD_DIM)
        scores = dot(queries[:, part], source[0, :, part], ((1,), (1,)))
        top = jnp.max(scores, axis=1, keepdims=True)
        weights = jnp.exp2((scores - top) * SHARPNESS).astype(BF16)
        values = jnp.concatenate([source[1, :, part], jnp.ones((source.shape[1], HEAD_DIM), BF16)], axis=1)
        summed = dot(weights, values)
        out[:, part] = (summed[:, :HEAD_DIM] / summed[:, HEAD_DIM:]).astype(BF16)


def attend(queries, source, block):
    rows, width = queries.shape
    if rows == block:
        return pl.pallas_call(
            attend_kernel,
            in_specs=[WHOLE] * 2,
            out_specs=WHOLE,
            out_shape=jax.ShapeDtypeStruct((rows, width), BF16),
            compiler_params=PARAMS,
        cost_estimate=CHEAP,
            name="attend",
        )(queries, source)
    return pl.pallas_call(
        attend_kernel,
        grid=(rows // block,),
        in_specs=[
            pl.BlockSpec((block, width), lambda i: (i, 0)),
            pl.BlockSpec(source.shape, lambda i: (0, 0, 0)),
        ],
        out_specs=pl.BlockSpec((block, width), lambda i: (i, 0)),
        out_shape=jax.ShapeDtypeStruct((rows, width), BF16),
        compiler_params=PARAMS,
        cost_estimate=CHEAP,
        name="attend",
    )(queries, source)


def pick_kernel(owner, *refs):
    backs, out = refs[:-1], refs[-1]
    here, _ = position()
    names = jnp.broadcast_to(owner[0:1, 0:1], out.shape)
    total = backs[0][...].astype(F32)
    for k in range(1, len(backs)):
        total = jnp.where(names == here ^ k, backs[k][...].astype(F32), total)
    out[...] = total.astype(BF16)


def pick(owner, backs):
    return pl.pallas_call(
        pick_kernel,
        in_specs=[WHOLE] * (1 + len(backs)),
        out_specs=WHOLE,
        out_shape=jax.ShapeDtypeStruct(backs[0].shape, BF16),
        compiler_params=PARAMS,
        cost_estimate=CHEAP,
        name="pick",
    )(owner, *backs)


def route_kernel(experts, parts, choice_t, choice, *outs):
    dispatch, first, second = outs[:parts], outs[parts : 2 * parts], outs[2 * parts :]
    tokens = choice_t.shape[1]
    slots = dispatch[0].shape[0]
    capacity = slots * parts // experts
    wide = lax.broadcasted_iota(jnp.int32, (tokens, experts), 1)
    tall = lax.broadcasted_iota(jnp.int32, (experts, tokens), 0)
    i = lax.broadcasted_iota(jnp.int32, (tokens, tokens), 0)
    j = lax.broadcasted_iota(jnp.int32, (tokens, tokens), 1)
    r0, r1 = choice_t[0:1, :], choice_t[1:2, :]
    turned = dot((i == j).astype(BF16), choice_t[...].astype(F32).astype(BF16), ((1,), (1,))).astype(jnp.int32)
    choice[...] = turned
    c0, c1 = turned[:, 0:1], turned[:, 1:2]
    named = ((wide == c0) | (wide == c1)).astype(BF16)
    named_t = ((tall == r0) | (tall == r1)).astype(BF16)
    rank = dot((j < i).astype(BF16), named).astype(jnp.int32)
    rank_t = dot(named_t, (i < j).astype(BF16)).astype(jnp.int32)
    place0 = c0 * capacity + jnp.sum(jnp.where(wide == c0, rank, 0), axis=1, keepdims=True)
    place1 = c1 * capacity + jnp.sum(jnp.where(wide == c1, rank, 0), axis=1, keepdims=True)
    across0 = r0 * capacity + jnp.sum(jnp.where(tall == r0, rank_t, 0), axis=0, keepdims=True)
    across1 = r1 * capacity + jnp.sum(jnp.where(tall == r1, rank_t, 0), axis=0, keepdims=True)
    lane = lax.broadcasted_iota(jnp.int32, (tokens, slots), 1)
    row = lax.broadcasted_iota(jnp.int32, (slots, tokens), 0)
    for k in range(parts):
        base = (position()[0] ^ k) * capacity if parts > 1 else 0
        dispatch[k][...] = ((row + base == across0) | (row + base == across1)).astype(BF16)
        first[k][...] = (lane + base == place0).astype(BF16)
        second[k][...] = (lane + base == place1).astype(BF16)


def route(choice, experts, parts, capacity):
    tokens = choice.shape[0]
    slots = experts * capacity // parts
    outs = pl.pallas_call(
        functools.partial(route_kernel, experts, parts),
        in_specs=[WHOLE],
        out_specs=[WHOLE] * (1 + 3 * parts),
        out_shape=[jax.ShapeDtypeStruct(choice.shape, jnp.int32)]
        + [jax.ShapeDtypeStruct((slots, tokens), BF16)] * parts
        + [jax.ShapeDtypeStruct((tokens, slots), BF16)] * (2 * parts),
        compiler_params=PARAMS,
        cost_estimate=CHEAP,
        name="route",
    )(choice.T)
    return outs[0], outs[1 : 1 + parts], outs[1 + parts : 1 + 2 * parts], outs[1 + 2 * parts :]


def state_kernel(count, sends, *refs):
    tokens = refs[0]
    contexts, weights = refs[1 : 1 + count], refs[1 + count : 1 + 2 * count]
    dispatch = refs[1 + 2 * count : 1 + 2 * count + sends]
    state, outs = refs[1 + 2 * count + sends], refs[2 + 2 * count + sends :]
    tile = min(TILE, state.shape[1])
    for at in range(0, state.shape[1], tile):
        part = slice(at, at + tile)
        total = tokens[:, part].astype(F32)
        for context, weight in zip(contexts, weights):
            total += dot(context[...], weight[:, part])
        state[:, part] = total.astype(BF16)
    for rows, out in zip(dispatch, outs):
        width = out.shape[1]
        at = (position()[1] & (state.shape[1] // width - 1)) * width
        out[...] = dot(rows[...], state[:, pl.ds(pl.multiple_of(at, width), width)]).astype(BF16)


def make_state(tokens, contexts, weights, dispatch, cuts):
    return pl.pallas_call(
        functools.partial(state_kernel, len(contexts), len(dispatch)),
        in_specs=[WHOLE] * (1 + 2 * len(contexts) + len(dispatch)),
        out_specs=[WHOLE] * (1 + len(dispatch)),
        out_shape=[jax.ShapeDtypeStruct(tokens.shape, BF16)]
        + [jax.ShapeDtypeStruct((rows.shape[0], tokens.shape[1] // cut), BF16) for rows, cut in zip(dispatch, cuts)],
        compiler_params=PARAMS,
        cost_estimate=CHEAP,
        name="state",
    )(tokens, *contexts, *weights, *dispatch)


def home_kernel(experts, state, dispatch, router, choice, own_a, own_b, gates, columns):
    half = own_a.shape[1]
    column = position()[1]
    core = column & 1
    own_a[...] = dot(dispatch[...], state[:, pl.ds(pl.multiple_of(core * half, half), half)]).astype(BF16)
    own_b[...] = dot(dispatch[...], state[:, pl.ds(pl.multiple_of((1 - core) * half, half), half)]).astype(BF16)
    logits = dot(state[...], router[...], ((1,), (1,)))
    wide = lax.broadcasted_iota(jnp.int32, logits.shape, 1)
    first = jnp.sum(jnp.where(wide == choice[:, 0:1], logits, 0.0), axis=1, keepdims=True)
    second = jnp.sum(jnp.where(wide == choice[:, 1:2], logits, 0.0), axis=1, keepdims=True)
    gates[:, 0:1] = jax.nn.sigmoid(first - second)
    gates[:, 1:2] = jax.nn.sigmoid(second - first)
    width = columns.shape[1]
    columns[...] = state[:, pl.ds(pl.multiple_of(column * width, width), width)].astype(F32)


def at_home(state, dispatch, router, choice, experts, width):
    tokens, features = state.shape
    slots = dispatch.shape[0]
    return pl.pallas_call(
        functools.partial(home_kernel, experts),
        in_specs=[WHOLE] * 4,
        out_specs=[WHOLE] * 4,
        out_shape=[
            jax.ShapeDtypeStruct((slots, features // 2), BF16),
            jax.ShapeDtypeStruct((slots, features // 2), BF16),
            jax.ShapeDtypeStruct((tokens, 2), F32),
            jax.ShapeDtypeStruct((tokens, width), F32),
        ],
        compiler_params=PARAMS,
        cost_estimate=CHEAP,
        name="home",
    )(state, dispatch, router, choice)


def expert_kernel(orders, *refs):
    blocks, at = [], 0
    for order in orders:
        blocks.append(refs[at : at + len(order)])
        at += len(order)
    column = position()[1]
    expand, shrink, keep, give, rows_here, hidden = refs[at:]
    count = blocks[0][0].shape[0]
    for block, (order, pieces) in enumerate(zip(orders, blocks)):
        for index, piece in zip(order, pieces):
            width = piece.shape[1]
            part = pl.ds(pl.multiple_of(((column & (len(order) - 1)) ^ index) * width, width), width)
            rows_here[block * count : (block + 1) * count, part] = piece[...]
    units = expand.shape[1]
    tile = min(TILE, units)
    for at in range(0, units, tile):
        total = dot(rows_here[...], expand[:, at : at + tile])
        hidden[:, at : at + tile] = jnp.maximum(total, 0.0).astype(BF16)
    width = keep.shape[2]
    for j in range(keep.shape[0]):
        at = pl.multiple_of((column ^ (2 * j) ^ 1) * width, width)
        give[j] = dot(hidden[...], shrink[:, pl.ds(at, width)]).astype(BF16)
    for j in range(keep.shape[0]):
        at = pl.multiple_of((column ^ (2 * j)) * width, width)
        keep[j] = dot(hidden[...], shrink[:, pl.ds(at, width)])


def run_expert(orders, blocks, expand, shrink, parts):
    pieces = [piece for block in blocks for piece in block]
    rows = pieces[0].shape[0] * len(blocks)
    features, units = expand.shape
    width = features // (2 * parts)
    return pl.pallas_call(
        functools.partial(expert_kernel, tuple(map(tuple, orders))),
        in_specs=[WHOLE] * (2 + len(pieces)),
        out_specs=[WHOLE] * 2,
        out_shape=[
            jax.ShapeDtypeStruct((parts, rows, width), F32),
            jax.ShapeDtypeStruct((parts, rows, width), BF16),
        ],
        scratch_shapes=[pltpu.VMEM((rows, features), BF16), pltpu.VMEM((rows, units), BF16)],
        compiler_params=PARAMS,
        cost_estimate=CHEAP,
        name="expert",
    )(*pieces, expand, shrink)


def combine_kernel(count, gates, base, first, second, *refs):
    parts, out = refs[:count], refs[count]
    total = parts[0][...].astype(F32)
    for part in parts[1:]:
        total += part[...].astype(F32)
    total = total.astype(BF16)
    result = base[...] + gates[:, 0:1] * dot(first[...], total) + gates[:, 1:2] * dot(second[...], total)
    out[...] = result.astype(out.dtype)


def combine(gates, base, first, second, parts, dtype):
    return pl.pallas_call(
        functools.partial(combine_kernel, len(parts)),
        in_specs=[WHOLE] * (4 + len(parts)),
        out_specs=WHOLE,
        out_shape=jax.ShapeDtypeStruct(base.shape, dtype),
        compiler_params=PARAMS,
        cost_estimate=CHEAP,
        name="combine",
    )(gates, base, first, second, *parts)


def bits_of(count):
    bits = []
    while 2 ** len(bits) < count:
        bits.insert(0, 2 ** len(bits))
    return bits


def local(
    tokens,
    encoder_states,
    source_owner,
    query_weight,
    output_weight,
    router_weight,
    expert_choice,
    expand_weight,
    shrink_weight,
):
    token_count, features = tokens.shape
    groups = lax.axis_size("expert")
    slices = lax.axis_size("mp")
    here, column = lax.axis_index("expert"), lax.axis_index("mp")
    width = features // slices
    experts = expand_weight.shape[0] * groups
    capacity = max(2, 3 * token_count // experts)
    direct = groups <= DIRECT
    pairs = slices // 2
    slots = capacity if direct else experts * capacity

    def hop(value, along_expert, along_mp):
        if along_expert == 0 and along_mp == 0:
            return value
        moves = [
            (e * slices + m, (e ^ along_expert) * slices + (m ^ along_mp))
            for e in range(groups)
            for m in range(slices)
        ]
        return lax.ppermute(value, ("expert", "mp"), moves)

    def spread(value):
        parts = value.reshape(groups, -1, value.shape[-1])
        return lax.all_to_all(parts, "expert", 0, 0, tiled=True).reshape(value.shape)

    def after(value, other):
        return lax.optimization_barrier((value, other))[0]

    steps = range(groups) if direct else [0]

    queries, source = ask(tokens, query_weight, encoder_states[0])
    expert_bits = bits_of(groups)
    bits = bits_of(slices)
    if direct:
        own = attend(queries, source, token_count)
        asked, steps_of = [queries], [0]
        for bit in expert_bits:
            asked = asked + [hop(value if k == 0 else after(value, own), bit, 0) for k, value in zip(steps_of, asked)]
            steps_of = steps_of + [k ^ bit for k in steps_of]
        asked = dict(zip(steps_of, asked))
        previous, backs = own, {}
        for k in sorted(range(1, groups), key=lambda k: (k & (k - 1) != 0, -k)):
            answer = previous = attend(after(asked[k], previous), source, token_count)
            backs[k] = hop(answer, k, 0)
        context = pick(source_owner.reshape(1, 1), [own] + [backs[k] for k in range(1, groups)])
    else:
        asked = lax.all_gather(queries, "expert", axis=0, tiled=True)
        previous = attend(asked, source, token_count)
        context = lax.dynamic_slice_in_dim(spread(previous), source_owner[0] * token_count, token_count, 0)

    choice, dispatch, first, second = route(after(expert_choice, previous), experts, len(steps), capacity)
    weights, order = [output_weight], [0]
    for bit in bits:
        if bit == 1:
            weights = [after(weight, context) for weight in weights]
        weights = weights + [hop(weight, 0, bit) for weight in weights]
        order = order + [index ^ bit for index in order]
    contexts = [context]
    for bit in bits:
        contexts = contexts + [hop(value if i == 0 else after(value, dispatch[0]), 0, bit) for i, value in enumerate(contexts)]

    far = set(range(2, groups)) if direct and pairs > 1 else set()
    sends = [k for k in range(2, groups)] + ([1] if groups > 1 else []) if direct else [0]
    relayed = {groups - 1} & far
    cuts = [slices if k in relayed else 2 for k in sends]
    state, *leaving = make_state(tokens, contexts, weights, [dispatch[k] for k in sends], cuts)
    own_a, own_b, gates, columns = at_home(
        state, dispatch[0], router_weight.T, choice, experts, width
    )
    expert = functools.partial(run_expert, expand=expand_weight[0], shrink=shrink_weight[0], parts=pairs)

    def sum_cores(keep, give):
        return keep + hop(give, 0, 1).astype(F32)

    def send_home(k, summed, wait=None):
        parts = [summed[j].astype(BF16) for j in range(pairs)]
        if wait is not None:
            parts = parts[:1] + [after(part, wait) for part in parts[1:]]
        return [hop(part, k, 2 * j) if direct else hop(spread(part), 0, 2 * j) for j, part in enumerate(parts)]

    home, order = {}, [0]
    if direct:
        arrived = {k: hop(rows, k, 0) for k, rows in zip(sends, leaving)}
        keep, give = expert([[0, 1]], [[own_a, own_b]])
        if sends:
            give = after(give, arrived[groups - 1])
        own_sum, wait = sum_cores(keep, give), None
        earlier = [own_sum]
        crossing, started, relays = {}, None, {}
        for k in sends:
            pieces, places = [arrived[k]], [0]
            for bit in bits[:-1] if k in relayed else []:
                pieces = pieces + [hop(piece, 0, bit) for piece in pieces]
                places = places + [index ^ bit for index in places]
            relays[k] = pieces, places
            if k in relayed:
                earlier.append(pieces[-1])
                wait = pieces[-1]
        home[0] = send_home(0, own_sum, wait)
        turns = [[k for k in sends if k < groups - 1], [groups - 1]] if groups > 2 else [sends]
        for turn in turns:
            blocks, orders = [], []
            for k in turn:
                pieces, places = relays[k]
                if started is not None:
                    pieces = [after(piece, started) for piece in pieces]
                pieces = pieces + [hop(piece, 0, 1) for piece in pieces]
                places = places + [index ^ 1 for index in places]
                blocks.append(pieces)
                orders.append(places)
            if turn:
                for value in earlier:
                    blocks[0][0] = after(blocks[0][0], value)
                keep, give = expert(orders, blocks)
                summed = sum_cores(keep, give)
                earlier, started = [summed], give
                for i, k in enumerate(turn):
                    rows = summed[:, i * slots : (i + 1) * slots]
                    if k in far:
                        crossed = [hop(rows[j].astype(BF16), 0, 2 * j) for j in range(1, pairs)]
                        crossing[k] = [rows[0]] + crossed
                    else:
                        near = k, rows
        for k, (total, *crossed) in crossing.items():
            for part in crossed:
                total += (part if k == groups - 1 else after(part, summed)).astype(F32)
            total = total.astype(BF16)
            home[k] = [hop(total, k, 0)]
        if sends:
            home[near[0]] = send_home(near[0], after(near[1], give))
        order = [0] + sorted(sends)
    else:
        mine = spread(leaving[0])
        home[0] = send_home(0, sum_cores(*expert([[0, 1]], [[mine, hop(mine, 0, 1)]])))
    results = columns
    for k in order:
        results = combine(gates, results, first[k], second[k], home[k], BF16 if k == order[-1] else F32)
    return results


def solution(mesh):
    return jax.shard_map(
        local,
        mesh=mesh,
        in_specs=(
            P(("groups", "expert"), None),
            P(("groups", "expert"), None, None, "mp"),
            P(("groups", "expert")),
            P(None, "mp"),
            P("mp", None),
            P(),
            P(("groups", "expert"), None),
            P("expert", None, "mp"),
            P("expert", "mp", None),
        ),
        out_specs=P(("groups", "expert"), "mp"),
        check_vma=False,
    )
```

```python
import functools
import math

import jax
import jax.numpy as jnp
from jax import lax
from jax.experimental import pallas as pl
from jax.experimental.pallas import tpu as pltpu
from jax.sharding import PartitionSpec as P

HEAD_DIM = 128
SHARPNESS = HEAD_DIM**-0.5 * math.log2(math.e)
DIRECT = 8
CUTS = 1
TILE = 256
F32, BF16 = jnp.float32, jnp.bfloat16
PARAMS = pltpu.CompilerParams(vmem_limit_bytes=20 * 2**20)
CHEAP = pl.CostEstimate(flops=0, bytes_accessed=0, transcendentals=0)
WHOLE = pl.BlockSpec(memory_space=pltpu.VMEM)


def dot(a, b, dims=((1,), (0,))):
    return lax.dot_general(a, b, (dims, ((), ())), preferred_element_type=F32)


def in_hbm(value):
    return pltpu.with_memory_space_constraint(value, pltpu.HBM)


def position():
    return lax.axis_index("expert"), lax.axis_index("mp")


def query_kernel(tokens, weight, source, out, staged, tokens_here, weight_here, sems):
    features = tokens.shape[1]
    depth = features // CUTS
    copies, later = [], []
    for i in range(CUTS):
        part = pl.ds(i * depth, depth)
        copies.append(
            (
                pltpu.make_async_copy(tokens.at[:, part], tokens_here.at[:, part], sems.at[0, i]),
                pltpu.make_async_copy(weight.at[part, :], weight_here.at[part, :], sems.at[1, i]),
            )
        )
        rows = pl.ds(i * (source.shape[1] // CUTS), source.shape[1] // CUTS)
        later.append(pltpu.make_async_copy(source.at[:, rows], staged.at[:, rows], sems.at[2, i]))
    for pair in copies:
        for copy in pair:
            copy.start()
    for copy in later:
        copy.start()
    total = jnp.zeros(out.shape, F32)
    for i, pair in enumerate(copies):
        for copy in pair:
            copy.wait()
        part = slice(i * depth, (i + 1) * depth)
        total += dot(tokens_here[:, part], weight_here[part, :])
    out[...] = total.astype(BF16)
    for copy in later:
        copy.wait()


def ask(tokens, weight, source):
    return pl.pallas_call(
        query_kernel,
        in_specs=[pl.BlockSpec(memory_space=pltpu.HBM)] * 3,
        out_specs=[WHOLE] * 2,
        out_shape=[
            jax.ShapeDtypeStruct((tokens.shape[0], weight.shape[1]), BF16),
            jax.ShapeDtypeStruct(source.shape, BF16),
        ],
        scratch_shapes=[
            pltpu.VMEM(tokens.shape, BF16),
            pltpu.VMEM(weight.shape, BF16),
            pltpu.SemaphoreType.DMA((3, CUTS)),
        ],
        compiler_params=PARAMS,
        cost_estimate=CHEAP,
        name="query",
    )(in_hbm(tokens), in_hbm(weight), in_hbm(source))


def attend_kernel(queries, source, out):
    for head in range(queries.shape[1] // HEAD_DIM):
        part = slice(head * HEAD_DIM, (head + 1) * HEAD_DIM)
        scores = dot(queries[:, part], source[0, :, part], ((1,), (1,)))
        top = jnp.max(scores, axis=1, keepdims=True)
        weights = jnp.exp2((scores - top) * SHARPNESS).astype(BF16)
        values = jnp.concatenate([source[1, :, part], jnp.ones((source.shape[1], HEAD_DIM), BF16)], axis=1)
        summed = dot(weights, values)
        out[:, part] = (summed[:, :HEAD_DIM] / summed[:, HEAD_DIM:]).astype(BF16)


def attend(queries, source, block):
    rows, width = queries.shape
    if rows == block:
        return pl.pallas_call(
            attend_kernel,
            in_specs=[WHOLE] * 2,
            out_specs=WHOLE,
            out_shape=jax.ShapeDtypeStruct((rows, width), BF16),
            compiler_params=PARAMS,
        cost_estimate=CHEAP,
            name="attend",
        )(queries, source)
    return pl.pallas_call(
        attend_kernel,
        grid=(rows // block,),
        in_specs=[
            pl.BlockSpec((block, width), lambda i: (i, 0)),
            pl.BlockSpec(source.shape, lambda i: (0, 0, 0)),
        ],
        out_specs=pl.BlockSpec((block, width), lambda i: (i, 0)),
        out_shape=jax.ShapeDtypeStruct((rows, width), BF16),
        compiler_params=PARAMS,
        cost_estimate=CHEAP,
        name="attend",
    )(queries, source)


def pick_kernel(owner, *refs):
    backs, out = refs[:-1], refs[-1]
    here, _ = position()
    names = jnp.broadcast_to(owner[0:1, 0:1], out.shape)
    total = backs[0][...].astype(F32)
    for k in range(1, len(backs)):
        total = jnp.where(names == here ^ k, backs[k][...].astype(F32), total)
    out[...] = total.astype(BF16)


def pick(owner, backs):
    return pl.pallas_call(
        pick_kernel,
        in_specs=[WHOLE] * (1 + len(backs)),
        out_specs=WHOLE,
        out_shape=jax.ShapeDtypeStruct(backs[0].shape, BF16),
        compiler_params=PARAMS,
        cost_estimate=CHEAP,
        name="pick",
    )(owner, *backs)


def route_kernel(experts, parts, choice_t, choice, *outs):
    dispatch, first, second = outs[:parts], outs[parts : 2 * parts], outs[2 * parts :]
    tokens = choice_t.shape[1]
    slots = dispatch[0].shape[0]
    capacity = slots * parts // experts
    wide = lax.broadcasted_iota(jnp.int32, (tokens, experts), 1)
    tall = lax.broadcasted_iota(jnp.int32, (experts, tokens), 0)
    i = lax.broadcasted_iota(jnp.int32, (tokens, tokens), 0)
    j = lax.broadcasted_iota(jnp.int32, (tokens, tokens), 1)
    r0, r1 = choice_t[0:1, :], choice_t[1:2, :]
    turned = dot((i == j).astype(BF16), choice_t[...].astype(F32).astype(BF16), ((1,), (1,))).astype(jnp.int32)
    choice[...] = turned
    c0, c1 = turned[:, 0:1], turned[:, 1:2]
    named = ((wide == c0) | (wide == c1)).astype(BF16)
    named_t = ((tall == r0) | (tall == r1)).astype(BF16)
    rank = dot((j < i).astype(BF16), named).astype(jnp.int32)
    rank_t = dot(named_t, (i < j).astype(BF16)).astype(jnp.int32)
    place0 = c0 * capacity + jnp.sum(jnp.where(wide == c0, rank, 0), axis=1, keepdims=True)
    place1 = c1 * capacity + jnp.sum(jnp.where(wide == c1, rank, 0), axis=1, keepdims=True)
    across0 = r0 * capacity + jnp.sum(jnp.where(tall == r0, rank_t, 0), axis=0, keepdims=True)
    across1 = r1 * capacity + jnp.sum(jnp.where(tall == r1, rank_t, 0), axis=0, keepdims=True)
    lane = lax.broadcasted_iota(jnp.int32, (tokens, slots), 1)
    row = lax.broadcasted_iota(jnp.int32, (slots, tokens), 0)
    for k in range(parts):
        base = (position()[0] ^ k) * capacity if parts > 1 else 0
        dispatch[k][...] = ((row + base == across0) | (row + base == across1)).astype(BF16)
        first[k][...] = (lane + base == place0).astype(BF16)
        second[k][...] = (lane + base == place1).astype(BF16)


def route(choice, experts, parts, capacity):
    tokens = choice.shape[0]
    slots = experts * capacity // parts
    outs = pl.pallas_call(
        functools.partial(route_kernel, experts, parts),
        in_specs=[WHOLE],
        out_specs=[WHOLE] * (1 + 3 * parts),
        out_shape=[jax.ShapeDtypeStruct(choice.shape, jnp.int32)]
        + [jax.ShapeDtypeStruct((slots, tokens), BF16)] * parts
        + [jax.ShapeDtypeStruct((tokens, slots), BF16)] * (2 * parts),
        compiler_params=PARAMS,
        cost_estimate=CHEAP,
        name="route",
    )(choice.T)
    return outs[0], outs[1 : 1 + parts], outs[1 + parts : 1 + 2 * parts], outs[1 + 2 * parts :]


def state_kernel(count, sends, *refs):
    tokens = refs[0]
    contexts, weights = refs[1 : 1 + count], refs[1 + count : 1 + 2 * count]
    dispatch = refs[1 + 2 * count : 1 + 2 * count + sends]
    state, outs = refs[1 + 2 * count + sends], refs[2 + 2 * count + sends :]
    tile = min(TILE, state.shape[1])
    for at in range(0, state.shape[1], tile):
        part = slice(at, at + tile)
        total = tokens[:, part].astype(F32)
        for context, weight in zip(contexts, weights):
            total += dot(context[...], weight[:, part])
        state[:, part] = total.astype(BF16)
    for rows, out in zip(dispatch, outs):
        width = out.shape[1]
        at = (position()[1] & (state.shape[1] // width - 1)) * width
        out[...] = dot(rows[...], state[:, pl.ds(pl.multiple_of(at, width), width)]).astype(BF16)


def make_state(tokens, contexts, weights, dispatch, cuts):
    return pl.pallas_call(
        functools.partial(state_kernel, len(contexts), len(dispatch)),
        in_specs=[WHOLE] * (1 + 2 * len(contexts) + len(dispatch)),
        out_specs=[WHOLE] * (1 + len(dispatch)),
        out_shape=[jax.ShapeDtypeStruct(tokens.shape, BF16)]
        + [jax.ShapeDtypeStruct((rows.shape[0], tokens.shape[1] // cut), BF16) for rows, cut in zip(dispatch, cuts)],
        compiler_params=PARAMS,
        cost_estimate=CHEAP,
        name="state",
    )(tokens, *contexts, *weights, *dispatch)


def home_kernel(experts, state, dispatch, router, choice, own_a, own_b, gates, columns):
    half = own_a.shape[1]
    column = position()[1]
    core = column & 1
    own_a[...] = dot(dispatch[...], state[:, pl.ds(pl.multiple_of(core * half, half), half)]).astype(BF16)
    own_b[...] = dot(dispatch[...], state[:, pl.ds(pl.multiple_of((1 - core) * half, half), half)]).astype(BF16)
    logits = dot(state[...], router[...], ((1,), (1,)))
    wide = lax.broadcasted_iota(jnp.int32, logits.shape, 1)
    first = jnp.sum(jnp.where(wide == choice[:, 0:1], logits, 0.0), axis=1, keepdims=True)
    second = jnp.sum(jnp.where(wide == choice[:, 1:2], logits, 0.0), axis=1, keepdims=True)
    gates[:, 0:1] = jax.nn.sigmoid(first - second)
    gates[:, 1:2] = jax.nn.sigmoid(second - first)
    width = columns.shape[1]
    columns[...] = state[:, pl.ds(pl.multiple_of(column * width, width), width)].astype(F32)


def at_home(state, dispatch, router, choice, experts, width):
    tokens, features = state.shape
    slots = dispatch.shape[0]
    return pl.pallas_call(
        functools.partial(home_kernel, experts),
        in_specs=[WHOLE] * 4,
        out_specs=[WHOLE] * 4,
        out_shape=[
            jax.ShapeDtypeStruct((slots, features // 2), BF16),
            jax.ShapeDtypeStruct((slots, features // 2), BF16),
            jax.ShapeDtypeStruct((tokens, 2), F32),
            jax.ShapeDtypeStruct((tokens, width), F32),
        ],
        compiler_params=PARAMS,
        cost_estimate=CHEAP,
        name="home",
    )(state, dispatch, router, choice)


def expert_kernel(orders, *refs):
    blocks, at = [], 0
    for order in orders:
        blocks.append(refs[at : at + len(order)])
        at += len(order)
    column = position()[1]
    expand, shrink, keep, give, rows_here, hidden = refs[at:]
    count = blocks[0][0].shape[0]
    for block, (order, pieces) in enumerate(zip(orders, blocks)):
        for index, piece in zip(order, pieces):
            width = piece.shape[1]
            part = pl.ds(pl.multiple_of(((column & (len(order) - 1)) ^ index) * width, width), width)
            rows_here[block * count : (block + 1) * count, part] = piece[...]
    units = expand.shape[1]
    tile = min(TILE, units)
    for at in range(0, units, tile):
        total = dot(rows_here[...], expand[:, at : at + tile])
        hidden[:, at : at + tile] = jnp.maximum(total, 0.0).astype(BF16)
    width = keep.shape[2]
    for j in range(keep.shape[0]):
        at = pl.multiple_of((column ^ (2 * j) ^ 1) * width, width)
        give[j] = dot(hidden[...], shrink[:, pl.ds(at, width)]).astype(BF16)
    for j in range(keep.shape[0]):
        at = pl.multiple_of((column ^ (2 * j)) * width, width)
        keep[j] = dot(hidden[...], shrink[:, pl.ds(at, width)])


def run_expert(orders, blocks, expand, shrink, parts):
    pieces = [piece for block in blocks for piece in block]
    rows = pieces[0].shape[0] * len(blocks)
    features, units = expand.shape
    width = features // (2 * parts)
    return pl.pallas_call(
        functools.partial(expert_kernel, tuple(map(tuple, orders))),
        in_specs=[WHOLE] * (2 + len(pieces)),
        out_specs=[WHOLE] * 2,
        out_shape=[
            jax.ShapeDtypeStruct((parts, rows, width), F32),
            jax.ShapeDtypeStruct((parts, rows, width), BF16),
        ],
        scratch_shapes=[pltpu.VMEM((rows, features), BF16), pltpu.VMEM((rows, units), BF16)],
        compiler_params=PARAMS,
        cost_estimate=CHEAP,
        name="expert",
    )(*pieces, expand, shrink)


def combine_kernel(count, gates, base, first, second, *refs):
    parts, out = refs[:count], refs[count]
    total = parts[0][...].astype(F32)
    for part in parts[1:]:
        total += part[...].astype(F32)
    total = total.astype(BF16)
    result = base[...] + gates[:, 0:1] * dot(first[...], total) + gates[:, 1:2] * dot(second[...], total)
    out[...] = result.astype(out.dtype)


def combine(gates, base, first, second, parts, dtype):
    return pl.pallas_call(
        functools.partial(combine_kernel, len(parts)),
        in_specs=[WHOLE] * (4 + len(parts)),
        out_specs=WHOLE,
        out_shape=jax.ShapeDtypeStruct(base.shape, dtype),
        compiler_params=PARAMS,
        cost_estimate=CHEAP,
        name="combine",
    )(gates, base, first, second, *parts)


def bits_of(count):
    bits = []
    while 2 ** len(bits) < count:
        bits.insert(0, 2 ** len(bits))
    return bits


def local(
    tokens,
    encoder_states,
    source_owner,
    query_weight,
    output_weight,
    router_weight,
    expert_choice,
    expand_weight,
    shrink_weight,
):
    token_count, features = tokens.shape
    groups = lax.axis_size("expert")
    slices = lax.axis_size("mp")
    here, column = lax.axis_index("expert"), lax.axis_index("mp")
    width = features // slices
    experts = expand_weight.shape[0] * groups
    capacity = max(2, 3 * token_count // experts)
    direct = groups <= DIRECT
    pairs = slices // 2
    slots = capacity if direct else experts * capacity

    def hop(value, along_expert, along_mp):
        if along_expert == 0 and along_mp == 0:
            return value
        moves = [
            (e * slices + m, (e ^ along_expert) * slices + (m ^ along_mp))
            for e in range(groups)
            for m in range(slices)
        ]
        return lax.ppermute(value, ("expert", "mp"), moves)

    def spread(value):
        parts = value.reshape(groups, -1, value.shape[-1])
        return lax.all_to_all(parts, "expert", 0, 0, tiled=True).reshape(value.shape)

    def after(value, other):
        return lax.optimization_barrier((value, other))[0]

    steps = range(groups) if direct else [0]

    queries, source = ask(tokens, query_weight, encoder_states[0])
    expert_bits = bits_of(groups)
    bits = bits_of(slices)
    if direct:
        own = attend(queries, source, token_count)
        asked, steps_of = [queries], [0]
        for bit in expert_bits:
            asked = asked + [hop(value if k == 0 else after(value, own), bit, 0) for k, value in zip(steps_of, asked)]
            steps_of = steps_of + [k ^ bit for k in steps_of]
        asked = dict(zip(steps_of, asked))
        previous, backs = own, {}
        for k in sorted(range(1, groups), key=lambda k: (k & (k - 1) != 0, -k)):
            answer = previous = attend(after(asked[k], previous), source, token_count)
            backs[k] = hop(answer, k, 0)
        context = pick(source_owner.reshape(1, 1), [own] + [backs[k] for k in range(1, groups)])
    else:
        asked = lax.all_gather(queries, "expert", axis=0, tiled=True)
        previous = attend(asked, source, token_count)
        context = lax.dynamic_slice_in_dim(spread(previous), source_owner[0] * token_count, token_count, 0)

    choice, dispatch, first, second = route(after(expert_choice, previous), experts, len(steps), capacity)
    weights, order = [output_weight], [0]
    for bit in bits:
        if bit == 1:
            weights = [after(weight, context) for weight in weights]
        weights = weights + [hop(weight, 0, bit) for weight in weights]
        order = order + [index ^ bit for index in order]
    contexts = [context]
    for bit in bits:
        contexts = contexts + [hop(value if i == 0 else after(value, dispatch[0]), 0, bit) for i, value in enumerate(contexts)]

    far = set(range(2, groups)) if direct and pairs > 1 else set()
    sends = [k for k in range(2, groups)] + ([1] if groups > 1 else []) if direct else [0]
    relayed = {groups - 1} & far
    cuts = [slices if k in relayed else 2 for k in sends]
    state, *leaving = make_state(tokens, contexts, weights, [dispatch[k] for k in sends], cuts)
    own_a, own_b, gates, columns = at_home(
        state, dispatch[0], router_weight.T, choice, experts, width
    )
    expert = functools.partial(run_expert, expand=expand_weight[0], shrink=shrink_weight[0], parts=pairs)

    def sum_cores(keep, give):
        return keep + hop(give, 0, 1).astype(F32)

    def send_home(k, summed, wait=None):
        parts = [summed[j].astype(BF16) for j in range(pairs)]
        if wait is not None:
            parts = parts[:1] + [after(part, wait) for part in parts[1:]]
        return [hop(part, k, 2 * j) if direct else hop(spread(part), 0, 2 * j) for j, part in enumerate(parts)]

    home, order = {}, [0]
    if direct:
        arrived = {k: hop(rows, k, 0) for k, rows in zip(sends, leaving)}
        keep, give = expert([[0, 1]], [[own_a, own_b]])
        if sends:
            give = after(give, arrived[groups - 1])
        own_sum, wait = sum_cores(keep, give), None
        earlier = [own_sum]
        crossing, started, relays = {}, None, {}
        for k in sends:
            pieces, places = [arrived[k]], [0]
            for bit in bits[:-1] if k in relayed else []:
                pieces = pieces + [hop(piece, 0, bit) for piece in pieces]
                places = places + [index ^ bit for index in places]
            relays[k] = pieces, places
            if k in relayed:
                earlier.append(pieces[-1])
                wait = pieces[-1]
        home[0] = send_home(0, own_sum)
        turns = [[k for k in sends if k < groups - 1], [groups - 1]] if groups > 2 else [sends]
        for turn in turns:
            blocks, orders = [], []
            for k in turn:
                pieces, places = relays[k]
                if started is not None:
                    pieces = [after(piece, started) for piece in pieces]
                pieces = pieces + [hop(piece, 0, 1) for piece in pieces]
                places = places + [index ^ 1 for index in places]
                blocks.append(pieces)
                orders.append(places)
            if turn:
                for value in earlier:
                    blocks[0][0] = after(blocks[0][0], value)
                keep, give = expert(orders, blocks)
                summed = sum_cores(keep, give)
                earlier, started = [summed], give
                for i, k in enumerate(turn):
                    rows = summed[:, i * slots : (i + 1) * slots]
                    if k in far:
                        crossed = [hop(rows[j].astype(BF16), 0, 2 * j) for j in range(1, pairs)]
                        crossing[k] = [rows[0]] + crossed
                    else:
                        near = k, rows
        for k, (total, *crossed) in crossing.items():
            for part in crossed:
                total += (part if k == groups - 1 else after(part, summed)).astype(F32)
            total = total.astype(BF16)
            home[k] = [hop(total, k, 0)]
        if sends:
            home[near[0]] = send_home(near[0], after(near[1], give))
        order = [0] + sorted(sends)
    else:
        mine = spread(leaving[0])
        home[0] = send_home(0, sum_cores(*expert([[0, 1]], [[mine, hop(mine, 0, 1)]])))
    results = columns
    for k in order:
        results = combine(gates, results, first[k], second[k], home[k], BF16 if k == order[-1] else F32)
    return results


def solution(mesh):
    return jax.shard_map(
        local,
        mesh=mesh,
        in_specs=(
            P(("groups", "expert"), None),
            P(("groups", "expert"), None, None, "mp"),
            P(("groups", "expert")),
            P(None, "mp"),
            P("mp", None),
            P(),
            P(("groups", "expert"), None),
            P("expert", None, "mp"),
            P("expert", "mp", None),
        ),
        out_specs=P(("groups", "expert"), "mp"),
        check_vma=False,
    )
```
